32 devices in a mesh: dp: 8 (over y, x, core), row: 4 (over z).
Axes of the slice: x: 2, y: 2, z: 4, core: 2. Of those that a mesh axis runs over, the one named last changes fastest.
Arguments:
- small_nodes: bfloat16 [96, 32, 512], P(('dp', 'row')), may hold values from -6 to 6
- small_edges: bfloat16 [96, 32, 2048], P(('dp', 'row')), may hold values from -6 to 6
- small_counts: int32 [96], P(('dp', 'row')), may hold values from 16 to 32
- big_nodes: bfloat16 [64, 64, 512], P('dp', 'row'), may hold values from -6 to 6
- big_edges: bfloat16 [64, 64, 4096], P('dp', 'row'), may hold values from -6 to 6
- big_counts: int32 [64], P('dp'), may hold values from 32 to 64
- small_node_cot: bfloat16 [96, 32, 512], P(('dp', 'row')), may hold values from -6 to 6
- small_edge_cot: bfloat16 [96, 32, 2048], P(('dp', 'row')), may hold values from -6 to 6
- big_node_cot: bfloat16 [64, 64, 512], P('dp', 'row'), may hold values from -6 to 6
- big_edge_cot: bfloat16 [64, 64, 4096], P('dp', 'row'), may hold values from -6 to 6
- master: float32 [66320, 128], P('dp'), may hold values from -3 to 3
- first_moment: float32 [66320, 128], P('dp')
- second_moment: float32 [66320, 128], P('dp'), as said below
- owner: int32 [8], replicated, may hold values from 0 to 7, as said below
- segment_rows: int32 [8], replicated, may hold values from 1 to 8290, as said below
- step_count: int32 [1], replicated, may hold values from 1 to 20
Outputs:
- small_nodes_out: bfloat16 [96, 32, 512], P(('dp', 'row'))
- small_edges_out: bfloat16 [96, 32, 2048], P(('dp', 'row'))
- big_nodes_out: bfloat16 [64, 64, 512], P('dp', 'row')
- big_edges_out: bfloat16 [64, 64, 4096], P('dp', 'row')
- small_nodes_grad: bfloat16 [96, 32, 512], P(('dp', 'row'))
- small_edges_grad: bfloat16 [96, 32, 2048], P(('dp', 'row'))
- big_nodes_grad: bfloat16 [64, 64, 512], P('dp', 'row')
- big_edges_grad: bfloat16 [64, 64, 4096], P('dp', 'row')
- new_master: float32 [66320, 128], P('dp')
- new_first: float32 [66320, 128], P('dp')
- new_second: float32 [66320, 128], P('dp')
- norm_grads: float32 [8, 576], replicated
The draws below stay inside these ranges and needn't reach their ends.
Inputs may be any that keep to these rules, and one draw needn't show every extreme that they name: owner[j] is the segment kept by index j of dp; every segment is named once. `segment_rows`: segments follow one another in order of s and together cover 33156 rows; one segment has exactly 8290 rows. `second_moment`: second moments are positive.
All inputs are finite; a program needn't handle non-finite values.
Results may differ from the reference program's by a relative error of at most 0.02.
Values may be sent and summed in bfloat16 or wider, within the bound.
No kernel may reach another device: no remote copies, remote signals or barrier semaphores. Data moves between devices by JAX's collectives and lax.ppermute only.
A program may use at most 256 MiB of HBM per device.

```python
import jax
import jax.numpy as jnp
from jax import lax

D = 512
H = 32
DE = 64
FF = 1024
FFE = 128
NS = 32
NB = 64
SMALL_GRAPHS = 96
BIG_GRAPHS = 64
PARAMS = 4243968
TOTAL_ROWS = 33156
OWN_ROWS = 8290
TOK_ALL = 7168
PAIR_ALL = 360448
N_DP = 8
N_ROW = 4


def piece_table():
    node_scale = TOK_ALL ** 0.5
    pair_scale = PAIR_ALL ** 0.5
    one_set = [(D * D, D ** (-0.5), 3.0 * node_scale, 0), (D * D, D ** (-0.5), 3.0 * node_scale, 0), (D * D, D ** (-0.5), node_scale, 0), (D * D, 4.0 * D ** (-0.5), 0.2 * node_scale, 0), (D * FF, D ** (-0.5), 0.45 * node_scale, 0), (FF * D, FF ** (-0.5), 0.65 * node_scale, 0), (DE * H, DE ** (-0.5), 1.5 * pair_scale, 0), (DE * H, DE ** (-0.5), 0.1 * pair_scale, 0), (H * DE, H ** (-0.5), 1.5 * pair_scale, 0), (DE * FFE, DE ** (-0.5), 0.4 * pair_scale, 0), (FFE * DE, FFE ** (-0.5), 0.65 * pair_scale, 0), (4 * D, 0.3, 2.0 * node_scale, 1), (4 * DE, 0.3, 1.5 * pair_scale, 1)]
    return one_set + one_set


def padding_size():
    return TOTAL_ROWS * 128 - PARAMS


def lookup_drawn(table, index):
    slot_ids = jnp.arange(table.shape[0], dtype=jnp.int32)
    return jnp.sum(jnp.where(index[:, None] == slot_ids[None, :], table[None, :], 0), axis=1).astype(jnp.int32)


def owner_of(key):
    return jax.random.permutation(jax.random.fold_in(key, 11), N_DP).astype(jnp.int32)


def segment_rows_of(key):
    pick_key = jax.random.fold_in(key, 51)
    share_key = jax.random.fold_in(key, 52)
    big_at = jax.random.randint(pick_key, (), 0, N_DP)
    slot_ids = jnp.arange(N_DP, dtype=jnp.int32)
    is_big = slot_ids == big_at
    shares = jnp.where(is_big, 0, jax.random.randint(share_key, (N_DP,), 2, 5)).astype(jnp.int32)
    rest_rows = TOTAL_ROWS - OWN_ROWS
    base_rows = (rest_rows * shares // jnp.sum(shares)).astype(jnp.int32)
    remain = rest_rows - jnp.sum(base_rows)
    order_among = jnp.cumsum(jnp.where(is_big, 0, 1)).astype(jnp.int32) - 1
    extra = jnp.where(jnp.logical_and(jnp.logical_not(is_big), order_among < remain), 1, 0)
    return jnp.where(is_big, OWN_ROWS, base_rows + extra).astype(jnp.int32)


def place_rows(flat_all, fill, key):
    owner = owner_of(key)
    segment_rows = segment_rows_of(key)
    ends = jnp.cumsum(segment_rows).astype(jnp.int32)
    starts = (ends - segment_rows).astype(jnp.int32)
    start_of = lookup_drawn(starts, owner)
    length_of = lookup_drawn(segment_rows, owner)
    inside = jnp.arange(OWN_ROWS, dtype=jnp.int32)
    targets = jnp.minimum(start_of[:, None] + inside[None, :], TOTAL_ROWS - 1).reshape(-1)
    live = (inside[None, :] < length_of[:, None]).reshape(-1)
    taken = jnp.take(flat_all.reshape(TOTAL_ROWS, 128), targets, axis=0)
    return jnp.where(live[:, None], taken, fill)


def draw_owner(key, part):
    return owner_of(key)


def draw_segment_rows(key, part):
    return segment_rows_of(key)


def draw_master(key, part):
    stream = jax.random.fold_in(key, 21)
    pieces = []
    for piece_index, (entries, spread, grad_size, piece_kind) in enumerate(piece_table()):
        sub_key = jax.random.fold_in(stream, piece_index)
        if piece_kind == 0:
            pieces.append(spread * jnp.clip(jax.random.normal(sub_key, (entries,), jnp.float32), -4.0, 4.0))
        else:
            offsets = jnp.repeat(jnp.array([1.0, 0.0, 1.0, 0.0], jnp.float32), entries // 4)
            pieces.append(offsets + spread * jax.random.uniform(sub_key, (entries,), jnp.float32, -1.0, 1.0))
    pieces.append(0.1 * jax.random.uniform(jax.random.fold_in(stream, 99), (padding_size(),), jnp.float32, -1.0, 1.0))
    fill = 0.1 * jax.random.uniform(jax.random.fold_in(stream, 98), (N_DP * OWN_ROWS, 128), jnp.float32, -1.0, 1.0)
    return place_rows(jnp.concatenate(pieces), fill, key)


def draw_first_moment(key, part):
    stream = jax.random.fold_in(key, 31)
    sizes_list = [(entries, grad_size) for entries, spread, grad_size, piece_kind in piece_table()]
    sizes_list.append((padding_size(), 0.001))
    pieces = []
    for piece_index, (entries, grad_size) in enumerate(sizes_list):
        sign_key = jax.random.fold_in(stream, 2 * piece_index)
        mag_key = jax.random.fold_in(stream, 2 * piece_index + 1)
        signs = jnp.where(jax.random.uniform(sign_key, (entries,), jnp.float32) < 0.5, -1.0, 1.0)
        magnitude = jax.random.uniform(mag_key, (entries,), jnp.float32, 0.5, 2.0)
        pieces.append(signs * magnitude * (0.1 / 0.9) * grad_size)
    fill = 0.001 * jax.random.uniform(jax.random.fold_in(stream, 998), (N_DP * OWN_ROWS, 128), jnp.float32, -1.0, 1.0)
    return place_rows(jnp.concatenate(pieces), fill, key)


def draw_second_moment(key, part):
    stream = jax.random.fold_in(key, 41)
    sizes_list = [(entries, grad_size) for entries, spread, grad_size, piece_kind in piece_table()]
    sizes_list.append((padding_size(), 0.001))
    pieces = []
    for piece_index, (entries, grad_size) in enumerate(sizes_list):
        sub_key = jax.random.fold_in(stream, piece_index)
        factor = jax.random.uniform(sub_key, (entries,), jnp.float32, 1.0, 4.0)
        pieces.append(factor * (0.05 / 0.95) * grad_size * grad_size)
    fill = 1e-07 * jax.random.uniform(jax.random.fold_in(stream, 998), (N_DP * OWN_ROWS, 128), jnp.float32, 1.0, 4.0)
    return place_rows(jnp.concatenate(pieces), fill, key)


def place_ends(drawn, own_key, smallest, top_value):
    longest = drawn.shape.index(max(drawn.shape))
    spots = []
    for shift in (0, 1):
        where = [jax.random.randint(jax.random.fold_in(own_key, axis), (), 0, length) for axis, length in enumerate(drawn.shape)]
        where[longest] = (where[longest] + shift) % drawn.shape[longest]
        spots.append(tuple(where))
    return drawn.at[spots[0]].set(smallest).at[spots[1]].set(top_value)


def shard_levels(stream_key, dims, cuts, smallest, largest):
    level, own = 1.0, jax.random.fold_in(stream_key, 6)
    for axis_at, parts in cuts:
        steps = jnp.exp(jax.random.uniform(jax.random.fold_in(own, axis_at), (parts,), jnp.float32, smallest / len(cuts), largest / len(cuts)))
        level = level * jnp.repeat(steps, dims[axis_at] // parts).reshape([-1 if axis == axis_at else 1 for axis in range(len(dims))])
    return level


def normal_values(stream_key, dims, width, bound, shards=(), kind=jnp.bfloat16):
    level = shard_levels(stream_key, dims, shards, -0.22, 0.18) if shards else 1.0
    values = jax.random.normal(stream_key, dims, jnp.float32) * width * level
    return jnp.minimum(jnp.maximum(values, -bound), bound).astype(kind)


def setup_inputs(seed: int = 0) -> dict:
    seeds = jax.random.split(jax.random.key(seed), 17)
    return {
        "small_nodes": normal_values(seeds[0], (SMALL_GRAPHS, NS, D), 1.0, 6.0, ((0, 32),)),
        "small_edges": normal_values(seeds[1], (SMALL_GRAPHS, NS, NS * DE), 1.0, 6.0, ((0, 32),)),
        "small_counts": place_ends(jax.random.randint(seeds[2], (SMALL_GRAPHS,), NS // 2, NS + 1), jax.random.fold_in(seeds[2], 1), NS // 2, NS).astype(jnp.int32),
        "big_nodes": normal_values(seeds[3], (BIG_GRAPHS, NB, D), 1.0, 6.0, ((0, 8), (1, 4))),
        "big_edges": normal_values(seeds[4], (BIG_GRAPHS, NB, NB * DE), 1.0, 6.0, ((0, 8), (1, 4))),
        "big_counts": place_ends(jax.random.randint(seeds[5], (BIG_GRAPHS,), NB // 2, NB + 1), jax.random.fold_in(seeds[5], 1), NB // 2, NB).astype(jnp.int32),
        "small_node_cot": normal_values(seeds[6], (SMALL_GRAPHS, NS, D), 1.0, 6.0, ((0, 32),)),
        "small_edge_cot": normal_values(seeds[7], (SMALL_GRAPHS, NS, NS * DE), 1.0, 6.0, ((0, 32),)),
        "big_node_cot": normal_values(seeds[8], (BIG_GRAPHS, NB, D), 1.0, 6.0, ((0, 8), (1, 4))),
        "big_edge_cot": normal_values(seeds[9], (BIG_GRAPHS, NB, NB * DE), 1.0, 6.0, ((0, 8), (1, 4))),
        "master": draw_master(jax.random.fold_in(seeds[16], 71), 0),
        "first_moment": draw_first_moment(jax.random.fold_in(seeds[16], 71), 0),
        "second_moment": draw_second_moment(jax.random.fold_in(seeds[16], 71), 0),
        "owner": draw_owner(jax.random.fold_in(seeds[16], 71), 0),
        "segment_rows": draw_segment_rows(jax.random.fold_in(seeds[16], 71), 0),
        "step_count": jax.random.randint(seeds[15], (1,), 1, 21).astype(jnp.int32),
    }


@jax.custom_vjp
def low(v):
    return lax.optimization_barrier(v.astype(jnp.bfloat16)).astype(jnp.float32)

@jax.custom_vjp
def low_back(v):
    return v

def low_keep(v):
    return (low(v), None)

def low_pass(kept, grad):
    return (grad,)

def back_keep(v):
    return (v, None)

def back_low(kept, grad):
    return (low(grad),)
low.defvjp(low_keep, low_pass)
low_back.defvjp(back_keep, back_low)
NORM_EPS = 1e-05
BETA_ONE = 0.9
BETA_TWO = 0.95
WEIGHT_DECAY = 0.1
ADAM_EPS = 1e-08
PAD_RATE = 0.05
MASK_FILL = -1e+30
SET_PIECES = 13

def layer_shapes():
    return [(D, D), (D, D), (D, D), (D, D), (D, FF), (FF, D), (DE, H), (DE, H), (H, DE), (DE, FFE), (FFE, DE), (4, D), (4, DE)]

def piece_shapes():
    return layer_shapes() + layer_shapes()

def piece_rates():
    one_set = [0.5 * D ** (-0.5), 0.5 * D ** (-0.5), 0.5 * D ** (-0.5), 2.0 * D ** (-0.5), 0.5 * D ** (-0.5), 0.5 * FF ** (-0.5), 0.5 * DE ** (-0.5), 0.5 * DE ** (-0.5), 0.5 * H ** (-0.5), 0.5 * DE ** (-0.5), 0.5 * FFE ** (-0.5), 0.25, 0.25]
    return one_set + one_set

def unpack(flat_all):
    result = []
    offset = 0
    for piece_shape in piece_shapes():
        entries = piece_shape[0] * piece_shape[1]
        result.append(flat_all[offset:offset + entries].reshape(piece_shape))
        offset += entries
    return result

def lookup(table, index):
    slot_ids = jnp.arange(table.shape[0], dtype=jnp.int32)
    return lax.optimization_barrier(jnp.sum(jnp.where(index[:, None] == slot_ids[None, :], table[None, :], 0), axis=1)).astype(jnp.int32)

def segment_bounds(segment_rows):
    ends = jnp.cumsum(segment_rows).astype(jnp.int32)
    return ((ends - segment_rows).astype(jnp.int32), ends)

def target_rows(owner, segment_rows, held_rows):
    starts, ends = segment_bounds(segment_rows)
    start_of = lookup(starts, owner)
    length_of = lookup(segment_rows, owner)
    inside = jnp.arange(held_rows, dtype=jnp.int32)
    targets = start_of[:, None] + inside[None, :]
    live = inside[None, :] < length_of[:, None]
    return (jnp.minimum(targets, TOTAL_ROWS - 1).reshape(-1), live.reshape(-1))

def source_rows(owner, segment_rows, held_rows):
    starts, ends = segment_bounds(segment_rows)
    flat_ids = jnp.arange(TOTAL_ROWS, dtype=jnp.int32)
    segment_of = lax.optimization_barrier(jnp.sum((ends[None, :] <= flat_ids[:, None]).astype(jnp.int32), axis=1)).astype(jnp.int32)
    slot_ids = jnp.arange(owner.shape[0], dtype=jnp.int32)
    holder = lax.optimization_barrier(jnp.sum(jnp.where(owner[None, :] == slot_ids[:, None], slot_ids[None, :], 0), axis=1)).astype(jnp.int32)
    return lookup(holder, segment_of) * held_rows + flat_ids - lookup(starts, segment_of)

def layer_norm(values, norm_gain, norm_bias):
    centred = values - lax.optimization_barrier(jnp.mean(values, axis=-1, keepdims=True))
    spread = lax.optimization_barrier(jnp.mean(centred * centred, axis=-1, keepdims=True))
    return centred * lax.rsqrt(spread + NORM_EPS) * norm_gain + norm_bias

def smooth_gate(values):
    return jax.nn.gelu(values, approximate=True)

def matmul(values, weight):
    return jnp.dot(values, weight, precision=lax.Precision.HIGHEST)

def block_forward(params, node_rows, edge_rows, counts):
    w_query, w_key, w_value, w_out, w_up, w_down, w_bias, w_gate, w_edge, w_edge_up, w_edge_down, node_norms, edge_norms = params
    graphs, per_graph, _ = node_rows.shape
    head_dim = D // H
    score_scale = head_dim ** (-0.5)
    normed = low(layer_norm(node_rows, node_norms[0], node_norms[1]))
    queries = low_back(low(matmul(normed, w_query))).reshape(graphs, per_graph, H, head_dim)
    keys_all = low_back(low(matmul(normed, w_key))).reshape(graphs, per_graph, H, head_dim)
    values_all = low_back(low(matmul(normed, w_value))).reshape(graphs, per_graph, H, head_dim)
    edge_in = edge_rows.reshape(graphs, per_graph, per_graph, DE)
    edge_normed = low(layer_norm(edge_in, edge_norms[0], edge_norms[1]))
    edge_bias = matmul(edge_normed, w_bias)
    gate_logit = low_back(matmul(edge_normed, w_gate))
    products = jnp.einsum('gihd,gjhd->gijh', queries, keys_all, precision=lax.Precision.HIGHEST)
    scores = low_back(products * score_scale + edge_bias)
    valid_keys = jnp.arange(per_graph, dtype=jnp.int32)[None, :] < counts[:, None]
    masked = jnp.where(valid_keys[:, None, :, None], scores, MASK_FILL)
    attn_weights = low(jax.nn.softmax(masked, axis=2) * jax.nn.sigmoid(gate_logit))
    mixed_heads = jnp.einsum('gijh,gjhd->gihd', attn_weights, values_all, precision=lax.Precision.HIGHEST)
    mixed_heads = low_back(low(mixed_heads)).reshape(graphs, per_graph, D)
    hidden = node_rows + low_back(matmul(mixed_heads, w_out))
    ffn_in = low(layer_norm(hidden, node_norms[2], node_norms[3]))
    ffn_act = low(smooth_gate(low_back(matmul(ffn_in, w_up))))
    node_out = hidden + matmul(ffn_act, w_down)
    edge_mid = edge_in + low_back(matmul(low(scores), w_edge))
    edge_ffn_in = low(layer_norm(edge_mid, edge_norms[2], edge_norms[3]))
    edge_act = low(smooth_gate(low_back(matmul(edge_ffn_in, w_edge_up))))
    edge_out = edge_mid + matmul(edge_act, w_edge_down)
    return (node_out, edge_out.reshape(graphs, per_graph, per_graph * DE))

def two_layers(params, node_rows, edge_rows, counts):
    node_mid, edge_mid = block_forward(params[:SET_PIECES], node_rows, edge_rows, counts)
    node_mid = low_back(low(node_mid))
    edge_mid = low_back(low(edge_mid))
    return block_forward(params[SET_PIECES:], node_mid, edge_mid, counts)

def bucket_pass(params, node_rows, edge_rows, counts, node_cot, edge_cot, blocks):

    def to_blocks(array):
        return array.reshape((blocks, array.shape[0] // blocks) + array.shape[1:])

    def one_block(totals, pieces):
        block_nodes, block_edges, block_counts, block_node_cot, block_edge_cot = pieces

        def forward(weights_in, nodes_in, edges_in):
            return two_layers(weights_in, nodes_in, edges_in, block_counts)
        outputs, pullback = jax.vjp(forward, params, block_nodes.astype(jnp.float32), block_edges.astype(jnp.float32))
        weight_grads, node_grads, edge_grads = pullback((block_node_cot.astype(jnp.float32), block_edge_cot.astype(jnp.float32)))
        totals = jax.tree.map(jnp.add, totals, weight_grads)
        return (totals, (outputs[0].astype(jnp.bfloat16), outputs[1].astype(jnp.bfloat16), node_grads.astype(jnp.bfloat16), edge_grads.astype(jnp.bfloat16)))
    starting = [jnp.zeros_like(p) for p in params]
    inputs = tuple((to_blocks(a) for a in (node_rows, edge_rows, counts, node_cot, edge_cot)))
    totals, stacked = lax.scan(one_block, starting, inputs)
    return (totals, tuple((s.reshape((-1,) + s.shape[2:]) for s in stacked)))

def reference(small_nodes, small_edges, small_counts, big_nodes, big_edges, big_counts, small_node_cot, small_edge_cot, big_node_cot, big_edge_cot, master, first_moment, second_moment, owner, segment_rows, step_count):
    source = source_rows(owner, segment_rows, OWN_ROWS)
    param_rows = jnp.take(low(master), source, axis=0)
    params = unpack(param_rows.reshape(-1))
    small_grads, small_outs = bucket_pass(params, small_nodes, small_edges, small_counts, small_node_cot, small_edge_cot, N_DP * N_ROW)
    big_grads, big_outs = bucket_pass(params, big_nodes, big_edges, big_counts, big_node_cot, big_edge_cot, N_DP)
    padding = TOTAL_ROWS * 128 - PARAMS
    summed = [a + b for a, b in zip(small_grads, big_grads)]
    norm_grads = jnp.concatenate([jnp.concatenate([summed[11], summed[12]], axis=1), jnp.concatenate([summed[11 + SET_PIECES], summed[12 + SET_PIECES]], axis=1)], axis=0)
    flat_grad = jnp.concatenate([g.reshape(-1) for g in summed] + [jnp.zeros((padding,), jnp.float32)])
    targets, live = target_rows(owner, segment_rows, OWN_ROWS)
    live_rows = live[:, None]
    owned_grad = jnp.where(live_rows, jnp.take(flat_grad.reshape(TOTAL_ROWS, 128), targets, axis=0), 0.0)
    rate_parts = [jnp.full((s[0] * s[1],), r, jnp.float32) for s, r in zip(piece_shapes(), piece_rates())]
    rate_flat = jnp.concatenate(rate_parts + [jnp.full((padding,), PAD_RATE, jnp.float32)])
    entry_rates = jnp.take(rate_flat.reshape(TOTAL_ROWS, 128), targets, axis=0)
    step_value = step_count[0].astype(jnp.float32)
    first_new = BETA_ONE * first_moment + (1.0 - BETA_ONE) * owned_grad
    second_new = BETA_TWO * second_moment + (1.0 - BETA_TWO) * owned_grad * owned_grad
    first_hat = first_new / (1.0 - jnp.power(jnp.float32(BETA_ONE), step_value))
    second_hat = second_new / (1.0 - jnp.power(jnp.float32(BETA_TWO), step_value))
    master_new = master - entry_rates * (first_hat / (jnp.sqrt(second_hat) + ADAM_EPS) + WEIGHT_DECAY * master)
    master_new = jnp.where(live_rows, master_new, master)
    first_new = jnp.where(live_rows, first_new, first_moment)
    second_new = jnp.where(live_rows, second_new, second_moment)
    return (small_outs[0], small_outs[1], big_outs[0], big_outs[1], small_outs[2], small_outs[3], big_outs[2], big_outs[3], master_new, first_new, second_new, norm_grads)
```

```python
import functools

import jax
import jax.numpy as jnp
from jax import lax
from jax.experimental import pallas as pl
from jax.experimental.pallas import tpu as pltpu
from jax.sharding import PartitionSpec as P

D = 512
H = 32
DE = 64
FF = 1024
FFE = 128
NS = 32
NB = 64
SET_ROWS = 16578
TOTAL_ROWS = 33156
NORM_EPS = 1e-05
BETA_ONE = 0.9
BETA_TWO = 0.95
WEIGHT_DECAY = 0.1
ADAM_EPS = 1e-08
MASK_FILL = -1e30
BF = jnp.bfloat16
F32 = jnp.float32
VMEM_LIMIT = 58 * 1024 * 1024
ROW_QKV, ROW_O, ROW_UP, ROW_DOWN = 0, 6144, 8192, 12288
ROW_BIAS, ROW_GATE, ROW_EDGE, ROW_EUP, ROW_EDOWN = 16384, 16400, 16416, 16432, 16496
ROW_NN, ROW_EN = 16560, 16576
GELU_C = 0.7978845608028654


def nn(a, b):
    return lax.dot_general(a, b, (((1,), (0,)), ((), ())), preferred_element_type=F32)


def nt(a, b):
    return lax.dot_general(a, b, (((1,), (1,)), ((), ())), preferred_element_type=F32)


def tn(a, b):
    return lax.dot_general(a, b, (((0,), (0,)), ((), ())), preferred_element_type=F32)


def iota(shape, axis):
    return lax.broadcasted_iota(jnp.int32, shape, axis)


def gelu_parts(u):
    u2 = u * u
    t = jnp.tanh(u * (GELU_C + (GELU_C * 0.044715) * u2))
    half = 0.5 + 0.5 * t
    value = u * half
    slope = half + value * (1.0 - t) * (GELU_C + (3.0 * GELU_C * 0.044715) * u2)
    return value, slope


def gelu_value(u):
    return u * (0.5 + 0.5 * jnp.tanh(u * (GELU_C + (GELU_C * 0.044715) * (u * u))))


def sigmoid(v):
    return 0.5 + 0.5 * jnp.tanh(0.5 * v)


def group_sum(v):
    v = v + pltpu.roll(v, 32, 1)
    return v + pltpu.roll(v, 64, 1)


def group_max(v):
    v = jnp.maximum(v, pltpu.roll(v, 32, 1))
    return jnp.maximum(v, pltpu.roll(v, 64, 1))


def fold8(v):
    return jnp.sum(v.reshape(v.shape[0] // 8, 8, v.shape[1]), axis=0)


class Bucket:
    def __init__(self, graphs, slots, node0, edge0, count0):
        self.graphs, self.slots = graphs, slots
        self.node0, self.edge0, self.count0 = node0, edge0, count0
        self.rows = graphs * slots
        self.chunks = slots // 4
        self.blocks = slots // 16
        self.edges = self.rows * self.chunks
        self.edge_lanes = slots * DE


class Dims:
    def __init__(self, small_graphs, big_graphs):
        self.small = Bucket(small_graphs, NS, 0, 0, 0)
        self.big = Bucket(
            big_graphs, NB, self.small.rows, self.small.edges, small_graphs
        )
        self.buckets = (self.small, self.big)
        self.nodes = self.small.rows + self.big.rows
        self.edges = self.small.edges + self.big.edges
        self.step = next(s for s in (256, 128, 64, 32) if self.edges % s == 0)
        self.blocks = sum(b.graphs * b.blocks for b in self.buckets)


def make_masks(mean_ref, head_ref, pick_ref):
    shape = (256, 256)
    same = (iota(shape, 0) >> 6) == (iota(shape, 1) >> 6)
    mean_ref[...] = jnp.where(same, 1.0 / DE, 0.0).astype(BF)
    shape = (512, 512)
    head_ref[...] = jnp.where((iota(shape, 0) >> 4) == (iota(shape, 1) & 31), 1.0, 0.0).astype(BF)
    shape = (16, 512)
    pick_ref[...] = jnp.where(iota(shape, 0) == (iota(shape, 1) >> 5), 1.0, 0.0).astype(BF)


def node_norm(v):
    centred = v - jnp.mean(v, axis=1, keepdims=True)
    r = lax.rsqrt(jnp.mean(centred * centred, axis=1, keepdims=True) + NORM_EPS)
    return centred * r, r


def node_norm_back(gdy, n, r):
    return r * (gdy - jnp.mean(gdy, axis=1, keepdims=True) - n * jnp.mean(gdy * n, axis=1, keepdims=True))


def aligned(value, by):
    return pl.multiple_of(value, by)


def block_of(bucket, t):
    g = t // bucket.blocks
    b = t % bucket.blocks
    rows = pl.ds(aligned(bucket.node0 + g * bucket.slots, 16), bucket.slots)
    keys = pl.ds(aligned(bucket.node0 + t * 16, 16), 16)
    chunk_rows = [
        pl.ds(
            aligned(bucket.edge0 + (4 * b + c) * bucket.rows + g * bucket.slots, 16),
            bucket.slots,
        )
        for c in range(4)
    ]
    return g, rows, keys, chunk_rows


def forward(dm, counts, w, io, res, scr):
    step = dm.step
    x = io.nodes[...].astype(F32)
    n, r = node_norm(x)
    res.node_n1[...] = n.astype(BF)
    res.node_r1[...] = jnp.broadcast_to(r, (dm.nodes, 128))
    hn = (n * w.nn[0:1, :] + w.nn[1:2, :]).astype(BF)
    res.qkv[...] = nn(hn, w.qkv[...]).astype(BF)

    @pl.loop(0, dm.edges // step)
    def _(i):
        rows = pl.ds(aligned(i * step, step), step)
        x = io.edges[rows, :]
        centred = x.astype(F32) - nn(x, scr.mean[...])
        r = lax.rsqrt(nn((centred * centred).astype(BF), scr.mean[...]) + NORM_EPS)
        n = centred * r
        res.edge_n1[rows, :] = n.astype(BF)
        res.edge_r1[rows, :] = r.astype(BF)
        xn = (n * w.en[0:1, :] + w.en[1:2, :]).astype(BF)
        both = nn(xn, w.eg[...])
        scr.scores[rows, :] = both[:, :128]
        res.gate[rows, :] = both[:, 128:]

    t0 = 0
    for bucket in dm.buckets:
        @pl.loop(0, bucket.graphs * bucket.blocks)
        def _(t, bucket=bucket, t0=t0):
            g, rows, keys, chunk_rows = block_of(bucket, t)
            kb = tn(res.qkv[keys, 512:1024], scr.pick[...]).astype(BF) * scr.head[...]
            scr.vbig[t0 + t] = tn(res.qkv[keys, 1024:1536], scr.pick[...]).astype(BF) * scr.head[...]
            s = nn(res.qkv[rows, 0:512], kb) * 0.25
            for c in range(4):
                scr.scores[chunk_rows[c], :] += s[:, 128 * c : 128 * (c + 1)]

        @pl.loop(0, bucket.rows // 32)
        def _(i, bucket=bucket):
            count = counts[bucket.count0 + i * 32 // bucket.slots]
            lane_key = iota((32, 128), 1) >> 5
            row = [
                pl.ds(aligned(bucket.edge0 + c * bucket.rows + i * 32, 32), 32)
                for c in range(bucket.chunks)
            ]
            top = jnp.full((32, 128), MASK_FILL, F32)
            for c in range(bucket.chunks):
                s = scr.scores[row[c], :]
                res.low[row[c], :] = s.astype(BF)
                top = jnp.maximum(top, jnp.where(lane_key < count - 4 * c, s, MASK_FILL))
            top = group_max(top)
            total = jnp.zeros((32, 128), F32)
            for c in range(bucket.chunks):
                s = jnp.where(lane_key < count - 4 * c, scr.scores[row[c], :], MASK_FILL)
                e = jnp.exp(s - top)
                total = total + e
                scr.scores[row[c], :] = e
            inv = 1.0 / group_sum(total)
            for c in range(bucket.chunks):
                p = scr.scores[row[c], :] * inv
                res.prob[row[c], :] = p.astype(BF)
                scr.attn[row[c], :] = (p * sigmoid(res.gate[row[c], :])).astype(BF)

        @pl.loop(0, bucket.graphs)
        def _(g, bucket=bucket, t0=t0):
            total = None
            for b in range(bucket.blocks):
                _, rows, _, chunk_rows = block_of(bucket, g * bucket.blocks + b)
                a = jnp.concatenate([scr.attn[chunk_rows[c], :] for c in range(4)], axis=1)
                part = nt(a, scr.vbig[t0 + g * bucket.blocks + b])
                total = part if total is None else total + part
            res.mixed[rows, :] = total.astype(BF)

        t0 += bucket.graphs * bucket.blocks

    y = io.nodes[...].astype(F32) + nn(res.mixed[...], w.o[...])
    n, r = node_norm(y)
    res.node_n2[...] = n.astype(BF)
    res.node_r2[...] = jnp.broadcast_to(r, (dm.nodes, 128))
    z = (n * w.nn[2:3, :] + w.nn[3:4, :]).astype(BF)
    u = nn(z, w.up[...])
    res.node_u[...] = u
    io.nodes_out[...] = (y + nn(gelu_value(u).astype(BF), w.down[...])).astype(BF)

    @pl.loop(0, dm.edges // step)
    def _(i):
        rows = pl.ds(aligned(i * step, step), step)
        m = io.edges[rows, :].astype(F32) + nn(res.low[rows, :], w.x[...])
        high = m.astype(BF)
        rest = (m - high.astype(F32)).astype(BF)
        centred = m - nn(high, scr.mean[...]) - nn(rest, scr.mean[...])
        r = lax.rsqrt(nn((centred * centred).astype(BF), scr.mean[...]) + NORM_EPS)
        n = centred * r
        res.edge_n2[rows, :] = n.astype(BF)
        res.edge_r2[rows, :] = r.astype(BF)
        mn = (n * w.en[2:3, :] + w.en[3:4, :]).astype(BF)
        ua = nn(mn, w.a[...])
        res.edge_u[rows, :] = ua.astype(BF)
        io.edges_out[rows, :] = (m + nn(gelu_value(ua).astype(BF), w.b[...])).astype(BF)


def put_strided(flat, first, value, parts):
    for q in range(parts):
        flat[pl.ds(first + q, value.shape[0], stride=parts), :] = value[:, 128 * q : 128 * (q + 1)]


def backward(dm, off, w, io, res, scr):
    step = dm.step
    flat = scr.flat
    gy = io.nodes_cot[...]
    act, slope = gelu_parts(res.node_u[...])
    du = (nt(gy, w.down[...]) * slope).astype(BF)
    put_strided(flat, off + ROW_DOWN, tn(act.astype(BF), gy), 4)
    n = res.node_n2[...].astype(F32)
    z = (n * w.nn[2:3, :] + w.nn[3:4, :]).astype(BF)
    put_strided(flat, off + ROW_UP, tn(z, du), 8)
    dz = nt(du, w.up[...])
    io.norms[2:3, 0:512] = jnp.sum(dz * n, axis=0, keepdims=True)
    io.norms[3:4, 0:512] = jnp.sum(dz, axis=0, keepdims=True)
    dy = gy.astype(F32) + node_norm_back(dz * w.nn[2:3, :], n, res.node_r2[:, 0:1])
    scr.dy[...] = dy
    dyl = dy.astype(BF)
    put_strided(flat, off + ROW_O, tn(res.mixed[...], dyl), 4)
    scr.do[...] = nt(dyl, w.o[...]).astype(BF)

    scr.gb[...] = jnp.zeros((512, 256), F32)
    scr.ga[...] = jnp.zeros((256, 512), F32)
    scr.gx[...] = jnp.zeros((128, 256), F32)
    scr.geg[...] = jnp.zeros((256, 256), F32)
    scr.en[...] = jnp.zeros((4, 8, 256), F32)

    @pl.loop(0, dm.edges // step)
    def _(i):
        rows = pl.ds(aligned(i * step, step), step)
        gx = io.edges_cot[rows, :]
        act, slope = gelu_parts(res.edge_u[rows, :].astype(F32))
        dua = (nt(gx, w.b[...]) * slope).astype(BF)
        scr.gb[...] += tn(act.astype(BF), gx)
        n = res.edge_n2[rows, :].astype(F32)
        mn = (n * w.en[2:3, :] + w.en[3:4, :]).astype(BF)
        scr.ga[...] += tn(mn, dua)
        dmn = nt(dua, w.a[...])
        scr.en[2] += fold8(dmn * n)
        scr.en[3] += fold8(dmn)
        gdy = dmn * w.en[2:3, :]
        m1 = nn(gdy.astype(BF), scr.mean[...])
        m2 = nn((gdy * n).astype(BF), scr.mean[...])
        dmid = gx.astype(F32) + res.edge_r2[rows, :].astype(F32) * (gdy - m1 - n * m2)
        scr.dmid[rows, :] = dmid
        dml = dmid.astype(BF)
        scr.gx[...] += tn(res.low[rows, :], dml)
        scr.scores[rows, :] = nt(dml, w.x[...])

    t0 = 0
    for bucket in dm.buckets:
        @pl.loop(0, bucket.graphs * bucket.blocks)
        def _(t, bucket=bucket, t0=t0):
            g, rows, keys, chunk_rows = block_of(bucket, t)
            scr.vbig[t0 + t] = tn(res.qkv[keys, 512:1024], scr.pick[...]).astype(BF) * scr.head[...]
            vb = tn(res.qkv[keys, 1024:1536], scr.pick[...]).astype(BF) * scr.head[...]
            da = nn(scr.do[rows, :], vb)
            for c in range(4):
                scr.da[chunk_rows[c], :] = da[:, 128 * c : 128 * (c + 1)]

        @pl.loop(0, bucket.rows // 32)
        def _(i, bucket=bucket):
            row = [
                pl.ds(aligned(bucket.edge0 + c * bucket.rows + i * 32, 32), 32)
                for c in range(bucket.chunks)
            ]
            total = jnp.zeros((32, 128), F32)
            for c in range(bucket.chunks):
                p = res.prob[row[c], :].astype(F32)
                s = sigmoid(res.gate[row[c], :])
                scr.attn[row[c], :] = (p * s).astype(BF)
                pt = p * scr.da[row[c], :] * s
                scr.da[row[c], :] = pt
                total = total + pt
                scr.dsg[row[c], 128:] = (pt * (1.0 - s)).astype(BF)
            total = group_sum(total)
            for c in range(bucket.chunks):
                p = res.prob[row[c], :].astype(F32)
                ds = scr.da[row[c], :] - p * total + scr.scores[row[c], :]
                scr.dsg[row[c], :128] = ds.astype(BF)

        @pl.loop(0, bucket.graphs)
        def _(g, bucket=bucket, t0=t0):
            total = None
            for b in range(bucket.blocks):
                t = g * bucket.blocks + b
                _, rows, keys, chunk_rows = block_of(bucket, t)
                ds = jnp.concatenate([scr.dsg[chunk_rows[c], :128] for c in range(4)], axis=1)
                part = nt(ds, scr.vbig[t0 + t])
                total = part if total is None else total + part
                gk = tn(res.qkv[rows, 0:512], ds).astype(BF) * scr.head[...]
                scr.dqkv[keys, 512:1024] = (nt(scr.pick[...], gk) * 0.25).astype(BF)
                a = jnp.concatenate([scr.attn[chunk_rows[c], :] for c in range(4)], axis=1)
                gv = tn(scr.do[rows, :], a).astype(BF) * scr.head[...]
                scr.dqkv[keys, 1024:1536] = nt(scr.pick[...], gv).astype(BF)
            scr.dqkv[rows, 0:512] = (total * 0.25).astype(BF)

        t0 += bucket.graphs * bucket.blocks

    n = res.node_n1[...].astype(F32)
    hn = (n * w.nn[0:1, :] + w.nn[1:2, :]).astype(BF)
    for m in range(3):
        put_strided(flat, off + ROW_QKV + 2048 * m, tn(hn, scr.dqkv[:, 512 * m : 512 * (m + 1)]), 4)
    dhn = nt(scr.dqkv[...], w.qkv[...])
    io.norms[0:1, 0:512] = jnp.sum(dhn * n, axis=0, keepdims=True)
    io.norms[1:2, 0:512] = jnp.sum(dhn, axis=0, keepdims=True)
    dx = scr.dy[...] + node_norm_back(dhn * w.nn[0:1, :], n, res.node_r1[:, 0:1])
    io.nodes_grad[...] = dx.astype(BF)

    @pl.loop(0, dm.edges // step)
    def _(i):
        rows = pl.ds(aligned(i * step, step), step)
        dsg = scr.dsg[rows, :]
        n = res.edge_n1[rows, :].astype(F32)
        xn = (n * w.en[0:1, :] + w.en[1:2, :]).astype(BF)
        scr.geg[...] += tn(xn, dsg)
        dxn = nt(dsg, w.eg[...])
        scr.en[0] += fold8(dxn * n)
        scr.en[1] += fold8(dxn)
        gdy = dxn * w.en[0:1, :]
        m1 = nn(gdy.astype(BF), scr.mean[...])
        m2 = nn((gdy * n).astype(BF), scr.mean[...])
        dx = scr.dmid[rows, :] + res.edge_r1[rows, :].astype(F32) * (gdy - m1 - n * m2)
        io.edges_grad[rows, :] = dx.astype(BF)

    small_grads(off, io, scr)
    io.grads[...] = scr.flat[...].astype(BF)


def small_grads(off, io, scr):
    flat, tmp = scr.flat, scr.tmp
    lane64 = lambda rows: iota((rows, 128), 1) >> 6
    lane32 = lambda rows: iota((rows, 128), 1) >> 5
    up = scr.ga[0:64, 0:128]
    for k in range(1, 4):
        up = up + scr.ga[64 * k : 64 * (k + 1), 128 * k : 128 * (k + 1)]
    flat[pl.ds(off + ROW_EUP, 64), :] = up

    def halves(ref, rows, first, out_rows):
        total = jnp.zeros((rows, 128), F32)
        for k in range(4):
            part = ref[rows * k : rows * (k + 1), 128 * (k // 2) : 128 * (k // 2 + 1)]
            total = total + jnp.where(lane64(rows) == k % 2, part, 0.0)
        tmp[0:rows, :] = total + pltpu.roll(total, 64, 1)
        even = tmp[pl.ds(0, out_rows, stride=2), :]
        odd = tmp[pl.ds(1, out_rows, stride=2), :]
        flat[pl.ds(off + first, out_rows), :] = jnp.where(lane64(out_rows) == 0, even, odd)

    halves(scr.gb, 128, ROW_EDOWN, 64)
    halves(scr.gx, 32, ROW_EDGE, 16)
    for half, first in ((0, ROW_BIAS), (1, ROW_GATE)):
        total = jnp.zeros((64, 128), F32)
        for k in range(4):
            part = scr.geg[64 * k : 64 * (k + 1), 128 * half : 128 * (half + 1)]
            total = total + jnp.where(lane32(64) == k, part, 0.0)
        tmp[0:64, :] = group_sum(total)
        rows = jnp.zeros((16, 128), F32)
        for b in range(4):
            rows = jnp.where(lane32(16) == b, tmp[pl.ds(b, 16, stride=4), :], rows)
        flat[pl.ds(off + first, 16), :] = rows
    sums = []
    for t in range(4):
        both = jnp.sum(scr.en[t], axis=0, keepdims=True)
        one = both[:, :128] + both[:, 128:]
        one = one + pltpu.roll(one, 64, 1)
        io.norms[t : t + 1, 512:576] = one[:, 0:64]
        sums.append(one)
    for t in range(2):
        flat[pl.ds(off + ROW_EN + t, 1), :] = jnp.where(lane64(1) == 0, sums[2 * t], sums[2 * t + 1])
    for t in range(4):
        for q in range(4):
            flat[pl.ds(off + ROW_NN + 4 * t + q, 1), :] = io.norms[t : t + 1, 128 * q : 128 * (q + 1)]
    if off:
        flat[pl.ds(0, off), :] = jnp.zeros((off, 128), F32)
    end = off + SET_ROWS
    flat[pl.ds(end, flat.shape[0] - end), :] = jnp.zeros((flat.shape[0] - end, 128), F32)


def assemble_set(off, flat, tmp, w):
    def strided(first, rows, parts, out, lane0=0):
        for q in range(parts):
            out[:, lane0 + 128 * q : lane0 + 128 * (q + 1)] = flat[
                pl.ds(off + first + q, rows, stride=parts), :
            ].astype(BF)

    for m in range(3):
        strided(ROW_QKV + 2048 * m, 512, 4, w.qkv, 512 * m)
    strided(ROW_O, 512, 4, w.o)
    strided(ROW_UP, 512, 8, w.up)
    strided(ROW_DOWN, 1024, 4, w.down)
    lane64 = lambda rows: iota((rows, 128), 1) >> 6
    lane32 = lambda rows: iota((rows, 128), 1) >> 5
    w.eg[...] = jnp.zeros((256, 256), BF)
    w.x[...] = jnp.zeros((128, 256), BF)
    w.a[...] = jnp.zeros((256, 512), BF)
    w.b[...] = jnp.zeros((512, 256), BF)
    up = flat[pl.ds(off + ROW_EUP, 64), :].astype(BF)
    for k in range(4):
        w.a[64 * k : 64 * (k + 1), 128 * k : 128 * (k + 1)] = up

    def halves(first, in_rows, out):
        rows = 2 * in_rows
        v = flat[pl.ds(off + first, in_rows), :]
        other = pltpu.roll(v, 64, 1)
        tmp[pl.ds(0, in_rows, stride=2), :] = jnp.where(lane64(in_rows) == 0, v, other)
        tmp[pl.ds(1, in_rows, stride=2), :] = jnp.where(lane64(in_rows) == 0, other, v)
        both = tmp[0:rows, :]
        for k in range(4):
            out[rows * k : rows * (k + 1), 128 * (k // 2) : 128 * (k // 2 + 1)] = jnp.where(
                lane64(rows) == k % 2, both, 0.0
            ).astype(BF)

    halves(ROW_EDOWN, 64, w.b)
    halves(ROW_EDGE, 16, w.x)
    for half, first in ((0, ROW_BIAS), (1, ROW_GATE)):
        v = flat[pl.ds(off + first, 16), :]
        for b in range(4):
            tmp[pl.ds(b, 16, stride=4), :] = group_sum(jnp.where(lane32(16) == b, v, 0.0))
        both = tmp[0:64, :]
        for k in range(4):
            w.eg[64 * k : 64 * (k + 1), 128 * half : 128 * (half + 1)] = jnp.where(
                lane32(64) == k, both, 0.0
            ).astype(BF)
    for t in range(4):
        for q in range(4):
            w.nn[t : t + 1, 128 * q : 128 * (q + 1)] = flat[pl.ds(off + ROW_NN + 4 * t + q, 1), :]
    for t in range(2):
        v = flat[pl.ds(off + ROW_EN + t, 1), :]
        other = pltpu.roll(v, 64, 1)
        gain = jnp.where(lane64(1) == 0, v, other)
        bias = jnp.where(lane64(1) == 0, other, v)
        for half in range(2):
            w.en[2 * t : 2 * t + 1, 128 * half : 128 * (half + 1)] = gain
            w.en[2 * t + 1 : 2 * t + 2, 128 * half : 128 * (half + 1)] = bias


class Group:
    def __init__(self, names, refs):
        for name, ref in zip(names, refs):
            setattr(self, name, ref)


WEIGHTS = {
    "qkv": ((D, 3 * D), BF),
    "o": ((D, D), BF),
    "up": ((D, FF), BF),
    "down": ((FF, D), BF),
    "eg": ((256, 256), BF),
    "x": ((128, 256), BF),
    "a": ((256, 512), BF),
    "b": ((512, 256), BF),
    "nn": ((4, D), F32),
    "en": ((4, 256), F32),
}


def residual_shapes(dm):
    return {
        "node_n1": ((dm.nodes, D), BF),
        "node_r1": ((dm.nodes, 128), F32),
        "qkv": ((dm.nodes, 3 * D), BF),
        "mixed": ((dm.nodes, D), BF),
        "node_n2": ((dm.nodes, D), BF),
        "node_r2": ((dm.nodes, 128), F32),
        "node_u": ((dm.nodes, FF), F32),
        "edge_n1": ((dm.edges, 256), BF),
        "edge_r1": ((dm.edges, 256), BF),
        "gate": ((dm.edges, 128), F32),
        "low": ((dm.edges, 128), BF),
        "prob": ((dm.edges, 128), BF),
        "edge_n2": ((dm.edges, 256), BF),
        "edge_r2": ((dm.edges, 256), BF),
        "edge_u": ((dm.edges, 512), BF),
    }


def mask_shapes():
    return {"mean": ((256, 256), BF), "head": ((512, 512), BF), "pick": ((16, 512), BF)}


def forward_scratch(dm):
    return {
        "scores": ((dm.edges, 128), F32),
        "attn": ((dm.edges, 128), BF),
        "vbig": ((dm.blocks, 512, 512), BF),
    }


def backward_scratch(dm, set_pad):
    return {
        "scores": ((dm.edges, 128), F32),
        "attn": ((dm.edges, 128), BF),
        "vbig": ((dm.blocks, 512, 512), BF),
        "da": ((dm.edges, 128), F32),
        "dsg": ((dm.edges, 256), BF),
        "dmid": ((dm.edges, 256), F32),
        "dy": ((dm.nodes, D), F32),
        "do": ((dm.nodes, D), BF),
        "dqkv": ((dm.nodes, 3 * D), BF),
        "gb": ((512, 256), F32),
        "ga": ((256, 512), F32),
        "gx": ((128, 256), F32),
        "geg": ((256, 256), F32),
        "en": ((4, 8, 256), F32),
        "tmp": ((128, 128), F32),
        "flat": ((set_pad, 128), F32),
    }


def structs(shapes):
    return [jax.ShapeDtypeStruct(s, t) for s, t in shapes.values()]


def vmem(shapes):
    return [pltpu.VMEM(s, t) for s, t in shapes.values()]


def whole(n):
    return [pl.BlockSpec(memory_space=pltpu.VMEM)] * n


def split(refs, *groups):
    out, at = [], 0
    for names in groups:
        out.append(Group(names, refs[at : at + len(names)]))
        at += len(names)
    assert at == len(refs)
    return out


def edge_copies(dm, whole_refs, stacked, sems, out):
    copies = []
    for bucket, ref in zip(dm.buckets, whole_refs):
        for c in range(bucket.chunks):
            a = ref.at[:, pl.ds(256 * c, 256)]
            b = stacked.at[pl.ds(bucket.edge0 + c * bucket.rows, bucket.rows), :]
            src, dst = (b, a) if out else (a, b)
            copies.append(pltpu.make_async_copy(src, dst, sems.at[len(copies)]))
    return copies


def copy_count(dm):
    return dm.small.chunks + dm.big.chunks


HBM = pl.BlockSpec(memory_space=pl.ANY)
SMEM = pl.BlockSpec(memory_space=pltpu.SMEM)


def compiler_params():
    return pltpu.CompilerParams(vmem_limit_bytes=VMEM_LIMIT)


def join_nodes(dm, small, big, out):
    out[0 : dm.small.rows, :] = small[...]
    out[dm.small.rows :, :] = big[...]


def part_nodes(dm, value, small, big):
    small[...] = value[0 : dm.small.rows, :]
    big[...] = value[dm.small.rows :, :]


def first_forward(dm, counts, weights, nodes, edges):
    res, masks = residual_shapes(dm), mask_shapes()
    out = {"nodes_out": ((dm.nodes, D), BF), "edges_out": ((dm.edges, 256), BF), **res}
    scr = {**masks, **forward_scratch(dm), "nodes": ((dm.nodes, D), BF), "edges": ((dm.edges, 256), BF)}

    def body(*refs):
        counts_ref, refs, sems = refs[0], refs[1:-1], refs[-1]
        w, src, dst, s = split(refs, WEIGHTS, ("sn", "bn", "se", "be"), out, scr)
        copies = edge_copies(dm, (src.se, src.be), s.edges, sems, False)
        for c in copies:
            c.start()
        make_masks(s.mean, s.head, s.pick)
        join_nodes(dm, src.sn, src.bn, s.nodes)
        io = Group(
            ("nodes", "edges", "nodes_out", "edges_out"),
            (s.nodes, s.edges, dst.nodes_out, dst.edges_out),
        )
        for c in copies:
            c.wait()
        forward(dm, counts_ref, w, io, dst, s)

    got = pl.pallas_call(
        body,
        out_shape=structs(out),
        in_specs=[SMEM] + whole(len(WEIGHTS) + 2) + [HBM] * 2,
        out_specs=whole(len(out)),
        scratch_shapes=vmem(scr) + [pltpu.SemaphoreType.DMA((copy_count(dm),))],
        compiler_params=compiler_params(),
    )(counts, *weights, *nodes, *edges)
    return got[0], got[1], got[2:]


def second_layer(dm, set_pad, off, counts, weights, nodes, edges, node_cots, edge_cots):
    out = {
        "sno": ((dm.small.rows, D), BF),
        "bno": ((dm.big.rows, D), BF),
        "seo": ((dm.small.rows, dm.small.edge_lanes), BF),
        "beo": ((dm.big.rows, dm.big.edge_lanes), BF),
        "nodes_grad": ((dm.nodes, D), BF),
        "edges_grad": ((dm.edges, 256), BF),
        "grads": ((set_pad, 128), BF),
        "norms": ((4, 576), F32),
    }
    res = residual_shapes(dm)
    scr = {
        **mask_shapes(),
        **forward_scratch(dm),
        **backward_scratch(dm, set_pad),
        **{"res_" + k: v for k, v in res.items()},
        "nodes_out": ((dm.nodes, D), BF),
        "edges_out": ((dm.edges, 256), BF),
        "node_cot": ((dm.nodes, D), BF),
        "edge_cot": ((dm.edges, 256), BF),
    }

    def body(*refs):
        counts_ref, refs, in_sems, out_sems = refs[0], refs[1:-2], refs[-2], refs[-1]
        w, src, dst, s = split(
            refs, WEIGHTS, ("nodes", "edges", "snc", "bnc", "sec", "bec"), out, scr
        )
        copies = edge_copies(dm, (src.sec, src.bec), s.edge_cot, in_sems, False)
        for c in copies:
            c.start()
        make_masks(s.mean, s.head, s.pick)
        join_nodes(dm, src.snc, src.bnc, s.node_cot)
        kept = Group(res, [getattr(s, "res_" + k) for k in res])
        io = Group(
            ("nodes", "edges", "nodes_out", "edges_out"),
            (src.nodes, src.edges, s.nodes_out, s.edges_out),
        )
        forward(dm, counts_ref, w, io, kept, s)
        outgoing = edge_copies(dm, (dst.seo, dst.beo), s.edges_out, out_sems, True)
        for c in outgoing:
            c.start()
        part_nodes(dm, s.nodes_out[...], dst.sno, dst.bno)
        for c in copies:
            c.wait()
        io = Group(
            ("nodes_cot", "edges_cot", "nodes_grad", "edges_grad", "grads", "norms"),
            (s.node_cot, s.edge_cot, dst.nodes_grad, dst.edges_grad, dst.grads, dst.norms),
        )
        backward(dm, off, w, io, kept, s)
        for c in outgoing:
            c.wait()

    count = copy_count(dm)
    return pl.pallas_call(
        body,
        out_shape=structs(out),
        in_specs=[SMEM] + whole(len(WEIGHTS) + 4) + [HBM] * 2,
        out_specs=whole(2) + [HBM] * 2 + whole(4),
        scratch_shapes=vmem(scr) + [pltpu.SemaphoreType.DMA((count,))] * 2,
        compiler_params=compiler_params(),
    )(counts, *weights, nodes, edges, *node_cots, *edge_cots)


def first_backward(dm, set_pad, off, weights, kept, nodes_cot, edges_cot):
    out = {
        "sng": ((dm.small.rows, D), BF),
        "bng": ((dm.big.rows, D), BF),
        "seg": ((dm.small.rows, dm.small.edge_lanes), BF),
        "beg": ((dm.big.rows, dm.big.edge_lanes), BF),
        "grads": ((set_pad, 128), BF),
        "norms": ((4, 576), F32),
    }
    res = residual_shapes(dm)
    scr = {
        **mask_shapes(),
        **backward_scratch(dm, set_pad),
        "nodes_grad": ((dm.nodes, D), BF),
        "edges_grad": ((dm.edges, 256), BF),
    }

    def body(*refs):
        refs, out_sems = refs[:-1], refs[-1]
        w, kept_refs, src, dst, s = split(refs, WEIGHTS, res, ("nodes_cot", "edges_cot"), out, scr)
        make_masks(s.mean, s.head, s.pick)
        io = Group(
            ("nodes_cot", "edges_cot", "nodes_grad", "edges_grad", "grads", "norms"),
            (src.nodes_cot, src.edges_cot, s.nodes_grad, s.edges_grad, dst.grads, dst.norms),
        )
        backward(dm, off, w, io, kept_refs, s)
        outgoing = edge_copies(dm, (dst.seg, dst.beg), s.edges_grad, out_sems, True)
        for c in outgoing:
            c.start()
        part_nodes(dm, s.nodes_grad[...], dst.sng, dst.bng)
        for c in outgoing:
            c.wait()

    return pl.pallas_call(
        body,
        out_shape=structs(out),
        in_specs=whole(len(WEIGHTS) + len(res) + 2),
        out_specs=whole(2) + [HBM] * 2 + whole(2),
        scratch_shapes=vmem(scr) + [pltpu.SemaphoreType.DMA((copy_count(dm),))],
        compiler_params=compiler_params(),
    )(*weights, *kept, nodes_cot, edges_cot)


def round_up(value, by):
    return -(-value // by) * by


def shifted_segment(master, shift, length):
    held = master.shape[0]
    padded = round_up(held + 15, 16)
    step = 1024

    def body(info, src, dst, window):
        i = pl.program_id(0)

        @pl.when(i == 0)
        def _():
            window[0:16, :] = jnp.zeros((16, 128), F32)

        window[16:, :] = src[...]
        moved = window[pl.ds(16 - info[0], step), :]
        index = i * step - info[0] + iota((step, 128), 0)
        live = (index >= 0) & (index < info[1])
        dst[...] = jnp.where(live, moved, 0.0).astype(BF)
        window[0:16, :] = window[step : step + 16, :]

    return pl.pallas_call(
        body,
        grid=(pl.cdiv(padded, step),),
        out_shape=jax.ShapeDtypeStruct((padded, 128), BF),
        in_specs=[
            SMEM,
            pl.BlockSpec((step, 128), lambda i: (jnp.minimum(i, (held - 1) // step), 0)),
        ],
        out_specs=pl.BlockSpec((step, 128), lambda i: (i, 0)),
        scratch_shapes=[pltpu.VMEM((step + 16, 128), F32)],
        compiler_params=compiler_params(),
    )(jnp.stack([shift, length]), master)


def assemble(first, last, parts):
    count = len(parts)
    padded = parts[0].shape[0]
    bits = (padded // 16).bit_length()
    tiles = -(-TOTAL_ROWS // 16)
    set_tiles = -(-(SET_ROWS + 2) // 16)
    out = {**{"one_" + k: v for k, v in WEIGHTS.items()}, **{"two_" + k: v for k, v in WEIGHTS.items()}}

    def body(first_ref, last_ref, *refs):
        srcs, refs = refs[:count], refs[count:]
        dsts, (rows, flat, tmp, edge, sems, edge_sems) = refs[: len(out)], refs[len(out) :]

        def each(act):
            for i in range(count):
                a, b = first_ref[i], last_ref[i]
                inner = b - a - 1
                for bit in range(bits):
                    size = 16 << bit
                    if size > padded:
                        continue
                    done = (inner >> (bit + 1)) << (bit + 1)

                    @pl.when((inner > 0) & (((inner >> bit) & 1) == 1))
                    def _(i=i, a=a, done=done, size=size, bit=bit):
                        act(
                            pltpu.make_async_copy(
                                srcs[i].at[pl.ds(aligned(16 * (1 + done), 16), size), :],
                                rows.at[pl.ds(aligned(16 * (a + 1 + done), 16), size), :],
                                sems.at[i, bit],
                            )
                        )

                act(pltpu.make_async_copy(srcs[i].at[pl.ds(0, 16), :], edge.at[2 * i], edge_sems.at[2 * i]))
                act(
                    pltpu.make_async_copy(
                        srcs[i].at[pl.ds(aligned(16 * (b - a), 16), 16), :],
                        edge.at[2 * i + 1],
                        edge_sems.at[2 * i + 1],
                    )
                )

        each(lambda c: c.start())
        each(lambda c: c.wait())
        tile = lambda t: pl.ds(aligned(16 * t, 16), 16)
        for i in range(count):
            rows[tile(first_ref[i]), :] = jnp.zeros((16, 128), BF)
            rows[tile(last_ref[i]), :] = jnp.zeros((16, 128), BF)
        for i in range(count):
            rows[tile(first_ref[i]), :] += edge[2 * i]

            @pl.when(last_ref[i] != first_ref[i])
            def _(i=i):
                rows[tile(last_ref[i]), :] += edge[2 * i + 1]

        for which in range(2):
            base = which * (SET_ROWS // 16) * 16
            flat[...] = rows[pl.ds(base, 16 * set_tiles), :].astype(F32)
            w = Group(WEIGHTS, dsts[which * len(WEIGHTS) : (which + 1) * len(WEIGHTS)])
            assemble_set(which * (SET_ROWS % 16), flat, tmp, w)

    got = pl.pallas_call(
        body,
        out_shape=structs(out),
        in_specs=[SMEM] * 2 + [HBM] * count,
        out_specs=whole(len(out)),
        scratch_shapes=[
            pltpu.VMEM((16 * tiles, 128), BF),
            pltpu.VMEM((16 * set_tiles, 128), F32),
            pltpu.VMEM((128, 128), F32),
            pltpu.VMEM((2 * count, 16, 128), BF),
            pltpu.SemaphoreType.DMA((count, bits)),
            pltpu.SemaphoreType.DMA((2 * count,)),
        ],
        compiler_params=compiler_params(),
    )(first, last, *parts)
    return got[: len(WEIGHTS)], got[len(WEIGHTS) :]


def adam(info, scales, places, grads, master, first, second):
    held = master.shape[0]
    step = 1040
    count = len(grads)
    each = count // 2
    block = grads[0].shape[0]
    base = (SET_ROWS // 16) * 16
    total = round_up(base + each * block + round_up(held + 16, step) + 16, 16)

    def body(info_ref, scale_ref, place_ref, *refs):
        srcs, refs = refs[:count], refs[count:]
        master_ref, first_ref, second_ref, o_master, o_first, o_second, rows, window, sems = refs
        i = pl.program_id(0)

        @pl.when(i == 0)
        def _():
            def copies(which):
                return [
                    pltpu.make_async_copy(
                        srcs[which * each + k],
                        rows.at[pl.ds(aligned(which * base + place_ref[which * each + k], 16), block), :],
                        sems.at[which * each + k],
                    )
                    for k in range(each)
                ]

            for c in copies(0):
                c.start()
            for c in copies(0):
                c.wait()
            kept = rows[base : base + 16, :]
            for c in copies(1):
                c.start()
            for c in copies(1):
                c.wait()
            rows[base : base + 16, :] += kept

        start, length = info_ref[0], info_ref[1]
        shift = start % 16
        from_row = aligned(start - shift + i * step, 16)
        window[...] = rows[pl.ds(from_row, step + 16), :].astype(F32)
        g = window[pl.ds(shift, step), :]
        index = i * step + iota((step, 128), 0)
        live = index < length
        at = start + index
        at = jnp.where(at >= SET_ROWS, at - SET_ROWS, at)
        rate = jnp.full((step, 128), 0.25, F32)
        for end, value in reversed(RATES):
            rate = jnp.where(at < end, value, rate)
        p, m, v = master_ref[...], first_ref[...], second_ref[...]
        m_new = BETA_ONE * m + (1.0 - BETA_ONE) * g
        v_new = BETA_TWO * v + (1.0 - BETA_TWO) * g * g
        move = (m_new * scale_ref[0]) / (jnp.sqrt(v_new * scale_ref[1]) + ADAM_EPS)
        o_master[...] = jnp.where(live, p - rate * (move + WEIGHT_DECAY * p), p)
        o_first[...] = jnp.where(live, m_new, m)
        o_second[...] = jnp.where(live, v_new, v)

    spec = pl.BlockSpec((step, 128), lambda i: (i, 0))
    shape = jax.ShapeDtypeStruct((held, 128), F32)
    return pl.pallas_call(
        body,
        grid=(pl.cdiv(held, step),),
        out_shape=[shape] * 3,
        in_specs=[SMEM] * 3 + [HBM] * count + [spec] * 3,
        out_specs=[spec] * 3,
        scratch_shapes=[
            pltpu.VMEM((total, 128), BF),
            pltpu.VMEM((step + 16, 128), F32),
            pltpu.SemaphoreType.DMA((count,)),
        ],
        compiler_params=compiler_params(),
    )(info, scales, places, *grads, master, first, second)


RATES = [
    (ROW_O, 0.5 * D ** (-0.5)),
    (ROW_UP, 2.0 * D ** (-0.5)),
    (ROW_DOWN, 0.5 * D ** (-0.5)),
    (ROW_BIAS, 0.5 * FF ** (-0.5)),
    (ROW_EDGE, 0.5 * DE ** (-0.5)),
    (ROW_EUP, 0.5 * H ** (-0.5)),
    (ROW_EDOWN, 0.5 * DE ** (-0.5)),
    (ROW_NN, 0.5 * FFE ** (-0.5)),
]


class Cube:
    def __init__(self, size):
        self.size = size
        self.bits = size.bit_length() - 1
        assert size == 1 << self.bits
        up = list(range(1, self.bits))
        self.order = (up, up[::-1])

    def pairs(self, step):
        return [(i, i ^ (1 << self.order[i & 1][step])) for i in range(self.size)]

    def core_pairs(self):
        return [(i, i ^ 1) for i in range(self.size)]

    def gather(self, value, backward=False):
        me = lax.axis_index("dp")
        core = me & 1
        held = [((), value)]
        steps = range(self.bits - 1)
        for step in reversed(steps) if backward else steps:
            held += [(used + (step,), lax.ppermute(v, "dp", self.pairs(step))) for used, v in held]
        out = []
        for other in (0, 1):
            for used, v in held:
                masks = [sum(1 << self.order[c][s] for s in used) for c in (0, 1)]
                if other:
                    v = lax.ppermute(v, "dp", self.core_pairs())
                    source = (me ^ 1) ^ jnp.where(core == 0, masks[1], masks[0])
                else:
                    source = me ^ jnp.where(core == 0, masks[0], masks[1])
                out.append((v, source))
        return [v for v, _ in out], jnp.stack([s for _, s in out])

    def place(self, index, rows):
        core = index & 1
        at, size = core * (rows // 2), rows // 2
        for step in range(self.bits - 1):
            size //= 2
            low, high = self.order[0][step], self.order[1][step]
            at = at + jnp.where(core == 0, (index >> low) & 1, (index >> high) & 1) * size
        return at

    def reduce(self, value):
        me = lax.axis_index("dp")
        core = me & 1
        value = exchange_half(value, "dp", core, self.core_pairs())
        for step in range(self.bits - 1):
            low, high = self.order[0][step], self.order[1][step]
            bit = jnp.where(core == 0, (me >> low) & 1, (me >> high) & 1)
            value = exchange_half(value, "dp", bit, self.pairs(step))
        return value


def exchange_half(value, axis, bit, pairs):
    halves = value.reshape((2, value.shape[0] // 2) + value.shape[1:])
    keep = lax.dynamic_index_in_dim(halves, bit, 0, keepdims=False)
    send = lax.dynamic_index_in_dim(halves, 1 - bit, 0, keepdims=False)
    got = lax.ppermute(send, axis, pairs)
    return (keep.astype(F32) + got.astype(F32)).astype(BF)


def sum_over_row(value):
    size = lax.axis_size("row")
    me = lax.axis_index("row")
    bits = size.bit_length() - 1
    assert size == 1 << bits
    for b in range(bits):
        value = exchange_half(value, "row", (me >> b) & 1, [(i, i ^ (1 << b)) for i in range(size)])
    for b in reversed(range(bits)):
        got = lax.ppermute(value, "row", [(i, i ^ (1 << b)) for i in range(size)])
        mine = ((me >> b) & 1) == 0
        value = jnp.concatenate([jnp.where(mine, value, got), jnp.where(mine, got, value)])
    return value


def pick_from(table, index):
    slots = jnp.arange(table.shape[0], dtype=jnp.int32)
    return jnp.sum(jnp.where(index[:, None] == slots[None, :], table[None, :], 0), axis=1)


def per_device(
    small_nodes,
    small_edges,
    small_counts,
    big_nodes,
    big_edges,
    big_counts,
    small_node_cot,
    small_edge_cot,
    big_node_cot,
    big_edge_cot,
    master,
    first_moment,
    second_moment,
    owner,
    segment_rows,
    step_count,
):
    n_dp, n_row = lax.axis_size("dp"), lax.axis_size("row")
    cube = Cube(n_dp)
    share = big_nodes.shape[0] // n_row
    dm = Dims(small_nodes.shape[0], share)
    set_pad = round_up(SET_ROWS + 2, 16 * n_dp)
    me = lax.axis_index("dp")

    ends = jnp.cumsum(segment_rows)
    start_of = pick_from(ends - segment_rows, owner)
    length_of = pick_from(segment_rows, owner)
    my_start = lax.dynamic_index_in_dim(start_of, me, keepdims=False)
    my_length = lax.dynamic_index_in_dim(length_of, me, keepdims=False)
    parts, sources = cube.gather(shifted_segment(master, my_start % 16, my_length))
    part_start = pick_from(start_of, sources)
    part_end = part_start + pick_from(length_of, sources) - 1
    one, two = assemble(part_start // 16, part_end // 16, parts)

    def to_whole(v):
        return lax.all_to_all(v, "row", split_axis=0, concat_axis=1, tiled=True)

    def to_rows(v, lanes):
        v = v.reshape(share, NB, lanes)
        return lax.all_to_all(v, "row", split_axis=1, concat_axis=0, tiled=True)

    def flat2(v):
        return v.reshape(-1, v.shape[-1])

    whole_edges, whole_nodes = to_whole(big_edges), to_whole(big_nodes)
    whole_edge_cot, whole_node_cot = to_whole(big_edge_cot), to_whole(big_node_cot)
    own_counts = lax.dynamic_slice_in_dim(big_counts, lax.axis_index("row") * share, share)
    counts = jnp.concatenate([small_counts, own_counts])

    mid_nodes, mid_edges, kept = first_forward(
        dm,
        counts,
        one,
        (flat2(small_nodes), flat2(whole_nodes)),
        (flat2(small_edges), flat2(whole_edges)),
    )
    sno, bno, seo, beo, node_grad, edge_grad, grads_two, norms_two = second_layer(
        dm,
        set_pad,
        SET_ROWS % 16,
        counts,
        two,
        mid_nodes,
        mid_edges,
        (flat2(small_node_cot), flat2(whole_node_cot)),
        (flat2(small_edge_cot), flat2(whole_edge_cot)),
    )
    sng, bng, seg, beg, grads_one, norms_one = first_backward(
        dm, set_pad, 0, one, kept, node_grad, edge_grad
    )
    norm_grads = lax.psum(jnp.concatenate([norms_one, norms_two]), ("dp", "row"))
    blocks, places = [], []
    for value in (grads_one, grads_two):
        got, sources = cube.gather(sum_over_row(cube.reduce(value)), backward=True)
        blocks += got
        places.append(cube.place(sources, set_pad))
    step_value = step_count[0].astype(F32)
    scales = jnp.stack(
        [
            1.0 / (1.0 - jnp.power(F32(BETA_ONE), step_value)),
            1.0 / (1.0 - jnp.power(F32(BETA_TWO), step_value)),
        ]
    )
    new_master, new_first, new_second = adam(
        jnp.stack([my_start, my_length]),
        scales,
        jnp.concatenate(places).astype(jnp.int32),
        blocks,
        master,
        first_moment,
        second_moment,
    )
    return (
        sno.reshape(small_nodes.shape),
        seo.reshape(small_edges.shape),
        to_rows(bno, D),
        to_rows(beo, NB * DE),
        sng.reshape(small_nodes.shape),
        seg.reshape(small_edges.shape),
        to_rows(bng, D),
        to_rows(beg, NB * DE),
        new_master,
        new_first,
        new_second,
        norm_grads,
    )


def solution(mesh):
    both = P(("dp", "row"), None, None)
    rows = P("dp", "row", None)
    held = P("dp", None)
    in_specs = (
        both, both, P(("dp", "row")), rows, rows, P("dp"), both, both, rows, rows,
        held, held, held, P(), P(), P(),
    )
    out_specs = (both, both, rows, rows, both, both, rows, rows, held, held, held, P())
    return jax.shard_map(
        per_device, mesh=mesh, in_specs=in_specs, out_specs=out_specs, check_vma=False
    )
```

```python
import functools

import jax
import jax.numpy as jnp
from jax import lax
from jax.experimental import pallas as pl
from jax.experimental.pallas import tpu as pltpu
from jax.sharding import PartitionSpec as P

D = 512
H = 32
DE = 64
FF = 1024
FFE = 128
NS = 32
NB = 64
SET_ROWS = 16578
TOTAL_ROWS = 33156
NORM_EPS = 1e-05
BETA_ONE = 0.9
BETA_TWO = 0.95
WEIGHT_DECAY = 0.1
ADAM_EPS = 1e-08
MASK_FILL = -1e30
BF = jnp.bfloat16
F32 = jnp.float32
VMEM_LIMIT = 58 * 1024 * 1024
ROW_QKV, ROW_O, ROW_UP, ROW_DOWN = 0, 6144, 8192, 12288
ROW_BIAS, ROW_GATE, ROW_EDGE, ROW_EUP, ROW_EDOWN = 16384, 16400, 16416, 16432, 16496
ROW_NN, ROW_EN = 16560, 16576
SMALL_USED, SMALL_ROWS = SET_ROWS - ROW_BIAS, 256
BIAS, GATE, EDGE, EUP, EDOWN = 0, 16, 32, 48, 112
NN, EN = ROW_NN - ROW_BIAS, ROW_EN - ROW_BIAS
UPPER_ROWS = ROW_BIAS - ROW_O
GELU_C = 0.7978845608028654


def nn(a, b):
    return lax.dot_general(a, b, (((1,), (0,)), ((), ())), preferred_element_type=F32)


def nt(a, b):
    return lax.dot_general(a, b, (((1,), (1,)), ((), ())), preferred_element_type=F32)


def tn(a, b):
    return lax.dot_general(a, b, (((0,), (0,)), ((), ())), preferred_element_type=F32)


def iota(shape, axis):
    return lax.broadcasted_iota(jnp.int32, shape, axis)


def gelu_parts(u):
    u2 = u * u
    t = jnp.tanh(u * (GELU_C + (GELU_C * 0.044715) * u2))
    half = 0.5 + 0.5 * t
    value = u * half
    slope = half + value * (1.0 - t) * (GELU_C + (3.0 * GELU_C * 0.044715) * u2)
    return value, slope


def gelu_value(u):
    return u * (0.5 + 0.5 * jnp.tanh(u * (GELU_C + (GELU_C * 0.044715) * (u * u))))


def sigmoid(v):
    return 0.5 + 0.5 * jnp.tanh(0.5 * v)


def group_sum(v, first=16):
    while first < 128:
        v = v + pltpu.roll(v, first, 1)
        first *= 2
    return v


def group_max(v):
    for shift in (16, 32, 64):
        v = jnp.maximum(v, pltpu.roll(v, shift, 1))
    return v


def fold8(v):
    return jnp.sum(v.reshape(v.shape[0] // 8, 8, v.shape[1]), axis=0)


class Bucket:
    def __init__(self, graphs, slots, node0, edge0, count0):
        self.graphs, self.slots = graphs, slots
        self.node0, self.edge0, self.count0 = node0, edge0, count0
        self.rows = graphs * slots
        self.chunks = slots // 4
        self.pairs = slots // 8
        self.blocks = slots // 16
        self.edges = self.rows * self.chunks
        self.edge_lanes = slots * DE


class Dims:
    def __init__(self, small_graphs, big_graphs, parts):
        self.lower = round_up(ROW_O + SMALL_ROWS, 16 * parts)
        self.small = Bucket(small_graphs, NS, 0, 0, 0)
        self.big = Bucket(big_graphs, NB, self.small.rows, self.small.edges, small_graphs)
        self.buckets = (self.small, self.big)
        self.nodes = self.small.rows + self.big.rows
        self.edges = self.small.edges + self.big.edges
        self.scores = self.edges // 2
        self.blocks = sum(b.graphs * b.blocks for b in self.buckets)

    def each_pair(self, body):
        for bucket in self.buckets:
            two = 2 * bucket.rows

            @pl.loop(0, bucket.pairs, unroll=4)
            def _(i, bucket=bucket, two=two):
                body(
                    pl.ds(aligned(bucket.edge0 + i * two, 32), two),
                    pl.ds(aligned(bucket.edge0 // 2 + i * bucket.rows, 16), bucket.rows),
                )


def beside(v):
    half = v.shape[0] // 2
    return jnp.concatenate([v[:half], v[half:]], axis=1)


def below(v):
    return jnp.concatenate([v[:, :256], v[:, 256:]], axis=0)


def make_masks(scr):
    make_mean(scr)
    make_heads(scr)


def make_mean(scr):
    shape = (256, 256)
    same = (iota(shape, 0) >> 6) == (iota(shape, 1) >> 6)
    scr.mean[...] = jnp.where(same, 1.0 / DE, 0.0).astype(BF)


def make_heads(scr):
    shape = (256, 256)
    scr.head[...] = jnp.where((iota(shape, 0) >> 4) == (iota(shape, 1) & 15), 1.0, 0.0).astype(BF)
    shape = (16, 256)
    scr.pick[...] = jnp.where(iota(shape, 0) == (iota(shape, 1) >> 4), 1.0, 0.0).astype(BF)


def node_norm(v):
    centred = v - jnp.mean(v, axis=1, keepdims=True)
    r = lax.rsqrt(jnp.mean(centred * centred, axis=1, keepdims=True) + NORM_EPS)
    return centred * r, r


def node_norm_back(gdy, n, r):
    return r * (gdy - jnp.mean(gdy, axis=1, keepdims=True) - n * jnp.mean(gdy * n, axis=1, keepdims=True))


def aligned(value, by):
    return pl.multiple_of(value, by)


def block_of(bucket, t):
    g = t // bucket.blocks
    b = t % bucket.blocks
    rows = pl.ds(aligned(bucket.node0 + g * bucket.slots, 16), bucket.slots)
    keys = pl.ds(aligned(bucket.node0 + t * 16, 16), 16)
    pair_rows = [
        pl.ds(
            aligned(bucket.edge0 // 2 + (2 * b + c) * bucket.rows + g * bucket.slots, 16),
            bucket.slots,
        )
        for c in range(2)
    ]
    return rows, keys, pair_rows


def side(first, half):
    return slice(first + 256 * half, first + 256 * (half + 1))


def lanes(half):
    return slice(128 * half, 128 * (half + 1))


def expand(values, scr):
    return tn(values, scr.pick[...]).astype(BF) * scr.head[...]


def joined(ref, pair_rows, half):
    return jnp.concatenate([ref[r, lanes(half)] for r in pair_rows], axis=1)


def forward(dm, counts, w, io, res, scr):
    x = io.nodes[...].astype(F32)
    n, r = node_norm(x)
    res.node_n1[...] = n.astype(BF)
    res.node_r1[...] = jnp.broadcast_to(r, (dm.nodes, 128))
    hn = (n * w.nn[0:1, :] + w.nn[1:2, :]).astype(BF)
    res.qkv[...] = nn(hn, w.qkv[...]).astype(BF)

    @dm.each_pair
    def _(rows, pair):
        x = io.edges[rows, :]
        centred = x.astype(F32) - nn(x, scr.mean[...])
        r = lax.rsqrt(nn((centred * centred).astype(BF), scr.mean[...]) + NORM_EPS)
        n = centred * r
        res.edge_n1[rows, :] = n.astype(BF)
        res.edge_r1[rows, :] = r.astype(BF)
        xn = (n * w.en[0:1, :] + w.en[1:2, :]).astype(BF)
        both = nn(beside(xn), w.eg[...])
        scr.scores[pair, :] = both[:, :256]
        res.gate[pair, :] = both[:, 256:]

    t0 = 0
    for bucket in dm.buckets:
        @pl.loop(0, bucket.graphs * bucket.blocks, unroll=True)
        def _(t, bucket=bucket, t0=t0):
            rows, keys, pair_rows = block_of(bucket, t)
            for half in range(2):
                kb = expand(res.qkv[keys, side(512, half)], scr)
                scr.vbig[t0 + t, half] = expand(res.qkv[keys, side(1024, half)], scr)
                s = nn(res.qkv[rows, side(0, half)], kb) * 0.25
                for c in range(2):
                    scr.scores[pair_rows[c], lanes(half)] += s[:, lanes(c)]

        @pl.loop(0, bucket.rows // 32, unroll=True)
        def _(i, bucket=bucket):
            count = counts[bucket.count0 + i * 32 // bucket.slots]
            lane_key = iota((32, 128), 1) >> 4
            row = [
                pl.ds(aligned(bucket.edge0 // 2 + c * bucket.rows + i * 32, 32), 32)
                for c in range(bucket.pairs)
            ]
            for half in range(2):
                at = lanes(half)
                top = jnp.full((32, 128), MASK_FILL, F32)
                for c in range(bucket.pairs):
                    s = scr.scores[row[c], at]
                    res.low[row[c], at] = s.astype(BF)
                    top = jnp.maximum(top, jnp.where(lane_key < count - 8 * c, s, MASK_FILL))
                top = group_max(top)
                sums = jnp.zeros((32, 128), F32)
                for c in range(bucket.pairs):
                    s = jnp.where(lane_key < count - 8 * c, scr.scores[row[c], at], MASK_FILL)
                    e = jnp.exp(s - top)
                    sums = sums + e
                    scr.scores[row[c], at] = e
                inv = 1.0 / group_sum(sums)
                for c in range(bucket.pairs):
                    p = scr.scores[row[c], at] * inv
                    res.prob[row[c], at] = p.astype(BF)
                    scr.attn[row[c], at] = (p * sigmoid(res.gate[row[c], at])).astype(BF)

        @pl.loop(0, bucket.graphs, unroll=True)
        def _(g, bucket=bucket, t0=t0):
            for half in range(2):
                sums = None
                for b in range(bucket.blocks):
                    t = g * bucket.blocks + b
                    rows, _, pair_rows = block_of(bucket, t)
                    part = nt(joined(scr.attn, pair_rows, half), scr.vbig[t0 + t, half])
                    sums = part if sums is None else sums + part
                res.mixed[rows, side(0, half)] = sums.astype(BF)

        t0 += bucket.graphs * bucket.blocks

    y = io.nodes[...].astype(F32) + nn(res.mixed[...], w.o[...])
    n, r = node_norm(y)
    res.node_n2[...] = n.astype(BF)
    res.node_r2[...] = jnp.broadcast_to(r, (dm.nodes, 128))
    z = (n * w.nn[2:3, :] + w.nn[3:4, :]).astype(BF)
    u = nn(z, w.up[...])
    res.node_u[...] = u
    io.nodes_out[...] = (y + nn(gelu_value(u).astype(BF), w.down[...])).astype(BF)

    @dm.each_pair
    def _(rows, pair):
        m = io.edges[rows, :].astype(F32) + below(nn(res.low[pair, :], w.x[...]))
        high = m.astype(BF)
        rest = (m - high.astype(F32)).astype(BF)
        centred = m - nn(high, scr.mean[...]) - nn(rest, scr.mean[...])
        r = lax.rsqrt(nn((centred * centred).astype(BF), scr.mean[...]) + NORM_EPS)
        n = centred * r
        res.edge_n2[rows, :] = n.astype(BF)
        res.edge_r2[rows, :] = r.astype(BF)
        mn = (n * w.en[2:3, :] + w.en[3:4, :]).astype(BF)
        ua = nn(mn, w.a[...])
        io.edges_out[rows, :] = (m + nn(gelu_value(ua).astype(BF), w.b[...])).astype(BF)


def put_strided(flat, first, value, parts):
    for q in range(parts):
        flat[pl.ds(first + q, value.shape[0], stride=parts), :] = value[:, 128 * q : 128 * (q + 1)]


def back_ffn(dm, w, io, res, scr):
    flat = scr.upper
    gy = io.nodes_cot[...]
    act, slope = gelu_parts(res.node_u[...])
    du = (nt(gy, w.down[...]) * slope).astype(BF)
    put_strided(flat, ROW_DOWN - ROW_O, tn(act.astype(BF), gy), 4)
    n = res.node_n2[...].astype(F32)
    z = (n * w.nn[2:3, :] + w.nn[3:4, :]).astype(BF)
    put_strided(flat, ROW_UP - ROW_O, tn(z, du), 8)
    dz = nt(du, w.up[...])
    gain = jnp.sum(dz * n, axis=0, keepdims=True)
    bias = jnp.sum(dz, axis=0, keepdims=True)
    dy = gy.astype(F32) + node_norm_back(dz * w.nn[2:3, :], n, res.node_r2[:, 0:1])
    io.dy[...] = dy
    dyl = dy.astype(BF)
    put_strided(flat, 0, tn(res.mixed[...], dyl), 4)
    io.do[...] = nt(dyl, w.o[...]).astype(BF)
    for q in range(4):
        io.sums[q : q + 1, :] = gain[:, 128 * q : 128 * (q + 1)]
        io.sums[4 + q : 5 + q, :] = bias[:, 128 * q : 128 * (q + 1)]
    if hasattr(io, "upper"):
        io.upper[...] = flat[...].astype(BF)
    else:
        put_halves(flat, io.keep, io.send)


def put_halves(flat, keep, send):
    half = keep.shape[0]
    core = lax.axis_index("dp") & 1
    keep[...] = flat[pl.ds(aligned(core * half, 16), half), :].astype(BF)
    send[...] = flat[pl.ds(aligned((1 - core) * half, 16), half), :].astype(BF)


def back_edges(dm, w, io, res, scr):
    io.small[NN + 8 : NN + 16, :] = io.sums[...]
    scr.gb[...] = jnp.zeros((512, 256), F32)
    scr.ga[...] = jnp.zeros((256, 512), F32)
    scr.gx[...] = jnp.zeros((256, 512), F32)
    scr.en[...] = jnp.zeros((2, 8, 256), F32)

    @dm.each_pair
    def _(rows, pair):
        gx = io.edges_cot[rows, :]
        n = res.edge_n2[rows, :].astype(F32)
        mn = (n * w.en[2:3, :] + w.en[3:4, :]).astype(BF)
        act, slope = gelu_parts(nn(mn, w.a[...]))
        dua = (nt(gx, w.b[...]) * slope).astype(BF)
        scr.gb[...] += tn(act.astype(BF), gx)
        scr.ga[...] += tn(mn, dua)
        dmn = nt(dua, w.a[...])
        scr.en[0] += fold8(dmn * n)
        scr.en[1] += fold8(dmn)
        gdy = dmn * w.en[2:3, :]
        m1 = nn(gdy.astype(BF), scr.mean[...])
        m2 = nn((gdy * n).astype(BF), scr.mean[...])
        dmid = gx.astype(F32) + res.edge_r2[rows, :].astype(F32) * (gdy - m1 - n * m2)
        dml = dmid.astype(BF)
        io.dmid[rows, :] = dml
        dml = beside(dml)
        scr.gx[...] += tn(res.low[pair, :], dml)
        io.scores[pair, :] = nt(dml, w.x[...])

    up = scr.ga[0:64, 0:128]
    for k in range(1, 4):
        up = up + scr.ga[64 * k : 64 * (k + 1), 128 * k : 128 * (k + 1)]
    io.small[EUP : EUP + 64, :] = up
    sums = jnp.zeros((128, 128), F32)
    for k in range(4):
        part = scr.gb[128 * k : 128 * (k + 1), 128 * (k // 2) : 128 * (k // 2 + 1)]
        sums = sums + jnp.where(lane_group(128, 6) == k % 2, part, 0.0)
    fold_halves(sums, scr.tmp, io.small, EDOWN)
    sides = []
    for half in range(2):
        sums = jnp.zeros((16, 128), F32)
        for k in range(8):
            at = 128 * half + 16 * k
            part = scr.gx[at : at + 16, 128 * (k // 2) : 128 * (k // 2 + 1)]
            sums = sums + jnp.where(lane_group(16, 6) == k % 2, part, 0.0)
        sides.append(sums)
    fold_halves(jnp.concatenate(sides), scr.tmp, io.small, EDGE)
    put_edge_norm(scr.en, io.small, EN + 1)
    io.small[SMALL_USED:, :] = jnp.zeros((SMALL_ROWS - SMALL_USED, 128), F32)


def back_attention(dm, io, res, scr):
    t0 = 0
    for bucket in dm.buckets:
        @pl.loop(0, bucket.graphs * bucket.blocks, unroll=True)
        def _(t, bucket=bucket, t0=t0):
            rows, keys, pair_rows = block_of(bucket, t)
            for half in range(2):
                scr.vbig[t0 + t, half] = expand(res.qkv[keys, side(512, half)], scr)
                vb = expand(res.qkv[keys, side(1024, half)], scr)
                da = nn(io.do[rows, side(0, half)], vb)
                for c in range(2):
                    scr.da[pair_rows[c], lanes(half)] = da[:, lanes(c)]

        @pl.loop(0, bucket.rows // 32, unroll=True)
        def _(i, bucket=bucket):
            row = [
                pl.ds(aligned(bucket.edge0 // 2 + c * bucket.rows + i * 32, 32), 32)
                for c in range(bucket.pairs)
            ]
            for half in range(2):
                at = lanes(half)
                sums = jnp.zeros((32, 128), F32)
                for c in range(bucket.pairs):
                    p = res.prob[row[c], at].astype(F32)
                    s = sigmoid(res.gate[row[c], at])
                    scr.attn[row[c], at] = (p * s).astype(BF)
                    pt = p * scr.da[row[c], at] * s
                    scr.da[row[c], at] = pt
                    sums = sums + pt
                    io.dsg[row[c], lanes(2 + half)] = (pt * (1.0 - s)).astype(BF)
                sums = group_sum(sums)
                for c in range(bucket.pairs):
                    p = res.prob[row[c], at].astype(F32)
                    ds = scr.da[row[c], at] - p * sums + io.scores[row[c], at]
                    io.dsg[row[c], at] = ds.astype(BF)

        @pl.loop(0, bucket.graphs, unroll=True)
        def _(g, bucket=bucket, t0=t0):
            for half in range(2):
                sums = None
                for b in range(bucket.blocks):
                    t = g * bucket.blocks + b
                    rows, keys, pair_rows = block_of(bucket, t)
                    ds = joined(io.dsg, pair_rows, half)
                    part = nt(ds, scr.vbig[t0 + t, half])
                    sums = part if sums is None else sums + part
                    gk = tn(res.qkv[rows, side(0, half)], ds).astype(BF) * scr.head[...]
                    io.dqkv[keys, side(512, half)] = (nt(scr.pick[...], gk) * 0.25).astype(BF)
                    gv = tn(io.do[rows, side(0, half)], joined(scr.attn, pair_rows, half))
                    gv = gv.astype(BF) * scr.head[...]
                    io.dqkv[keys, side(1024, half)] = nt(scr.pick[...], gv).astype(BF)
                io.dqkv[rows, side(0, half)] = (sums * 0.25).astype(BF)

        t0 += bucket.graphs * bucket.blocks


def back_last(dm, w, io, res, scr):
    flat = scr.lower
    n = res.node_n1[...].astype(F32)
    hn = (n * w.nn[0:1, :] + w.nn[1:2, :]).astype(BF)
    for m in range(3):
        put_strided(flat, 2048 * m, tn(hn, io.dqkv[:, 512 * m : 512 * (m + 1)]), 4)
    dhn = nt(io.dqkv[...], w.qkv[...])
    gain = jnp.sum(dhn * n, axis=0, keepdims=True)
    bias = jnp.sum(dhn, axis=0, keepdims=True)
    small = flat.at[pl.ds(ROW_O, SMALL_ROWS), :]
    small[...] = io.small[...]
    for q in range(4):
        small[NN + q : NN + 1 + q, :] = gain[:, 128 * q : 128 * (q + 1)]
        small[NN + 4 + q : NN + 5 + q, :] = bias[:, 128 * q : 128 * (q + 1)]
    dx = io.dy[...] + node_norm_back(dhn * w.nn[0:1, :], n, res.node_r1[:, 0:1])
    io.nodes_grad[...] = dx.astype(BF)

    scr.geg[...] = jnp.zeros((512, 512), F32)
    scr.en[...] = jnp.zeros((2, 8, 256), F32)

    @dm.each_pair
    def _(rows, pair):
        dsg = io.dsg[pair, :]
        n = res.edge_n1[rows, :].astype(F32)
        xn = (n * w.en[0:1, :] + w.en[1:2, :]).astype(BF)
        scr.geg[...] += tn(beside(xn), dsg)
        dxn = below(nt(dsg, w.eg[...]))
        scr.en[0] += fold8(dxn * n)
        scr.en[1] += fold8(dxn)
        gdy = dxn * w.en[0:1, :]
        m1 = nn(gdy.astype(BF), scr.mean[...])
        m2 = nn((gdy * n).astype(BF), scr.mean[...])
        dx = io.dmid[rows, :].astype(F32) + res.edge_r1[rows, :].astype(F32) * (gdy - m1 - n * m2)
        io.edges_grad[rows, :] = dx.astype(BF)

    for which, first in ((0, BIAS), (1, GATE)):
        sides = []
        for half in range(2):
            sums = jnp.zeros((64, 128), F32)
            for k in range(8):
                part = scr.geg[64 * k : 64 * (k + 1), lanes(2 * which + half)]
                sums = sums + jnp.where(lane_group(64, 4) == k, part, 0.0)
            sides.append(group_sum(sums))
        scr.tmp[0:64, :] = jnp.where(lane_group(64, 4) % 2 == 0, sides[0], sides[1])
        rows = jnp.zeros((16, 128), F32)
        for b in range(4):
            rows = jnp.where(lane_group(16, 5) == b, scr.tmp[pl.ds(b, 16, stride=4), :], rows)
        small[first : first + 16, :] = rows
    put_edge_norm(scr.en, small, EN)
    end = ROW_O + SMALL_ROWS
    if dm.lower > end:
        flat[end:, :] = jnp.zeros((dm.lower - end, 128), F32)
    put_halves(flat, io.keep, io.send)


def lane_group(rows, bits):
    return iota((rows, 128), 1) >> bits


def fold_halves(sums, tmp, out, first):
    rows, half = sums.shape[0], sums.shape[0] // 2
    tmp[0:rows, :] = sums + pltpu.roll(sums, 64, 1)
    even = tmp[pl.ds(0, half, stride=2), :]
    odd = tmp[pl.ds(1, half, stride=2), :]
    out[first : first + half, :] = jnp.where(lane_group(half, 6) == 0, even, odd)


def put_edge_norm(sums, out, at):
    ones = []
    for t in range(2):
        both = jnp.sum(sums[t], axis=0, keepdims=True)
        one = both[:, :128] + both[:, 128:]
        ones.append(one + pltpu.roll(one, 64, 1))
    out[at : at + 1, :] = jnp.where(lane_group(1, 6) == 0, ones[0], ones[1])


def assemble_set(off, flat, tmp, w):
    def strided(first, rows, parts, out, lane0=0):
        for q in range(parts):
            out[:, lane0 + 128 * q : lane0 + 128 * (q + 1)] = flat[
                pl.ds(off + first + q, rows, stride=parts), :
            ].astype(BF)

    for m in range(3):
        strided(ROW_QKV + 2048 * m, 512, 4, w.qkv, 512 * m)
    strided(ROW_O, 512, 4, w.o)
    strided(ROW_UP, 512, 8, w.up)
    strided(ROW_DOWN, 1024, 4, w.down)
    w.eg[...] = jnp.zeros((512, 512), BF)
    w.x[...] = jnp.zeros((256, 512), BF)
    w.a[...] = jnp.zeros((256, 512), BF)
    w.b[...] = jnp.zeros((512, 256), BF)
    up = flat[pl.ds(off + ROW_EUP, 64), :].astype(BF)
    for k in range(4):
        w.a[64 * k : 64 * (k + 1), 128 * k : 128 * (k + 1)] = up

    def doubled(first, in_rows):
        v = flat[pl.ds(off + first, in_rows), :]
        other = pltpu.roll(v, 64, 1)
        low = lane_group(in_rows, 6) == 0
        tmp[pl.ds(0, in_rows, stride=2), :] = jnp.where(low, v, other)
        tmp[pl.ds(1, in_rows, stride=2), :] = jnp.where(low, other, v)
        return tmp[0 : 2 * in_rows, :]

    both = doubled(ROW_EDOWN, 64)
    for k in range(4):
        w.b[128 * k : 128 * (k + 1), 128 * (k // 2) : 128 * (k // 2 + 1)] = jnp.where(
            lane_group(128, 6) == k % 2, both, 0.0
        ).astype(BF)
    both = doubled(ROW_EDGE, 16)
    for half in range(2):
        for k in range(8):
            at = 128 * half + 16 * k
            w.x[at : at + 16, 128 * (k // 2) : 128 * (k // 2 + 1)] = jnp.where(
                lane_group(16, 6) == k % 2, both[16 * half : 16 * (half + 1)], 0.0
            ).astype(BF)
    for which, first in ((0, ROW_BIAS), (1, ROW_GATE)):
        v = flat[pl.ds(off + first, 16), :]
        for b in range(4):
            tmp[pl.ds(b, 16, stride=4), :] = group_sum(jnp.where(lane_group(16, 5) == b, v, 0.0), 32)
        both = tmp[0:64, :]
        even = lane_group(64, 4) % 2 == 0
        sides = (
            jnp.where(even, both, pltpu.roll(both, 16, 1)),
            jnp.where(even, pltpu.roll(both, 112, 1), both),
        )
        for half in range(2):
            for k in range(8):
                w.eg[64 * k : 64 * (k + 1), lanes(2 * which + half)] = jnp.where(
                    lane_group(64, 4) == k, sides[half], 0.0
                ).astype(BF)
    for t in range(4):
        for q in range(4):
            w.nn[t : t + 1, 128 * q : 128 * (q + 1)] = flat[pl.ds(off + ROW_NN + 4 * t + q, 1), :]
    for t in range(2):
        v = flat[pl.ds(off + ROW_EN + t, 1), :]
        other = pltpu.roll(v, 64, 1)
        gain = jnp.where(lane_group(1, 6) == 0, v, other)
        bias = jnp.where(lane_group(1, 6) == 0, other, v)
        for half in range(2):
            w.en[2 * t : 2 * t + 1, 128 * half : 128 * (half + 1)] = gain
            w.en[2 * t + 1 : 2 * t + 2, 128 * half : 128 * (half + 1)] = bias


class Group:
    def __init__(self, names, refs):
        for name, ref in zip(names, refs):
            setattr(self, name, ref)


WEIGHTS = {
    "qkv": ((D, 3 * D), BF),
    "o": ((D, D), BF),
    "up": ((D, FF), BF),
    "down": ((FF, D), BF),
    "eg": ((512, 512), BF),
    "x": ((256, 512), BF),
    "a": ((256, 512), BF),
    "b": ((512, 256), BF),
    "nn": ((4, D), F32),
    "en": ((4, 256), F32),
}


def residual_shapes(dm):
    return {
        "node_n1": ((dm.nodes, D), BF),
        "node_r1": ((dm.nodes, 128), F32),
        "qkv": ((dm.nodes, 3 * D), BF),
        "mixed": ((dm.nodes, D), BF),
        "node_n2": ((dm.nodes, D), BF),
        "node_r2": ((dm.nodes, 128), F32),
        "node_u": ((dm.nodes, FF), F32),
        "edge_n1": ((dm.edges, 256), BF),
        "edge_r1": ((dm.edges, 256), BF),
        "gate": ((dm.scores, 256), F32),
        "low": ((dm.scores, 256), BF),
        "prob": ((dm.scores, 256), BF),
        "edge_n2": ((dm.edges, 256), BF),
        "edge_r2": ((dm.edges, 256), BF),
    }


def mean_shapes():
    return {"mean": ((256, 256), BF)}


def head_shapes():
    return {"head": ((256, 256), BF), "pick": ((16, 256), BF)}


def mask_shapes():
    return {**mean_shapes(), **head_shapes()}


def forward_scratch(dm):
    return {
        "scores": ((dm.scores, 256), F32),
        "attn": ((dm.scores, 256), BF),
        "vbig": ((dm.blocks, 2, 256, 256), BF),
    }


def ffn_shapes(dm, halves):
    half = ((UPPER_ROWS // 2, 128), BF)
    grads = {"keep": half, "send": half} if halves else {"upper": ((UPPER_ROWS, 128), BF)}
    return {
        "dy": ((dm.nodes, D), F32),
        "do": ((dm.nodes, D), BF),
        "sums": ((8, 128), F32),
        **grads,
    }


def edge_shapes(dm):
    return {
        "dmid": ((dm.edges, 256), BF),
        "scores": ((dm.scores, 256), F32),
        "small": ((SMALL_ROWS, 128), F32),
    }


def attention_shapes(dm):
    return {"dsg": ((dm.scores, 512), BF), "dqkv": ((dm.nodes, 3 * D), BF)}


def ffn_scratch():
    return {"upper": ((UPPER_ROWS, 128), F32)}


def edge_scratch():
    return {
        "gb": ((512, 256), F32),
        "ga": ((256, 512), F32),
        "gx": ((256, 512), F32),
        "en": ((2, 8, 256), F32),
        "tmp": ((128, 128), F32),
    }


def attention_scratch(dm):
    return {
        "attn": ((dm.scores, 256), BF),
        "vbig": ((dm.blocks, 2, 256, 256), BF),
        "da": ((dm.scores, 256), F32),
    }


def last_scratch(dm):
    return {
        "geg": ((512, 512), F32),
        "en": ((2, 8, 256), F32),
        "tmp": ((128, 128), F32),
        "lower": ((dm.lower, 128), F32),
    }


def structs(shapes):
    return [jax.ShapeDtypeStruct(s, t) for s, t in shapes.values()]


def vmem(shapes):
    return [pltpu.VMEM(s, t) for s, t in shapes.values()]


def whole(n):
    return [pl.BlockSpec(memory_space=pltpu.VMEM)] * n


def split(refs, *groups):
    out, at = [], 0
    for names in groups:
        out.append(Group(names, refs[at : at + len(names)]))
        at += len(names)
    assert at == len(refs)
    return out


def edge_copies(dm, small, big, big_lane, stacked, sems, out):
    copies = []
    for bucket, ref, lane in ((dm.small, small, 0), (dm.big, big, big_lane)):
        for c in range(bucket.chunks):
            a = ref.at[:, pl.ds(lane + 256 * c, 256)]
            b = stacked.at[pl.ds(bucket.edge0 + c * bucket.rows, bucket.rows), :]
            src, dst = (b, a) if out else (a, b)
            copies.append(pltpu.make_async_copy(src, dst, sems.at[len(copies)]))
    return copies


def node_copies(dm, small, big, big_lane, nodes, sems, at, out):
    copies = []
    for bucket, ref in ((dm.small, small), (dm.big, big.at[:, pl.ds(big_lane, D)])):
        b = nodes.at[pl.ds(bucket.node0, bucket.rows), :]
        src, dst = (b, ref) if out else (ref, b)
        copies.append(pltpu.make_async_copy(src, dst, sems.at[at + len(copies)]))
    return copies


def copy_sems(dm):
    return pltpu.SemaphoreType.DMA((dm.small.chunks + dm.big.chunks + 2,))


def all_copies(dm, small_nodes, small_edges, big, edge_lane, node_lane, nodes, edges, sems, out):
    copies = edge_copies(dm, small_edges, big, edge_lane, edges, sems, out)
    return node_copies(dm, small_nodes, big, node_lane, nodes, sems, len(copies), out) + copies


def start(copies):
    for c in copies:
        c.start()


def wait(copies):
    for c in copies:
        c.wait()


HBM = pl.BlockSpec(memory_space=pl.ANY)
SMEM = pl.BlockSpec(memory_space=pltpu.SMEM)
EDGE_LANES = NB * DE
IN_LANES = 2 * EDGE_LANES + 2 * D
OUT_LANES = EDGE_LANES + D


def compiler_params():
    return pltpu.CompilerParams(vmem_limit_bytes=VMEM_LIMIT)


def cost(us):
    return pl.CostEstimate(flops=0, bytes_accessed=int(us * 3.4e6), transcendentals=0)


def take(group, names):
    return [getattr(group, k) for k in names]


NODE_BACK = ("node_n2", "node_r2", "node_u", "mixed")
EDGE_BACK = ("edge_n2", "edge_r2", "low")
ATTENTION_BACK = ("qkv", "prob", "gate")
LAST_BACK = ("node_n1", "node_r1", "edge_n1", "edge_r1")
W_NODE = ("o", "up", "down", "nn")
W_EDGE = ("x", "a", "b", "en")
W_LAST = ("qkv", "eg", "nn", "en")


def kernel(body, inputs, out, scr, us, counts=None, hbm_in=0, hbm_out=(), sems=()):
    smem = [] if counts is None else [counts]
    return Group(
        out,
        pl.pallas_call(
            body,
            out_shape=structs(out),
            in_specs=[SMEM] * len(smem) + whole(len(inputs) - hbm_in) + [HBM] * hbm_in,
            out_specs=[HBM if k in hbm_out else pl.BlockSpec(memory_space=pltpu.VMEM) for k in out],
            scratch_shapes=vmem(scr) + list(sems),
            compiler_params=compiler_params(),
            cost_estimate=cost(us),
        )(*smem, *inputs),
    )


def first_forward(dm, counts, weights, small_nodes, small_edges, big):
    res = residual_shapes(dm)
    out = {"nodes_out": ((dm.nodes, D), BF), "edges_out": ((dm.edges, 256), BF), **res}
    scr = {
        **mask_shapes(),
        **forward_scratch(dm),
        "nodes": ((dm.nodes, D), BF),
        "edges": ((dm.edges, 256), BF),
    }

    def body(*refs):
        counts_ref, refs, sems = refs[0], refs[1:-1], refs[-1]
        w, src, dst, s = split(refs, WEIGHTS, ("sn", "se", "big"), out, scr)
        copies = all_copies(
            dm, src.sn, src.se, src.big, 0, 2 * EDGE_LANES, s.nodes, s.edges, sems, False
        )
        start(copies)
        make_masks(s)
        io = Group(
            ("nodes", "edges", "nodes_out", "edges_out"),
            (s.nodes, s.edges, dst.nodes_out, dst.edges_out),
        )
        wait(copies)
        forward(dm, counts_ref, w, io, dst, s)

    inputs = take(weights, WEIGHTS) + [small_nodes, small_edges, big]
    got = kernel(body, inputs, out, scr, 38, counts, 3, (), [copy_sems(dm)])
    return got.nodes_out, got.edges_out, got


def second_forward(dm, counts, weights, nodes, edges, small_node_cot, small_edge_cot, big):
    res, ffn = residual_shapes(dm), ffn_shapes(dm, False)
    whole_outs = {
        "sno": ((dm.small.rows, D), BF),
        "seo": ((dm.small.rows, dm.small.edge_lanes), BF),
        "bout": ((dm.big.rows, OUT_LANES), BF),
    }
    node_res = [k for k in res if k in NODE_BACK]
    kept = {k: v for k, v in res.items() if k not in NODE_BACK}
    out = {**whole_outs, "edge_cot": ((dm.edges, 256), BF), **kept, **ffn}
    scr = {
        **mask_shapes(),
        **forward_scratch(dm),
        **ffn_scratch(),
        **{k: res[k] for k in node_res},
        "nodes_out": ((dm.nodes, D), BF),
        "edges_out": ((dm.edges, 256), BF),
        "node_cot": ((dm.nodes, D), BF),
    }

    def body(*refs):
        counts_ref, refs, in_sems, out_sems = refs[0], refs[1:-2], refs[-2], refs[-1]
        w, src, dst, s = split(refs, WEIGHTS, ("nodes", "edges", "snc", "sec", "big"), out, scr)
        copies = all_copies(
            dm, src.snc, src.sec, src.big, EDGE_LANES, 2 * EDGE_LANES + D, s.node_cot, dst.edge_cot, in_sems, False
        )
        start(copies)
        make_masks(s)
        every = Group(
            [*kept, *node_res], [getattr(dst, k) for k in kept] + [getattr(s, k) for k in node_res]
        )
        io = Group(
            ("nodes", "edges", "nodes_out", "edges_out"),
            (src.nodes, src.edges, s.nodes_out, s.edges_out),
        )
        forward(dm, counts_ref, w, io, every, s)
        outgoing = all_copies(
            dm, dst.sno, dst.seo, dst.bout, 0, EDGE_LANES, s.nodes_out, s.edges_out, out_sems, True
        )
        start(outgoing)
        wait(copies)
        back_ffn(dm, w, Group(("nodes_cot", *ffn), (s.node_cot, *take(dst, ffn))), every, s)
        wait(outgoing)

    inputs = take(weights, WEIGHTS) + [nodes, edges, small_node_cot, small_edge_cot, big]
    got = kernel(body, inputs, out, scr, 46, counts, 3, tuple(whole_outs), [copy_sems(dm)] * 2)
    return got.sno, got.seo, got.bout, None, got.edge_cot, got, got


def between(dm, weights_two, weights_one, kept_two, kept_one, ffn_two, edges_cot):
    half = {k: ((dm.lower // 2, 128), BF) for k in ("keep", "send")}
    ffn = ffn_shapes(dm, True)
    out = {
        "edges_grad": ((dm.edges, 256), BF),
        **{"two_" + k: v for k, v in half.items()},
        **ffn,
    }
    edge, att = edge_shapes(dm), attention_shapes(dm)
    scr = {
        **mask_shapes(),
        **edge_scratch(),
        **attention_scratch(dm),
        **last_scratch(dm),
        **ffn_scratch(),
        **edge,
        **att,
        "nodes_grad": ((dm.nodes, D), BF),
    }
    w_two = ("qkv", *W_EDGE, "eg", "nn")
    res_two = EDGE_BACK + ATTENTION_BACK + LAST_BACK

    def body(*refs):
        w, w_one, res, res_one, src, dst, s = split(
            refs, w_two, W_NODE, res_two, NODE_BACK, ("edges_cot", "sums", "do", "dy"), out, scr
        )
        make_masks(s)
        io = Group(
            ("edges_cot", "sums", "do", "dy", *edge, *att, "nodes_grad", "edges_grad", "keep", "send"),
            (src.edges_cot, src.sums, src.do, src.dy, *take(s, edge), *take(s, att))
            + (s.nodes_grad, dst.edges_grad, dst.two_keep, dst.two_send),
        )
        back_edges(dm, w, io, res, s)
        back_attention(dm, io, res, s)
        back_last(dm, w, io, res, s)
        back_ffn(dm, w_one, Group(("nodes_cot", *ffn), (s.nodes_grad, *take(dst, ffn))), res_one, s)

    inputs = take(weights_two, w_two) + take(weights_one, W_NODE)
    inputs += take(kept_two, res_two) + take(kept_one, NODE_BACK)
    inputs += [edges_cot, ffn_two.sums, ffn_two.do, ffn_two.dy]
    return kernel(body, inputs, out, scr, 45)


def call_edges(dm, weights, kept, ffn, edges_cot):
    out, scr = edge_shapes(dm), {**mean_shapes(), **edge_scratch()}

    def body(*refs):
        w, res, src, dst, s = split(refs, W_EDGE, EDGE_BACK, ("edges_cot", "sums"), out, scr)
        make_mean(s)
        io = Group(("edges_cot", "sums", *out), (src.edges_cot, src.sums, *take(dst, out)))
        back_edges(dm, w, io, res, s)

    inputs = take(weights, W_EDGE) + take(kept, EDGE_BACK) + [edges_cot, ffn.sums]
    return kernel(body, inputs, out, scr, 16)


def call_attention(dm, kept, ffn, edge):
    out, scr = attention_shapes(dm), {**head_shapes(), **attention_scratch(dm)}

    def body(*refs):
        res, src, dst, s = split(refs, ATTENTION_BACK, ("do", "scores"), out, scr)
        make_heads(s)
        back_attention(dm, Group(("do", "scores", *out), (src.do, src.scores, *take(dst, out))), res, s)

    return kernel(body, take(kept, ATTENTION_BACK) + [ffn.do, edge.scores], out, scr, 14)


def call_last(dm, weights, kept, ffn, edge, att):
    half = {k: ((dm.lower // 2, 128), BF) for k in ("keep", "send")}
    outs = {
        "sng": ((dm.small.rows, D), BF),
        "seg": ((dm.small.rows, dm.small.edge_lanes), BF),
        "bgrad": ((dm.big.rows, OUT_LANES), BF),
    }
    out = {**outs, **half}
    scr = {
        **mean_shapes(),
        **last_scratch(dm),
        "nodes_grad": ((dm.nodes, D), BF),
        "edges_grad": ((dm.edges, 256), BF),
    }
    given = ("dy", "dmid", "small", "dsg", "dqkv")

    def body(*refs):
        refs, sems = refs[:-1], refs[-1]
        w, res, src, dst, s = split(refs, W_LAST, LAST_BACK, given, out, scr)
        make_mean(s)
        io = Group(
            (*given, "nodes_grad", "edges_grad", "keep", "send"),
            (*take(src, given), s.nodes_grad, s.edges_grad, dst.keep, dst.send),
        )
        back_last(dm, w, io, res, s)
        outgoing = all_copies(
            dm, dst.sng, dst.seg, dst.bgrad, 0, EDGE_LANES, s.nodes_grad, s.edges_grad, sems, True
        )
        start(outgoing)
        wait(outgoing)

    inputs = take(weights, W_LAST) + take(kept, LAST_BACK)
    inputs += [ffn.dy, edge.dmid, edge.small, att.dsg, att.dqkv]
    got = kernel(body, inputs, out, scr, 13, hbm_out=tuple(outs), sems=[copy_sems(dm)])
    return take(got, out)


def round_up(value, by):
    return -(-value // by) * by


def segment_of(owner, rows, index, count):
    name = owner[index]
    first = jnp.int32(0)
    for t in range(count):
        first = first + jnp.where(t < name, rows[t], 0)
    return first, rows[name]


def shifted_segment(owner, segment_rows, master):
    held = master.shape[0]
    count = owner.shape[0]
    padded = round_up(held + 15, 16)
    step = 1664

    def body(owner_ref, rows_ref, src, dst, window):
        i = pl.program_id(0)
        first, length = segment_of(owner_ref, rows_ref, lax.axis_index("dp"), count)
        shift = first % 16

        @pl.when(i == 0)
        def _():
            window[0:16, :] = jnp.zeros((16, 128), F32)

        window[16:, :] = src[...]
        moved = window[pl.ds(16 - shift, step), :]
        index = i * step - shift + iota((step, 128), 0)
        live = (index >= 0) & (index < length)
        dst[...] = jnp.where(live, moved, 0.0).astype(BF)
        window[0:16, :] = window[step : step + 16, :]

    return pl.pallas_call(
        body,
        grid=(pl.cdiv(padded, step),),
        out_shape=jax.ShapeDtypeStruct((padded, 128), BF),
        in_specs=[
            SMEM,
            SMEM,
            pl.BlockSpec((step, 128), lambda i: (jnp.minimum(i, (held - 1) // step), 0)),
        ],
        out_specs=pl.BlockSpec((step, 128), lambda i: (i, 0)),
        scratch_shapes=[pltpu.VMEM((step + 16, 128), F32)],
        compiler_params=compiler_params(),
    )(owner, segment_rows, master)


def assemble(cube, owner, segment_rows, parts, sources):
    count = len(parts)
    padded = parts[0].shape[0]
    bits = (padded // 16).bit_length()
    tiles = -(-TOTAL_ROWS // 16)
    set_tiles = -(-(SET_ROWS + 2) // 16)
    out = {**{"one_" + k: v for k, v in WEIGHTS.items()}, **{"two_" + k: v for k, v in WEIGHTS.items()}}

    def body(owner_ref, rows_ref, *refs):
        srcs, refs = refs[:count], refs[count:]
        dsts, (rows, flat, tmp, edge, sems, edge_sems) = refs[: len(out)], refs[len(out) :]
        me = lax.axis_index("dp")
        spans = []
        for i in range(count):
            first, length = segment_of(owner_ref, rows_ref, cube.source(me, sources[i]), count)
            spans.append((first // 16, (first + length - 1) // 16))

        def each(act):
            for i, (a, b) in enumerate(spans):
                inner = b - a - 1
                for bit in range(bits):
                    size = 16 << bit
                    if size > padded:
                        continue
                    done = (inner >> (bit + 1)) << (bit + 1)

                    @pl.when((inner > 0) & (((inner >> bit) & 1) == 1))
                    def _(i=i, a=a, done=done, size=size, bit=bit):
                        act(
                            pltpu.make_async_copy(
                                srcs[i].at[pl.ds(aligned(16 * (1 + done), 16), size), :],
                                rows.at[pl.ds(aligned(16 * (a + 1 + done), 16), size), :],
                                sems.at[i, bit],
                            )
                        )

                act(pltpu.make_async_copy(srcs[i].at[pl.ds(0, 16), :], edge.at[2 * i], edge_sems.at[2 * i]))
                act(
                    pltpu.make_async_copy(
                        srcs[i].at[pl.ds(aligned(16 * (b - a), 16), 16), :],
                        edge.at[2 * i + 1],
                        edge_sems.at[2 * i + 1],
                    )
                )

        each(lambda c: c.start())
        each(lambda c: c.wait())
        tile = lambda t: pl.ds(aligned(16 * t, 16), 16)
        for a, b in spans:
            rows[tile(a), :] = jnp.zeros((16, 128), BF)
            rows[tile(b), :] = jnp.zeros((16, 128), BF)
        for i, (a, b) in enumerate(spans):
            rows[tile(a), :] += edge[2 * i]

            @pl.when(b != a)
            def _(i=i, b=b):
                rows[tile(b), :] += edge[2 * i + 1]

        for which in range(2):
            base = which * (SET_ROWS // 16) * 16
            flat[...] = rows[pl.ds(base, 16 * set_tiles), :].astype(F32)
            w = Group(WEIGHTS, dsts[which * len(WEIGHTS) : (which + 1) * len(WEIGHTS)])
            assemble_set(which * (SET_ROWS % 16), flat, tmp, w)

    got = pl.pallas_call(
        body,
        out_shape=structs(out),
        in_specs=[SMEM] * 2 + [HBM] * count,
        out_specs=whole(len(out)),
        scratch_shapes=[
            pltpu.VMEM((16 * tiles, 128), BF),
            pltpu.VMEM((16 * set_tiles, 128), F32),
            pltpu.VMEM((128, 128), F32),
            pltpu.VMEM((2 * count, 16, 128), BF),
            pltpu.SemaphoreType.DMA((count, bits)),
            pltpu.SemaphoreType.DMA((2 * count,)),
        ],
        compiler_params=compiler_params(),
        cost_estimate=cost(10),
    )(owner, segment_rows, *parts)
    return Group(WEIGHTS, got[: len(WEIGHTS)]), Group(WEIGHTS, got[len(WEIGHTS) :])


def adam(n_row, lower, owner, segment_rows, scales, whole_upper, blocks, master, first, second):
    held = master.shape[0]
    step = 1040
    front = step + 16
    count = len(blocks)
    n_dp = owner.shape[0]
    set_rows = ROW_BIAS - ROW_O + lower
    total_rows = front + set_rows + step + 32
    ways = 3 * n_row
    arrivals = sum(len(keys) for _, _, keys, _ in blocks)

    def body(owner_ref, rows_ref, scale_ref, *refs):
        upper, srcs, refs = refs[0], refs[1 : 1 + count], refs[1 + count :]
        master_ref, first_ref, second_ref, o_master, o_first, o_second, o_norms, rows, window, grad, rate, sems, upper_sem = refs
        i = pl.program_id(0)
        me, row = lax.axis_index("dp"), lax.axis_index("row")
        begin, length = segment_of(owner_ref, rows_ref, me, n_dp)

        @pl.when(i == 0)
        def _():
            def each(act):
                copy = pltpu.make_async_copy(
                    upper, rows.at[1, pl.ds(front + ROW_O, UPPER_ROWS), :], upper_sem
                )
                pl.when(begin + length > SET_ROWS + ROW_O)(functools.partial(act, copy))
                every = [
                    (k, core, key, n, sections)
                    for k, (_, core, keys, sections) in enumerate(blocks)
                    for n, key in enumerate(keys)
                ]
                for at_sem, (k, core, key, n, sections) in enumerate(every):
                    mine = (me ^ core) & 1
                    source = me ^ core ^ jnp.where(mine == 0, key[0], key[1])
                    stride = sum(size for _, _, size in sections)
                    offset = n * stride * n_row
                    for number, (which, part, size) in enumerate(sections):
                        block = ((source & 1) * (n_dp // 2) + (source >> 1)) * size * n_row
                        for z in range(n_row):
                            at = block + (row ^ z) * size
                            dest = at + ROW_O if part else jnp.where(at >= ROW_O, at - ROW_O + ROW_BIAS, at)
                            wanted = (dest + which * SET_ROWS < begin + length) & (
                                dest + size + which * SET_ROWS > begin
                            )
                            wanted = wanted | (dest + size > ROW_NN)
                            lies = z * stride + offset

                            def move(frm, extent, to, way, k=k, which=which, at_sem=at_sem):
                                act(
                                    pltpu.make_async_copy(
                                        srcs[k].at[pl.ds(frm, extent), :],
                                        rows.at[which, pl.ds(aligned(front + to, 16), extent), :],
                                        sems.at[at_sem, way],
                                    )
                                )

                            cut = 0 if part else ROW_O % size
                            way = number * n_row + z
                            if not cut:
                                pl.when(wanted)(functools.partial(move, lies, size, dest, way))
                                continue
                            split_here = (at < ROW_O) & (at + size > ROW_O)
                            pl.when(wanted & jnp.logical_not(split_here))(
                                functools.partial(move, lies, size, dest, way)
                            )

                            @pl.when(split_here)
                            def _(move=move, lies=lies, size=size, at=at, cut=cut, way=way, z=z):
                                move(lies, cut, at, way)
                                move(lies + cut, size - cut, ROW_BIAS, 2 * n_row + z)

                        offset += size

            each(lambda c: c.start())
            each(lambda c: c.wait())
            for which in range(2):
                v = rows[which, front + ROW_NN : front + ROW_NN + 32, :].astype(F32)
                for t in range(4):
                    for q in range(4):
                        o_norms[4 * which + t : 4 * which + t + 1, 128 * q : 128 * (q + 1)] = v[
                            4 * t + q : 4 * t + q + 1, :
                        ]
                for t in range(2):
                    both = v[16 + t : 17 + t, :]
                    at = 4 * which + 2 * t
                    o_norms[at : at + 1, 512:576] = both[:, 0:64]
                    o_norms[at + 1 : at + 2, 512:576] = pltpu.roll(both, 64, 1)[:, 0:64]

        low = begin + i * step
        high = low + step
        some = i * step < length

        @pl.when(jnp.logical_not(some))
        def _():
            o_master[...] = master_ref[...]
            o_first[...] = first_ref[...]
            o_second[...] = second_ref[...]

        @pl.when(some)
        def _():
            def shifted(which):
                local = low - which * SET_ROWS + front
                shift = local % 16
                window[...] = rows[which, pl.ds(aligned(local - shift, 16), step + 16), :].astype(F32)
                return window[pl.ds(shift, step), :]

            index = iota((step, 128), 0)

            @pl.when(low < SET_ROWS)
            def _():
                grad[...] = shifted(0)

            @pl.when(low >= SET_ROWS)
            def _():
                grad[...] = shifted(1)

            @pl.when((low < SET_ROWS) & (high > SET_ROWS))
            def _():
                grad[...] = jnp.where(index + low >= SET_ROWS, shifted(1), grad[...])

            at = index + low
            at = jnp.where(at >= SET_ROWS, at - SET_ROWS, at)
            a, b, c = RATES[0][1], RATES[1][1], RATES[3][1]
            far = jnp.where(at < ROW_DOWN, a, c)
            rate[...] = jnp.where(at < ROW_O, a, jnp.where(at < ROW_UP, b, far))
            near = (low < SET_ROWS) & (high > ROW_BIAS)

            @pl.when(near | (high > SET_ROWS + ROW_BIAS))
            def _():
                value = jnp.full((step, 128), 0.25, F32)
                for end, one in reversed(RATES[4:]):
                    value = jnp.where(at < end, one, value)
                rate[...] = jnp.where(at < ROW_BIAS, rate[...], value)

            g = grad[...]
            p, m, v = master_ref[...], first_ref[...], second_ref[...]
            m_new = BETA_ONE * m + (1.0 - BETA_ONE) * g
            v_new = BETA_TWO * v + (1.0 - BETA_TWO) * g * g
            move = (m_new * scale_ref[0]) / (jnp.sqrt(v_new * scale_ref[1]) + ADAM_EPS)
            live = index < length - i * step
            o_master[...] = jnp.where(live, p - rate[...] * (move + WEIGHT_DECAY * p), p)
            o_first[...] = jnp.where(live, m_new, m)
            o_second[...] = jnp.where(live, v_new, v)

    spec = pl.BlockSpec((step, 128), lambda i: (i, 0))
    shape = jax.ShapeDtypeStruct((held, 128), F32)
    return pl.pallas_call(
        body,
        grid=(pl.cdiv(held, step),),
        out_shape=[shape] * 3 + [jax.ShapeDtypeStruct((8, D + DE), F32)],
        in_specs=[SMEM] * 3 + [HBM] * (count + 1) + [spec] * 3,
        out_specs=[spec] * 3 + [pl.BlockSpec((8, D + DE), lambda i: (0, 0))],
        scratch_shapes=[
            pltpu.VMEM((2, total_rows, 128), BF),
            pltpu.VMEM((step + 16, 128), F32),
            pltpu.VMEM((step, 128), F32),
            pltpu.VMEM((step, 128), F32),
            pltpu.SemaphoreType.DMA((arrivals, ways)),
            pltpu.SemaphoreType.DMA(()),
        ],
        compiler_params=compiler_params(),
        cost_estimate=cost(10),
    )(owner, segment_rows, scales, whole_upper, *[b[0] for b in blocks], master, first, second)


RATES = [
    (ROW_O, 0.5 * D ** (-0.5)),
    (ROW_UP, 2.0 * D ** (-0.5)),
    (ROW_DOWN, 0.5 * D ** (-0.5)),
    (ROW_BIAS, 0.5 * FF ** (-0.5)),
    (ROW_EDGE, 0.5 * DE ** (-0.5)),
    (ROW_EUP, 0.5 * H ** (-0.5)),
    (ROW_EDOWN, 0.5 * DE ** (-0.5)),
    (ROW_NN, 0.5 * FFE ** (-0.5)),
]


class Cube:
    def __init__(self, size):
        self.size = size
        self.bits = size.bit_length() - 1
        assert size == 1 << self.bits
        up = list(range(1, self.bits))
        self.order = (up, up[::-1])

    def pairs(self, step):
        return [(i, i ^ (1 << self.order[i & 1][step])) for i in range(self.size)]

    def core_pairs(self):
        return [(i, i ^ 1) for i in range(self.size)]

    def source(self, me, key):
        other, used = key
        even, odd = [sum(1 << self.order[c][s] for s in used) for c in (0, 1)]
        if other:
            even, odd = odd, even
        return me ^ jnp.where(me & 1 == 0, even, odd) ^ other

    def gather(self, value, also):
        steps = range(self.bits - 1)
        new, done = [((), value)], []
        while new:
            sent = []
            for used, v in new:
                done.append(((0, used), v))
                for step in steps:
                    if not used or step > used[-1]:
                        sent.append((0, used + (step,), lax.ppermute(v, "dp", self.pairs(step))))
            for used, v in new:
                sent.append((1, used, lax.ppermute(v, "dp", self.core_pairs())))
            moved, also = lax.optimization_barrier(([v for _, _, v in sent], also))
            new = []
            for (other, used, _), v in zip(sent, moved):
                if other:
                    done.append(((1, used), v))
                else:
                    new.append((used, v))
        return done, also


def total(values):
    out = values[0].astype(F32)
    for v in values[1:]:
        out = out + v.astype(F32)
    return out.astype(BF)


class Chain:
    def __init__(self, cube, direct, *halves):
        self.cube, self.direct = cube, direct
        self.kept = [k for k, _ in halves]
        self.value = [s for _, s in halves]
        self.step, self.done = 0, False
        self.sides = lax.axis_size("dp") // 2
        self.rows = lax.axis_size("row")

    def swap(self, value):
        return lax.ppermute(value, "dp", [(i, i ^ 1) for i in range(2 * self.sides)])

    def to_chip(self, value, k):
        return lax.ppermute(value, "dp", [(i, i ^ (k << 1)) for i in range(2 * self.sides)])

    def to_row(self, value, k):
        return lax.ppermute(value, "row", [(i, i ^ k) for i in range(self.rows)])

    def scatter(self, index, count, send):
        def at(k):
            parts = [v.reshape(count, v.shape[0] // count, 128) for v in self.value]
            parts = [lax.dynamic_index_in_dim(v, index ^ k, 0, keepdims=False) for v in parts]
            return jnp.concatenate(parts) if len(parts) > 1 else parts[0]

        self.sizes = [v.shape[0] // count for v in self.value]
        self.kept = at(0)
        return [send(at(k), k) for k in range(1, count)]

    def launch(self):
        self.step += 1
        if self.step == 1:
            return [self.swap(v) for v in self.value]
        if self.step == 2:
            return self.scatter(lax.axis_index("dp") >> 1, self.sides, self.to_chip)
        if self.step == 3:
            return self.scatter(lax.axis_index("row"), self.rows, self.to_row)
        if self.step == 4:
            return [self.to_row(self.value, k) for k in range(1, self.rows)]
        if not self.spread():
            return [self.swap(self.value)]
        if self.direct:
            return [self.to_chip(self.value, k) for k in range(1, self.sides)]
        return [lax.ppermute(self.value, "dp", self.cube.pairs(self.step - 5))]

    def spread(self):
        return self.step < 6 if self.direct else self.step < 5 + self.cube.bits - 1

    def land(self, got):
        if self.step == 1:
            self.value = [total(pair) for pair in zip(self.kept, got)]
        elif self.step <= 3:
            value = total([self.kept, *got])
            if self.step == 3:
                self.value = value
            else:
                self.value, at = [], 0
                for size in self.sizes:
                    self.value.append(value[at : at + size])
                    at += size
        elif self.step == 4:
            self.value = jnp.concatenate([self.value, *got])
            self.size = self.value.shape[0]
        elif self.spread():
            self.value = jnp.concatenate([self.value, *got])
            if self.direct:
                self.keys = [(k << 1, k << 1) for k in range(self.sides)]
            else:
                bit = [1 << order[self.step - 5] for order in self.cube.order]
                keys = self.keys if self.step > 5 else [(0, 0)]
                self.keys = keys + [(a ^ bit[0], b ^ bit[1]) for a, b in keys]
        else:
            self.value, self.done = [self.value, *got], True

    def blocks(self, *names):
        sections = [(which, part, size) for (which, part), size in zip(names, self.sizes)]
        return [(v, core, self.keys, sections) for core, v in enumerate(self.value)]


def phase(chains, *ready):
    chains = [c for c in chains if not c.done]
    sent = [c.launch() for c in chains]
    got, ready = lax.optimization_barrier((sent, ready))
    for c, g in zip(chains, got):
        c.land(g)
    return ready


def per_device(
    small_nodes,
    small_edges,
    small_counts,
    big_nodes,
    big_edges,
    big_counts,
    small_node_cot,
    small_edge_cot,
    big_node_cot,
    big_edge_cot,
    master,
    first_moment,
    second_moment,
    owner,
    segment_rows,
    step_count,
):
    n_dp, n_row = lax.axis_size("dp"), lax.axis_size("row")
    cube = Cube(n_dp)
    share = big_nodes.shape[0] // n_row
    dm = Dims(small_nodes.shape[0], share, n_dp * n_row)

    def flat2(v):
        return v.reshape(-1, v.shape[-1])

    def to_rows(v):
        v = v.reshape(share, NB, OUT_LANES)
        v = lax.all_to_all(v, "row", split_axis=1, concat_axis=0, tiled=True)
        return v[..., EDGE_LANES:], v[..., :EDGE_LANES]

    own = shifted_segment(owner, segment_rows, master)
    own, big = lax.optimization_barrier((own, (big_edges, big_edge_cot, big_nodes, big_node_cot)))
    big = jnp.concatenate(big, axis=2)
    big = flat2(lax.all_to_all(big, "row", split_axis=0, concat_axis=1, tiled=True))
    held, big = cube.gather(own, big)
    one, two = assemble(cube, owner, segment_rows, [v for _, v in held], [k for k, _ in held])

    own_counts = lax.dynamic_slice_in_dim(big_counts, lax.axis_index("row") * share, share)
    counts = jnp.concatenate([small_counts, own_counts])

    mid_nodes, mid_edges, kept = first_forward(
        dm, counts, one, flat2(small_nodes), flat2(small_edges), big
    )
    sno, seo, bout, node_cot, edge_cot, kept_two, ffn_two = second_forward(
        dm, counts, two, mid_nodes, mid_edges, flat2(small_node_cot), flat2(small_edge_cot), big
    )
    spread = lax.psum_scatter(ffn_two.upper, "dp", scatter_dimension=0, tiled=True)
    got = between(dm, two, one, kept_two, kept, ffn_two, edge_cot)
    outs = to_rows(bout)
    names = tuple(k for k in vars(got))
    *values, bno, beo = phase([], *take(got, names), *outs)
    got = Group(names, values)
    middle = Chain(cube, False, (got.keep, got.send), (got.two_keep, got.two_send))
    names = tuple(edge_shapes(dm))
    edge_one = call_edges(dm, one, kept, got, got.edges_grad)
    spread, *edge = phase([middle], spread, *take(edge_one, names))
    edge_one = Group(names, edge)
    spread = lax.psum(spread, "row")
    names = tuple(attention_shapes(dm))
    att_one = Group(names, phase([middle], *take(call_attention(dm, kept, got, edge_one), names)))
    sng, seg, bgrad, keep, send = call_last(dm, one, kept, got, edge_one, att_one)
    spread, sng, seg, bgrad, keep, send = phase([middle], spread, sng, seg, bgrad, keep, send)
    upper_two = lax.all_gather(spread, "dp", axis=0, tiled=True)
    last = Chain(cube, True, (keep, send))
    for _ in range(4):
        phase([last, middle])
    bgrad, upper_two = phase([last, middle], bgrad, upper_two)
    bng, beg = to_rows(bgrad)
    while not (last.done and middle.done):
        phase([last, middle])
    blocks = last.blocks((0, 0)) + middle.blocks((0, 1), (1, 0))
    step_value = step_count[0].astype(F32)
    scales = jnp.stack(
        [
            1.0 / (1.0 - jnp.power(F32(BETA_ONE), step_value)),
            1.0 / (1.0 - jnp.power(F32(BETA_TWO), step_value)),
        ]
    )
    new_master, new_first, new_second, norm_grads = adam(
        n_row, dm.lower, owner, segment_rows, scales, upper_two, blocks, master, first_moment, second_moment
    )
    return (
        sno.reshape(small_nodes.shape),
        seo.reshape(small_edges.shape),
        bno,
        beo,
        sng.reshape(small_nodes.shape),
        seg.reshape(small_edges.shape),
        bng,
        beg,
        new_master,
        new_first,
        new_second,
        norm_grads,
    )


def solution(mesh):
    both = P(("dp", "row"), None, None)
    rows = P("dp", "row", None)
    held = P("dp", None)
    in_specs = (
        both, both, P(("dp", "row")), rows, rows, P("dp"), both, both, rows, rows,
        held, held, held, P(), P(), P(),
    )
    out_specs = (both, both, rows, rows, both, both, rows, rows, held, held, held, P())
    return jax.shard_map(
        per_device, mesh=mesh, in_specs=in_specs, out_specs=out_specs, check_vma=False
    )
```

```python
import functools

import jax
import jax.numpy as jnp
from jax import lax
from jax.experimental import pallas as pl
from jax.experimental.pallas import tpu as pltpu
from jax.sharding import PartitionSpec as P

D = 512
H = 32
DE = 64
FF = 1024
FFE = 128
NS = 32
NB = 64
SET_ROWS = 16578
TOTAL_ROWS = 33156
NORM_EPS = 1e-05
BETA_ONE = 0.9
BETA_TWO = 0.95
WEIGHT_DECAY = 0.1
ADAM_EPS = 1e-08
MASK_FILL = -1e30
BF = jnp.bfloat16
F32 = jnp.float32
VMEM_LIMIT = 58 * 1024 * 1024
ROW_QKV, ROW_O, ROW_UP, ROW_DOWN = 0, 6144, 8192, 12288
ROW_BIAS, ROW_GATE, ROW_EDGE, ROW_EUP, ROW_EDOWN = 16384, 16400, 16416, 16432, 16496
ROW_NN, ROW_EN = 16560, 16576
SMALL_USED, SMALL_ROWS = SET_ROWS - ROW_BIAS, 256
BIAS, GATE, EDGE, EUP, EDOWN = 0, 16, 32, 48, 112
NN, EN = ROW_NN - ROW_BIAS, ROW_EN - ROW_BIAS
UPPER_ROWS = ROW_BIAS - ROW_O
GELU_C = 0.7978845608028654


def nn(a, b):
    return lax.dot_general(a, b, (((1,), (0,)), ((), ())), preferred_element_type=F32)


def nt(a, b):
    return lax.dot_general(a, b, (((1,), (1,)), ((), ())), preferred_element_type=F32)


def tn(a, b):
    return lax.dot_general(a, b, (((0,), (0,)), ((), ())), preferred_element_type=F32)


def iota(shape, axis):
    return lax.broadcasted_iota(jnp.int32, shape, axis)


def gelu_parts(u):
    u2 = u * u
    t = jnp.tanh(u * (GELU_C + (GELU_C * 0.044715) * u2))
    half = 0.5 + 0.5 * t
    value = u * half
    slope = half + value * (1.0 - t) * (GELU_C + (3.0 * GELU_C * 0.044715) * u2)
    return value, slope


def gelu_value(u):
    return u * (0.5 + 0.5 * jnp.tanh(u * (GELU_C + (GELU_C * 0.044715) * (u * u))))


def sigmoid(v):
    return 0.5 + 0.5 * jnp.tanh(0.5 * v)


def group_sum(v, first=16):
    while first < 128:
        v = v + pltpu.roll(v, first, 1)
        first *= 2
    return v


def group_max(v):
    for shift in (16, 32, 64):
        v = jnp.maximum(v, pltpu.roll(v, shift, 1))
    return v


def fold8(v):
    return jnp.sum(v.reshape(v.shape[0] // 8, 8, v.shape[1]), axis=0)


class Bucket:
    def __init__(self, graphs, slots, node0, edge0, count0):
        self.graphs, self.slots = graphs, slots
        self.node0, self.edge0, self.count0 = node0, edge0, count0
        self.rows = graphs * slots
        self.chunks = slots // 4
        self.pairs = slots // 8
        self.blocks = slots // 16
        self.edges = self.rows * self.chunks
        self.edge_lanes = slots * DE


class Dims:
    def __init__(self, small_graphs, big_graphs, parts):
        self.lower = round_up(ROW_O + SMALL_ROWS, 16 * parts)
        self.small = Bucket(small_graphs, NS, 0, 0, 0)
        self.big = Bucket(big_graphs, NB, self.small.rows, self.small.edges, small_graphs)
        self.buckets = (self.small, self.big)
        self.nodes = self.small.rows + self.big.rows
        self.edges = self.small.edges + self.big.edges
        self.scores = self.edges // 2
        self.blocks = sum(b.graphs * b.blocks for b in self.buckets)

    def each_pair(self, body):
        for bucket in self.buckets:
            two = 2 * bucket.rows

            @pl.loop(0, bucket.pairs, unroll=4)
            def _(i, bucket=bucket, two=two):
                body(
                    pl.ds(aligned(bucket.edge0 + i * two, 32), two),
                    pl.ds(aligned(bucket.edge0 // 2 + i * bucket.rows, 16), bucket.rows),
                )


def beside(v):
    half = v.shape[0] // 2
    return jnp.concatenate([v[:half], v[half:]], axis=1)


def below(v):
    return jnp.concatenate([v[:, :256], v[:, 256:]], axis=0)


def make_masks(scr):
    make_mean(scr)
    make_heads(scr)


def make_mean(scr):
    shape = (256, 256)
    same = (iota(shape, 0) >> 6) == (iota(shape, 1) >> 6)
    scr.mean[...] = jnp.where(same, 1.0 / DE, 0.0).astype(BF)


def make_heads(scr):
    shape = (16, 256)
    scr.head[...] = jnp.where(iota(shape, 0) == (iota(shape, 1) >> 4), 1.0, 0.0)


def node_norm(v):
    centred = v - jnp.mean(v, axis=1, keepdims=True)
    r = lax.rsqrt(jnp.mean(centred * centred, axis=1, keepdims=True) + NORM_EPS)
    return centred * r, r


def node_norm_back(gdy, n, r):
    return r * (gdy - jnp.mean(gdy, axis=1, keepdims=True) - n * jnp.mean(gdy * n, axis=1, keepdims=True))


def aligned(value, by):
    return pl.multiple_of(value, by)


def block_of(bucket, t):
    g = t // bucket.blocks
    b = t % bucket.blocks
    rows = pl.ds(aligned(bucket.node0 + g * bucket.slots, 16), bucket.slots)
    keys = pl.ds(aligned(bucket.node0 + t * 16, 16), 16)
    pair_rows = [
        pl.ds(
            aligned(bucket.edge0 // 2 + (2 * b + c) * bucket.rows + g * bucket.slots, 16),
            bucket.slots,
        )
        for c in range(2)
    ]
    return rows, keys, pair_rows


def side(first, half):
    return slice(first + 256 * half, first + 256 * (half + 1))


def lanes(half):
    return slice(128 * half, 128 * (half + 1))


def expand(values, scr):
    spread = values.astype(F32)[:, None, :] * scr.head[...][None]
    return spread.reshape(256, 256).astype(BF)


def collect(values, scr):
    return jnp.sum(values.reshape(16, 16, 256) * scr.head[...][None], axis=1)


def joined(ref, pair_rows, half):
    return jnp.concatenate([ref[r, lanes(half)] for r in pair_rows], axis=1)


def forward(dm, counts, w, io, res, scr):
    x = io.nodes[...].astype(F32)
    n, r = node_norm(x)
    res.node_n1[...] = n.astype(BF)
    res.node_r1[...] = jnp.broadcast_to(r, (dm.nodes, 128))
    hn = (n * w.nn[0:1, :] + w.nn[1:2, :]).astype(BF)
    res.qkv[...] = nn(hn, w.qkv[...]).astype(BF)

    @dm.each_pair
    def _(rows, pair):
        x = io.edges[rows, :]
        centred = x.astype(F32) - nn(x, scr.mean[...])
        r = lax.rsqrt(nn((centred * centred).astype(BF), scr.mean[...]) + NORM_EPS)
        n = centred * r
        res.edge_n1[rows, :] = n.astype(BF)
        res.edge_r1[rows, :] = r.astype(BF)
        xn = (n * w.en[0:1, :] + w.en[1:2, :]).astype(BF)
        both = nn(beside(xn), w.eg[...])
        scr.scores[pair, :] = both[:, :256]
        res.gate[pair, :] = both[:, 256:]

    t0 = 0
    for bucket in dm.buckets:
        @pl.loop(0, bucket.graphs * bucket.blocks, unroll=True)
        def _(t, bucket=bucket, t0=t0):
            rows, keys, pair_rows = block_of(bucket, t)
            for half in range(2):
                kb = expand(res.qkv[keys, side(512, half)], scr)
                scr.vbig[t0 + t, half] = expand(res.qkv[keys, side(1024, half)], scr)
                s = nt(res.qkv[rows, side(0, half)], kb) * 0.25
                for c in range(2):
                    scr.scores[pair_rows[c], lanes(half)] += s[:, lanes(c)]

        @pl.loop(0, bucket.rows // 32, unroll=True)
        def _(i, bucket=bucket):
            count = counts[bucket.count0 + i * 32 // bucket.slots]
            lane_key = iota((32, 128), 1) >> 4
            row = [
                pl.ds(aligned(bucket.edge0 // 2 + c * bucket.rows + i * 32, 32), 32)
                for c in range(bucket.pairs)
            ]
            for half in range(2):
                at = lanes(half)
                top = jnp.full((32, 128), MASK_FILL, F32)
                for c in range(bucket.pairs):
                    s = scr.scores[row[c], at]
                    res.low[row[c], at] = s.astype(BF)
                    top = jnp.maximum(top, jnp.where(lane_key < count - 8 * c, s, MASK_FILL))
                top = group_max(top)
                sums = jnp.zeros((32, 128), F32)
                for c in range(bucket.pairs):
                    s = jnp.where(lane_key < count - 8 * c, scr.scores[row[c], at], MASK_FILL)
                    e = jnp.exp(s - top)
                    sums = sums + e
                    scr.scores[row[c], at] = e
                inv = 1.0 / group_sum(sums)
                for c in range(bucket.pairs):
                    p = scr.scores[row[c], at] * inv
                    res.prob[row[c], at] = p.astype(BF)
                    scr.attn[row[c], at] = (p * sigmoid(res.gate[row[c], at])).astype(BF)

        @pl.loop(0, bucket.graphs, unroll=True)
        def _(g, bucket=bucket, t0=t0):
            for half in range(2):
                sums = None
                for b in range(bucket.blocks):
                    t = g * bucket.blocks + b
                    rows, _, pair_rows = block_of(bucket, t)
                    part = nn(joined(scr.attn, pair_rows, half), scr.vbig[t0 + t, half])
                    sums = part if sums is None else sums + part
                res.mixed[rows, side(0, half)] = sums.astype(BF)

        t0 += bucket.graphs * bucket.blocks

    y = io.nodes[...].astype(F32) + nn(res.mixed[...], w.o[...])
    n, r = node_norm(y)
    res.node_n2[...] = n.astype(BF)
    res.node_r2[...] = jnp.broadcast_to(r, (dm.nodes, 128))
    z = (n * w.nn[2:3, :] + w.nn[3:4, :]).astype(BF)
    u = nn(z, w.up[...])
    res.node_u[...] = u
    io.nodes_out[...] = (y + nn(gelu_value(u).astype(BF), w.down[...])).astype(BF)

    @dm.each_pair
    def _(rows, pair):
        m = io.edges[rows, :].astype(F32) + below(nn(res.low[pair, :], w.x[...]))
        high = m.astype(BF)
        rest = (m - high.astype(F32)).astype(BF)
        centred = m - nn(high, scr.mean[...]) - nn(rest, scr.mean[...])
        r = lax.rsqrt(nn((centred * centred).astype(BF), scr.mean[...]) + NORM_EPS)
        n = centred * r
        res.edge_n2[rows, :] = n.astype(BF)
        res.edge_r2[rows, :] = r.astype(BF)
        mn = (n * w.en[2:3, :] + w.en[3:4, :]).astype(BF)
        ua = nn(mn, w.a[...])
        io.edges_out[rows, :] = (m + nn(gelu_value(ua).astype(BF), w.b[...])).astype(BF)


def put_strided(flat, first, value, parts):
    for q in range(parts):
        flat[pl.ds(first + q, value.shape[0], stride=parts), :] = value[:, 128 * q : 128 * (q + 1)]


def back_ffn(dm, w, io, res, scr):
    flat = scr.upper
    gy = io.nodes_cot[...]
    act, slope = gelu_parts(res.node_u[...])
    du = (nt(gy, w.down[...]) * slope).astype(BF)
    put_strided(flat, ROW_DOWN - ROW_O, tn(act.astype(BF), gy), 4)
    n = res.node_n2[...].astype(F32)
    z = (n * w.nn[2:3, :] + w.nn[3:4, :]).astype(BF)
    put_strided(flat, ROW_UP - ROW_O, tn(z, du), 8)
    dz = nt(du, w.up[...])
    gain = jnp.sum(dz * n, axis=0, keepdims=True)
    bias = jnp.sum(dz, axis=0, keepdims=True)
    dy = gy.astype(F32) + node_norm_back(dz * w.nn[2:3, :], n, res.node_r2[:, 0:1])
    io.dy[...] = dy
    dyl = dy.astype(BF)
    put_strided(flat, 0, tn(res.mixed[...], dyl), 4)
    io.do[...] = nt(dyl, w.o[...]).astype(BF)
    for q in range(4):
        io.sums[q : q + 1, :] = gain[:, 128 * q : 128 * (q + 1)]
        io.sums[4 + q : 5 + q, :] = bias[:, 128 * q : 128 * (q + 1)]
    if hasattr(io, "upper"):
        io.upper[...] = flat[...].astype(BF)
    else:
        put_halves(flat, io.keep, io.send)


def put_halves(flat, keep, send):
    half = keep.shape[0]
    core = lax.axis_index("dp") & 1
    keep[...] = flat[pl.ds(aligned(core * half, 16), half), :].astype(BF)
    send[...] = flat[pl.ds(aligned((1 - core) * half, 16), half), :].astype(BF)


def back_edges(dm, w, io, res, scr):
    io.small[NN + 8 : NN + 16, :] = io.sums[...]
    scr.gb[...] = jnp.zeros((512, 256), F32)
    scr.ga[...] = jnp.zeros((256, 512), F32)
    scr.gx[...] = jnp.zeros((256, 512), F32)
    scr.en[...] = jnp.zeros((2, 8, 256), F32)

    @dm.each_pair
    def _(rows, pair):
        gx = io.edges_cot[rows, :]
        n = res.edge_n2[rows, :].astype(F32)
        mn = (n * w.en[2:3, :] + w.en[3:4, :]).astype(BF)
        act, slope = gelu_parts(nn(mn, w.a[...]))
        dua = (nt(gx, w.b[...]) * slope).astype(BF)
        scr.gb[...] += tn(act.astype(BF), gx)
        scr.ga[...] += tn(mn, dua)
        dmn = nt(dua, w.a[...])
        scr.en[0] += fold8(dmn * n)
        scr.en[1] += fold8(dmn)
        gdy = dmn * w.en[2:3, :]
        m1 = nn(gdy.astype(BF), scr.mean[...])
        m2 = nn((gdy * n).astype(BF), scr.mean[...])
        dmid = gx.astype(F32) + res.edge_r2[rows, :].astype(F32) * (gdy - m1 - n * m2)
        dml = dmid.astype(BF)
        io.dmid[rows, :] = dml
        dml = beside(dml)
        scr.gx[...] += tn(res.low[pair, :], dml)
        io.scores[pair, :] = nt(dml, w.x[...])

    up = scr.ga[0:64, 0:128]
    for k in range(1, 4):
        up = up + scr.ga[64 * k : 64 * (k + 1), 128 * k : 128 * (k + 1)]
    io.small[EUP : EUP + 64, :] = up
    sums = jnp.zeros((128, 128), F32)
    for k in range(4):
        part = scr.gb[128 * k : 128 * (k + 1), 128 * (k // 2) : 128 * (k // 2 + 1)]
        sums = sums + jnp.where(lane_group(128, 6) == k % 2, part, 0.0)
    fold_halves(sums, scr.tmp, io.small, EDOWN)
    sides = []
    for half in range(2):
        sums = jnp.zeros((16, 128), F32)
        for k in range(8):
            at = 128 * half + 16 * k
            part = scr.gx[at : at + 16, 128 * (k // 2) : 128 * (k // 2 + 1)]
            sums = sums + jnp.where(lane_group(16, 6) == k % 2, part, 0.0)
        sides.append(sums)
    fold_halves(jnp.concatenate(sides), scr.tmp, io.small, EDGE)
    put_edge_norm(scr.en, io.small, EN + 1)
    io.small[SMALL_USED:, :] = jnp.zeros((SMALL_ROWS - SMALL_USED, 128), F32)


def back_attention(dm, io, res, scr):
    t0 = 0
    for bucket in dm.buckets:
        @pl.loop(0, bucket.graphs * bucket.blocks, unroll=True)
        def _(t, bucket=bucket, t0=t0):
            rows, keys, pair_rows = block_of(bucket, t)
            for half in range(2):
                scr.vbig[t0 + t, half] = expand(res.qkv[keys, side(512, half)], scr)
                vb = expand(res.qkv[keys, side(1024, half)], scr)
                da = nt(io.do[rows, side(0, half)], vb)
                for c in range(2):
                    scr.da[pair_rows[c], lanes(half)] = da[:, lanes(c)]

        @pl.loop(0, bucket.rows // 32, unroll=True)
        def _(i, bucket=bucket):
            row = [
                pl.ds(aligned(bucket.edge0 // 2 + c * bucket.rows + i * 32, 32), 32)
                for c in range(bucket.pairs)
            ]
            for half in range(2):
                at = lanes(half)
                sums = jnp.zeros((32, 128), F32)
                for c in range(bucket.pairs):
                    p = res.prob[row[c], at].astype(F32)
                    s = sigmoid(res.gate[row[c], at])
                    scr.attn[row[c], at] = (p * s).astype(BF)
                    pt = p * scr.da[row[c], at] * s
                    scr.da[row[c], at] = pt
                    sums = sums + pt
                    io.dsg[row[c], lanes(2 + half)] = (pt * (1.0 - s)).astype(BF)
                sums = group_sum(sums)
                for c in range(bucket.pairs):
                    p = res.prob[row[c], at].astype(F32)
                    ds = scr.da[row[c], at] - p * sums + io.scores[row[c], at]
                    io.dsg[row[c], at] = ds.astype(BF)

        @pl.loop(0, bucket.graphs, unroll=True)
        def _(g, bucket=bucket, t0=t0):
            for half in range(2):
                sums = None
                for b in range(bucket.blocks):
                    t = g * bucket.blocks + b
                    rows, keys, pair_rows = block_of(bucket, t)
                    ds = joined(io.dsg, pair_rows, half)
                    part = nn(ds, scr.vbig[t0 + t, half])
                    sums = part if sums is None else sums + part
                    gk = collect(tn(ds, res.qkv[rows, side(0, half)]), scr)
                    io.dqkv[keys, side(512, half)] = (gk * 0.25).astype(BF)
                    gv = tn(joined(scr.attn, pair_rows, half), io.do[rows, side(0, half)])
                    io.dqkv[keys, side(1024, half)] = collect(gv, scr).astype(BF)
                io.dqkv[rows, side(0, half)] = (sums * 0.25).astype(BF)

        t0 += bucket.graphs * bucket.blocks


def back_last(dm, w, io, res, scr):
    flat = scr.lower
    n = res.node_n1[...].astype(F32)
    hn = (n * w.nn[0:1, :] + w.nn[1:2, :]).astype(BF)
    for m in range(3):
        put_strided(flat, 2048 * m, tn(hn, io.dqkv[:, 512 * m : 512 * (m + 1)]), 4)
    dhn = nt(io.dqkv[...], w.qkv[...])
    gain = jnp.sum(dhn * n, axis=0, keepdims=True)
    bias = jnp.sum(dhn, axis=0, keepdims=True)
    small = flat.at[pl.ds(ROW_O, SMALL_ROWS), :]
    small[...] = io.small[...]
    for q in range(4):
        small[NN + q : NN + 1 + q, :] = gain[:, 128 * q : 128 * (q + 1)]
        small[NN + 4 + q : NN + 5 + q, :] = bias[:, 128 * q : 128 * (q + 1)]
    dx = io.dy[...] + node_norm_back(dhn * w.nn[0:1, :], n, res.node_r1[:, 0:1])
    io.nodes_grad[...] = dx.astype(BF)

    scr.geg[...] = jnp.zeros((512, 512), F32)
    scr.en[...] = jnp.zeros((2, 8, 256), F32)

    @dm.each_pair
    def _(rows, pair):
        dsg = io.dsg[pair, :]
        n = res.edge_n1[rows, :].astype(F32)
        xn = (n * w.en[0:1, :] + w.en[1:2, :]).astype(BF)
        scr.geg[...] += tn(beside(xn), dsg)
        dxn = below(nt(dsg, w.eg[...]))
        scr.en[0] += fold8(dxn * n)
        scr.en[1] += fold8(dxn)
        gdy = dxn * w.en[0:1, :]
        m1 = nn(gdy.astype(BF), scr.mean[...])
        m2 = nn((gdy * n).astype(BF), scr.mean[...])
        dx = io.dmid[rows, :].astype(F32) + res.edge_r1[rows, :].astype(F32) * (gdy - m1 - n * m2)
        io.edges_grad[rows, :] = dx.astype(BF)

    for which, first in ((0, BIAS), (1, GATE)):
        sides = []
        for half in range(2):
            sums = jnp.zeros((64, 128), F32)
            for k in range(8):
                part = scr.geg[64 * k : 64 * (k + 1), lanes(2 * which + half)]
                sums = sums + jnp.where(lane_group(64, 4) == k, part, 0.0)
            sides.append(group_sum(sums))
        scr.tmp[0:64, :] = jnp.where(lane_group(64, 4) % 2 == 0, sides[0], sides[1])
        rows = jnp.zeros((16, 128), F32)
        for b in range(4):
            rows = jnp.where(lane_group(16, 5) == b, scr.tmp[pl.ds(b, 16, stride=4), :], rows)
        small[first : first + 16, :] = rows
    put_edge_norm(scr.en, small, EN)
    end = ROW_O + SMALL_ROWS
    if dm.lower > end:
        flat[end:, :] = jnp.zeros((dm.lower - end, 128), F32)
    put_halves(flat, io.keep, io.send)


def lane_group(rows, bits):
    return iota((rows, 128), 1) >> bits


def fold_halves(sums, tmp, out, first):
    rows, half = sums.shape[0], sums.shape[0] // 2
    tmp[0:rows, :] = sums + pltpu.roll(sums, 64, 1)
    even = tmp[pl.ds(0, half, stride=2), :]
    odd = tmp[pl.ds(1, half, stride=2), :]
    out[first : first + half, :] = jnp.where(lane_group(half, 6) == 0, even, odd)


def put_edge_norm(sums, out, at):
    ones = []
    for t in range(2):
        both = jnp.sum(sums[t], axis=0, keepdims=True)
        one = both[:, :128] + both[:, 128:]
        ones.append(one + pltpu.roll(one, 64, 1))
    out[at : at + 1, :] = jnp.where(lane_group(1, 6) == 0, ones[0], ones[1])


def assemble_set(off, flat, tmp, w):
    def strided(first, rows, parts, out, lane0=0):
        for q in range(parts):
            out[:, lane0 + 128 * q : lane0 + 128 * (q + 1)] = flat[
                pl.ds(off + first + q, rows, stride=parts), :
            ].astype(BF)

    for m in range(3):
        strided(ROW_QKV + 2048 * m, 512, 4, w.qkv, 512 * m)
    strided(ROW_O, 512, 4, w.o)
    strided(ROW_UP, 512, 8, w.up)
    strided(ROW_DOWN, 1024, 4, w.down)
    w.eg[...] = jnp.zeros((512, 512), BF)
    w.x[...] = jnp.zeros((256, 512), BF)
    w.a[...] = jnp.zeros((256, 512), BF)
    w.b[...] = jnp.zeros((512, 256), BF)
    up = flat[pl.ds(off + ROW_EUP, 64), :].astype(BF)
    for k in range(4):
        w.a[64 * k : 64 * (k + 1), 128 * k : 128 * (k + 1)] = up

    def doubled(first, in_rows):
        v = flat[pl.ds(off + first, in_rows), :]
        other = pltpu.roll(v, 64, 1)
        low = lane_group(in_rows, 6) == 0
        tmp[pl.ds(0, in_rows, stride=2), :] = jnp.where(low, v, other)
        tmp[pl.ds(1, in_rows, stride=2), :] = jnp.where(low, other, v)
        return tmp[0 : 2 * in_rows, :]

    both = doubled(ROW_EDOWN, 64)
    for k in range(4):
        w.b[128 * k : 128 * (k + 1), 128 * (k // 2) : 128 * (k // 2 + 1)] = jnp.where(
            lane_group(128, 6) == k % 2, both, 0.0
        ).astype(BF)
    both = doubled(ROW_EDGE, 16)
    for half in range(2):
        for k in range(8):
            at = 128 * half + 16 * k
            w.x[at : at + 16, 128 * (k // 2) : 128 * (k // 2 + 1)] = jnp.where(
                lane_group(16, 6) == k % 2, both[16 * half : 16 * (half + 1)], 0.0
            ).astype(BF)
    for which, first in ((0, ROW_BIAS), (1, ROW_GATE)):
        v = flat[pl.ds(off + first, 16), :]
        for b in range(4):
            tmp[pl.ds(b, 16, stride=4), :] = group_sum(jnp.where(lane_group(16, 5) == b, v, 0.0), 32)
        both = tmp[0:64, :]
        even = lane_group(64, 4) % 2 == 0
        sides = (
            jnp.where(even, both, pltpu.roll(both, 16, 1)),
            jnp.where(even, pltpu.roll(both, 112, 1), both),
        )
        for half in range(2):
            for k in range(8):
                w.eg[64 * k : 64 * (k + 1), lanes(2 * which + half)] = jnp.where(
                    lane_group(64, 4) == k, sides[half], 0.0
                ).astype(BF)
    for t in range(4):
        for q in range(4):
            w.nn[t : t + 1, 128 * q : 128 * (q + 1)] = flat[pl.ds(off + ROW_NN + 4 * t + q, 1), :]
    for t in range(2):
        v = flat[pl.ds(off + ROW_EN + t, 1), :]
        other = pltpu.roll(v, 64, 1)
        gain = jnp.where(lane_group(1, 6) == 0, v, other)
        bias = jnp.where(lane_group(1, 6) == 0, other, v)
        for half in range(2):
            w.en[2 * t : 2 * t + 1, 128 * half : 128 * (half + 1)] = gain
            w.en[2 * t + 1 : 2 * t + 2, 128 * half : 128 * (half + 1)] = bias


class Group:
    def __init__(self, names, refs):
        for name, ref in zip(names, refs):
            setattr(self, name, ref)


WEIGHTS = {
    "qkv": ((D, 3 * D), BF),
    "o": ((D, D), BF),
    "up": ((D, FF), BF),
    "down": ((FF, D), BF),
    "eg": ((512, 512), BF),
    "x": ((256, 512), BF),
    "a": ((256, 512), BF),
    "b": ((512, 256), BF),
    "nn": ((4, D), F32),
    "en": ((4, 256), F32),
}


def residual_shapes(dm):
    return {
        "node_n1": ((dm.nodes, D), BF),
        "node_r1": ((dm.nodes, 128), F32),
        "qkv": ((dm.nodes, 3 * D), BF),
        "mixed": ((dm.nodes, D), BF),
        "node_n2": ((dm.nodes, D), BF),
        "node_r2": ((dm.nodes, 128), F32),
        "node_u": ((dm.nodes, FF), F32),
        "edge_n1": ((dm.edges, 256), BF),
        "edge_r1": ((dm.edges, 256), BF),
        "gate": ((dm.scores, 256), F32),
        "low": ((dm.scores, 256), BF),
        "prob": ((dm.scores, 256), BF),
        "edge_n2": ((dm.edges, 256), BF),
        "edge_r2": ((dm.edges, 256), BF),
    }


def mean_shapes():
    return {"mean": ((256, 256), BF)}


def head_shapes():
    return {"head": ((16, 256), F32)}


def mask_shapes():
    return {**mean_shapes(), **head_shapes()}


def forward_scratch(dm):
    return {
        "scores": ((dm.scores, 256), F32),
        "attn": ((dm.scores, 256), BF),
        "vbig": ((dm.blocks, 2, 256, 256), BF),
    }


def ffn_shapes(dm, halves):
    half = ((UPPER_ROWS // 2, 128), BF)
    grads = {"keep": half, "send": half} if halves else {"upper": ((UPPER_ROWS, 128), BF)}
    return {
        "dy": ((dm.nodes, D), F32),
        "do": ((dm.nodes, D), BF),
        "sums": ((8, 128), F32),
        **grads,
    }


def edge_shapes(dm):
    return {
        "dmid": ((dm.edges, 256), BF),
        "scores": ((dm.scores, 256), F32),
        "small": ((SMALL_ROWS, 128), F32),
    }


def attention_shapes(dm):
    return {"dsg": ((dm.scores, 512), BF), "dqkv": ((dm.nodes, 3 * D), BF)}


def ffn_scratch():
    return {"upper": ((UPPER_ROWS, 128), F32)}


def edge_scratch():
    return {
        "gb": ((512, 256), F32),
        "ga": ((256, 512), F32),
        "gx": ((256, 512), F32),
        "en": ((2, 8, 256), F32),
        "tmp": ((128, 128), F32),
    }


def attention_scratch(dm):
    return {
        "attn": ((dm.scores, 256), BF),
        "vbig": ((dm.blocks, 2, 256, 256), BF),
        "da": ((dm.scores, 256), F32),
    }


def last_scratch(dm):
    return {
        "geg": ((512, 512), F32),
        "en": ((2, 8, 256), F32),
        "tmp": ((128, 128), F32),
        "lower": ((dm.lower, 128), F32),
    }


def structs(shapes):
    return [jax.ShapeDtypeStruct(s, t) for s, t in shapes.values()]


def vmem(shapes):
    return [pltpu.VMEM(s, t) for s, t in shapes.values()]


def whole(n):
    return [pl.BlockSpec(memory_space=pltpu.VMEM)] * n


def split(refs, *groups):
    out, at = [], 0
    for names in groups:
        out.append(Group(names, refs[at : at + len(names)]))
        at += len(names)
    assert at == len(refs)
    return out


def edge_copies(dm, small, big, big_lane, stacked, sems, out):
    copies = []
    for bucket, ref, lane in ((dm.small, small, 0), (dm.big, big, big_lane)):
        for c in range(bucket.chunks):
            a = ref.at[:, pl.ds(lane + 256 * c, 256)]
            b = stacked.at[pl.ds(bucket.edge0 + c * bucket.rows, bucket.rows), :]
            src, dst = (b, a) if out else (a, b)
            copies.append(pltpu.make_async_copy(src, dst, sems.at[len(copies)]))
    return copies


def node_copies(dm, small, big, big_lane, nodes, sems, at, out):
    copies = []
    for bucket, ref in ((dm.small, small), (dm.big, big.at[:, pl.ds(big_lane, D)])):
        b = nodes.at[pl.ds(bucket.node0, bucket.rows), :]
        src, dst = (b, ref) if out else (ref, b)
        copies.append(pltpu.make_async_copy(src, dst, sems.at[at + len(copies)]))
    return copies


def copy_sems(dm):
    return pltpu.SemaphoreType.DMA((dm.small.chunks + dm.big.chunks + 2,))


def all_copies(dm, small_nodes, small_edges, big, edge_lane, node_lane, nodes, edges, sems, out):
    copies = edge_copies(dm, small_edges, big, edge_lane, edges, sems, out)
    return node_copies(dm, small_nodes, big, node_lane, nodes, sems, len(copies), out) + copies


def start(copies):
    for c in copies:
        c.start()


def wait(copies):
    for c in copies:
        c.wait()


HBM = pl.BlockSpec(memory_space=pl.ANY)
SMEM = pl.BlockSpec(memory_space=pltpu.SMEM)
EDGE_LANES = NB * DE
IN_LANES = 2 * EDGE_LANES + 2 * D
OUT_LANES = EDGE_LANES + D


def compiler_params():
    return pltpu.CompilerParams(vmem_limit_bytes=VMEM_LIMIT)


def cost(us):
    return pl.CostEstimate(flops=0, bytes_accessed=int(us * 3.4e6), transcendentals=0)


def take(group, names):
    return [getattr(group, k) for k in names]


NODE_BACK = ("node_n2", "node_r2", "node_u", "mixed")
EDGE_BACK = ("edge_n2", "edge_r2", "low")
ATTENTION_BACK = ("qkv", "prob", "gate")
LAST_BACK = ("node_n1", "node_r1", "edge_n1", "edge_r1")
W_NODE = ("o", "up", "down", "nn")
W_EDGE = ("x", "a", "b", "en")
W_LAST = ("qkv", "eg", "nn", "en")


def kernel(body, inputs, out, scr, us, counts=None, hbm_in=0, hbm_out=(), sems=()):
    smem = [] if counts is None else [counts]
    return Group(
        out,
        pl.pallas_call(
            body,
            out_shape=structs(out),
            in_specs=[SMEM] * len(smem) + whole(len(inputs) - hbm_in) + [HBM] * hbm_in,
            out_specs=[HBM if k in hbm_out else pl.BlockSpec(memory_space=pltpu.VMEM) for k in out],
            scratch_shapes=vmem(scr) + list(sems),
            compiler_params=compiler_params(),
            cost_estimate=cost(us),
        )(*smem, *inputs),
    )


def first_forward(dm, counts, weights, small_nodes, small_edges, big):
    res = residual_shapes(dm)
    out = {"nodes_out": ((dm.nodes, D), BF), "edges_out": ((dm.edges, 256), BF), **res}
    scr = {
        **mask_shapes(),
        **forward_scratch(dm),
        "nodes": ((dm.nodes, D), BF),
        "edges": ((dm.edges, 256), BF),
    }

    def body(*refs):
        counts_ref, refs, sems = refs[0], refs[1:-1], refs[-1]
        w, src, dst, s = split(refs, WEIGHTS, ("sn", "se", "big"), out, scr)
        copies = all_copies(
            dm, src.sn, src.se, src.big, 0, 2 * EDGE_LANES, s.nodes, s.edges, sems, False
        )
        start(copies)
        make_masks(s)
        io = Group(
            ("nodes", "edges", "nodes_out", "edges_out"),
            (s.nodes, s.edges, dst.nodes_out, dst.edges_out),
        )
        wait(copies)
        forward(dm, counts_ref, w, io, dst, s)

    inputs = take(weights, WEIGHTS) + [small_nodes, small_edges, big]
    got = kernel(body, inputs, out, scr, 38, counts, 3, (), [copy_sems(dm)])
    return got.nodes_out, got.edges_out, got


def second_forward(dm, counts, weights, nodes, edges, small_node_cot, small_edge_cot, big):
    res, ffn = residual_shapes(dm), ffn_shapes(dm, False)
    whole_outs = {
        "sno": ((dm.small.rows, D), BF),
        "seo": ((dm.small.rows, dm.small.edge_lanes), BF),
        "bout": ((dm.big.rows, OUT_LANES), BF),
    }
    node_res = [k for k in res if k in NODE_BACK]
    kept = {k: v for k, v in res.items() if k not in NODE_BACK}
    out = {**whole_outs, "edge_cot": ((dm.edges, 256), BF), **kept, **ffn}
    scr = {
        **mask_shapes(),
        **forward_scratch(dm),
        **ffn_scratch(),
        **{k: res[k] for k in node_res},
        "nodes_out": ((dm.nodes, D), BF),
        "edges_out": ((dm.edges, 256), BF),
        "node_cot": ((dm.nodes, D), BF),
    }

    def body(*refs):
        counts_ref, refs, in_sems, out_sems = refs[0], refs[1:-2], refs[-2], refs[-1]
        w, src, dst, s = split(refs, WEIGHTS, ("nodes", "edges", "snc", "sec", "big"), out, scr)
        copies = all_copies(
            dm, src.snc, src.sec, src.big, EDGE_LANES, 2 * EDGE_LANES + D, s.node_cot, dst.edge_cot, in_sems, False
        )
        start(copies)
        make_masks(s)
        every = Group(
            [*kept, *node_res], [getattr(dst, k) for k in kept] + [getattr(s, k) for k in node_res]
        )
        io = Group(
            ("nodes", "edges", "nodes_out", "edges_out"),
            (src.nodes, src.edges, s.nodes_out, s.edges_out),
        )
        forward(dm, counts_ref, w, io, every, s)
        outgoing = all_copies(
            dm, dst.sno, dst.seo, dst.bout, 0, EDGE_LANES, s.nodes_out, s.edges_out, out_sems, True
        )
        start(outgoing)
        wait(copies)
        back_ffn(dm, w, Group(("nodes_cot", *ffn), (s.node_cot, *take(dst, ffn))), every, s)
        wait(outgoing)

    inputs = take(weights, WEIGHTS) + [nodes, edges, small_node_cot, small_edge_cot, big]
    got = kernel(body, inputs, out, scr, 46, counts, 3, tuple(whole_outs), [copy_sems(dm)] * 2)
    return got.sno, got.seo, got.bout, None, got.edge_cot, got, got


def between(dm, weights_two, weights_one, kept_two, kept_one, ffn_two, edges_cot):
    half = {k: ((dm.lower // 2, 128), BF) for k in ("keep", "send")}
    ffn = ffn_shapes(dm, True)
    out = {
        "edges_grad": ((dm.edges, 256), BF),
        **{"two_" + k: v for k, v in half.items()},
        **ffn,
    }
    edge, att = edge_shapes(dm), attention_shapes(dm)
    scr = {
        **mask_shapes(),
        **edge_scratch(),
        **attention_scratch(dm),
        **last_scratch(dm),
        **ffn_scratch(),
        **edge,
        **att,
        "nodes_grad": ((dm.nodes, D), BF),
    }
    w_two = ("qkv", *W_EDGE, "eg", "nn")
    res_two = EDGE_BACK + ATTENTION_BACK + LAST_BACK

    def body(*refs):
        w, w_one, res, res_one, src, dst, s = split(
            refs, w_two, W_NODE, res_two, NODE_BACK, ("edges_cot", "sums", "do", "dy"), out, scr
        )
        make_masks(s)
        io = Group(
            ("edges_cot", "sums", "do", "dy", *edge, *att, "nodes_grad", "edges_grad", "keep", "send"),
            (src.edges_cot, src.sums, src.do, src.dy, *take(s, edge), *take(s, att))
            + (s.nodes_grad, dst.edges_grad, dst.two_keep, dst.two_send),
        )
        back_edges(dm, w, io, res, s)
        back_attention(dm, io, res, s)
        back_last(dm, w, io, res, s)
        back_ffn(dm, w_one, Group(("nodes_cot", *ffn), (s.nodes_grad, *take(dst, ffn))), res_one, s)

    inputs = take(weights_two, w_two) + take(weights_one, W_NODE)
    inputs += take(kept_two, res_two) + take(kept_one, NODE_BACK)
    inputs += [edges_cot, ffn_two.sums, ffn_two.do, ffn_two.dy]
    return kernel(body, inputs, out, scr, 45)


def call_edges(dm, weights, kept, ffn, edges_cot):
    out, scr = edge_shapes(dm), {**mean_shapes(), **edge_scratch()}

    def body(*refs):
        w, res, src, dst, s = split(refs, W_EDGE, EDGE_BACK, ("edges_cot", "sums"), out, scr)
        make_mean(s)
        io = Group(("edges_cot", "sums", *out), (src.edges_cot, src.sums, *take(dst, out)))
        back_edges(dm, w, io, res, s)

    inputs = take(weights, W_EDGE) + take(kept, EDGE_BACK) + [edges_cot, ffn.sums]
    return kernel(body, inputs, out, scr, 16)


def call_attention(dm, kept, ffn, edge):
    out, scr = attention_shapes(dm), {**head_shapes(), **attention_scratch(dm)}

    def body(*refs):
        res, src, dst, s = split(refs, ATTENTION_BACK, ("do", "scores"), out, scr)
        make_heads(s)
        back_attention(dm, Group(("do", "scores", *out), (src.do, src.scores, *take(dst, out))), res, s)

    return kernel(body, take(kept, ATTENTION_BACK) + [ffn.do, edge.scores], out, scr, 14)


def call_last(dm, weights, kept, ffn, edge, att):
    half = {k: ((dm.lower // 2, 128), BF) for k in ("keep", "send")}
    outs = {
        "sng": ((dm.small.rows, D), BF),
        "seg": ((dm.small.rows, dm.small.edge_lanes), BF),
        "bgrad": ((dm.big.rows, OUT_LANES), BF),
    }
    out = {**outs, **half}
    scr = {
        **mean_shapes(),
        **last_scratch(dm),
        "nodes_grad": ((dm.nodes, D), BF),
        "edges_grad": ((dm.edges, 256), BF),
    }
    given = ("dy", "dmid", "small", "dsg", "dqkv")

    def body(*refs):
        refs, sems = refs[:-1], refs[-1]
        w, res, src, dst, s = split(refs, W_LAST, LAST_BACK, given, out, scr)
        make_mean(s)
        io = Group(
            (*given, "nodes_grad", "edges_grad", "keep", "send"),
            (*take(src, given), s.nodes_grad, s.edges_grad, dst.keep, dst.send),
        )
        back_last(dm, w, io, res, s)
        outgoing = all_copies(
            dm, dst.sng, dst.seg, dst.bgrad, 0, EDGE_LANES, s.nodes_grad, s.edges_grad, sems, True
        )
        start(outgoing)
        wait(outgoing)

    inputs = take(weights, W_LAST) + take(kept, LAST_BACK)
    inputs += [ffn.dy, edge.dmid, edge.small, att.dsg, att.dqkv]
    got = kernel(body, inputs, out, scr, 13, hbm_out=tuple(outs), sems=[copy_sems(dm)])
    return take(got, out)


def round_up(value, by):
    return -(-value // by) * by


def segment_of(owner, rows, index, count):
    name = owner[index]
    first = jnp.int32(0)
    for t in range(count):
        first = first + jnp.where(t < name, rows[t], 0)
    return first, rows[name]


def shifted_segment(owner, segment_rows, master):
    held = master.shape[0]
    count = owner.shape[0]
    padded = round_up(held + 15, 16)
    step = 1664

    def body(owner_ref, rows_ref, src, dst, window):
        i = pl.program_id(0)
        first, length = segment_of(owner_ref, rows_ref, lax.axis_index("dp"), count)
        shift = first % 16

        @pl.when(i == 0)
        def _():
            window[0:16, :] = jnp.zeros((16, 128), F32)

        window[16:, :] = src[...]
        moved = window[pl.ds(16 - shift, step), :]
        index = i * step - shift + iota((step, 128), 0)
        live = (index >= 0) & (index < length)
        dst[...] = jnp.where(live, moved, 0.0).astype(BF)
        window[0:16, :] = window[step : step + 16, :]

    return pl.pallas_call(
        body,
        grid=(pl.cdiv(padded, step),),
        out_shape=jax.ShapeDtypeStruct((padded, 128), BF),
        in_specs=[
            SMEM,
            SMEM,
            pl.BlockSpec((step, 128), lambda i: (jnp.minimum(i, (held - 1) // step), 0)),
        ],
        out_specs=pl.BlockSpec((step, 128), lambda i: (i, 0)),
        scratch_shapes=[pltpu.VMEM((step + 16, 128), F32)],
        compiler_params=compiler_params(),
    )(owner, segment_rows, master)


def assemble(cube, owner, segment_rows, parts, sources):
    count = len(parts)
    padded = parts[0].shape[0]
    bits = (padded // 16).bit_length()
    tiles = -(-TOTAL_ROWS // 16)
    set_tiles = -(-(SET_ROWS + 2) // 16)
    out = {**{"one_" + k: v for k, v in WEIGHTS.items()}, **{"two_" + k: v for k, v in WEIGHTS.items()}}

    def body(owner_ref, rows_ref, *refs):
        srcs, refs = refs[:count], refs[count:]
        dsts, (rows, flat, tmp, edge, sems, edge_sems) = refs[: len(out)], refs[len(out) :]
        me = lax.axis_index("dp")
        spans = []
        for i in range(count):
            first, length = segment_of(owner_ref, rows_ref, cube.source(me, sources[i]), count)
            spans.append((first // 16, (first + length - 1) // 16))

        def each(act):
            for i, (a, b) in enumerate(spans):
                inner = b - a - 1
                for bit in range(bits):
                    size = 16 << bit
                    if size > padded:
                        continue
                    done = (inner >> (bit + 1)) << (bit + 1)

                    @pl.when((inner > 0) & (((inner >> bit) & 1) == 1))
                    def _(i=i, a=a, done=done, size=size, bit=bit):
                        act(
                            pltpu.make_async_copy(
                                srcs[i].at[pl.ds(aligned(16 * (1 + done), 16), size), :],
                                rows.at[pl.ds(aligned(16 * (a + 1 + done), 16), size), :],
                                sems.at[i, bit],
                            )
                        )

                act(pltpu.make_async_copy(srcs[i].at[pl.ds(0, 16), :], edge.at[2 * i], edge_sems.at[2 * i]))
                act(
                    pltpu.make_async_copy(
                        srcs[i].at[pl.ds(aligned(16 * (b - a), 16), 16), :],
                        edge.at[2 * i + 1],
                        edge_sems.at[2 * i + 1],
                    )
                )

        each(lambda c: c.start())
        each(lambda c: c.wait())
        tile = lambda t: pl.ds(aligned(16 * t, 16), 16)
        for a, b in spans:
            rows[tile(a), :] = jnp.zeros((16, 128), BF)
            rows[tile(b), :] = jnp.zeros((16, 128), BF)
        for i, (a, b) in enumerate(spans):
            rows[tile(a), :] += edge[2 * i]

            @pl.when(b != a)
            def _(i=i, b=b):
                rows[tile(b), :] += edge[2 * i + 1]

        for which in range(2):
            base = which * (SET_ROWS // 16) * 16
            flat[...] = rows[pl.ds(base, 16 * set_tiles), :].astype(F32)
            w = Group(WEIGHTS, dsts[which * len(WEIGHTS) : (which + 1) * len(WEIGHTS)])
            assemble_set(which * (SET_ROWS % 16), flat, tmp, w)

    got = pl.pallas_call(
        body,
        out_shape=structs(out),
        in_specs=[SMEM] * 2 + [HBM] * count,
        out_specs=whole(len(out)),
        scratch_shapes=[
            pltpu.VMEM((16 * tiles, 128), BF),
            pltpu.VMEM((16 * set_tiles, 128), F32),
            pltpu.VMEM((128, 128), F32),
            pltpu.VMEM((2 * count, 16, 128), BF),
            pltpu.SemaphoreType.DMA((count, bits)),
            pltpu.SemaphoreType.DMA((2 * count,)),
        ],
        compiler_params=compiler_params(),
        cost_estimate=cost(10),
    )(owner, segment_rows, *parts)
    return Group(WEIGHTS, got[: len(WEIGHTS)]), Group(WEIGHTS, got[len(WEIGHTS) :])


def adam(n_row, lower, owner, segment_rows, scales, whole_upper, blocks, master, first, second):
    held = master.shape[0]
    step = 2080
    front = step + 16
    count = len(blocks)
    n_dp = owner.shape[0]
    set_rows = ROW_BIAS - ROW_O + lower
    total_rows = front + set_rows + step + 32
    ways = 3 * n_row
    arrivals = sum(len(keys) for _, _, keys, _ in blocks)

    def body(owner_ref, rows_ref, scale_ref, *refs):
        upper, srcs, refs = refs[0], refs[1 : 1 + count], refs[1 + count :]
        master_ref, first_ref, second_ref, o_master, o_first, o_second, o_norms, rows, window, grad, rate, sems, upper_sem = refs
        i = pl.program_id(0)
        me, row = lax.axis_index("dp"), lax.axis_index("row")
        begin, length = segment_of(owner_ref, rows_ref, me, n_dp)

        @pl.when(i == 0)
        def _():
            def each(act):
                copy = pltpu.make_async_copy(
                    upper, rows.at[1, pl.ds(front + ROW_O, UPPER_ROWS), :], upper_sem
                )
                pl.when(begin + length > SET_ROWS + ROW_O)(functools.partial(act, copy))
                every = [
                    (k, core, key, n, sections)
                    for k, (_, core, keys, sections) in enumerate(blocks)
                    for n, key in enumerate(keys)
                ]
                for at_sem, (k, core, key, n, sections) in enumerate(every):
                    mine = (me ^ core) & 1
                    source = me ^ core ^ jnp.where(mine == 0, key[0], key[1])
                    stride = sum(size for _, _, size in sections)
                    offset = n * stride * n_row
                    for number, (which, part, size) in enumerate(sections):
                        block = ((source & 1) * (n_dp // 2) + (source >> 1)) * size * n_row
                        for z in range(n_row):
                            at = block + (row ^ z) * size
                            dest = at + ROW_O if part else jnp.where(at >= ROW_O, at - ROW_O + ROW_BIAS, at)
                            wanted = (dest + which * SET_ROWS < begin + length) & (
                                dest + size + which * SET_ROWS > begin
                            )
                            wanted = wanted | (dest + size > ROW_NN)
                            lies = z * stride + offset

                            def move(frm, extent, to, way, k=k, which=which, at_sem=at_sem):
                                act(
                                    pltpu.make_async_copy(
                                        srcs[k].at[pl.ds(frm, extent), :],
                                        rows.at[which, pl.ds(aligned(front + to, 16), extent), :],
                                        sems.at[at_sem, way],
                                    )
                                )

                            cut = 0 if part else ROW_O % size
                            way = number * n_row + z
                            if not cut:
                                pl.when(wanted)(functools.partial(move, lies, size, dest, way))
                                continue
                            split_here = (at < ROW_O) & (at + size > ROW_O)
                            pl.when(wanted & jnp.logical_not(split_here))(
                                functools.partial(move, lies, size, dest, way)
                            )

                            @pl.when(split_here)
                            def _(move=move, lies=lies, size=size, at=at, cut=cut, way=way, z=z):
                                move(lies, cut, at, way)
                                move(lies + cut, size - cut, ROW_BIAS, 2 * n_row + z)

                        offset += size

            each(lambda c: c.start())
            each(lambda c: c.wait())
            for which in range(2):
                v = rows[which, front + ROW_NN : front + ROW_NN + 32, :].astype(F32)
                for t in range(4):
                    for q in range(4):
                        o_norms[4 * which + t : 4 * which + t + 1, 128 * q : 128 * (q + 1)] = v[
                            4 * t + q : 4 * t + q + 1, :
                        ]
                for t in range(2):
                    both = v[16 + t : 17 + t, :]
                    at = 4 * which + 2 * t
                    o_norms[at : at + 1, 512:576] = both[:, 0:64]
                    o_norms[at + 1 : at + 2, 512:576] = pltpu.roll(both, 64, 1)[:, 0:64]

        low = begin + i * step
        high = low + step
        some = i * step < length

        @pl.when(jnp.logical_not(some))
        def _():
            o_master[...] = master_ref[...]
            o_first[...] = first_ref[...]
            o_second[...] = second_ref[...]

        @pl.when(some)
        def _():
            def shifted(which):
                local = low - which * SET_ROWS + front
                shift = local % 16
                window[...] = rows[which, pl.ds(aligned(local - shift, 16), step + 16), :].astype(F32)
                return window[pl.ds(shift, step), :]

            index = iota((step, 128), 0)

            @pl.when(low < SET_ROWS)
            def _():
                grad[...] = shifted(0)

            @pl.when(low >= SET_ROWS)
            def _():
                grad[...] = shifted(1)

            @pl.when((low < SET_ROWS) & (high > SET_ROWS))
            def _():
                grad[...] = jnp.where(index + low >= SET_ROWS, shifted(1), grad[...])

            at = index + low
            at = jnp.where(at >= SET_ROWS, at - SET_ROWS, at)
            a, b, c = RATES[0][1], RATES[1][1], RATES[3][1]
            far = jnp.where(at < ROW_DOWN, a, c)
            rate[...] = jnp.where(at < ROW_O, a, jnp.where(at < ROW_UP, b, far))
            near = (low < SET_ROWS) & (high > ROW_BIAS)

            @pl.when(near | (high > SET_ROWS + ROW_BIAS))
            def _():
                value = jnp.full((step, 128), 0.25, F32)
                for end, one in reversed(RATES[4:]):
                    value = jnp.where(at < end, one, value)
                rate[...] = jnp.where(at < ROW_BIAS, rate[...], value)

            g = grad[...]
            p, m, v = master_ref[...], first_ref[...], second_ref[...]
            m_new = BETA_ONE * m + (1.0 - BETA_ONE) * g
            v_new = BETA_TWO * v + (1.0 - BETA_TWO) * g * g
            move = (m_new * scale_ref[0]) / (jnp.sqrt(v_new * scale_ref[1]) + ADAM_EPS)
            live = index < length - i * step
            o_master[...] = jnp.where(live, p - rate[...] * (move + WEIGHT_DECAY * p), p)
            o_first[...] = jnp.where(live, m_new, m)
            o_second[...] = jnp.where(live, v_new, v)

    spec = pl.BlockSpec((step, 128), lambda i: (i, 0))
    shape = jax.ShapeDtypeStruct((held, 128), F32)
    return pl.pallas_call(
        body,
        grid=(pl.cdiv(held, step),),
        out_shape=[shape] * 3 + [jax.ShapeDtypeStruct((8, D + DE), F32)],
        in_specs=[SMEM] * 3 + [HBM] * (count + 1) + [spec] * 3,
        out_specs=[spec] * 3 + [pl.BlockSpec((8, D + DE), lambda i: (0, 0))],
        scratch_shapes=[
            pltpu.VMEM((2, total_rows, 128), BF),
            pltpu.VMEM((step + 16, 128), F32),
            pltpu.VMEM((step, 128), F32),
            pltpu.VMEM((step, 128), F32),
            pltpu.SemaphoreType.DMA((arrivals, ways)),
            pltpu.SemaphoreType.DMA(()),
        ],
        compiler_params=compiler_params(),
        cost_estimate=cost(10),
    )(owner, segment_rows, scales, whole_upper, *[b[0] for b in blocks], master, first, second)


RATES = [
    (ROW_O, 0.5 * D ** (-0.5)),
    (ROW_UP, 2.0 * D ** (-0.5)),
    (ROW_DOWN, 0.5 * D ** (-0.5)),
    (ROW_BIAS, 0.5 * FF ** (-0.5)),
    (ROW_EDGE, 0.5 * DE ** (-0.5)),
    (ROW_EUP, 0.5 * H ** (-0.5)),
    (ROW_EDOWN, 0.5 * DE ** (-0.5)),
    (ROW_NN, 0.5 * FFE ** (-0.5)),
]


class Cube:
    def __init__(self, size):
        self.size = size
        self.bits = size.bit_length() - 1
        assert size == 1 << self.bits
        up = list(range(1, self.bits))
        self.order = (up, up[::-1])

    def pairs(self, step):
        return [(i, i ^ (1 << self.order[i & 1][step])) for i in range(self.size)]

    def core_pairs(self):
        return [(i, i ^ 1) for i in range(self.size)]

    def source(self, me, key):
        other, used = key
        even, odd = [sum(1 << self.order[c][s] for s in used) for c in (0, 1)]
        if other:
            even, odd = odd, even
        return me ^ jnp.where(me & 1 == 0, even, odd) ^ other

    def gather(self, value, meanwhile):
        steps = range(self.bits - 1)
        new, done, also = [((), value)], [], None
        while new:
            sent = []
            for used, v in new:
                done.append(((0, used), v))
                for step in steps:
                    if not used or step > used[-1]:
                        sent.append((0, used + (step,), lax.ppermute(v, "dp", self.pairs(step))))
            for used, v in new:
                sent.append((1, used, lax.ppermute(v, "dp", self.core_pairs())))
            beside = None
            if also is None:
                also = meanwhile(lax.ppermute(value[:16], "dp", self.core_pairs()))
            else:
                beside = also
            moved, beside = lax.optimization_barrier(([v for _, _, v in sent], beside))
            also = also if beside is None else beside
            new = []
            for (other, used, _), v in zip(sent, moved):
                if other:
                    done.append(((1, used), v))
                else:
                    new.append((used, v))
        return done, also


def total(values):
    out = values[0].astype(F32)
    for v in values[1:]:
        out = out + v.astype(F32)
    return out.astype(BF)


class Chain:
    def __init__(self, cube, direct, *halves):
        self.cube, self.direct = cube, direct
        self.kept = [k for k, _ in halves]
        self.value = [s for _, s in halves]
        self.step, self.done = 0, False
        self.sides = lax.axis_size("dp") // 2
        self.rows = lax.axis_size("row")

    def swap(self, value):
        return lax.ppermute(value, "dp", [(i, i ^ 1) for i in range(2 * self.sides)])

    def to_chip(self, value, k):
        return lax.ppermute(value, "dp", [(i, i ^ (k << 1)) for i in range(2 * self.sides)])

    def to_row(self, value, k):
        return lax.ppermute(value, "row", [(i, i ^ k) for i in range(self.rows)])

    def scatter(self, index, count, send):
        def at(k):
            parts = [v.reshape(count, v.shape[0] // count, 128) for v in self.value]
            parts = [lax.dynamic_index_in_dim(v, index ^ k, 0, keepdims=False) for v in parts]
            return jnp.concatenate(parts) if len(parts) > 1 else parts[0]

        self.sizes = [v.shape[0] // count for v in self.value]
        self.kept = at(0)
        return [send(at(k), k) for k in range(1, count)]

    def launch(self):
        self.step += 1
        if self.step == 1:
            return [self.swap(v) for v in self.value]
        if self.step == 2:
            return self.scatter(lax.axis_index("dp") >> 1, self.sides, self.to_chip)
        if self.step == 3:
            return self.scatter(lax.axis_index("row"), self.rows, self.to_row)
        if self.step == 4:
            return [self.to_row(self.value, k) for k in range(1, self.rows)]
        if not self.spread():
            return [self.swap(self.value)]
        if self.direct:
            return [self.to_chip(self.value, k) for k in range(1, self.sides)]
        return [lax.ppermute(self.value, "dp", self.cube.pairs(self.step - 5))]

    def spread(self):
        return self.step < 6 if self.direct else self.step < 5 + self.cube.bits - 1

    def land(self, got):
        if self.step == 1:
            self.value = [total(pair) for pair in zip(self.kept, got)]
        elif self.step <= 3:
            value = total([self.kept, *got])
            if self.step == 3:
                self.value = value
            else:
                self.value, at = [], 0
                for size in self.sizes:
                    self.value.append(value[at : at + size])
                    at += size
        elif self.step == 4:
            self.value = jnp.concatenate([self.value, *got])
            self.size = self.value.shape[0]
        elif self.spread():
            self.value = jnp.concatenate([self.value, *got])
            if self.direct:
                self.keys = [(k << 1, k << 1) for k in range(self.sides)]
            else:
                bit = [1 << order[self.step - 5] for order in self.cube.order]
                keys = self.keys if self.step > 5 else [(0, 0)]
                self.keys = keys + [(a ^ bit[0], b ^ bit[1]) for a, b in keys]
        else:
            self.value, self.done = [self.value, *got], True

    def blocks(self, *names):
        sections = [(which, part, size) for (which, part), size in zip(names, self.sizes)]
        return [(v, core, self.keys, sections) for core, v in enumerate(self.value)]


def phase(chains, *ready):
    chains = [c for c in chains if not c.done]
    sent = [c.launch() for c in chains]
    got, ready = lax.optimization_barrier((sent, ready))
    for c, g in zip(chains, got):
        c.land(g)
    return ready


def per_device(
    small_nodes,
    small_edges,
    small_counts,
    big_nodes,
    big_edges,
    big_counts,
    small_node_cot,
    small_edge_cot,
    big_node_cot,
    big_edge_cot,
    master,
    first_moment,
    second_moment,
    owner,
    segment_rows,
    step_count,
):
    n_dp, n_row = lax.axis_size("dp"), lax.axis_size("row")
    cube = Cube(n_dp)
    share = big_nodes.shape[0] // n_row
    dm = Dims(small_nodes.shape[0], share, n_dp * n_row)

    def flat2(v):
        return v.reshape(-1, v.shape[-1])

    def to_rows(v):
        v = v.reshape(share, NB, OUT_LANES)
        v = lax.all_to_all(v, "row", split_axis=1, concat_axis=0, tiled=True)
        return v[..., EDGE_LANES:], v[..., :EDGE_LANES]

    def to_whole(first):
        big = (big_edges, big_edge_cot, big_nodes, big_node_cot)
        _, big = lax.optimization_barrier((first, big))
        big = jnp.concatenate(big, axis=2)
        return flat2(lax.all_to_all(big, "row", split_axis=0, concat_axis=1, tiled=True))

    held, big = cube.gather(shifted_segment(owner, segment_rows, master), to_whole)
    one, two = assemble(cube, owner, segment_rows, [v for _, v in held], [k for k, _ in held])

    own_counts = lax.dynamic_slice_in_dim(big_counts, lax.axis_index("row") * share, share)
    counts = jnp.concatenate([small_counts, own_counts])

    mid_nodes, mid_edges, kept = first_forward(
        dm, counts, one, flat2(small_nodes), flat2(small_edges), big
    )
    sno, seo, bout, node_cot, edge_cot, kept_two, ffn_two = second_forward(
        dm, counts, two, mid_nodes, mid_edges, flat2(small_node_cot), flat2(small_edge_cot), big
    )
    spread = lax.psum_scatter(ffn_two.upper, "dp", scatter_dimension=0, tiled=True)
    got = between(dm, two, one, kept_two, kept, ffn_two, edge_cot)
    outs = to_rows(bout)
    names = tuple(k for k in vars(got))
    spread, *values, bno, beo = phase([], spread, *take(got, names), *outs)
    spread = lax.psum(spread, "row")
    got = Group(names, values)
    middle = Chain(cube, False, (got.keep, got.send), (got.two_keep, got.two_send))
    names = tuple(edge_shapes(dm))
    edge_one = call_edges(dm, one, kept, got, got.edges_grad)
    edge_one = Group(names, phase([middle], *take(edge_one, names)))
    names = tuple(attention_shapes(dm))
    att_one = Group(names, phase([middle], *take(call_attention(dm, kept, got, edge_one), names)))
    sng, seg, bgrad, keep, send = call_last(dm, one, kept, got, edge_one, att_one)
    spread, sng, seg, bgrad, keep, send = phase([middle], spread, sng, seg, bgrad, keep, send)
    upper_two = lax.all_gather(spread, "dp", axis=0, tiled=True)
    last = Chain(cube, True, (keep, send))
    bgrad, = phase([last, middle], bgrad)
    outs = to_rows(bgrad)
    phase([last, middle])
    sent = middle.launch()
    phase([last])
    sent, bng, beg, upper_two = phase([last], sent, *outs, upper_two)
    middle.land(sent)
    while not (last.done and middle.done):
        phase([last, middle])
    blocks = last.blocks((0, 0)) + middle.blocks((0, 1), (1, 0))
    step_value = step_count[0].astype(F32)
    scales = jnp.stack(
        [
            1.0 / (1.0 - jnp.power(F32(BETA_ONE), step_value)),
            1.0 / (1.0 - jnp.power(F32(BETA_TWO), step_value)),
        ]
    )
    new_master, new_first, new_second, norm_grads = adam(
        n_row, dm.lower, owner, segment_rows, scales, upper_two, blocks, master, first_moment, second_moment
    )
    return (
        sno.reshape(small_nodes.shape),
        seo.reshape(small_edges.shape),
        bno,
        beo,
        sng.reshape(small_nodes.shape),
        seg.reshape(small_edges.shape),
        bng,
        beg,
        new_master,
        new_first,
        new_second,
        norm_grads,
    )


def solution(mesh):
    both = P(("dp", "row"), None, None)
    rows = P("dp", "row", None)
    held = P("dp", None)
    in_specs = (
        both, both, P(("dp", "row")), rows, rows, P("dp"), both, both, rows, rows,
        held, held, held, P(), P(), P(),
    )
    out_specs = (both, both, rows, rows, both, both, rows, rows, held, held, held, P())
    return jax.shard_map(
        per_device, mesh=mesh, in_specs=in_specs, out_specs=out_specs, check_vma=False
    )
```

```python
import functools

import jax
import jax.numpy as jnp
from jax import lax
from jax.experimental import pallas as pl
from jax.experimental.pallas import tpu as pltpu
from jax.sharding import PartitionSpec as P

D = 512
H = 32
DE = 64
FF = 1024
FFE = 128
NS = 32
NB = 64
SET_ROWS = 16578
TOTAL_ROWS = 33156
NORM_EPS = 1e-05
BETA_ONE = 0.9
BETA_TWO = 0.95
WEIGHT_DECAY = 0.1
ADAM_EPS = 1e-08
MASK_FILL = -1e30
BF = jnp.bfloat16
F32 = jnp.float32
VMEM_LIMIT = 58 * 1024 * 1024
ROW_QKV, ROW_O, ROW_UP, ROW_DOWN = 0, 6144, 8192, 12288
ROW_BIAS, ROW_GATE, ROW_EDGE, ROW_EUP, ROW_EDOWN = 16384, 16400, 16416, 16432, 16496
ROW_NN, ROW_EN = 16560, 16576
SMALL_USED, SMALL_ROWS = SET_ROWS - ROW_BIAS, 256
BIAS, GATE, EDGE, EUP, EDOWN = 0, 16, 32, 48, 112
NN, EN = ROW_NN - ROW_BIAS, ROW_EN - ROW_BIAS
UPPER_ROWS = ROW_BIAS - ROW_O
GELU_C = 0.7978845608028654
PAIRS = 4


def nn(a, b):
    return lax.dot_general(a, b, (((1,), (0,)), ((), ())), preferred_element_type=F32)


def nt(a, b):
    return lax.dot_general(a, b, (((1,), (1,)), ((), ())), preferred_element_type=F32)


def tn(a, b):
    return lax.dot_general(a, b, (((0,), (0,)), ((), ())), preferred_element_type=F32)


def iota(shape, axis):
    return lax.broadcasted_iota(jnp.int32, shape, axis)


def gelu_parts(u):
    u2 = u * u
    t = jnp.tanh(u * (GELU_C + (GELU_C * 0.044715) * u2))
    half = 0.5 + 0.5 * t
    value = u * half
    slope = half + value * (1.0 - t) * (GELU_C + (3.0 * GELU_C * 0.044715) * u2)
    return value, slope


def gelu_value(u):
    return u * (0.5 + 0.5 * jnp.tanh(u * (GELU_C + (GELU_C * 0.044715) * (u * u))))


def sigmoid(v):
    return 0.5 + 0.5 * jnp.tanh(0.5 * v)


def group_sum(v, first=16):
    while first < 128:
        v = v + pltpu.roll(v, first, 1)
        first *= 2
    return v


def group_max(v):
    for shift in (16, 32, 64):
        v = jnp.maximum(v, pltpu.roll(v, shift, 1))
    return v


def fold8(v):
    return jnp.sum(v.reshape(v.shape[0] // 8, 8, v.shape[1]), axis=0)


class Bucket:
    def __init__(self, graphs, slots, node0, edge0, count0):
        self.graphs, self.slots = graphs, slots
        self.node0, self.edge0, self.count0 = node0, edge0, count0
        self.rows = graphs * slots
        self.chunks = slots // 4
        self.pairs = slots // 8
        self.blocks = slots // 16
        self.edges = self.rows * self.chunks
        self.edge_lanes = slots * DE


class Dims:
    def __init__(self, small_graphs, big_graphs, parts):
        self.lower = round_up(ROW_O + SMALL_ROWS, 16 * parts)
        self.small = Bucket(small_graphs, NS, 0, 0, 0)
        self.big = Bucket(big_graphs, NB, self.small.rows, self.small.edges, small_graphs)
        self.buckets = (self.small, self.big)
        self.nodes = self.small.rows + self.big.rows
        self.edges = self.small.edges + self.big.edges
        self.scores = self.edges // 2
        self.blocks = sum(b.graphs * b.blocks for b in self.buckets)

    def each_pair(self, body):
        for bucket in self.buckets:
            two = 2 * PAIRS * bucket.rows

            @pl.loop(0, bucket.pairs // PAIRS, unroll=True)
            def _(i, bucket=bucket, two=two):
                body(
                    pl.ds(aligned(bucket.edge0 + i * two, 32), two),
                    pl.ds(aligned((bucket.edge0 + i * two) // 2, 16), two // 2),
                )


def beside(v):
    one = v.shape[0] // (2 * PAIRS)
    at = lambda c: v[c * one : (c + 1) * one]
    sides = [[at(2 * p + c) for p in range(PAIRS)] for c in range(2)]
    return jnp.concatenate([jnp.concatenate(s) for s in sides], axis=1)


def below(v):
    one = v.shape[0] // PAIRS
    at = lambda p, c: v[p * one : (p + 1) * one, 256 * c : 256 * (c + 1)]
    return jnp.concatenate([at(p, c) for p in range(PAIRS) for c in range(2)])


def make_masks(scr):
    make_mean(scr)
    make_heads(scr)


def make_mean(scr):
    shape = (256, 256)
    same = (iota(shape, 0) >> 6) == (iota(shape, 1) >> 6)
    scr.mean[...] = jnp.where(same, 1.0 / DE, 0.0).astype(BF)


def make_heads(scr):
    shape = (16, 256)
    scr.head[...] = jnp.where(iota(shape, 0) == (iota(shape, 1) >> 4), 1.0, 0.0)


def node_norm(v):
    centred = v - jnp.mean(v, axis=1, keepdims=True)
    r = lax.rsqrt(jnp.mean(centred * centred, axis=1, keepdims=True) + NORM_EPS)
    return centred * r, r


def node_norm_back(gdy, n, r):
    return r * (gdy - jnp.mean(gdy, axis=1, keepdims=True) - n * jnp.mean(gdy * n, axis=1, keepdims=True))


def aligned(value, by):
    return pl.multiple_of(value, by)


def block_of(bucket, t):
    g = t // bucket.blocks
    b = t % bucket.blocks
    rows = pl.ds(aligned(bucket.node0 + g * bucket.slots, 16), bucket.slots)
    keys = pl.ds(aligned(bucket.node0 + t * 16, 16), 16)
    pair_rows = [
        pl.ds(
            aligned(bucket.edge0 // 2 + (2 * b + c) * bucket.rows + g * bucket.slots, 16),
            bucket.slots,
        )
        for c in range(2)
    ]
    return rows, keys, pair_rows


def side(first, half):
    return slice(first + 256 * half, first + 256 * (half + 1))


def lanes(half):
    return slice(128 * half, 128 * (half + 1))


def expand(values, scr):
    spread = values.astype(F32)[:, None, :] * scr.head[...][None]
    return spread.reshape(256, 256).astype(BF)


def collect(values, scr):
    return jnp.sum(values.reshape(16, 16, 256) * scr.head[...][None], axis=1)


def joined(ref, pair_rows, half):
    return jnp.concatenate([ref[r, lanes(half)] for r in pair_rows], axis=1)


def forward(dm, counts, w, io, res, scr):
    x = io.nodes[...].astype(F32)
    n, r = node_norm(x)
    res.node_n1[...] = n.astype(BF)
    res.node_r1[...] = jnp.broadcast_to(r, (dm.nodes, 128))
    hn = (n * w.nn[0:1, :] + w.nn[1:2, :]).astype(BF)
    res.qkv[...] = nn(hn, w.qkv[...]).astype(BF)

    @dm.each_pair
    def _(rows, pair):
        x = io.edges[rows, :]
        centred = x.astype(F32) - nn(x, scr.mean[...])
        r = lax.rsqrt(nn((centred * centred).astype(BF), scr.mean[...]) + NORM_EPS)
        n = centred * r
        res.edge_n1[rows, :] = n.astype(BF)
        res.edge_r1[rows, :] = r.astype(BF)
        xn = (n * w.en[0:1, :] + w.en[1:2, :]).astype(BF)
        both = nn(beside(xn), w.eg[...])
        scr.scores[pair, :] = both[:, :256]
        res.gate[pair, :] = both[:, 256:]

    t0 = 0
    for bucket in dm.buckets:
        @pl.loop(0, bucket.graphs * bucket.blocks, unroll=True)
        def _(t, bucket=bucket, t0=t0):
            rows, keys, pair_rows = block_of(bucket, t)
            for half in range(2):
                kb = expand(res.qkv[keys, side(512, half)], scr)
                scr.vbig[t0 + t, half] = expand(res.qkv[keys, side(1024, half)], scr)
                s = nt(res.qkv[rows, side(0, half)], kb) * 0.25
                for c in range(2):
                    scr.scores[pair_rows[c], lanes(half)] += s[:, lanes(c)]

        @pl.loop(0, bucket.rows // 32, unroll=True)
        def _(i, bucket=bucket):
            count = counts[bucket.count0 + i * 32 // bucket.slots]
            lane_key = iota((32, 128), 1) >> 4
            row = [
                pl.ds(aligned(bucket.edge0 // 2 + c * bucket.rows + i * 32, 32), 32)
                for c in range(bucket.pairs)
            ]
            for half in range(2):
                at = lanes(half)
                top = jnp.full((32, 128), MASK_FILL, F32)
                for c in range(bucket.pairs):
                    s = scr.scores[row[c], at]
                    res.low[row[c], at] = s.astype(BF)
                    top = jnp.maximum(top, jnp.where(lane_key < count - 8 * c, s, MASK_FILL))
                top = group_max(top)
                sums = jnp.zeros((32, 128), F32)
                for c in range(bucket.pairs):
                    s = jnp.where(lane_key < count - 8 * c, scr.scores[row[c], at], MASK_FILL)
                    e = jnp.exp(s - top)
                    sums = sums + e
                    scr.scores[row[c], at] = e
                inv = 1.0 / group_sum(sums)
                for c in range(bucket.pairs):
                    p = scr.scores[row[c], at] * inv
                    res.prob[row[c], at] = p.astype(BF)
                    scr.attn[row[c], at] = (p * sigmoid(res.gate[row[c], at])).astype(BF)

        @pl.loop(0, bucket.graphs, unroll=True)
        def _(g, bucket=bucket, t0=t0):
            for half in range(2):
                sums = None
                for b in range(bucket.blocks):
                    t = g * bucket.blocks + b
                    rows, _, pair_rows = block_of(bucket, t)
                    part = nn(joined(scr.attn, pair_rows, half), scr.vbig[t0 + t, half])
                    sums = part if sums is None else sums + part
                res.mixed[rows, side(0, half)] = sums.astype(BF)

        t0 += bucket.graphs * bucket.blocks

    y = io.nodes[...].astype(F32) + nn(res.mixed[...], w.o[...])
    n, r = node_norm(y)
    res.node_n2[...] = n.astype(BF)
    res.node_r2[...] = jnp.broadcast_to(r, (dm.nodes, 128))
    z = (n * w.nn[2:3, :] + w.nn[3:4, :]).astype(BF)
    u = nn(z, w.up[...])
    res.node_u[...] = u
    io.nodes_out[...] = (y + nn(gelu_value(u).astype(BF), w.down[...])).astype(BF)

    @dm.each_pair
    def _(rows, pair):
        m = io.edges[rows, :].astype(F32) + below(nn(res.low[pair, :], w.x[...]))
        high = m.astype(BF)
        rest = (m - high.astype(F32)).astype(BF)
        centred = m - nn(high, scr.mean[...]) - nn(rest, scr.mean[...])
        r = lax.rsqrt(nn((centred * centred).astype(BF), scr.mean[...]) + NORM_EPS)
        n = centred * r
        res.edge_n2[rows, :] = n.astype(BF)
        res.edge_r2[rows, :] = r.astype(BF)
        mn = (n * w.en[2:3, :] + w.en[3:4, :]).astype(BF)
        ua = nn(mn, w.a[...])
        io.edges_out[rows, :] = (m + nn(gelu_value(ua).astype(BF), w.b[...])).astype(BF)


def put_strided(flat, first, value, parts):
    for q in range(parts):
        flat[pl.ds(first + q, value.shape[0], stride=parts), :] = value[:, 128 * q : 128 * (q + 1)]


def back_ffn(dm, w, io, res, scr):
    flat = scr.upper
    gy = io.nodes_cot[...]
    act, slope = gelu_parts(res.node_u[...])
    du = (nt(gy, w.down[...]) * slope).astype(BF)
    put_strided(flat, ROW_DOWN - ROW_O, tn(act.astype(BF), gy), 4)
    n = res.node_n2[...].astype(F32)
    z = (n * w.nn[2:3, :] + w.nn[3:4, :]).astype(BF)
    put_strided(flat, ROW_UP - ROW_O, tn(z, du), 8)
    dz = nt(du, w.up[...])
    gain = jnp.sum(dz * n, axis=0, keepdims=True)
    bias = jnp.sum(dz, axis=0, keepdims=True)
    dy = gy.astype(F32) + node_norm_back(dz * w.nn[2:3, :], n, res.node_r2[:, 0:1])
    io.dy[...] = dy
    dyl = dy.astype(BF)
    put_strided(flat, 0, tn(res.mixed[...], dyl), 4)
    io.do[...] = nt(dyl, w.o[...]).astype(BF)
    for q in range(4):
        io.sums[q : q + 1, :] = gain[:, 128 * q : 128 * (q + 1)]
        io.sums[4 + q : 5 + q, :] = bias[:, 128 * q : 128 * (q + 1)]
    if hasattr(io, "upper"):
        io.upper[...] = flat[...].astype(BF)
    else:
        put_halves(flat, io.keep, io.send)


def put_halves(flat, keep, send):
    half = keep.shape[0]
    core = lax.axis_index("dp") & 1
    keep[...] = flat[pl.ds(aligned(core * half, 16), half), :].astype(BF)
    send[...] = flat[pl.ds(aligned((1 - core) * half, 16), half), :].astype(BF)


def stacked(v, width):
    return jnp.concatenate([v[:, i : i + width] for i in range(0, v.shape[1], width)])


def back_edges(dm, w, io, res, scr):
    io.small[NN + 8 : NN + 16, :] = io.sums[...]
    scr.gb[...] = jnp.zeros((256, 128), F32)
    scr.ga[...] = jnp.zeros((128, 256), F32)
    scr.gx[...] = jnp.zeros((256, 512), F32)
    scr.en[...] = jnp.zeros((2, 8, 256), F32)

    @dm.each_pair
    def _(rows, pair):
        gx = io.edges_cot[rows, :]
        n = res.edge_n2[rows, :].astype(F32)
        mn = (n * w.en[2:3, :] + w.en[3:4, :]).astype(BF)
        act, slope = gelu_parts(nn(mn, w.a[...]))
        dua = (nt(gx, w.b[...]) * slope).astype(BF)
        act = act.astype(BF)
        scr.gb[...] += tn(stacked(act, 256), stacked(gx, 128))
        scr.ga[...] += tn(stacked(mn, 128), stacked(dua, 256))
        dmn = nt(dua, w.a[...])
        scr.en[0] += fold8(dmn * n)
        scr.en[1] += fold8(dmn)
        gdy = dmn * w.en[2:3, :]
        m1 = nn(gdy.astype(BF), scr.mean[...])
        m2 = nn((gdy * n).astype(BF), scr.mean[...])
        dmid = gx.astype(F32) + res.edge_r2[rows, :].astype(F32) * (gdy - m1 - n * m2)
        dml = dmid.astype(BF)
        io.dmid[rows, :] = dml
        dml = beside(dml)
        scr.gx[...] += tn(res.low[pair, :], dml)
        io.scores[pair, :] = nt(dml, w.x[...])

    io.small[EUP : EUP + 64, :] = scr.ga[0:64, 0:128] + scr.ga[64:128, 128:256]
    sums = jnp.where(lane_group(128, 6) == 0, scr.gb[0:128, :], scr.gb[128:256, :])
    fold_halves(sums, scr.tmp, io.small, EDOWN)
    sides = []
    for half in range(2):
        sums = jnp.zeros((16, 128), F32)
        for k in range(8):
            at = 128 * half + 16 * k
            part = scr.gx[at : at + 16, 128 * (k // 2) : 128 * (k // 2 + 1)]
            sums = sums + jnp.where(lane_group(16, 6) == k % 2, part, 0.0)
        sides.append(sums)
    fold_halves(jnp.concatenate(sides), scr.tmp, io.small, EDGE)
    put_edge_norm(scr.en, io.small, EN + 1)
    io.small[SMALL_USED:, :] = jnp.zeros((SMALL_ROWS - SMALL_USED, 128), F32)


def back_attention(dm, io, res, scr):
    t0 = 0
    for bucket in dm.buckets:
        @pl.loop(0, bucket.graphs * bucket.blocks, unroll=True)
        def _(t, bucket=bucket, t0=t0):
            rows, keys, pair_rows = block_of(bucket, t)
            for half in range(2):
                scr.vbig[t0 + t, half] = expand(res.qkv[keys, side(512, half)], scr)
                vb = expand(res.qkv[keys, side(1024, half)], scr)
                da = nt(io.do[rows, side(0, half)], vb)
                for c in range(2):
                    scr.da[pair_rows[c], lanes(half)] = da[:, lanes(c)]

        @pl.loop(0, bucket.rows // 32, unroll=True)
        def _(i, bucket=bucket):
            row = [
                pl.ds(aligned(bucket.edge0 // 2 + c * bucket.rows + i * 32, 32), 32)
                for c in range(bucket.pairs)
            ]
            for half in range(2):
                at = lanes(half)
                sums = jnp.zeros((32, 128), F32)
                for c in range(bucket.pairs):
                    p = res.prob[row[c], at].astype(F32)
                    s = sigmoid(res.gate[row[c], at])
                    scr.attn[row[c], at] = (p * s).astype(BF)
                    pt = p * scr.da[row[c], at] * s
                    scr.da[row[c], at] = pt
                    sums = sums + pt
                    io.dsg[row[c], lanes(2 + half)] = (pt * (1.0 - s)).astype(BF)
                sums = group_sum(sums)
                for c in range(bucket.pairs):
                    p = res.prob[row[c], at].astype(F32)
                    ds = scr.da[row[c], at] - p * sums + io.scores[row[c], at]
                    io.dsg[row[c], at] = ds.astype(BF)

        @pl.loop(0, bucket.graphs, unroll=True)
        def _(g, bucket=bucket, t0=t0):
            for half in range(2):
                sums = None
                for b in range(bucket.blocks):
                    t = g * bucket.blocks + b
                    rows, keys, pair_rows = block_of(bucket, t)
                    ds = joined(io.dsg, pair_rows, half)
                    part = nn(ds, scr.vbig[t0 + t, half])
                    sums = part if sums is None else sums + part
                    gk = collect(tn(ds, res.qkv[rows, side(0, half)]), scr)
                    io.dqkv[keys, side(512, half)] = (gk * 0.25).astype(BF)
                    gv = tn(joined(scr.attn, pair_rows, half), io.do[rows, side(0, half)])
                    io.dqkv[keys, side(1024, half)] = collect(gv, scr).astype(BF)
                io.dqkv[rows, side(0, half)] = (sums * 0.25).astype(BF)

        t0 += bucket.graphs * bucket.blocks


def back_nodes(dm, w, io, res, scr):
    n = res.node_n1[...].astype(F32)
    dhn = nt(io.dqkv[...], w.qkv[...])
    gain = jnp.sum(dhn * n, axis=0, keepdims=True)
    bias = jnp.sum(dhn, axis=0, keepdims=True)
    for q in range(4):
        io.sums_one[q : q + 1, :] = gain[:, 128 * q : 128 * (q + 1)]
        io.sums_one[4 + q : 5 + q, :] = bias[:, 128 * q : 128 * (q + 1)]
    dx = io.dy[...] + node_norm_back(dhn * w.nn[0:1, :], n, res.node_r1[:, 0:1])
    io.nodes_grad[...] = dx.astype(BF)


def back_last(dm, w, io, res, scr):
    flat = scr.lower
    n = res.node_n1[...].astype(F32)
    hn = (n * w.nn[0:1, :] + w.nn[1:2, :]).astype(BF)
    for m in range(3):
        put_strided(flat, 2048 * m, tn(hn, io.dqkv[:, 512 * m : 512 * (m + 1)]), 4)
    small = flat.at[pl.ds(ROW_O, SMALL_ROWS), :]
    small[...] = io.small[...]
    small[NN : NN + 8, :] = io.sums_one[...]

    scr.geg[...] = jnp.zeros((512, 512), F32)
    scr.en[...] = jnp.zeros((2, 8, 256), F32)

    @dm.each_pair
    def _(rows, pair):
        dsg = io.dsg[pair, :]
        n = res.edge_n1[rows, :].astype(F32)
        xn = (n * w.en[0:1, :] + w.en[1:2, :]).astype(BF)
        scr.geg[...] += tn(beside(xn), dsg)
        dxn = below(nt(dsg, w.eg[...]))
        scr.en[0] += fold8(dxn * n)
        scr.en[1] += fold8(dxn)
        gdy = dxn * w.en[0:1, :]
        m1 = nn(gdy.astype(BF), scr.mean[...])
        m2 = nn((gdy * n).astype(BF), scr.mean[...])
        dx = io.dmid[rows, :].astype(F32) + res.edge_r1[rows, :].astype(F32) * (gdy - m1 - n * m2)
        io.edges_grad[rows, :] = dx.astype(BF)

    for which, first in ((0, BIAS), (1, GATE)):
        sides = []
        for half in range(2):
            sums = jnp.zeros((64, 128), F32)
            for k in range(8):
                part = scr.geg[64 * k : 64 * (k + 1), lanes(2 * which + half)]
                sums = sums + jnp.where(lane_group(64, 4) == k, part, 0.0)
            sides.append(group_sum(sums))
        scr.tmp[0:64, :] = jnp.where(lane_group(64, 4) % 2 == 0, sides[0], sides[1])
        rows = jnp.zeros((16, 128), F32)
        for b in range(4):
            rows = jnp.where(lane_group(16, 5) == b, scr.tmp[pl.ds(b, 16, stride=4), :], rows)
        small[first : first + 16, :] = rows
    put_edge_norm(scr.en, small, EN)
    end = ROW_O + SMALL_ROWS
    if dm.lower > end:
        flat[end:, :] = jnp.zeros((dm.lower - end, 128), F32)
    put_halves(flat, io.keep, io.send)


def lane_group(rows, bits):
    return iota((rows, 128), 1) >> bits


def fold_halves(sums, tmp, out, first):
    rows, half = sums.shape[0], sums.shape[0] // 2
    tmp[0:rows, :] = sums + pltpu.roll(sums, 64, 1)
    even = tmp[pl.ds(0, half, stride=2), :]
    odd = tmp[pl.ds(1, half, stride=2), :]
    out[first : first + half, :] = jnp.where(lane_group(half, 6) == 0, even, odd)


def put_edge_norm(sums, out, at):
    ones = []
    for t in range(2):
        both = jnp.sum(sums[t], axis=0, keepdims=True)
        one = both[:, :128] + both[:, 128:]
        ones.append(one + pltpu.roll(one, 64, 1))
    out[at : at + 1, :] = jnp.where(lane_group(1, 6) == 0, ones[0], ones[1])


def assemble_set(off, flat, tmp, w):
    def strided(first, rows, parts, out, lane0=0):
        for q in range(parts):
            out[:, lane0 + 128 * q : lane0 + 128 * (q + 1)] = flat[
                pl.ds(off + first + q, rows, stride=parts), :
            ].astype(BF)

    for m in range(3):
        strided(ROW_QKV + 2048 * m, 512, 4, w.qkv, 512 * m)
    strided(ROW_O, 512, 4, w.o)
    strided(ROW_UP, 512, 8, w.up)
    strided(ROW_DOWN, 1024, 4, w.down)
    w.eg[...] = jnp.zeros((512, 512), BF)
    w.x[...] = jnp.zeros((256, 512), BF)
    w.a[...] = jnp.zeros((256, 512), BF)
    w.b[...] = jnp.zeros((512, 256), BF)
    up = flat[pl.ds(off + ROW_EUP, 64), :].astype(BF)
    for k in range(4):
        w.a[64 * k : 64 * (k + 1), 128 * k : 128 * (k + 1)] = up

    def doubled(first, in_rows):
        v = flat[pl.ds(off + first, in_rows), :]
        other = pltpu.roll(v, 64, 1)
        low = lane_group(in_rows, 6) == 0
        tmp[pl.ds(0, in_rows, stride=2), :] = jnp.where(low, v, other)
        tmp[pl.ds(1, in_rows, stride=2), :] = jnp.where(low, other, v)
        return tmp[0 : 2 * in_rows, :]

    both = doubled(ROW_EDOWN, 64)
    for k in range(4):
        w.b[128 * k : 128 * (k + 1), 128 * (k // 2) : 128 * (k // 2 + 1)] = jnp.where(
            lane_group(128, 6) == k % 2, both, 0.0
        ).astype(BF)
    both = doubled(ROW_EDGE, 16)
    for half in range(2):
        for k in range(8):
            at = 128 * half + 16 * k
            w.x[at : at + 16, 128 * (k // 2) : 128 * (k // 2 + 1)] = jnp.where(
                lane_group(16, 6) == k % 2, both[16 * half : 16 * (half + 1)], 0.0
            ).astype(BF)
    for which, first in ((0, ROW_BIAS), (1, ROW_GATE)):
        v = flat[pl.ds(off + first, 16), :]
        for b in range(4):
            tmp[pl.ds(b, 16, stride=4), :] = group_sum(jnp.where(lane_group(16, 5) == b, v, 0.0), 32)
        both = tmp[0:64, :]
        even = lane_group(64, 4) % 2 == 0
        sides = (
            jnp.where(even, both, pltpu.roll(both, 16, 1)),
            jnp.where(even, pltpu.roll(both, 112, 1), both),
        )
        for half in range(2):
            for k in range(8):
                w.eg[64 * k : 64 * (k + 1), lanes(2 * which + half)] = jnp.where(
                    lane_group(64, 4) == k, sides[half], 0.0
                ).astype(BF)
    for t in range(4):
        for q in range(4):
            w.nn[t : t + 1, 128 * q : 128 * (q + 1)] = flat[pl.ds(off + ROW_NN + 4 * t + q, 1), :]
    for t in range(2):
        v = flat[pl.ds(off + ROW_EN + t, 1), :]
        other = pltpu.roll(v, 64, 1)
        gain = jnp.where(lane_group(1, 6) == 0, v, other)
        bias = jnp.where(lane_group(1, 6) == 0, other, v)
        for half in range(2):
            w.en[2 * t : 2 * t + 1, 128 * half : 128 * (half + 1)] = gain
            w.en[2 * t + 1 : 2 * t + 2, 128 * half : 128 * (half + 1)] = bias


class Group:
    def __init__(self, names, refs):
        for name, ref in zip(names, refs):
            setattr(self, name, ref)


WEIGHTS = {
    "qkv": ((D, 3 * D), BF),
    "o": ((D, D), BF),
    "up": ((D, FF), BF),
    "down": ((FF, D), BF),
    "eg": ((512, 512), BF),
    "x": ((256, 512), BF),
    "a": ((256, 512), BF),
    "b": ((512, 256), BF),
    "nn": ((4, D), F32),
    "en": ((4, 256), F32),
}


def residual_shapes(dm):
    return {
        "node_n1": ((dm.nodes, D), BF),
        "node_r1": ((dm.nodes, 128), F32),
        "qkv": ((dm.nodes, 3 * D), BF),
        "mixed": ((dm.nodes, D), BF),
        "node_n2": ((dm.nodes, D), BF),
        "node_r2": ((dm.nodes, 128), F32),
        "node_u": ((dm.nodes, FF), F32),
        "edge_n1": ((dm.edges, 256), BF),
        "edge_r1": ((dm.edges, 256), BF),
        "gate": ((dm.scores, 256), F32),
        "low": ((dm.scores, 256), BF),
        "prob": ((dm.scores, 256), BF),
        "edge_n2": ((dm.edges, 256), BF),
        "edge_r2": ((dm.edges, 256), BF),
    }


def mean_shapes():
    return {"mean": ((256, 256), BF)}


def head_shapes():
    return {"head": ((16, 256), F32)}


def mask_shapes():
    return {**mean_shapes(), **head_shapes()}


def forward_scratch(dm):
    return {
        "scores": ((dm.scores, 256), F32),
        "attn": ((dm.scores, 256), BF),
        "vbig": ((dm.blocks, 2, 256, 256), BF),
    }


def ffn_shapes(dm, halves):
    half = ((UPPER_ROWS // 2, 128), BF)
    grads = {"keep": half, "send": half} if halves else {"upper": ((UPPER_ROWS, 128), BF)}
    return {
        "dy": ((dm.nodes, D), F32),
        "do": ((dm.nodes, D), BF),
        "sums": ((8, 128), F32),
        **grads,
    }


def edge_shapes(dm):
    return {
        "dmid": ((dm.edges, 256), BF),
        "scores": ((dm.scores, 256), F32),
        "small": ((SMALL_ROWS, 128), F32),
    }


def attention_shapes(dm):
    return {"dsg": ((dm.scores, 512), BF), "dqkv": ((dm.nodes, 3 * D), BF)}


def ffn_scratch():
    return {"upper": ((UPPER_ROWS, 128), F32)}


def edge_scratch():
    return {
        "gb": ((256, 128), F32),
        "ga": ((128, 256), F32),
        "gx": ((256, 512), F32),
        "en": ((2, 8, 256), F32),
        "tmp": ((128, 128), F32),
    }


def attention_scratch(dm):
    return {
        "attn": ((dm.scores, 256), BF),
        "vbig": ((dm.blocks, 2, 256, 256), BF),
        "da": ((dm.scores, 256), F32),
    }


def last_scratch(dm):
    return {
        "geg": ((512, 512), F32),
        "en": ((2, 8, 256), F32),
        "tmp": ((128, 128), F32),
        "lower": ((dm.lower, 128), F32),
    }


def structs(shapes):
    return [jax.ShapeDtypeStruct(s, t) for s, t in shapes.values()]


def vmem(shapes):
    return [pltpu.VMEM(s, t) for s, t in shapes.values()]


def whole(n):
    return [pl.BlockSpec(memory_space=pltpu.VMEM)] * n


def split(refs, *groups):
    out, at = [], 0
    for names in groups:
        out.append(Group(names, refs[at : at + len(names)]))
        at += len(names)
    assert at == len(refs)
    return out


def edge_copies(dm, small, big, big_lane, stacked, sems, out):
    copies = []
    for bucket, ref, lane in ((dm.small, small, 0), (dm.big, big, big_lane)):
        for c in range(bucket.chunks):
            a = ref.at[:, pl.ds(lane + 256 * c, 256)]
            b = stacked.at[pl.ds(bucket.edge0 + c * bucket.rows, bucket.rows), :]
            src, dst = (b, a) if out else (a, b)
            copies.append(pltpu.make_async_copy(src, dst, sems.at[len(copies)]))
    return copies


def node_copies(dm, small, big, big_lane, nodes, sems, at, out):
    copies = []
    for bucket, ref in ((dm.small, small), (dm.big, big.at[:, pl.ds(big_lane, D)])):
        b = nodes.at[pl.ds(bucket.node0, bucket.rows), :]
        src, dst = (b, ref) if out else (ref, b)
        copies.append(pltpu.make_async_copy(src, dst, sems.at[at + len(copies)]))
    return copies


def copy_sems(dm):
    return pltpu.SemaphoreType.DMA((dm.small.chunks + dm.big.chunks + 2,))


def all_copies(dm, small_nodes, small_edges, big, edge_lane, node_lane, nodes, edges, sems, out):
    copies = edge_copies(dm, small_edges, big, edge_lane, edges, sems, out)
    return node_copies(dm, small_nodes, big, node_lane, nodes, sems, len(copies), out) + copies


def start(copies):
    for c in copies:
        c.start()


def wait(copies):
    for c in copies:
        c.wait()


HBM = pl.BlockSpec(memory_space=pl.ANY)
SMEM = pl.BlockSpec(memory_space=pltpu.SMEM)
EDGE_LANES = NB * DE
IN_LANES = 2 * EDGE_LANES + 2 * D
OUT_LANES = EDGE_LANES + D


def compiler_params():
    return pltpu.CompilerParams(vmem_limit_bytes=VMEM_LIMIT)


def cost(us):
    return pl.CostEstimate(flops=0, bytes_accessed=int(us * 3.4e6), transcendentals=0)


def take(group, names):
    return [getattr(group, k) for k in names]


NODE_BACK = ("node_n2", "node_r2", "node_u", "mixed")
EDGE_BACK = ("edge_n2", "edge_r2", "low")
ATTENTION_BACK = ("qkv", "prob", "gate")
LAST_BACK = ("node_n1", "node_r1", "edge_n1", "edge_r1")
W_NODE = ("o", "up", "down", "nn")
W_EDGE = ("x", "a", "b", "en")
W_LAST = ("qkv", "eg", "nn", "en")


def kernel(body, inputs, out, scr, us, counts=None, hbm_in=0, hbm_out=(), sems=()):
    smem = [] if counts is None else [counts]
    return Group(
        out,
        pl.pallas_call(
            body,
            out_shape=structs(out),
            in_specs=[SMEM] * len(smem) + whole(len(inputs) - hbm_in) + [HBM] * hbm_in,
            out_specs=[HBM if k in hbm_out else pl.BlockSpec(memory_space=pltpu.VMEM) for k in out],
            scratch_shapes=vmem(scr) + list(sems),
            compiler_params=compiler_params(),
            cost_estimate=cost(us),
        )(*smem, *inputs),
    )


def first_forward(dm, counts, weights, small_nodes, small_edges, big):
    res = residual_shapes(dm)
    out = {"nodes_out": ((dm.nodes, D), BF), "edges_out": ((dm.edges, 256), BF), **res}
    scr = {
        **mask_shapes(),
        **forward_scratch(dm),
        "nodes": ((dm.nodes, D), BF),
        "edges": ((dm.edges, 256), BF),
    }

    def body(*refs):
        counts_ref, refs, sems = refs[0], refs[1:-1], refs[-1]
        w, src, dst, s = split(refs, WEIGHTS, ("sn", "se", "big"), out, scr)
        copies = all_copies(
            dm, src.sn, src.se, src.big, 0, 2 * EDGE_LANES, s.nodes, s.edges, sems, False
        )
        start(copies)
        make_masks(s)
        io = Group(
            ("nodes", "edges", "nodes_out", "edges_out"),
            (s.nodes, s.edges, dst.nodes_out, dst.edges_out),
        )
        wait(copies)
        forward(dm, counts_ref, w, io, dst, s)

    inputs = take(weights, WEIGHTS) + [small_nodes, small_edges, big]
    got = kernel(body, inputs, out, scr, 38, counts, 3, (), [copy_sems(dm)])
    return got.nodes_out, got.edges_out, got


def second_forward(dm, counts, weights, nodes, edges, small_node_cot, small_edge_cot, big):
    res, ffn = residual_shapes(dm), ffn_shapes(dm, False)
    whole_outs = {
        "sno": ((dm.small.rows, D), BF),
        "seo": ((dm.small.rows, dm.small.edge_lanes), BF),
        "bout": ((dm.big.rows, OUT_LANES), BF),
    }
    node_res = [k for k in res if k in NODE_BACK]
    kept = {k: v for k, v in res.items() if k not in NODE_BACK}
    out = {**whole_outs, "edge_cot": ((dm.edges, 256), BF), **kept, **ffn}
    scr = {
        **mask_shapes(),
        **forward_scratch(dm),
        **ffn_scratch(),
        **{k: res[k] for k in node_res},
        "nodes_out": ((dm.nodes, D), BF),
        "edges_out": ((dm.edges, 256), BF),
        "node_cot": ((dm.nodes, D), BF),
    }

    def body(*refs):
        counts_ref, refs, in_sems, out_sems = refs[0], refs[1:-2], refs[-2], refs[-1]
        w, src, dst, s = split(refs, WEIGHTS, ("nodes", "edges", "snc", "sec", "big"), out, scr)
        copies = all_copies(
            dm, src.snc, src.sec, src.big, EDGE_LANES, 2 * EDGE_LANES + D, s.node_cot, dst.edge_cot, in_sems, False
        )
        start(copies)
        make_masks(s)
        every = Group(
            [*kept, *node_res], [getattr(dst, k) for k in kept] + [getattr(s, k) for k in node_res]
        )
        io = Group(
            ("nodes", "edges", "nodes_out", "edges_out"),
            (src.nodes, src.edges, s.nodes_out, s.edges_out),
        )
        forward(dm, counts_ref, w, io, every, s)
        outgoing = all_copies(
            dm, dst.sno, dst.seo, dst.bout, 0, EDGE_LANES, s.nodes_out, s.edges_out, out_sems, True
        )
        start(outgoing)
        wait(copies)
        back_ffn(dm, w, Group(("nodes_cot", *ffn), (s.node_cot, *take(dst, ffn))), every, s)
        wait(outgoing)

    inputs = take(weights, WEIGHTS) + [nodes, edges, small_node_cot, small_edge_cot, big]
    got = kernel(body, inputs, out, scr, 46, counts, 3, tuple(whole_outs), [copy_sems(dm)] * 2)
    return got.sno, got.seo, got.bout, None, got.edge_cot, got, got


def between(dm, weights_two, weights_one, kept_two, kept_one, ffn_two, edges_cot):
    ffn, edge, att = ffn_shapes(dm, True), edge_shapes(dm), attention_shapes(dm)
    handed = {"dmid": edge["dmid"], "small": edge["small"], **att, "sums_one": ((8, 128), F32)}
    out = {**{"two_" + k: v for k, v in handed.items()}, **ffn}
    scr = {
        **mask_shapes(),
        **edge_scratch(),
        **attention_scratch(dm),
        **ffn_scratch(),
        "scores": edge["scores"],
        "nodes_grad": ((dm.nodes, D), BF),
    }
    w_two = ("qkv", *W_EDGE, "nn")
    res_two = EDGE_BACK + ATTENTION_BACK + ("node_n1", "node_r1")

    def body(*refs):
        w, w_one, res, res_one, src, dst, s = split(
            refs, w_two, W_NODE, res_two, NODE_BACK, ("edges_cot", "sums", "do", "dy"), out, scr
        )
        make_masks(s)
        io = Group(
            ("edges_cot", "sums", "do", "dy", "scores", "nodes_grad", *handed),
            (src.edges_cot, src.sums, src.do, src.dy, s.scores, s.nodes_grad)
            + tuple(getattr(dst, "two_" + k) for k in handed),
        )
        back_edges(dm, w, io, res, s)
        back_attention(dm, io, res, s)
        back_nodes(dm, w, io, res, s)
        back_ffn(dm, w_one, Group(("nodes_cot", *ffn), (s.nodes_grad, *take(dst, ffn))), res_one, s)

    inputs = take(weights_two, w_two) + take(weights_one, W_NODE)
    inputs += take(kept_two, res_two) + take(kept_one, NODE_BACK)
    inputs += [edges_cot, ffn_two.sums, ffn_two.do, ffn_two.dy]
    return kernel(body, inputs, out, scr, 25)


def second_last(dm, weights, kept, got):
    half = {k: ((dm.lower // 2, 128), BF) for k in ("keep", "send")}
    out = {"edges_grad": ((dm.edges, 256), BF), **half}
    scr = {**mean_shapes(), **last_scratch(dm)}
    given = ("dmid", "small", "dsg", "dqkv", "sums_one")
    w_last = ("eg", "nn", "en")
    last_res = ("node_n1", "edge_n1", "edge_r1")

    def body(*refs):
        w, res, src, dst, s = split(refs, w_last, last_res, given, out, scr)
        make_mean(s)
        back_last(dm, w, Group((*given, *out), (*take(src, given), *take(dst, out))), res, s)

    inputs = take(weights, w_last) + take(kept, last_res)
    inputs += [getattr(got, "two_" + k) for k in given]
    return kernel(body, inputs, out, scr, 9)


def call_edges(dm, weights, kept, ffn, edges_cot):
    out, scr = edge_shapes(dm), {**mean_shapes(), **edge_scratch()}

    def body(*refs):
        w, res, src, dst, s = split(refs, W_EDGE, EDGE_BACK, ("edges_cot", "sums"), out, scr)
        make_mean(s)
        io = Group(("edges_cot", "sums", *out), (src.edges_cot, src.sums, *take(dst, out)))
        back_edges(dm, w, io, res, s)

    inputs = take(weights, W_EDGE) + take(kept, EDGE_BACK) + [edges_cot, ffn.sums]
    return kernel(body, inputs, out, scr, 16)


def call_attention(dm, kept, ffn, edge):
    out, scr = attention_shapes(dm), {**head_shapes(), **attention_scratch(dm)}

    def body(*refs):
        res, src, dst, s = split(refs, ATTENTION_BACK, ("do", "scores"), out, scr)
        make_heads(s)
        back_attention(dm, Group(("do", "scores", *out), (src.do, src.scores, *take(dst, out))), res, s)

    return kernel(body, take(kept, ATTENTION_BACK) + [ffn.do, edge.scores], out, scr, 14)


def call_last(dm, weights, kept, ffn, edge, att):
    half = {k: ((dm.lower // 2, 128), BF) for k in ("keep", "send")}
    outs = {
        "sng": ((dm.small.rows, D), BF),
        "seg": ((dm.small.rows, dm.small.edge_lanes), BF),
        "bgrad": ((dm.big.rows, OUT_LANES), BF),
    }
    out = {**outs, **half}
    scr = {
        **mean_shapes(),
        **last_scratch(dm),
        "nodes_grad": ((dm.nodes, D), BF),
        "edges_grad": ((dm.edges, 256), BF),
        "sums_one": ((8, 128), F32),
    }
    given = ("dy", "dmid", "small", "dsg", "dqkv")

    def body(*refs):
        refs, sems = refs[:-1], refs[-1]
        w, res, src, dst, s = split(refs, W_LAST, LAST_BACK, given, out, scr)
        make_mean(s)
        io = Group(
            (*given, "nodes_grad", "edges_grad", "keep", "send", "sums_one"),
            (*take(src, given), s.nodes_grad, s.edges_grad, dst.keep, dst.send, s.sums_one),
        )
        back_nodes(dm, w, io, res, s)
        back_last(dm, w, io, res, s)
        outgoing = all_copies(
            dm, dst.sng, dst.seg, dst.bgrad, 0, EDGE_LANES, s.nodes_grad, s.edges_grad, sems, True
        )
        start(outgoing)
        wait(outgoing)

    inputs = take(weights, W_LAST) + take(kept, LAST_BACK)
    inputs += [ffn.dy, edge.dmid, edge.small, att.dsg, att.dqkv]
    got = kernel(body, inputs, out, scr, 13, hbm_out=tuple(outs), sems=[copy_sems(dm)])
    return take(got, out)


def round_up(value, by):
    return -(-value // by) * by


def segment_of(owner, rows, index, count):
    name = owner[index]
    first = jnp.int32(0)
    for t in range(count):
        first = first + jnp.where(t < name, rows[t], 0)
    return first, rows[name]


def shifted_segment(owner, segment_rows, master):
    held = master.shape[0]
    count = owner.shape[0]
    padded = round_up(held + 15, 16)
    step = 1664

    def body(owner_ref, rows_ref, src, dst, window):
        i = pl.program_id(0)
        first, length = segment_of(owner_ref, rows_ref, lax.axis_index("dp"), count)
        shift = first % 16

        @pl.when(i == 0)
        def _():
            window[0:16, :] = jnp.zeros((16, 128), F32)

        window[16:, :] = src[...]
        moved = window[pl.ds(16 - shift, step), :]
        index = i * step - shift + iota((step, 128), 0)
        live = (index >= 0) & (index < length)
        dst[...] = jnp.where(live, moved, 0.0).astype(BF)
        window[0:16, :] = window[step : step + 16, :]

    return pl.pallas_call(
        body,
        grid=(pl.cdiv(padded, step),),
        out_shape=jax.ShapeDtypeStruct((padded, 128), BF),
        in_specs=[
            SMEM,
            SMEM,
            pl.BlockSpec((step, 128), lambda i: (jnp.minimum(i, (held - 1) // step), 0)),
        ],
        out_specs=pl.BlockSpec((step, 128), lambda i: (i, 0)),
        scratch_shapes=[pltpu.VMEM((step + 16, 128), F32)],
        compiler_params=compiler_params(),
    )(owner, segment_rows, master)


def assemble(cube, owner, segment_rows, parts, sources):
    count = len(parts)
    padded = parts[0].shape[0]
    bits = (padded // 16).bit_length()
    tiles = -(-TOTAL_ROWS // 16)
    set_tiles = -(-(SET_ROWS + 2) // 16)
    out = {**{"one_" + k: v for k, v in WEIGHTS.items()}, **{"two_" + k: v for k, v in WEIGHTS.items()}}

    def body(owner_ref, rows_ref, *refs):
        srcs, refs = refs[:count], refs[count:]
        dsts, (rows, flat, tmp, edge, sems, edge_sems) = refs[: len(out)], refs[len(out) :]
        me = lax.axis_index("dp")
        spans = []
        for i in range(count):
            first, length = segment_of(owner_ref, rows_ref, cube.source(me, sources[i]), count)
            spans.append((first // 16, (first + length - 1) // 16))

        def each(act):
            for i, (a, b) in enumerate(spans):
                inner = b - a - 1
                for bit in range(bits):
                    size = 16 << bit
                    if size > padded:
                        continue
                    done = (inner >> (bit + 1)) << (bit + 1)

                    @pl.when((inner > 0) & (((inner >> bit) & 1) == 1))
                    def _(i=i, a=a, done=done, size=size, bit=bit):
                        act(
                            pltpu.make_async_copy(
                                srcs[i].at[pl.ds(aligned(16 * (1 + done), 16), size), :],
                                rows.at[pl.ds(aligned(16 * (a + 1 + done), 16), size), :],
                                sems.at[i, bit],
                            )
                        )

                act(pltpu.make_async_copy(srcs[i].at[pl.ds(0, 16), :], edge.at[2 * i], edge_sems.at[2 * i]))
                act(
                    pltpu.make_async_copy(
                        srcs[i].at[pl.ds(aligned(16 * (b - a), 16), 16), :],
                        edge.at[2 * i + 1],
                        edge_sems.at[2 * i + 1],
                    )
                )

        each(lambda c: c.start())
        each(lambda c: c.wait())
        tile = lambda t: pl.ds(aligned(16 * t, 16), 16)
        for a, b in spans:
            rows[tile(a), :] = jnp.zeros((16, 128), BF)
            rows[tile(b), :] = jnp.zeros((16, 128), BF)
        for i, (a, b) in enumerate(spans):
            rows[tile(a), :] += edge[2 * i]

            @pl.when(b != a)
            def _(i=i, b=b):
                rows[tile(b), :] += edge[2 * i + 1]

        for which in range(2):
            base = which * (SET_ROWS // 16) * 16
            flat[...] = rows[pl.ds(base, 16 * set_tiles), :].astype(F32)
            w = Group(WEIGHTS, dsts[which * len(WEIGHTS) : (which + 1) * len(WEIGHTS)])
            assemble_set(which * (SET_ROWS % 16), flat, tmp, w)

    got = pl.pallas_call(
        body,
        out_shape=structs(out),
        in_specs=[SMEM] * 2 + [HBM] * count,
        out_specs=whole(len(out)),
        scratch_shapes=[
            pltpu.VMEM((16 * tiles, 128), BF),
            pltpu.VMEM((16 * set_tiles, 128), F32),
            pltpu.VMEM((128, 128), F32),
            pltpu.VMEM((2 * count, 16, 128), BF),
            pltpu.SemaphoreType.DMA((count, bits)),
            pltpu.SemaphoreType.DMA((2 * count,)),
        ],
        compiler_params=compiler_params(),
        cost_estimate=cost(10),
    )(owner, segment_rows, *parts)
    return Group(WEIGHTS, got[: len(WEIGHTS)]), Group(WEIGHTS, got[len(WEIGHTS) :])


def adam(n_row, lower, owner, segment_rows, scales, whole_upper, blocks, master, first, second):
    held = master.shape[0]
    step = 2080
    front = step + 16
    count = len(blocks)
    n_dp = owner.shape[0]
    set_rows = ROW_BIAS - ROW_O + lower
    total_rows = front + set_rows + step + 32
    ways = 3
    arrivals = sum(len(keys) for _, _, keys, _ in blocks)

    def body(owner_ref, rows_ref, scale_ref, *refs):
        upper, srcs, refs = refs[0], refs[1 : 1 + count], refs[1 + count :]
        master_ref, first_ref, second_ref, o_master, o_first, o_second, o_norms, rows, window, grad, rate, sems, upper_sem = refs
        i = pl.program_id(0)
        me, row = lax.axis_index("dp"), lax.axis_index("row")
        begin, length = segment_of(owner_ref, rows_ref, me, n_dp)

        @pl.when(i == 0)
        def _():
            def each(act):
                copy = pltpu.make_async_copy(
                    upper, rows.at[1, pl.ds(front + ROW_O, UPPER_ROWS), :], upper_sem
                )
                pl.when(begin + length > SET_ROWS + ROW_O)(functools.partial(act, copy))
                every = [
                    (k, core, key, n, sections)
                    for k, (_, core, keys, sections) in enumerate(blocks)
                    for n, key in enumerate(keys)
                ]
                for at_sem, (k, core, key, n, sections) in enumerate(every):
                    mine = (me ^ core) & 1
                    source = me ^ core ^ jnp.where(mine == 0, key[0], key[1])
                    offset = n * n_row * sum(size for _, _, size in sections)
                    place = (source & 1) * (n_dp // 2) + (source >> 1)
                    for number, (which, part, size) in enumerate(sections):
                        size = size * n_row
                        at = place * size
                        dest = at + ROW_O if part else jnp.where(at >= ROW_O, at - ROW_O + ROW_BIAS, at)
                        wanted = (dest + which * SET_ROWS < begin + length) & (
                            dest + size + which * SET_ROWS > begin
                        )
                        wanted = wanted | (dest + size > ROW_NN)

                        def move(frm, extent, to, way, k=k, which=which, at_sem=at_sem):
                            act(
                                pltpu.make_async_copy(
                                    srcs[k].at[pl.ds(frm, extent), :],
                                    rows.at[which, pl.ds(aligned(front + to, 16), extent), :],
                                    sems.at[at_sem, way],
                                )
                            )

                        cut = 0 if part else ROW_O % size
                        if cut:
                            split_here = (at < ROW_O) & (at + size > ROW_O)
                            wanted = wanted & jnp.logical_not(split_here)

                            @pl.when(split_here)
                            def _(move=move, offset=offset, size=size, at=at, cut=cut, number=number):
                                move(offset, cut, at, number)
                                move(offset + cut, size - cut, ROW_BIAS, 2)

                        pl.when(wanted)(functools.partial(move, offset, size, dest, number))
                        offset += size

            each(lambda c: c.start())
            each(lambda c: c.wait())
            for which in range(2):
                v = rows[which, front + ROW_NN : front + ROW_NN + 32, :].astype(F32)
                for t in range(4):
                    for q in range(4):
                        o_norms[4 * which + t : 4 * which + t + 1, 128 * q : 128 * (q + 1)] = v[
                            4 * t + q : 4 * t + q + 1, :
                        ]
                for t in range(2):
                    both = v[16 + t : 17 + t, :]
                    at = 4 * which + 2 * t
                    o_norms[at : at + 1, 512:576] = both[:, 0:64]
                    o_norms[at + 1 : at + 2, 512:576] = pltpu.roll(both, 64, 1)[:, 0:64]

        low = begin + i * step
        high = low + step
        some = i * step < length

        @pl.when(jnp.logical_not(some))
        def _():
            o_master[...] = master_ref[...]
            o_first[...] = first_ref[...]
            o_second[...] = second_ref[...]

        @pl.when(some)
        def _():
            def shifted(which):
                local = low - which * SET_ROWS + front
                shift = local % 16
                window[...] = rows[which, pl.ds(aligned(local - shift, 16), step + 16), :].astype(F32)
                return window[pl.ds(shift, step), :]

            index = iota((step, 128), 0)

            @pl.when(low < SET_ROWS)
            def _():
                grad[...] = shifted(0)

            @pl.when(low >= SET_ROWS)
            def _():
                grad[...] = shifted(1)

            @pl.when((low < SET_ROWS) & (high > SET_ROWS))
            def _():
                grad[...] = jnp.where(index + low >= SET_ROWS, shifted(1), grad[...])

            at = index + low
            at = jnp.where(at >= SET_ROWS, at - SET_ROWS, at)
            a, b, c = RATES[0][1], RATES[1][1], RATES[3][1]
            far = jnp.where(at < ROW_DOWN, a, c)
            rate[...] = jnp.where(at < ROW_O, a, jnp.where(at < ROW_UP, b, far))
            near = (low < SET_ROWS) & (high > ROW_BIAS)

            @pl.when(near | (high > SET_ROWS + ROW_BIAS))
            def _():
                value = jnp.full((step, 128), 0.25, F32)
                for end, one in reversed(RATES[4:]):
                    value = jnp.where(at < end, one, value)
                rate[...] = jnp.where(at < ROW_BIAS, rate[...], value)

            g = grad[...]
            p, m, v = master_ref[...], first_ref[...], second_ref[...]
            m_new = BETA_ONE * m + (1.0 - BETA_ONE) * g
            v_new = BETA_TWO * v + (1.0 - BETA_TWO) * g * g
            move = (m_new * scale_ref[0]) / (jnp.sqrt(v_new * scale_ref[1]) + ADAM_EPS)
            live = index < length - i * step
            o_master[...] = jnp.where(live, p - rate[...] * (move + WEIGHT_DECAY * p), p)
            o_first[...] = jnp.where(live, m_new, m)
            o_second[...] = jnp.where(live, v_new, v)

    spec = pl.BlockSpec((step, 128), lambda i: (i, 0))
    shape = jax.ShapeDtypeStruct((held, 128), F32)
    return pl.pallas_call(
        body,
        grid=(pl.cdiv(held, step),),
        out_shape=[shape] * 3 + [jax.ShapeDtypeStruct((8, D + DE), F32)],
        in_specs=[SMEM] * 3 + [HBM] * (count + 1) + [spec] * 3,
        out_specs=[spec] * 3 + [pl.BlockSpec((8, D + DE), lambda i: (0, 0))],
        scratch_shapes=[
            pltpu.VMEM((2, total_rows, 128), BF),
            pltpu.VMEM((step + 16, 128), F32),
            pltpu.VMEM((step, 128), F32),
            pltpu.VMEM((step, 128), F32),
            pltpu.SemaphoreType.DMA((arrivals, ways)),
            pltpu.SemaphoreType.DMA(()),
        ],
        compiler_params=compiler_params(),
        cost_estimate=cost(10),
    )(owner, segment_rows, scales, whole_upper, *[b[0] for b in blocks], master, first, second)


RATES = [
    (ROW_O, 0.5 * D ** (-0.5)),
    (ROW_UP, 2.0 * D ** (-0.5)),
    (ROW_DOWN, 0.5 * D ** (-0.5)),
    (ROW_BIAS, 0.5 * FF ** (-0.5)),
    (ROW_EDGE, 0.5 * DE ** (-0.5)),
    (ROW_EUP, 0.5 * H ** (-0.5)),
    (ROW_EDOWN, 0.5 * DE ** (-0.5)),
    (ROW_NN, 0.5 * FFE ** (-0.5)),
]


class Cube:
    def __init__(self, size):
        self.size = size
        self.bits = size.bit_length() - 1
        assert size == 1 << self.bits
        up = list(range(1, self.bits))
        self.order = (up, up[::-1])

    def pairs(self, step):
        return [(i, i ^ (1 << self.order[i & 1][step])) for i in range(self.size)]

    def core_pairs(self):
        return [(i, i ^ 1) for i in range(self.size)]

    def source(self, me, key):
        other, used = key
        even, odd = [sum(1 << self.order[c][s] for s in used) for c in (0, 1)]
        if other:
            even, odd = odd, even
        return me ^ jnp.where(me & 1 == 0, even, odd) ^ other

    def gather(self, value, meanwhile):
        steps = range(self.bits - 1)
        new, done, also = [((), value)], [], None
        while new:
            sent = []
            for used, v in new:
                done.append(((0, used), v))
                for step in steps:
                    if not used or step > used[-1]:
                        sent.append((0, used + (step,), lax.ppermute(v, "dp", self.pairs(step))))
            for used, v in new:
                sent.append((1, used, lax.ppermute(v, "dp", self.core_pairs())))
            beside = None
            if also is None:
                also = meanwhile(lax.ppermute(value[:16], "dp", self.core_pairs()))
            else:
                beside = also
            moved, beside = lax.optimization_barrier(([v for _, _, v in sent], beside))
            also = also if beside is None else beside
            new = []
            for (other, used, _), v in zip(sent, moved):
                if other:
                    done.append(((1, used), v))
                else:
                    new.append((used, v))
        return done, also


def total(values):
    out = values[0].astype(F32)
    for v in values[1:]:
        out = out + v.astype(F32)
    return out.astype(BF)


def side_by_side(parts, sections, row_order):
    count, total_rows = len(parts), len(parts) * parts[0].shape[0]

    def body(*refs):
        srcs, dst, sems = refs[:count], refs[count], refs[count + 1]
        row = lax.axis_index("row")
        copies = []
        for k in range(count):
            inside = 0
            for number, size in enumerate(sections):
                if row_order:
                    to = aligned(count * inside + (row ^ k) * size, 16)
                else:
                    to = k * parts[0].shape[0] + inside
                copies.append(
                    pltpu.make_async_copy(
                        srcs[k].at[pl.ds(inside, size), :],
                        dst.at[pl.ds(to, size), :],
                        sems.at[k, number],
                    )
                )
                inside += size
        start(copies)
        wait(copies)

    return pl.pallas_call(
        body,
        out_shape=jax.ShapeDtypeStruct((total_rows, 128), BF),
        in_specs=[HBM] * count,
        out_specs=HBM,
        scratch_shapes=[pltpu.SemaphoreType.DMA((count, len(sections)))],
        compiler_params=pltpu.CompilerParams(vmem_limit_bytes=4 * 1024 * 1024),
        cost_estimate=cost(1),
    )(*parts)


class Chain:
    def __init__(self, cube, direct, *halves):
        self.cube, self.direct = cube, direct
        self.kept = [k for k, _ in halves]
        self.value = [s for _, s in halves]
        self.step, self.done = 0, False
        self.sides = lax.axis_size("dp") // 2
        self.rows = lax.axis_size("row")

    def swap(self, value):
        return lax.ppermute(value, "dp", [(i, i ^ 1) for i in range(2 * self.sides)])

    def to_chip(self, value, k):
        return lax.ppermute(value, "dp", [(i, i ^ (k << 1)) for i in range(2 * self.sides)])

    def to_row(self, value, k):
        return lax.ppermute(value, "row", [(i, i ^ k) for i in range(self.rows)])

    def scatter(self, index, count, send):
        def at(k):
            parts = [v.reshape(count, v.shape[0] // count, 128) for v in self.value]
            parts = [lax.dynamic_index_in_dim(v, index ^ k, 0, keepdims=False) for v in parts]
            return jnp.concatenate(parts) if len(parts) > 1 else parts[0]

        self.sizes = [v.shape[0] // count for v in self.value]
        self.kept = at(0)
        return [send(at(k), k) for k in range(1, count)]

    def join(self, other):
        assert self.step == other.step == 2
        self.value = self.value + other.value

    def launch(self):
        self.step += 1
        if self.step == 1:
            return [self.swap(v) for v in self.value]
        if self.step == 2:
            return self.scatter(lax.axis_index("dp") >> 1, self.sides, self.to_chip)
        if self.step == 3:
            return self.scatter(lax.axis_index("row"), self.rows, self.to_row)
        if self.step == 4:
            return [self.to_row(self.value, k) for k in range(1, self.rows)]
        if not self.spread():
            return [self.swap(self.value)]
        if self.direct:
            return [self.to_chip(self.value, k) for k in range(1, self.sides)]
        return [lax.ppermute(self.value, "dp", self.cube.pairs(self.step - 5))]

    def spread(self):
        return self.step < 6 if self.direct else self.step < 5 + self.cube.bits - 1

    def land(self, got):
        if self.step == 1:
            self.value = [total(pair) for pair in zip(self.kept, got)]
        elif self.step <= 3:
            value = total([self.kept, *got])
            if self.step == 3:
                self.value = value
            else:
                self.value, at = [], 0
                for size in self.sizes:
                    self.value.append(value[at : at + size])
                    at += size
        elif self.step == 4:
            self.value = side_by_side([self.value, *got], self.sizes, True)
        elif self.spread():
            self.value = side_by_side([self.value, *got], [self.value.shape[0]], False)
            if self.direct:
                self.keys = [(k << 1, k << 1) for k in range(self.sides)]
            else:
                bit = [1 << order[self.step - 5] for order in self.cube.order]
                keys = self.keys if self.step > 5 else [(0, 0)]
                self.keys = keys + [(a ^ bit[0], b ^ bit[1]) for a, b in keys]
        else:
            self.value, self.done = [self.value, *got], True

    def blocks(self, *names):
        sections = [(which, part, size) for (which, part), size in zip(names, self.sizes)]
        return [(v, core, self.keys, sections) for core, v in enumerate(self.value)]


def phase(chains, *ready):
    chains = [c for c in chains if not c.done]
    sent = [c.launch() for c in chains]
    got, ready = lax.optimization_barrier((sent, ready))
    for c, g in zip(chains, got):
        c.land(g)
    return ready


def per_device(
    small_nodes,
    small_edges,
    small_counts,
    big_nodes,
    big_edges,
    big_counts,
    small_node_cot,
    small_edge_cot,
    big_node_cot,
    big_edge_cot,
    master,
    first_moment,
    second_moment,
    owner,
    segment_rows,
    step_count,
):
    n_dp, n_row = lax.axis_size("dp"), lax.axis_size("row")
    cube = Cube(n_dp)
    share = big_nodes.shape[0] // n_row
    dm = Dims(small_nodes.shape[0], share, n_dp * n_row)

    def flat2(v):
        return v.reshape(-1, v.shape[-1])

    def to_rows(v):
        v = v.reshape(share, NB, OUT_LANES)
        v = lax.all_to_all(v, "row", split_axis=1, concat_axis=0, tiled=True)
        return v[..., EDGE_LANES:], v[..., :EDGE_LANES]

    def to_whole(first):
        big = (big_edges, big_edge_cot, big_nodes, big_node_cot)
        _, big = lax.optimization_barrier((first, big))
        big = jnp.concatenate(big, axis=2)
        return flat2(lax.all_to_all(big, "row", split_axis=0, concat_axis=1, tiled=True))

    held, big = cube.gather(shifted_segment(owner, segment_rows, master), to_whole)
    one, two = assemble(cube, owner, segment_rows, [v for _, v in held], [k for k, _ in held])

    own_counts = lax.dynamic_slice_in_dim(big_counts, lax.axis_index("row") * share, share)
    counts = jnp.concatenate([small_counts, own_counts])

    mid_nodes, mid_edges, kept = first_forward(
        dm, counts, one, flat2(small_nodes), flat2(small_edges), big
    )
    sno, seo, bout, node_cot, edge_cot, kept_two, ffn_two = second_forward(
        dm, counts, two, mid_nodes, mid_edges, flat2(small_node_cot), flat2(small_edge_cot), big
    )
    spread = lax.psum_scatter(ffn_two.upper, "dp", scatter_dimension=0, tiled=True)
    got = between(dm, two, one, kept_two, kept, ffn_two, edge_cot)
    names = tuple(vars(got))
    outs = to_rows(bout)
    *values, bno, beo = phase([], *take(got, names), *outs)
    got = Group(names, values)
    middle = Chain(cube, False, (got.keep, got.send))
    rest = second_last(dm, two, kept_two, got)
    spread, edge_grad, keep, send = phase([middle], spread, rest.edges_grad, rest.keep, rest.send)
    spread = lax.psum(spread, "row")
    lower_two = Chain(cube, False, (keep, send))
    names = tuple(edge_shapes(dm))
    edge_one = call_edges(dm, one, kept, got, edge_grad)
    edge_one = Group(names, phase([middle, lower_two], *take(edge_one, names)))
    names = tuple(attention_shapes(dm))
    att_one = Group(names, phase([lower_two], *take(call_attention(dm, kept, got, edge_one), names)))
    middle.join(lower_two)
    sng, seg, bgrad, keep, send = call_last(dm, one, kept, got, edge_one, att_one)
    spread, sng, seg, bgrad, keep, send = phase([middle], spread, sng, seg, bgrad, keep, send)
    upper_two = lax.all_gather(spread, "dp", axis=0, tiled=True)
    last = Chain(cube, True, (keep, send))
    sent = middle.launch()
    bgrad, = phase([last], bgrad)
    outs = to_rows(bgrad)
    sent, = phase([last], sent)
    middle.land(sent)
    phase([last, middle])
    sent = middle.launch()
    bng, beg, upper_two = phase([last], *outs, upper_two)
    sent, = phase([last], sent)
    middle.land(sent)
    while not (last.done and middle.done):
        phase([last, middle])
    blocks = last.blocks((0, 0)) + middle.blocks((0, 1), (1, 0))
    step_value = step_count[0].astype(F32)
    scales = jnp.stack(
        [
            1.0 / (1.0 - jnp.power(F32(BETA_ONE), step_value)),
            1.0 / (1.0 - jnp.power(F32(BETA_TWO), step_value)),
        ]
    )
    new_master, new_first, new_second, norm_grads = adam(
        n_row, dm.lower, owner, segment_rows, scales, upper_two, blocks, master, first_moment, second_moment
    )
    return (
        sno.reshape(small_nodes.shape),
        seo.reshape(small_edges.shape),
        bno,
        beo,
        sng.reshape(small_nodes.shape),
        seg.reshape(small_edges.shape),
        bng,
        beg,
        new_master,
        new_first,
        new_second,
        norm_grads,
    )


def solution(mesh):
    both = P(("dp", "row"), None, None)
    rows = P("dp", "row", None)
    held = P("dp", None)
    in_specs = (
        both, both, P(("dp", "row")), rows, rows, P("dp"), both, both, rows, rows,
        held, held, held, P(), P(), P(),
    )
    out_specs = (both, both, rows, rows, both, both, rows, rows, held, held, held, P())
    return jax.shard_map(
        per_device, mesh=mesh, in_specs=in_specs, out_specs=out_specs, check_vma=False
    )
```

```python
import functools

import jax
import jax.numpy as jnp
from jax import lax
from jax.experimental import pallas as pl
from jax.experimental.pallas import tpu as pltpu
from jax.sharding import PartitionSpec as P

D = 512
H = 32
DE = 64
FF = 1024
FFE = 128
NS = 32
NB = 64
SET_ROWS = 16578
TOTAL_ROWS = 33156
NORM_EPS = 1e-05
BETA_ONE = 0.9
BETA_TWO = 0.95
WEIGHT_DECAY = 0.1
ADAM_EPS = 1e-08
MASK_FILL = -1e30
BF = jnp.bfloat16
F32 = jnp.float32
VMEM_LIMIT = 58 * 1024 * 1024
ROW_QKV, ROW_O, ROW_UP, ROW_DOWN = 0, 6144, 8192, 12288
ROW_BIAS, ROW_GATE, ROW_EDGE, ROW_EUP, ROW_EDOWN = 16384, 16400, 16416, 16432, 16496
ROW_NN, ROW_EN = 16560, 16576
SMALL_USED, SMALL_ROWS = SET_ROWS - ROW_BIAS, 256
BIAS, GATE, EDGE, EUP, EDOWN = 0, 16, 32, 48, 112
NN, EN = ROW_NN - ROW_BIAS, ROW_EN - ROW_BIAS
UPPER_ROWS = ROW_BIAS - ROW_O
GELU_C = 0.7978845608028654
PAIRS = 4


def nn(a, b):
    return lax.dot_general(a, b, (((1,), (0,)), ((), ())), preferred_element_type=F32)


def nt(a, b):
    return lax.dot_general(a, b, (((1,), (1,)), ((), ())), preferred_element_type=F32)


def tn(a, b):
    return lax.dot_general(a, b, (((0,), (0,)), ((), ())), preferred_element_type=F32)


def iota(shape, axis):
    return lax.broadcasted_iota(jnp.int32, shape, axis)


def gelu_parts(u):
    u2 = u * u
    t = jnp.tanh(u * (GELU_C + (GELU_C * 0.044715) * u2))
    half = 0.5 + 0.5 * t
    value = u * half
    slope = half + value * (1.0 - t) * (GELU_C + (3.0 * GELU_C * 0.044715) * u2)
    return value, slope


def gelu_value(u):
    return u * (0.5 + 0.5 * jnp.tanh(u * (GELU_C + (GELU_C * 0.044715) * (u * u))))


def sigmoid(v):
    return 0.5 + 0.5 * jnp.tanh(0.5 * v)


def group_sum(v, first=16):
    while first < 128:
        v = v + pltpu.roll(v, first, 1)
        first *= 2
    return v


def group_max(v):
    for shift in (16, 32, 64):
        v = jnp.maximum(v, pltpu.roll(v, shift, 1))
    return v


def fold8(v):
    return jnp.sum(v.reshape(v.shape[0] // 8, 8, v.shape[1]), axis=0)


class Bucket:
    def __init__(self, graphs, slots, node0, edge0, count0):
        self.graphs, self.slots = graphs, slots
        self.node0, self.edge0, self.count0 = node0, edge0, count0
        self.rows = graphs * slots
        self.chunks = slots // 4
        self.pairs = slots // 8
        self.blocks = slots // 16
        self.edges = self.rows * self.chunks
        self.edge_lanes = slots * DE


class Dims:
    def __init__(self, small_graphs, big_graphs, parts):
        self.lower = round_up(ROW_O + SMALL_ROWS, 16 * parts)
        self.small = Bucket(small_graphs, NS, 0, 0, 0)
        self.big = Bucket(big_graphs, NB, self.small.rows, self.small.edges, small_graphs)
        self.buckets = (self.small, self.big)
        self.nodes = self.small.rows + self.big.rows
        self.edges = self.small.edges + self.big.edges
        self.scores = self.edges // 2
        self.blocks = sum(b.graphs * b.blocks for b in self.buckets)

    def each_pair(self, body):
        for bucket in self.buckets:
            two = 2 * PAIRS * bucket.rows

            @pl.loop(0, bucket.pairs // PAIRS, unroll=True)
            def _(i, bucket=bucket, two=two):
                body(
                    pl.ds(aligned(bucket.edge0 + i * two, 32), two),
                    pl.ds(aligned((bucket.edge0 + i * two) // 2, 16), two // 2),
                )


def beside(v):
    one = v.shape[0] // (2 * PAIRS)
    at = lambda c: v[c * one : (c + 1) * one]
    sides = [[at(2 * p + c) for p in range(PAIRS)] for c in range(2)]
    return jnp.concatenate([jnp.concatenate(s) for s in sides], axis=1)


def below(v):
    one = v.shape[0] // PAIRS
    at = lambda p, c: v[p * one : (p + 1) * one, 256 * c : 256 * (c + 1)]
    return jnp.concatenate([at(p, c) for p in range(PAIRS) for c in range(2)])


def make_masks(scr):
    make_mean(scr)
    make_heads(scr)


def make_mean(scr):
    shape = (256, 256)
    same = (iota(shape, 0) >> 6) == (iota(shape, 1) >> 6)
    scr.mean[...] = jnp.where(same, 1.0 / DE, 0.0).astype(BF)


def make_heads(scr):
    shape = (16, 256)
    scr.head[...] = jnp.where(iota(shape, 0) == (iota(shape, 1) >> 4), 1.0, 0.0)


def node_norm(v):
    centred = v - jnp.mean(v, axis=1, keepdims=True)
    r = lax.rsqrt(jnp.mean(centred * centred, axis=1, keepdims=True) + NORM_EPS)
    return centred * r, r


def node_norm_back(gdy, n, r):
    return r * (gdy - jnp.mean(gdy, axis=1, keepdims=True) - n * jnp.mean(gdy * n, axis=1, keepdims=True))


def aligned(value, by):
    return pl.multiple_of(value, by)


def block_of(bucket, t):
    g = t // bucket.blocks
    b = t % bucket.blocks
    rows = pl.ds(aligned(bucket.node0 + g * bucket.slots, 16), bucket.slots)
    keys = pl.ds(aligned(bucket.node0 + t * 16, 16), 16)
    pair_rows = [
        pl.ds(
            aligned(bucket.edge0 // 2 + (2 * b + c) * bucket.rows + g * bucket.slots, 16),
            bucket.slots,
        )
        for c in range(2)
    ]
    return rows, keys, pair_rows


def side(first, half):
    return slice(first + 256 * half, first + 256 * (half + 1))


def lanes(half):
    return slice(128 * half, 128 * (half + 1))


def expand(values, scr):
    spread = values.astype(F32)[:, None, :] * scr.head[...][None]
    return spread.reshape(256, 256).astype(BF)


def collect(values, scr):
    return jnp.sum(values.reshape(16, 16, 256) * scr.head[...][None], axis=1)


def joined(ref, pair_rows, half):
    return jnp.concatenate([ref[r, lanes(half)] for r in pair_rows], axis=1)


def forward(dm, counts, w, io, res, scr, ready):
    x = io.nodes[...].astype(F32)
    n, r = node_norm(x)
    res.node_n1[...] = n.astype(BF)
    res.node_r1[...] = jnp.broadcast_to(r, (dm.nodes, 128))
    hn = (n * w.nn[0:1, :] + w.nn[1:2, :]).astype(BF)
    res.qkv[...] = nn(hn, w.qkv[...]).astype(BF)
    ready("node_n1", "node_r1", "qkv")

    @dm.each_pair
    def _(rows, pair):
        x = io.edges[rows, :]
        centred = x.astype(F32) - nn(x, scr.mean[...])
        r = lax.rsqrt(nn((centred * centred).astype(BF), scr.mean[...]) + NORM_EPS)
        n = centred * r
        res.edge_n1[rows, :] = n.astype(BF)
        res.edge_r1[rows, :] = r.astype(BF)
        xn = (n * w.en[0:1, :] + w.en[1:2, :]).astype(BF)
        both = nn(beside(xn), w.eg[...])
        scr.scores[pair, :] = both[:, :256]
        res.gate[pair, :] = both[:, 256:]

    ready("edge_n1", "edge_r1", "gate")
    t0 = 0
    for bucket in dm.buckets:
        @pl.loop(0, bucket.graphs * bucket.blocks, unroll=True)
        def _(t, bucket=bucket, t0=t0):
            rows, keys, pair_rows = block_of(bucket, t)
            for half in range(2):
                kb = expand(res.qkv[keys, side(512, half)], scr)
                scr.vbig[t0 + t, half] = expand(res.qkv[keys, side(1024, half)], scr)
                s = nt(res.qkv[rows, side(0, half)], kb) * 0.25
                for c in range(2):
                    scr.scores[pair_rows[c], lanes(half)] += s[:, lanes(c)]

        @pl.loop(0, bucket.rows // 32, unroll=True)
        def _(i, bucket=bucket):
            count = counts[bucket.count0 + i * 32 // bucket.slots]
            lane_key = iota((32, 128), 1) >> 4
            row = [
                pl.ds(aligned(bucket.edge0 // 2 + c * bucket.rows + i * 32, 32), 32)
                for c in range(bucket.pairs)
            ]
            for half in range(2):
                at = lanes(half)
                top = jnp.full((32, 128), MASK_FILL, F32)
                for c in range(bucket.pairs):
                    s = scr.scores[row[c], at]
                    res.low[row[c], at] = s.astype(BF)
                    top = jnp.maximum(top, jnp.where(lane_key < count - 8 * c, s, MASK_FILL))
                top = group_max(top)
                sums = jnp.zeros((32, 128), F32)
                for c in range(bucket.pairs):
                    s = jnp.where(lane_key < count - 8 * c, scr.scores[row[c], at], MASK_FILL)
                    e = jnp.exp(s - top)
                    sums = sums + e
                    scr.scores[row[c], at] = e
                inv = 1.0 / group_sum(sums)
                for c in range(bucket.pairs):
                    p = scr.scores[row[c], at] * inv
                    res.prob[row[c], at] = p.astype(BF)
                    scr.attn[row[c], at] = (p * sigmoid(res.gate[row[c], at])).astype(BF)

        @pl.loop(0, bucket.graphs, unroll=True)
        def _(g, bucket=bucket, t0=t0):
            for half in range(2):
                sums = None
                for b in range(bucket.blocks):
                    t = g * bucket.blocks + b
                    rows, _, pair_rows = block_of(bucket, t)
                    part = nn(joined(scr.attn, pair_rows, half), scr.vbig[t0 + t, half])
                    sums = part if sums is None else sums + part
                res.mixed[rows, side(0, half)] = sums.astype(BF)

        t0 += bucket.graphs * bucket.blocks

    ready("low", "prob", "mixed")
    y = io.nodes[...].astype(F32) + nn(res.mixed[...], w.o[...])
    n, r = node_norm(y)
    res.node_n2[...] = n.astype(BF)
    res.node_r2[...] = jnp.broadcast_to(r, (dm.nodes, 128))
    z = (n * w.nn[2:3, :] + w.nn[3:4, :]).astype(BF)
    u = nn(z, w.up[...])
    res.node_u[...] = u
    ready("node_n2", "node_r2", "node_u")
    io.nodes_out[...] = (y + nn(gelu_value(u).astype(BF), w.down[...])).astype(BF)

    @dm.each_pair
    def _(rows, pair):
        m = io.edges[rows, :].astype(F32) + below(nn(res.low[pair, :], w.x[...]))
        high = m.astype(BF)
        rest = (m - high.astype(F32)).astype(BF)
        centred = m - nn(high, scr.mean[...]) - nn(rest, scr.mean[...])
        r = lax.rsqrt(nn((centred * centred).astype(BF), scr.mean[...]) + NORM_EPS)
        n = centred * r
        res.edge_n2[rows, :] = n.astype(BF)
        res.edge_r2[rows, :] = r.astype(BF)
        mn = (n * w.en[2:3, :] + w.en[3:4, :]).astype(BF)
        ua = nn(mn, w.a[...])
        io.edges_out[rows, :] = (m + nn(gelu_value(ua).astype(BF), w.b[...])).astype(BF)

    ready("edge_n2", "edge_r2")


def put_strided(flat, first, value, parts):
    for q in range(parts):
        flat[pl.ds(first + q, value.shape[0], stride=parts), :] = value[:, 128 * q : 128 * (q + 1)]


def back_ffn(dm, w, io, res, scr):
    flat = scr.upper
    gy = io.nodes_cot[...]
    act, slope = gelu_parts(res.node_u[...])
    du = (nt(gy, w.down[...]) * slope).astype(BF)
    put_strided(flat, ROW_DOWN - ROW_O, tn(act.astype(BF), gy), 4)
    n = res.node_n2[...].astype(F32)
    z = (n * w.nn[2:3, :] + w.nn[3:4, :]).astype(BF)
    put_strided(flat, ROW_UP - ROW_O, tn(z, du), 8)
    dz = nt(du, w.up[...])
    gain = jnp.sum(dz * n, axis=0, keepdims=True)
    bias = jnp.sum(dz, axis=0, keepdims=True)
    dy = gy.astype(F32) + node_norm_back(dz * w.nn[2:3, :], n, res.node_r2[:, 0:1])
    io.dy[...] = dy
    dyl = dy.astype(BF)
    put_strided(flat, 0, tn(res.mixed[...], dyl), 4)
    io.do[...] = nt(dyl, w.o[...]).astype(BF)
    for q in range(4):
        io.sums[q : q + 1, :] = gain[:, 128 * q : 128 * (q + 1)]
        io.sums[4 + q : 5 + q, :] = bias[:, 128 * q : 128 * (q + 1)]
    if hasattr(io, "upper"):
        io.upper[...] = flat[...].astype(BF)
    else:
        put_halves(flat, io.keep, io.send)


def put_halves(flat, keep, send):
    half = keep.shape[0]
    core = lax.axis_index("dp") & 1
    keep[...] = flat[pl.ds(aligned(core * half, 16), half), :].astype(BF)
    send[...] = flat[pl.ds(aligned((1 - core) * half, 16), half), :].astype(BF)


def stacked(v, width):
    return jnp.concatenate([v[:, i : i + width] for i in range(0, v.shape[1], width)])


def back_edges(dm, w, io, res, scr):
    io.small[NN + 8 : NN + 16, :] = io.sums[...]
    scr.gb[...] = jnp.zeros((256, 128), F32)
    scr.ga[...] = jnp.zeros((128, 256), F32)
    scr.gx[...] = jnp.zeros((256, 512), F32)
    scr.en[...] = jnp.zeros((2, 8, 256), F32)

    @dm.each_pair
    def _(rows, pair):
        gx = io.edges_cot[rows, :]
        n = res.edge_n2[rows, :].astype(F32)
        mn = (n * w.en[2:3, :] + w.en[3:4, :]).astype(BF)
        act, slope = gelu_parts(nn(mn, w.a[...]))
        dua = (nt(gx, w.b[...]) * slope).astype(BF)
        act = act.astype(BF)
        scr.gb[...] += tn(stacked(act, 256), stacked(gx, 128))
        scr.ga[...] += tn(stacked(mn, 128), stacked(dua, 256))
        dmn = nt(dua, w.a[...])
        scr.en[0] += fold8(dmn * n)
        scr.en[1] += fold8(dmn)
        gdy = dmn * w.en[2:3, :]
        m1 = nn(gdy.astype(BF), scr.mean[...])
        m2 = nn((gdy * n).astype(BF), scr.mean[...])
        dmid = gx.astype(F32) + res.edge_r2[rows, :].astype(F32) * (gdy - m1 - n * m2)
        dml = dmid.astype(BF)
        io.dmid[rows, :] = dml
        dml = beside(dml)
        scr.gx[...] += tn(res.low[pair, :], dml)
        io.scores[pair, :] = nt(dml, w.x[...])

    io.small[EUP : EUP + 64, :] = scr.ga[0:64, 0:128] + scr.ga[64:128, 128:256]
    sums = jnp.where(lane_group(128, 6) == 0, scr.gb[0:128, :], scr.gb[128:256, :])
    fold_halves(sums, scr.tmp, io.small, EDOWN)
    sides = []
    for half in range(2):
        sums = jnp.zeros((16, 128), F32)
        for k in range(8):
            at = 128 * half + 16 * k
            part = scr.gx[at : at + 16, 128 * (k // 2) : 128 * (k // 2 + 1)]
            sums = sums + jnp.where(lane_group(16, 6) == k % 2, part, 0.0)
        sides.append(sums)
    fold_halves(jnp.concatenate(sides), scr.tmp, io.small, EDGE)
    put_edge_norm(scr.en, io.small, EN + 1)
    io.small[SMALL_USED:, :] = jnp.zeros((SMALL_ROWS - SMALL_USED, 128), F32)


def back_attention(dm, io, res, scr):
    t0 = 0
    for bucket in dm.buckets:
        @pl.loop(0, bucket.graphs * bucket.blocks, unroll=True)
        def _(t, bucket=bucket, t0=t0):
            rows, keys, pair_rows = block_of(bucket, t)
            for half in range(2):
                scr.vbig[t0 + t, half] = expand(res.qkv[keys, side(512, half)], scr)
                vb = expand(res.qkv[keys, side(1024, half)], scr)
                da = nt(io.do[rows, side(0, half)], vb)
                for c in range(2):
                    scr.da[pair_rows[c], lanes(half)] = da[:, lanes(c)]

        @pl.loop(0, bucket.rows // 32, unroll=True)
        def _(i, bucket=bucket):
            row = [
                pl.ds(aligned(bucket.edge0 // 2 + c * bucket.rows + i * 32, 32), 32)
                for c in range(bucket.pairs)
            ]
            for half in range(2):
                at = lanes(half)
                sums = jnp.zeros((32, 128), F32)
                for c in range(bucket.pairs):
                    p = res.prob[row[c], at].astype(F32)
                    s = sigmoid(res.gate[row[c], at])
                    scr.attn[row[c], at] = (p * s).astype(BF)
                    pt = p * scr.da[row[c], at] * s
                    scr.da[row[c], at] = pt
                    sums = sums + pt
                    io.dsg[row[c], lanes(2 + half)] = (pt * (1.0 - s)).astype(BF)
                sums = group_sum(sums)
                for c in range(bucket.pairs):
                    p = res.prob[row[c], at].astype(F32)
                    ds = scr.da[row[c], at] - p * sums + io.scores[row[c], at]
                    io.dsg[row[c], at] = ds.astype(BF)

        @pl.loop(0, bucket.graphs, unroll=True)
        def _(g, bucket=bucket, t0=t0):
            for half in range(2):
                sums = None
                for b in range(bucket.blocks):
                    t = g * bucket.blocks + b
                    rows, keys, pair_rows = block_of(bucket, t)
                    ds = joined(io.dsg, pair_rows, half)
                    part = nn(ds, scr.vbig[t0 + t, half])
                    sums = part if sums is None else sums + part
                    gk = collect(tn(ds, res.qkv[rows, side(0, half)]), scr)
                    io.dqkv[keys, side(512, half)] = (gk * 0.25).astype(BF)
                    gv = tn(joined(scr.attn, pair_rows, half), io.do[rows, side(0, half)])
                    io.dqkv[keys, side(1024, half)] = collect(gv, scr).astype(BF)
                io.dqkv[rows, side(0, half)] = (sums * 0.25).astype(BF)

        t0 += bucket.graphs * bucket.blocks


def back_nodes(dm, w, io, res, scr):
    n = res.node_n1[...].astype(F32)
    dhn = nt(io.dqkv[...], w.qkv[...])
    gain = jnp.sum(dhn * n, axis=0, keepdims=True)
    bias = jnp.sum(dhn, axis=0, keepdims=True)
    for q in range(4):
        io.sums_one[q : q + 1, :] = gain[:, 128 * q : 128 * (q + 1)]
        io.sums_one[4 + q : 5 + q, :] = bias[:, 128 * q : 128 * (q + 1)]
    dx = io.dy[...] + node_norm_back(dhn * w.nn[0:1, :], n, res.node_r1[:, 0:1])
    io.nodes_grad[...] = dx.astype(BF)


def back_last(dm, w, io, res, scr):
    flat = scr.lower
    n = res.node_n1[...].astype(F32)
    hn = (n * w.nn[0:1, :] + w.nn[1:2, :]).astype(BF)
    for m in range(3):
        put_strided(flat, 2048 * m, tn(hn, io.dqkv[:, 512 * m : 512 * (m + 1)]), 4)
    small = flat.at[pl.ds(ROW_O, SMALL_ROWS), :]
    small[...] = io.small[...]
    small[NN : NN + 8, :] = io.sums_one[...]

    scr.geg[...] = jnp.zeros((512, 512), F32)
    scr.en[...] = jnp.zeros((2, 8, 256), F32)

    @dm.each_pair
    def _(rows, pair):
        dsg = io.dsg[pair, :]
        n = res.edge_n1[rows, :].astype(F32)
        xn = (n * w.en[0:1, :] + w.en[1:2, :]).astype(BF)
        scr.geg[...] += tn(beside(xn), dsg)
        dxn = below(nt(dsg, w.eg[...]))
        scr.en[0] += fold8(dxn * n)
        scr.en[1] += fold8(dxn)
        gdy = dxn * w.en[0:1, :]
        m1 = nn(gdy.astype(BF), scr.mean[...])
        m2 = nn((gdy * n).astype(BF), scr.mean[...])
        dx = io.dmid[rows, :].astype(F32) + res.edge_r1[rows, :].astype(F32) * (gdy - m1 - n * m2)
        io.edges_grad[rows, :] = dx.astype(BF)

    for which, first in ((0, BIAS), (1, GATE)):
        sides = []
        for half in range(2):
            sums = jnp.zeros((64, 128), F32)
            for k in range(8):
                part = scr.geg[64 * k : 64 * (k + 1), lanes(2 * which + half)]
                sums = sums + jnp.where(lane_group(64, 4) == k, part, 0.0)
            sides.append(group_sum(sums))
        scr.tmp[0:64, :] = jnp.where(lane_group(64, 4) % 2 == 0, sides[0], sides[1])
        rows = jnp.zeros((16, 128), F32)
        for b in range(4):
            rows = jnp.where(lane_group(16, 5) == b, scr.tmp[pl.ds(b, 16, stride=4), :], rows)
        small[first : first + 16, :] = rows
    put_edge_norm(scr.en, small, EN)
    end = ROW_O + SMALL_ROWS
    if dm.lower > end:
        flat[end:, :] = jnp.zeros((dm.lower - end, 128), F32)
    put_halves(flat, io.keep, io.send)


def lane_group(rows, bits):
    return iota((rows, 128), 1) >> bits


def fold_halves(sums, tmp, out, first):
    rows, half = sums.shape[0], sums.shape[0] // 2
    tmp[0:rows, :] = sums + pltpu.roll(sums, 64, 1)
    even = tmp[pl.ds(0, half, stride=2), :]
    odd = tmp[pl.ds(1, half, stride=2), :]
    out[first : first + half, :] = jnp.where(lane_group(half, 6) == 0, even, odd)


def put_edge_norm(sums, out, at):
    ones = []
    for t in range(2):
        both = jnp.sum(sums[t], axis=0, keepdims=True)
        one = both[:, :128] + both[:, 128:]
        ones.append(one + pltpu.roll(one, 64, 1))
    out[at : at + 1, :] = jnp.where(lane_group(1, 6) == 0, ones[0], ones[1])


def assemble_set(off, flat, tmp, w):
    def strided(first, rows, parts, out, lane0=0):
        for q in range(parts):
            out[:, lane0 + 128 * q : lane0 + 128 * (q + 1)] = flat[
                pl.ds(off + first + q, rows, stride=parts), :
            ].astype(BF)

    for m in range(3):
        strided(ROW_QKV + 2048 * m, 512, 4, w.qkv, 512 * m)
    strided(ROW_O, 512, 4, w.o)
    strided(ROW_UP, 512, 8, w.up)
    strided(ROW_DOWN, 1024, 4, w.down)
    w.eg[...] = jnp.zeros((512, 512), BF)
    w.x[...] = jnp.zeros((256, 512), BF)
    w.a[...] = jnp.zeros((256, 512), BF)
    w.b[...] = jnp.zeros((512, 256), BF)
    up = flat[pl.ds(off + ROW_EUP, 64), :].astype(BF)
    for k in range(4):
        w.a[64 * k : 64 * (k + 1), 128 * k : 128 * (k + 1)] = up

    def doubled(first, in_rows):
        v = flat[pl.ds(off + first, in_rows), :]
        other = pltpu.roll(v, 64, 1)
        low = lane_group(in_rows, 6) == 0
        tmp[pl.ds(0, in_rows, stride=2), :] = jnp.where(low, v, other)
        tmp[pl.ds(1, in_rows, stride=2), :] = jnp.where(low, other, v)
        return tmp[0 : 2 * in_rows, :]

    both = doubled(ROW_EDOWN, 64)
    for k in range(4):
        w.b[128 * k : 128 * (k + 1), 128 * (k // 2) : 128 * (k // 2 + 1)] = jnp.where(
            lane_group(128, 6) == k % 2, both, 0.0
        ).astype(BF)
    both = doubled(ROW_EDGE, 16)
    for half in range(2):
        for k in range(8):
            at = 128 * half + 16 * k
            w.x[at : at + 16, 128 * (k // 2) : 128 * (k // 2 + 1)] = jnp.where(
                lane_group(16, 6) == k % 2, both[16 * half : 16 * (half + 1)], 0.0
            ).astype(BF)
    for which, first in ((0, ROW_BIAS), (1, ROW_GATE)):
        v = flat[pl.ds(off + first, 16), :]
        for b in range(4):
            tmp[pl.ds(b, 16, stride=4), :] = group_sum(jnp.where(lane_group(16, 5) == b, v, 0.0), 32)
        both = tmp[0:64, :]
        even = lane_group(64, 4) % 2 == 0
        sides = (
            jnp.where(even, both, pltpu.roll(both, 16, 1)),
            jnp.where(even, pltpu.roll(both, 112, 1), both),
        )
        for half in range(2):
            for k in range(8):
                w.eg[64 * k : 64 * (k + 1), lanes(2 * which + half)] = jnp.where(
                    lane_group(64, 4) == k, sides[half], 0.0
                ).astype(BF)
    for t in range(4):
        for q in range(4):
            w.nn[t : t + 1, 128 * q : 128 * (q + 1)] = flat[pl.ds(off + ROW_NN + 4 * t + q, 1), :]
    for t in range(2):
        v = flat[pl.ds(off + ROW_EN + t, 1), :]
        other = pltpu.roll(v, 64, 1)
        gain = jnp.where(lane_group(1, 6) == 0, v, other)
        bias = jnp.where(lane_group(1, 6) == 0, other, v)
        for half in range(2):
            w.en[2 * t : 2 * t + 1, 128 * half : 128 * (half + 1)] = gain
            w.en[2 * t + 1 : 2 * t + 2, 128 * half : 128 * (half + 1)] = bias


class Group:
    def __init__(self, names, refs):
        for name, ref in zip(names, refs):
            setattr(self, name, ref)


WEIGHTS = {
    "qkv": ((D, 3 * D), BF),
    "o": ((D, D), BF),
    "up": ((D, FF), BF),
    "down": ((FF, D), BF),
    "eg": ((512, 512), BF),
    "x": ((256, 512), BF),
    "a": ((256, 512), BF),
    "b": ((512, 256), BF),
    "nn": ((4, D), F32),
    "en": ((4, 256), F32),
}


def residual_shapes(dm):
    return {
        "node_n1": ((dm.nodes, D), BF),
        "node_r1": ((dm.nodes, 128), F32),
        "qkv": ((dm.nodes, 3 * D), BF),
        "mixed": ((dm.nodes, D), BF),
        "node_n2": ((dm.nodes, D), BF),
        "node_r2": ((dm.nodes, 128), F32),
        "node_u": ((dm.nodes, FF), F32),
        "edge_n1": ((dm.edges, 256), BF),
        "edge_r1": ((dm.edges, 256), BF),
        "gate": ((dm.scores, 256), F32),
        "low": ((dm.scores, 256), BF),
        "prob": ((dm.scores, 256), BF),
        "edge_n2": ((dm.edges, 256), BF),
        "edge_r2": ((dm.edges, 256), BF),
    }


def mean_shapes():
    return {"mean": ((256, 256), BF)}


def head_shapes():
    return {"head": ((16, 256), F32)}


def mask_shapes():
    return {**mean_shapes(), **head_shapes()}


def forward_scratch(dm):
    return {
        "scores": ((dm.scores, 256), F32),
        "attn": ((dm.scores, 256), BF),
        "vbig": ((dm.blocks, 2, 256, 256), BF),
    }


def ffn_shapes(dm, halves):
    half = ((UPPER_ROWS // 2, 128), BF)
    grads = {"keep": half, "send": half} if halves else {"upper": ((UPPER_ROWS, 128), BF)}
    return {
        "dy": ((dm.nodes, D), F32),
        "do": ((dm.nodes, D), BF),
        "sums": ((8, 128), F32),
        **grads,
    }


def edge_shapes(dm):
    return {
        "dmid": ((dm.edges, 256), BF),
        "scores": ((dm.scores, 256), F32),
        "small": ((SMALL_ROWS, 128), F32),
    }


def attention_shapes(dm):
    return {"dsg": ((dm.scores, 512), BF), "dqkv": ((dm.nodes, 3 * D), BF)}


def ffn_scratch():
    return {"upper": ((UPPER_ROWS, 128), F32)}


def edge_scratch():
    return {
        "gb": ((256, 128), F32),
        "ga": ((128, 256), F32),
        "gx": ((256, 512), F32),
        "en": ((2, 8, 256), F32),
        "tmp": ((128, 128), F32),
    }


def attention_scratch(dm):
    return {
        "attn": ((dm.scores, 256), BF),
        "vbig": ((dm.blocks, 2, 256, 256), BF),
        "da": ((dm.scores, 256), F32),
    }


def last_scratch(dm):
    return {
        "geg": ((512, 512), F32),
        "en": ((2, 8, 256), F32),
        "tmp": ((128, 128), F32),
        "lower": ((dm.lower, 128), F32),
    }


def structs(shapes):
    return [jax.ShapeDtypeStruct(s, t) for s, t in shapes.values()]


def vmem(shapes):
    return [pltpu.VMEM(s, t) for s, t in shapes.values()]


def whole(n):
    return [pl.BlockSpec(memory_space=pltpu.VMEM)] * n


def split(refs, *groups):
    out, at = [], 0
    for names in groups:
        out.append(Group(names, refs[at : at + len(names)]))
        at += len(names)
    assert at == len(refs)
    return out


def edge_copies(dm, small, big, big_lane, stacked, sems, out):
    copies = []
    for bucket, ref, lane in ((dm.small, small, 0), (dm.big, big, big_lane)):
        for c in range(bucket.chunks):
            a = ref.at[:, pl.ds(lane + 256 * c, 256)]
            b = stacked.at[pl.ds(bucket.edge0 + c * bucket.rows, bucket.rows), :]
            src, dst = (b, a) if out else (a, b)
            copies.append(pltpu.make_async_copy(src, dst, sems.at[len(copies)]))
    return copies


def node_copies(dm, small, big, big_lane, nodes, sems, at, out):
    copies = []
    for bucket, ref in ((dm.small, small), (dm.big, big.at[:, pl.ds(big_lane, D)])):
        b = nodes.at[pl.ds(bucket.node0, bucket.rows), :]
        src, dst = (b, ref) if out else (ref, b)
        copies.append(pltpu.make_async_copy(src, dst, sems.at[at + len(copies)]))
    return copies


def copy_sems(dm):
    return pltpu.SemaphoreType.DMA((dm.small.chunks + dm.big.chunks + 2,))


def all_copies(dm, small_nodes, small_edges, big, edge_lane, node_lane, nodes, edges, sems, out):
    copies = edge_copies(dm, small_edges, big, edge_lane, edges, sems, out)
    return node_copies(dm, small_nodes, big, node_lane, nodes, sems, len(copies), out) + copies


def start(copies):
    for c in copies:
        c.start()


def wait(copies):
    for c in copies:
        c.wait()


HBM = pl.BlockSpec(memory_space=pl.ANY)
SMEM = pl.BlockSpec(memory_space=pltpu.SMEM)
EDGE_LANES = NB * DE
IN_LANES = 2 * EDGE_LANES + 2 * D
OUT_LANES = EDGE_LANES + D


def compiler_params():
    return pltpu.CompilerParams(vmem_limit_bytes=VMEM_LIMIT)


def cost(us):
    return pl.CostEstimate(flops=0, bytes_accessed=int(us * 3.4e6), transcendentals=0)


def take(group, names):
    return [getattr(group, k) for k in names]


NODE_BACK = ("node_n2", "node_r2", "node_u", "mixed")
EDGE_BACK = ("edge_n2", "edge_r2", "low")
ATTENTION_BACK = ("qkv", "prob", "gate")
LAST_BACK = ("node_n1", "node_r1", "edge_n1", "edge_r1")
W_NODE = ("o", "up", "down", "nn")
W_EDGE = ("x", "a", "b", "en")
W_LAST = ("qkv", "eg", "nn", "en")


def kernel(body, inputs, out, scr, us, counts=None, hbm_in=0, hbm_out=(), sems=()):
    smem = [] if counts is None else [counts]
    return Group(
        out,
        pl.pallas_call(
            body,
            out_shape=structs(out),
            in_specs=[SMEM] * len(smem) + whole(len(inputs) - hbm_in) + [HBM] * hbm_in,
            out_specs=[HBM if k in hbm_out else pl.BlockSpec(memory_space=pltpu.VMEM) for k in out],
            scratch_shapes=vmem(scr) + list(sems),
            compiler_params=compiler_params(),
            cost_estimate=cost(us),
        )(*smem, *inputs),
    )


class Leaving:
    def __init__(self, names, held, outs, sems):
        self.names, self.held, self.outs, self.sems = tuple(names), held, outs, sems
        self.copies = []

    def __call__(self, *names):
        for k in names:
            if k in self.names:
                sem = self.sems.at[len(self.copies)]
                self.copies.append(
                    pltpu.make_async_copy(getattr(self.held, k), getattr(self.outs, k), sem)
                )
                self.copies[-1].start()

    def wait(self):
        assert len(self.copies) == len(self.names)
        wait(self.copies)


def first_forward(dm, counts, weights, small_nodes, small_edges, big):
    res = residual_shapes(dm)
    out = {"nodes_out": ((dm.nodes, D), BF), "edges_out": ((dm.edges, 256), BF), **res}
    scr = {
        **mask_shapes(),
        **forward_scratch(dm),
        "nodes": ((dm.nodes, D), BF),
        "edges": ((dm.edges, 256), BF),
        **res,
    }

    def body(*refs):
        counts_ref, refs, sems, out_sems = refs[0], refs[1:-2], refs[-2], refs[-1]
        w, src, dst, s = split(refs, WEIGHTS, ("sn", "se", "big"), out, scr)
        copies = all_copies(
            dm, src.sn, src.se, src.big, 0, 2 * EDGE_LANES, s.nodes, s.edges, sems, False
        )
        start(copies)
        make_masks(s)
        io = Group(
            ("nodes", "edges", "nodes_out", "edges_out"),
            (s.nodes, s.edges, dst.nodes_out, dst.edges_out),
        )
        leaving = Leaving(res, s, dst, out_sems)
        wait(copies)
        forward(dm, counts_ref, w, io, s, s, leaving)
        leaving.wait()

    inputs = take(weights, WEIGHTS) + [small_nodes, small_edges, big]
    sems = [copy_sems(dm), pltpu.SemaphoreType.DMA((len(res),))]
    got = kernel(body, inputs, out, scr, 16, counts, 3, tuple(res), sems)
    return got.nodes_out, got.edges_out, got


def second_forward(dm, counts, weights, nodes, edges, small_node_cot, small_edge_cot, big):
    res, ffn = residual_shapes(dm), ffn_shapes(dm, False)
    whole_outs = {
        "sno": ((dm.small.rows, D), BF),
        "seo": ((dm.small.rows, dm.small.edge_lanes), BF),
        "bout": ((dm.big.rows, OUT_LANES), BF),
    }
    kept = {k: v for k, v in res.items() if k not in NODE_BACK}
    out = {**whole_outs, "edge_cot": ((dm.edges, 256), BF), **kept, **ffn}
    scr = {
        **mask_shapes(),
        **forward_scratch(dm),
        **ffn_scratch(),
        **res,
        "nodes_out": ((dm.nodes, D), BF),
        "edges_out": ((dm.edges, 256), BF),
        "node_cot": ((dm.nodes, D), BF),
    }

    def body(*refs):
        counts_ref, refs, in_sems, out_sems, res_sems = refs[0], refs[1:-3], *refs[-3:]
        w, src, dst, s = split(refs, WEIGHTS, ("nodes", "edges", "snc", "sec", "big"), out, scr)
        copies = all_copies(
            dm, src.snc, src.sec, src.big, EDGE_LANES, 2 * EDGE_LANES + D, s.node_cot, dst.edge_cot, in_sems, False
        )
        start(copies)
        make_masks(s)
        leaving = Leaving(kept, s, dst, res_sems)
        io = Group(
            ("nodes", "edges", "nodes_out", "edges_out"),
            (src.nodes, src.edges, s.nodes_out, s.edges_out),
        )
        forward(dm, counts_ref, w, io, s, s, leaving)
        outgoing = all_copies(
            dm, dst.sno, dst.seo, dst.bout, 0, EDGE_LANES, s.nodes_out, s.edges_out, out_sems, True
        )
        start(outgoing)
        wait(copies)
        back_ffn(dm, w, Group(("nodes_cot", *ffn), (s.node_cot, *take(dst, ffn))), s, s)
        wait(outgoing)
        leaving.wait()

    inputs = take(weights, WEIGHTS) + [nodes, edges, small_node_cot, small_edge_cot, big]
    sems = [copy_sems(dm), copy_sems(dm), pltpu.SemaphoreType.DMA((len(kept),))]
    got = kernel(body, inputs, out, scr, 22, counts, 3, (*whole_outs, *kept), sems)
    return got.sno, got.seo, got.bout, None, got.edge_cot, got, got


def between(dm, weights_two, weights_one, kept_two, kept_one, ffn_two, edges_cot):
    ffn, edge, att = ffn_shapes(dm, True), edge_shapes(dm), attention_shapes(dm)
    handed = {"dmid": edge["dmid"], "small": edge["small"], **att, "sums_one": ((8, 128), F32)}
    out = {**{"two_" + k: v for k, v in handed.items()}, **ffn}
    scr = {
        **mask_shapes(),
        **edge_scratch(),
        **attention_scratch(dm),
        **ffn_scratch(),
        "scores": edge["scores"],
        "nodes_grad": ((dm.nodes, D), BF),
    }
    w_two = ("qkv", *W_EDGE, "nn")
    res_two = EDGE_BACK + ATTENTION_BACK + ("node_n1", "node_r1")

    def body(*refs):
        w, w_one, res, res_one, src, dst, s = split(
            refs, w_two, W_NODE, res_two, NODE_BACK, ("edges_cot", "sums", "do", "dy"), out, scr
        )
        make_masks(s)
        io = Group(
            ("edges_cot", "sums", "do", "dy", "scores", "nodes_grad", *handed),
            (src.edges_cot, src.sums, src.do, src.dy, s.scores, s.nodes_grad)
            + tuple(getattr(dst, "two_" + k) for k in handed),
        )
        back_edges(dm, w, io, res, s)
        back_attention(dm, io, res, s)
        back_nodes(dm, w, io, res, s)
        back_ffn(dm, w_one, Group(("nodes_cot", *ffn), (s.nodes_grad, *take(dst, ffn))), res_one, s)

    inputs = take(weights_two, w_two) + take(weights_one, W_NODE)
    inputs += take(kept_two, res_two) + take(kept_one, NODE_BACK)
    inputs += [edges_cot, ffn_two.sums, ffn_two.do, ffn_two.dy]
    return kernel(body, inputs, out, scr, 25)


def second_last(dm, weights, kept, got):
    half = {k: ((dm.lower // 2, 128), BF) for k in ("keep", "send")}
    out = {"edges_grad": ((dm.edges, 256), BF), **half}
    scr = {**mean_shapes(), **last_scratch(dm)}
    given = ("dmid", "small", "dsg", "dqkv", "sums_one")
    w_last = ("eg", "nn", "en")
    last_res = ("node_n1", "edge_n1", "edge_r1")

    def body(*refs):
        w, res, src, dst, s = split(refs, w_last, last_res, given, out, scr)
        make_mean(s)
        back_last(dm, w, Group((*given, *out), (*take(src, given), *take(dst, out))), res, s)

    inputs = take(weights, w_last) + take(kept, last_res)
    inputs += [getattr(got, "two_" + k) for k in given]
    return kernel(body, inputs, out, scr, 9)


def call_edges(dm, weights, kept, ffn, edges_cot):
    out, scr = edge_shapes(dm), {**mean_shapes(), **edge_scratch()}

    def body(*refs):
        w, res, src, dst, s = split(refs, W_EDGE, EDGE_BACK, ("edges_cot", "sums"), out, scr)
        make_mean(s)
        io = Group(("edges_cot", "sums", *out), (src.edges_cot, src.sums, *take(dst, out)))
        back_edges(dm, w, io, res, s)

    inputs = take(weights, W_EDGE) + take(kept, EDGE_BACK) + [edges_cot, ffn.sums]
    return kernel(body, inputs, out, scr, 16)


def call_attention(dm, kept, ffn, edge):
    out, scr = attention_shapes(dm), {**head_shapes(), **attention_scratch(dm)}

    def body(*refs):
        res, src, dst, s = split(refs, ATTENTION_BACK, ("do", "scores"), out, scr)
        make_heads(s)
        back_attention(dm, Group(("do", "scores", *out), (src.do, src.scores, *take(dst, out))), res, s)

    return kernel(body, take(kept, ATTENTION_BACK) + [ffn.do, edge.scores], out, scr, 14)


def call_last(dm, weights, kept, ffn, edge, att):
    half = {k: ((dm.lower // 2, 128), BF) for k in ("keep", "send")}
    outs = {
        "sng": ((dm.small.rows, D), BF),
        "seg": ((dm.small.rows, dm.small.edge_lanes), BF),
        "bgrad": ((dm.big.rows, OUT_LANES), BF),
    }
    out = {**outs, **half}
    scr = {
        **mean_shapes(),
        **last_scratch(dm),
        "nodes_grad": ((dm.nodes, D), BF),
        "edges_grad": ((dm.edges, 256), BF),
        "sums_one": ((8, 128), F32),
    }
    given = ("dy", "dmid", "small", "dsg", "dqkv")

    def body(*refs):
        refs, sems = refs[:-1], refs[-1]
        w, res, src, dst, s = split(refs, W_LAST, LAST_BACK, given, out, scr)
        make_mean(s)
        io = Group(
            (*given, "nodes_grad", "edges_grad", "keep", "send", "sums_one"),
            (*take(src, given), s.nodes_grad, s.edges_grad, dst.keep, dst.send, s.sums_one),
        )
        back_nodes(dm, w, io, res, s)
        back_last(dm, w, io, res, s)
        outgoing = all_copies(
            dm, dst.sng, dst.seg, dst.bgrad, 0, EDGE_LANES, s.nodes_grad, s.edges_grad, sems, True
        )
        start(outgoing)
        wait(outgoing)

    inputs = take(weights, W_LAST) + take(kept, LAST_BACK)
    inputs += [ffn.dy, edge.dmid, edge.small, att.dsg, att.dqkv]
    got = kernel(body, inputs, out, scr, 13, hbm_out=tuple(outs), sems=[copy_sems(dm)])
    return take(got, out)


def round_up(value, by):
    return -(-value // by) * by


def segment_of(owner, rows, index, count):
    name = owner[index]
    first = jnp.int32(0)
    for t in range(count):
        first = first + jnp.where(t < name, rows[t], 0)
    return first, rows[name]


def shifted_segment(owner, segment_rows, master):
    held = master.shape[0]
    count = owner.shape[0]
    padded = round_up(held + 15, 16)
    step = round_up(-(-padded // 2), 16)

    def body(owner_ref, rows_ref, src, dst, window):
        i = pl.program_id(0)
        first, length = segment_of(owner_ref, rows_ref, lax.axis_index("dp"), count)
        shift = first % 16

        @pl.when(i == 0)
        def _():
            window[0:16, :] = jnp.zeros((16, 128), F32)

        window[16:, :] = src[...]
        moved = window[pl.ds(16 - shift, step), :]
        index = i * step - shift + iota((step, 128), 0)
        live = (index >= 0) & (index < length)
        dst[...] = jnp.where(live, moved, 0.0).astype(BF)
        window[0:16, :] = window[step : step + 16, :]

    return pl.pallas_call(
        body,
        grid=(pl.cdiv(padded, step),),
        out_shape=jax.ShapeDtypeStruct((padded, 128), BF),
        in_specs=[
            SMEM,
            SMEM,
            pl.BlockSpec((step, 128), lambda i: (jnp.minimum(i, (held - 1) // step), 0)),
        ],
        out_specs=pl.BlockSpec((step, 128), lambda i: (i, 0)),
        scratch_shapes=[pltpu.VMEM((step + 16, 128), F32)],
        compiler_params=compiler_params(),
    )(owner, segment_rows, master)


def assemble(cube, owner, segment_rows, parts, sources):
    count = len(parts)
    padded = parts[0].shape[0]
    bits = (padded // 16).bit_length()
    tiles = -(-TOTAL_ROWS // 16)
    set_tiles = -(-(SET_ROWS + 2) // 16)
    out = {**{"one_" + k: v for k, v in WEIGHTS.items()}, **{"two_" + k: v for k, v in WEIGHTS.items()}}

    def body(owner_ref, rows_ref, *refs):
        srcs, refs = refs[:count], refs[count:]
        dsts, (rows, flat, tmp, edge, sems, edge_sems) = refs[: len(out)], refs[len(out) :]
        me = lax.axis_index("dp")
        spans = []
        for i in range(count):
            first, length = segment_of(owner_ref, rows_ref, cube.source(me, sources[i]), count)
            spans.append((first // 16, (first + length - 1) // 16))

        def each(act):
            for i, (a, b) in enumerate(spans):
                inner = b - a - 1
                for bit in range(bits):
                    size = 16 << bit
                    if size > padded:
                        continue
                    done = (inner >> (bit + 1)) << (bit + 1)

                    @pl.when((inner > 0) & (((inner >> bit) & 1) == 1))
                    def _(i=i, a=a, done=done, size=size, bit=bit):
                        act(
                            pltpu.make_async_copy(
                                srcs[i].at[pl.ds(aligned(16 * (1 + done), 16), size), :],
                                rows.at[pl.ds(aligned(16 * (a + 1 + done), 16), size), :],
                                sems.at[i, bit],
                            )
                        )

                act(pltpu.make_async_copy(srcs[i].at[pl.ds(0, 16), :], edge.at[2 * i], edge_sems.at[2 * i]))
                act(
                    pltpu.make_async_copy(
                        srcs[i].at[pl.ds(aligned(16 * (b - a), 16), 16), :],
                        edge.at[2 * i + 1],
                        edge_sems.at[2 * i + 1],
                    )
                )

        each(lambda c: c.start())
        each(lambda c: c.wait())
        tile = lambda t: pl.ds(aligned(16 * t, 16), 16)
        for a, b in spans:
            rows[tile(a), :] = jnp.zeros((16, 128), BF)
            rows[tile(b), :] = jnp.zeros((16, 128), BF)
        for i, (a, b) in enumerate(spans):
            rows[tile(a), :] += edge[2 * i]

            @pl.when(b != a)
            def _(i=i, b=b):
                rows[tile(b), :] += edge[2 * i + 1]

        for which in range(2):
            base = which * (SET_ROWS // 16) * 16
            flat[...] = rows[pl.ds(base, 16 * set_tiles), :].astype(F32)
            w = Group(WEIGHTS, dsts[which * len(WEIGHTS) : (which + 1) * len(WEIGHTS)])
            assemble_set(which * (SET_ROWS % 16), flat, tmp, w)

    got = pl.pallas_call(
        body,
        out_shape=structs(out),
        in_specs=[SMEM] * 2 + [HBM] * count,
        out_specs=whole(len(out)),
        scratch_shapes=[
            pltpu.VMEM((16 * tiles, 128), BF),
            pltpu.VMEM((16 * set_tiles, 128), F32),
            pltpu.VMEM((128, 128), F32),
            pltpu.VMEM((2 * count, 16, 128), BF),
            pltpu.SemaphoreType.DMA((count, bits)),
            pltpu.SemaphoreType.DMA((2 * count,)),
        ],
        compiler_params=compiler_params(),
        cost_estimate=cost(10),
    )(owner, segment_rows, *parts)
    return Group(WEIGHTS, got[: len(WEIGHTS)]), Group(WEIGHTS, got[len(WEIGHTS) :])


def adam(n_row, lower, owner, segment_rows, scales, whole_upper, blocks, master, first, second):
    held = master.shape[0]
    step = 2080
    front = step + 16
    count = len(blocks)
    n_dp = owner.shape[0]
    set_rows = ROW_BIAS - ROW_O + lower
    total_rows = front + set_rows + step + 32
    ways = 3
    arrivals = sum(len(keys) for _, _, keys, _ in blocks)

    def body(owner_ref, rows_ref, scale_ref, *refs):
        upper, srcs, refs = refs[0], refs[1 : 1 + count], refs[1 + count :]
        master_ref, first_ref, second_ref, o_master, o_first, o_second, o_norms, rows, window, grad, rate, sems, upper_sem = refs
        i = pl.program_id(0)
        me, row = lax.axis_index("dp"), lax.axis_index("row")
        begin, length = segment_of(owner_ref, rows_ref, me, n_dp)

        @pl.when(i == 0)
        def _():
            def each(act):
                copy = pltpu.make_async_copy(
                    upper, rows.at[1, pl.ds(front + ROW_O, UPPER_ROWS), :], upper_sem
                )
                pl.when(begin + length > SET_ROWS + ROW_O)(functools.partial(act, copy))
                every = [
                    (k, core, key, n, sections)
                    for k, (_, core, keys, sections) in enumerate(blocks)
                    for n, key in enumerate(keys)
                ]
                for at_sem, (k, core, key, n, sections) in enumerate(every):
                    mine = (me ^ core) & 1
                    source = me ^ core ^ jnp.where(mine == 0, key[0], key[1])
                    offset = n * n_row * sum(size for _, _, size in sections)
                    place = (source & 1) * (n_dp // 2) + (source >> 1)
                    for number, (which, part, size) in enumerate(sections):
                        size = size * n_row
                        at = place * size
                        dest = at + ROW_O if part else jnp.where(at >= ROW_O, at - ROW_O + ROW_BIAS, at)
                        wanted = (dest + which * SET_ROWS < begin + length) & (
                            dest + size + which * SET_ROWS > begin
                        )
                        wanted = wanted | (dest + size > ROW_NN)

                        def move(frm, extent, to, way, k=k, which=which, at_sem=at_sem):
                            act(
                                pltpu.make_async_copy(
                                    srcs[k].at[pl.ds(frm, extent), :],
                                    rows.at[which, pl.ds(aligned(front + to, 16), extent), :],
                                    sems.at[at_sem, way],
                                )
                            )

                        cut = 0 if part else ROW_O % size
                        if cut:
                            split_here = (at < ROW_O) & (at + size > ROW_O)
                            wanted = wanted & jnp.logical_not(split_here)

                            @pl.when(split_here)
                            def _(move=move, offset=offset, size=size, at=at, cut=cut, number=number):
                                move(offset, cut, at, number)
                                move(offset + cut, size - cut, ROW_BIAS, 2)

                        pl.when(wanted)(functools.partial(move, offset, size, dest, number))
                        offset += size

            each(lambda c: c.start())
            each(lambda c: c.wait())
            for which in range(2):
                v = rows[which, front + ROW_NN : front + ROW_NN + 32, :].astype(F32)
                for t in range(4):
                    for q in range(4):
                        o_norms[4 * which + t : 4 * which + t + 1, 128 * q : 128 * (q + 1)] = v[
                            4 * t + q : 4 * t + q + 1, :
                        ]
                for t in range(2):
                    both = v[16 + t : 17 + t, :]
                    at = 4 * which + 2 * t
                    o_norms[at : at + 1, 512:576] = both[:, 0:64]
                    o_norms[at + 1 : at + 2, 512:576] = pltpu.roll(both, 64, 1)[:, 0:64]

        low = begin + i * step
        high = low + step
        some = i * step < length

        @pl.when(jnp.logical_not(some))
        def _():
            o_master[...] = master_ref[...]
            o_first[...] = first_ref[...]
            o_second[...] = second_ref[...]

        @pl.when(some)
        def _():
            def shifted(which):
                local = low - which * SET_ROWS + front
                shift = local % 16
                window[...] = rows[which, pl.ds(aligned(local - shift, 16), step + 16), :].astype(F32)
                return window[pl.ds(shift, step), :]

            index = iota((step, 128), 0)

            @pl.when(low < SET_ROWS)
            def _():
                grad[...] = shifted(0)

            @pl.when(low >= SET_ROWS)
            def _():
                grad[...] = shifted(1)

            @pl.when((low < SET_ROWS) & (high > SET_ROWS))
            def _():
                grad[...] = jnp.where(index + low >= SET_ROWS, shifted(1), grad[...])

            at = index + low
            at = jnp.where(at >= SET_ROWS, at - SET_ROWS, at)
            a, b, c = RATES[0][1], RATES[1][1], RATES[3][1]
            far = jnp.where(at < ROW_DOWN, a, c)
            rate[...] = jnp.where(at < ROW_O, a, jnp.where(at < ROW_UP, b, far))
            near = (low < SET_ROWS) & (high > ROW_BIAS)

            @pl.when(near | (high > SET_ROWS + ROW_BIAS))
            def _():
                value = jnp.full((step, 128), 0.25, F32)
                for end, one in reversed(RATES[4:]):
                    value = jnp.where(at < end, one, value)
                rate[...] = jnp.where(at < ROW_BIAS, rate[...], value)

            g = grad[...]
            p, m, v = master_ref[...], first_ref[...], second_ref[...]
            m_new = BETA_ONE * m + (1.0 - BETA_ONE) * g
            v_new = BETA_TWO * v + (1.0 - BETA_TWO) * g * g
            move = (m_new * scale_ref[0]) / (jnp.sqrt(v_new * scale_ref[1]) + ADAM_EPS)
            live = index < length - i * step
            o_master[...] = jnp.where(live, p - rate[...] * (move + WEIGHT_DECAY * p), p)
            o_first[...] = jnp.where(live, m_new, m)
            o_second[...] = jnp.where(live, v_new, v)

    spec = pl.BlockSpec((step, 128), lambda i: (i, 0))
    shape = jax.ShapeDtypeStruct((held, 128), F32)
    return pl.pallas_call(
        body,
        grid=(pl.cdiv(held, step),),
        out_shape=[shape] * 3 + [jax.ShapeDtypeStruct((8, D + DE), F32)],
        in_specs=[SMEM] * 3 + [HBM] * (count + 1) + [spec] * 3,
        out_specs=[spec] * 3 + [pl.BlockSpec((8, D + DE), lambda i: (0, 0))],
        scratch_shapes=[
            pltpu.VMEM((2, total_rows, 128), BF),
            pltpu.VMEM((step + 16, 128), F32),
            pltpu.VMEM((step, 128), F32),
            pltpu.VMEM((step, 128), F32),
            pltpu.SemaphoreType.DMA((arrivals, ways)),
            pltpu.SemaphoreType.DMA(()),
        ],
        compiler_params=compiler_params(),
        cost_estimate=cost(10),
    )(owner, segment_rows, scales, whole_upper, *[b[0] for b in blocks], master, first, second)


RATES = [
    (ROW_O, 0.5 * D ** (-0.5)),
    (ROW_UP, 2.0 * D ** (-0.5)),
    (ROW_DOWN, 0.5 * D ** (-0.5)),
    (ROW_BIAS, 0.5 * FF ** (-0.5)),
    (ROW_EDGE, 0.5 * DE ** (-0.5)),
    (ROW_EUP, 0.5 * H ** (-0.5)),
    (ROW_EDOWN, 0.5 * DE ** (-0.5)),
    (ROW_NN, 0.5 * FFE ** (-0.5)),
]


class Cube:
    def __init__(self, size):
        self.size = size
        self.bits = size.bit_length() - 1
        assert size == 1 << self.bits
        up = list(range(1, self.bits))
        self.order = (up, up[::-1])

    def pairs(self, step):
        return [(i, i ^ (1 << self.order[i & 1][step])) for i in range(self.size)]

    def core_pairs(self):
        return [(i, i ^ 1) for i in range(self.size)]

    def source(self, me, key):
        other, used = key
        even, odd = [sum(1 << self.order[c][s] for s in used) for c in (0, 1)]
        if other:
            even, odd = odd, even
        return me ^ jnp.where(me & 1 == 0, even, odd) ^ other

    def gather(self, value, meanwhile):
        steps = range(self.bits - 1)
        new, done, also = [((), value)], [], None
        while new:
            sent = []
            for used, v in new:
                done.append(((0, used), v))
                for step in steps:
                    if not used or step > used[-1]:
                        sent.append((0, used + (step,), lax.ppermute(v, "dp", self.pairs(step))))
            for used, v in new:
                sent.append((1, used, lax.ppermute(v, "dp", self.core_pairs())))
            beside = None
            if also is None:
                also = meanwhile(lax.ppermute(value[:16], "dp", self.core_pairs()))
            else:
                beside = also
            moved, beside = lax.optimization_barrier(([v for _, _, v in sent], beside))
            also = also if beside is None else beside
            new = []
            for (other, used, _), v in zip(sent, moved):
                if other:
                    done.append(((1, used), v))
                else:
                    new.append((used, v))
        return done, also


def total(values):
    out = values[0].astype(F32)
    for v in values[1:]:
        out = out + v.astype(F32)
    return out.astype(BF)


def side_by_side(parts, sections, row_order):
    count, total_rows = len(parts), len(parts) * parts[0].shape[0]

    def body(*refs):
        srcs, dst, sems = refs[:count], refs[count], refs[count + 1]
        row = lax.axis_index("row")
        copies = []
        for k in range(count):
            inside = 0
            for number, size in enumerate(sections):
                if row_order:
                    to = aligned(count * inside + (row ^ k) * size, 16)
                else:
                    to = k * parts[0].shape[0] + inside
                copies.append(
                    pltpu.make_async_copy(
                        srcs[k].at[pl.ds(inside, size), :],
                        dst.at[pl.ds(to, size), :],
                        sems.at[k, number],
                    )
                )
                inside += size
        start(copies)
        wait(copies)

    return pl.pallas_call(
        body,
        out_shape=jax.ShapeDtypeStruct((total_rows, 128), BF),
        in_specs=[HBM] * count,
        out_specs=HBM,
        scratch_shapes=[pltpu.SemaphoreType.DMA((count, len(sections)))],
        compiler_params=pltpu.CompilerParams(vmem_limit_bytes=4 * 1024 * 1024),
        cost_estimate=cost(1),
    )(*parts)


class Chain:
    def __init__(self, cube, direct, *halves):
        self.cube, self.direct = cube, direct
        self.kept = [k for k, _ in halves]
        self.value = [s for _, s in halves]
        self.step, self.done = 0, False
        self.sides = lax.axis_size("dp") // 2
        self.rows = lax.axis_size("row")

    def swap(self, value):
        return lax.ppermute(value, "dp", [(i, i ^ 1) for i in range(2 * self.sides)])

    def to_chip(self, value, k):
        return lax.ppermute(value, "dp", [(i, i ^ (k << 1)) for i in range(2 * self.sides)])

    def to_row(self, value, k):
        return lax.ppermute(value, "row", [(i, i ^ k) for i in range(self.rows)])

    def scatter(self, index, count, send):
        def at(k):
            parts = [v.reshape(count, v.shape[0] // count, 128) for v in self.value]
            parts = [lax.dynamic_index_in_dim(v, index ^ k, 0, keepdims=False) for v in parts]
            return jnp.concatenate(parts) if len(parts) > 1 else parts[0]

        self.sizes = [v.shape[0] // count for v in self.value]
        self.kept = at(0)
        return [send(at(k), k) for k in range(1, count)]

    def join(self, other):
        assert self.step == other.step == 2
        self.value = self.value + other.value

    def launch(self):
        self.step += 1
        if self.step == 1:
            return [self.swap(v) for v in self.value]
        if self.step == 2:
            return self.scatter(lax.axis_index("dp") >> 1, self.sides, self.to_chip)
        if self.step == 3:
            return self.scatter(lax.axis_index("row"), self.rows, self.to_row)
        if self.step == 4:
            return [self.to_row(self.value, k) for k in range(1, self.rows)]
        if not self.spread():
            return [self.swap(self.value)]
        if self.direct:
            return [self.to_chip(self.value, k) for k in range(1, self.sides)]
        return [lax.ppermute(self.value, "dp", self.cube.pairs(self.step - 5))]

    def spread(self):
        return self.step < 6 if self.direct else self.step < 5 + self.cube.bits - 1

    def land(self, got):
        if self.step == 1:
            self.value = [total(pair) for pair in zip(self.kept, got)]
        elif self.step <= 3:
            value = total([self.kept, *got])
            if self.step == 3:
                self.value = value
            else:
                self.value, at = [], 0
                for size in self.sizes:
                    self.value.append(value[at : at + size])
                    at += size
        elif self.step == 4:
            self.value = side_by_side([self.value, *got], self.sizes, True)
        elif self.spread():
            self.value = side_by_side([self.value, *got], [self.value.shape[0]], False)
            if self.direct:
                self.keys = [(k << 1, k << 1) for k in range(self.sides)]
            else:
                bit = [1 << order[self.step - 5] for order in self.cube.order]
                keys = self.keys if self.step > 5 else [(0, 0)]
                self.keys = keys + [(a ^ bit[0], b ^ bit[1]) for a, b in keys]
        else:
            self.value, self.done = [self.value, *got], True

    def blocks(self, *names):
        sections = [(which, part, size) for (which, part), size in zip(names, self.sizes)]
        return [(v, core, self.keys, sections) for core, v in enumerate(self.value)]


def phase(chains, *ready):
    chains = [c for c in chains if not c.done]
    sent = [c.launch() for c in chains]
    got, ready = lax.optimization_barrier((sent, ready))
    for c, g in zip(chains, got):
        c.land(g)
    return ready


def per_device(
    small_nodes,
    small_edges,
    small_counts,
    big_nodes,
    big_edges,
    big_counts,
    small_node_cot,
    small_edge_cot,
    big_node_cot,
    big_edge_cot,
    master,
    first_moment,
    second_moment,
    owner,
    segment_rows,
    step_count,
):
    n_dp, n_row = lax.axis_size("dp"), lax.axis_size("row")
    cube = Cube(n_dp)
    share = big_nodes.shape[0] // n_row
    dm = Dims(small_nodes.shape[0], share, n_dp * n_row)

    def flat2(v):
        return v.reshape(-1, v.shape[-1])

    def packed(v, first, lanes):
        v = v[:, first : first + lanes].reshape(share, n_row, NB // n_row, lanes)
        return v.swapaxes(0, 1)

    def to_rows(v):
        v = lax.all_to_all(v, "row", split_axis=0, concat_axis=0, tiled=True)
        return v.reshape(n_row * share, NB // n_row, v.shape[-1])

    row = lax.axis_index("row")

    def row_pieces(v):
        v = v.reshape(share, n_row, NB // n_row, OUT_LANES)
        return [lax.dynamic_index_in_dim(v, row ^ k, 1, keepdims=False) for k in range(n_row)]

    def send_pieces(pieces):
        pairs = lambda k: [(i, i ^ k) for i in range(n_row)]
        return pieces[:1] + [lax.ppermute(pieces[k], "row", pairs(k)) for k in range(1, n_row)]

    def in_order(pieces, first, lanes):
        pieces = [p[..., first : first + lanes] for p in pieces]
        for k in range(n_row.bit_length() - 1):
            odd = (row >> k) & 1 == 1
            pieces = [jnp.where(odd, pieces[i ^ (1 << k)], p) for i, p in enumerate(pieces)]
        return jnp.concatenate(pieces)

    def to_whole(first):
        big = (big_edges, big_edge_cot, big_nodes, big_node_cot)
        _, big = lax.optimization_barrier((first, big))
        big = jnp.concatenate(big, axis=2)
        return flat2(lax.all_to_all(big, "row", split_axis=0, concat_axis=1, tiled=True))

    held, big = cube.gather(shifted_segment(owner, segment_rows, master), to_whole)
    one, two = assemble(cube, owner, segment_rows, [v for _, v in held], [k for k, _ in held])

    own_counts = lax.dynamic_slice_in_dim(big_counts, lax.axis_index("row") * share, share)
    counts = jnp.concatenate([small_counts, own_counts])

    mid_nodes, mid_edges, kept = first_forward(
        dm, counts, one, flat2(small_nodes), flat2(small_edges), big
    )
    sno, seo, bout, node_cot, edge_cot, kept_two, ffn_two = second_forward(
        dm, counts, two, mid_nodes, mid_edges, flat2(small_node_cot), flat2(small_edge_cot), big
    )
    spread = lax.psum_scatter(ffn_two.upper, "dp", scatter_dimension=0, tiled=True)
    got = between(dm, two, one, kept_two, kept, ffn_two, edge_cot)
    names = tuple(vars(got))
    values, out_pieces = phase([], take(got, names), send_pieces(row_pieces(bout)))
    got = Group(names, values)
    middle = Chain(cube, False, (got.keep, got.send))
    rest = second_last(dm, two, kept_two, got)
    spread, edge_grad, keep, send = phase([middle], spread, rest.edges_grad, rest.keep, rest.send)
    spread = lax.psum(spread, "row")
    lower_two = Chain(cube, False, (keep, send))
    names = tuple(edge_shapes(dm))
    edge_one = call_edges(dm, one, kept, got, edge_grad)
    edge_one = Group(names, phase([middle, lower_two], *take(edge_one, names)))
    names = tuple(attention_shapes(dm))
    att_one = Group(names, phase([lower_two], *take(call_attention(dm, kept, got, edge_one), names)))
    middle.join(lower_two)
    sng, seg, bgrad, keep, send = call_last(dm, one, kept, got, edge_one, att_one)
    spread, sng, seg, bgrad, keep, send = phase([middle], spread, sng, seg, bgrad, keep, send)
    upper_two = lax.all_gather(spread, "dp", axis=0, tiled=True)
    last = Chain(cube, True, (keep, send))
    sent = middle.launch()
    early = EDGE_LANES // 2
    bgrad, = phase([last], bgrad)
    one_part, two_part = packed(bgrad, 0, early), packed(bgrad, early, OUT_LANES - early)
    one_part = to_rows(one_part)
    sent, out_pieces = phase([last], sent, out_pieces)
    bno, beo = in_order(out_pieces, EDGE_LANES, D), in_order(out_pieces, 0, EDGE_LANES)
    middle.land(sent)
    phase([last, middle])
    sent = middle.launch()
    one_part, upper_two, bno, beo = phase([last], one_part, upper_two, bno, beo)
    sent, two_part = phase([last], sent, two_part)
    middle.land(sent)
    while not (last.done and middle.done):
        two_part, = phase([last, middle], two_part)
    two_part = to_rows(two_part)
    bng = two_part[..., EDGE_LANES - early :]
    beg = jnp.concatenate([one_part, two_part[..., : EDGE_LANES - early]], axis=-1)
    blocks = last.blocks((0, 0)) + middle.blocks((0, 1), (1, 0))
    step_value = step_count[0].astype(F32)
    scales = jnp.stack(
        [
            1.0 / (1.0 - jnp.power(F32(BETA_ONE), step_value)),
            1.0 / (1.0 - jnp.power(F32(BETA_TWO), step_value)),
        ]
    )
    new_master, new_first, new_second, norm_grads = adam(
        n_row, dm.lower, owner, segment_rows, scales, upper_two, blocks, master, first_moment, second_moment
    )
    return (
        sno.reshape(small_nodes.shape),
        seo.reshape(small_edges.shape),
        bno,
        beo,
        sng.reshape(small_nodes.shape),
        seg.reshape(small_edges.shape),
        bng,
        beg,
        new_master,
        new_first,
        new_second,
        norm_grads,
    )


def solution(mesh):
    both = P(("dp", "row"), None, None)
    rows = P("dp", "row", None)
    held = P("dp", None)
    in_specs = (
        both, both, P(("dp", "row")), rows, rows, P("dp"), both, both, rows, rows,
        held, held, held, P(), P(), P(),
    )
    out_specs = (both, both, rows, rows, both, both, rows, rows, held, held, held, P())
    return jax.shard_map(
        per_device, mesh=mesh, in_specs=in_specs, out_specs=out_specs, check_vma=False
    )
```

```python
import functools

import jax
import jax.numpy as jnp
from jax import lax
from jax.experimental import pallas as pl
from jax.experimental.pallas import tpu as pltpu
from jax.sharding import PartitionSpec as P

D = 512
H = 32
DE = 64
FF = 1024
FFE = 128
NS = 32
NB = 64
SET_ROWS = 16578
TOTAL_ROWS = 33156
NORM_EPS = 1e-05
BETA_ONE = 0.9
BETA_TWO = 0.95
WEIGHT_DECAY = 0.1
ADAM_EPS = 1e-08
MASK_FILL = -1e30
BF = jnp.bfloat16
F32 = jnp.float32
VMEM_LIMIT = 58 * 1024 * 1024
ROW_QKV, ROW_O, ROW_UP, ROW_DOWN = 0, 6144, 8192, 12288
ROW_BIAS, ROW_GATE, ROW_EDGE, ROW_EUP, ROW_EDOWN = 16384, 16400, 16416, 16432, 16496
ROW_NN, ROW_EN = 16560, 16576
SMALL_USED, SMALL_ROWS = SET_ROWS - ROW_BIAS, 256
BIAS, GATE, EDGE, EUP, EDOWN = 0, 16, 32, 48, 112
NN, EN = ROW_NN - ROW_BIAS, ROW_EN - ROW_BIAS
UPPER_ROWS = ROW_BIAS - ROW_O
GELU_C = 0.7978845608028654
PAIRS = 4


def nn(a, b):
    return lax.dot_general(a, b, (((1,), (0,)), ((), ())), preferred_element_type=F32)


def nt(a, b):
    return lax.dot_general(a, b, (((1,), (1,)), ((), ())), preferred_element_type=F32)


def tn(a, b):
    return lax.dot_general(a, b, (((0,), (0,)), ((), ())), preferred_element_type=F32)


def iota(shape, axis):
    return lax.broadcasted_iota(jnp.int32, shape, axis)


def gelu_parts(u):
    u2 = u * u
    t = jnp.tanh(u * (GELU_C + (GELU_C * 0.044715) * u2))
    half = 0.5 + 0.5 * t
    value = u * half
    slope = half + value * (1.0 - t) * (GELU_C + (3.0 * GELU_C * 0.044715) * u2)
    return value, slope


def gelu_value(u):
    return u * (0.5 + 0.5 * jnp.tanh(u * (GELU_C + (GELU_C * 0.044715) * (u * u))))


def sigmoid(v):
    return 0.5 + 0.5 * jnp.tanh(0.5 * v)


def group_sum(v, first=16):
    while first < 128:
        v = v + pltpu.roll(v, first, 1)
        first *= 2
    return v


def group_max(v):
    for shift in (16, 32, 64):
        v = jnp.maximum(v, pltpu.roll(v, shift, 1))
    return v


def fold8(v):
    return jnp.sum(v.reshape(v.shape[0] // 8, 8, v.shape[1]), axis=0)


class Bucket:
    def __init__(self, graphs, slots, node0, edge0, count0):
        self.graphs, self.slots = graphs, slots
        self.node0, self.edge0, self.count0 = node0, edge0, count0
        self.rows = graphs * slots
        self.chunks = slots // 4
        self.pairs = slots // 8
        self.blocks = slots // 16
        self.edges = self.rows * self.chunks
        self.edge_lanes = slots * DE


class Dims:
    def __init__(self, small_graphs, big_graphs, parts):
        self.lower = round_up(ROW_O + SMALL_ROWS, 16 * parts)
        self.small = Bucket(small_graphs, NS, 0, 0, 0)
        self.big = Bucket(big_graphs, NB, self.small.rows, self.small.edges, small_graphs)
        self.buckets = (self.small, self.big)
        self.nodes = self.small.rows + self.big.rows
        self.edges = self.small.edges + self.big.edges
        self.scores = self.edges // 2
        self.blocks = sum(b.graphs * b.blocks for b in self.buckets)

    def each_pair(self, body):
        for bucket in self.buckets:
            two = 2 * PAIRS * bucket.rows

            @pl.loop(0, bucket.pairs // PAIRS, unroll=True)
            def _(i, bucket=bucket, two=two):
                body(
                    pl.ds(aligned(bucket.edge0 + i * two, 32), two),
                    pl.ds(aligned((bucket.edge0 + i * two) // 2, 16), two // 2),
                )


def beside(v):
    one = v.shape[0] // (2 * PAIRS)
    at = lambda c: v[c * one : (c + 1) * one]
    sides = [[at(2 * p + c) for p in range(PAIRS)] for c in range(2)]
    return jnp.concatenate([jnp.concatenate(s) for s in sides], axis=1)


def below(v):
    one = v.shape[0] // PAIRS
    at = lambda p, c: v[p * one : (p + 1) * one, 256 * c : 256 * (c + 1)]
    return jnp.concatenate([at(p, c) for p in range(PAIRS) for c in range(2)])


def make_masks(scr):
    make_mean(scr)
    make_heads(scr)


def make_mean(scr):
    shape = (256, 256)
    same = (iota(shape, 0) >> 6) == (iota(shape, 1) >> 6)
    scr.mean[...] = jnp.where(same, 1.0 / DE, 0.0).astype(BF)


def make_heads(scr):
    shape = (16, 256)
    scr.head[...] = jnp.where(iota(shape, 0) == (iota(shape, 1) >> 4), 1.0, 0.0)


def node_norm(v):
    centred = v - jnp.mean(v, axis=1, keepdims=True)
    r = lax.rsqrt(jnp.mean(centred * centred, axis=1, keepdims=True) + NORM_EPS)
    return centred * r, r


def node_norm_back(gdy, n, r):
    return r * (gdy - jnp.mean(gdy, axis=1, keepdims=True) - n * jnp.mean(gdy * n, axis=1, keepdims=True))


def aligned(value, by):
    return pl.multiple_of(value, by)


def block_of(bucket, t):
    g = t // bucket.blocks
    b = t % bucket.blocks
    rows = pl.ds(aligned(bucket.node0 + g * bucket.slots, 16), bucket.slots)
    keys = pl.ds(aligned(bucket.node0 + t * 16, 16), 16)
    pair_rows = [
        pl.ds(
            aligned(bucket.edge0 // 2 + (2 * b + c) * bucket.rows + g * bucket.slots, 16),
            bucket.slots,
        )
        for c in range(2)
    ]
    return rows, keys, pair_rows


def side(first, half):
    return slice(first + 256 * half, first + 256 * (half + 1))


def lanes(half):
    return slice(128 * half, 128 * (half + 1))


def expand(values, scr):
    spread = values.astype(F32)[:, None, :] * scr.head[...][None]
    return spread.reshape(256, 256).astype(BF)


def collect(values, scr):
    return jnp.sum(values.reshape(16, 16, 256) * scr.head[...][None], axis=1)


def joined(ref, pair_rows, half):
    return jnp.concatenate([ref[r, lanes(half)] for r in pair_rows], axis=1)


def forward(dm, counts, w, io, res, scr, ready):
    x = io.nodes[...].astype(F32)
    n, r = node_norm(x)
    res.node_n1[...] = n.astype(BF)
    res.node_r1[...] = jnp.broadcast_to(r, (dm.nodes, 128))
    hn = (n * w.nn[0:1, :] + w.nn[1:2, :]).astype(BF)
    res.qkv[...] = nn(hn, w.qkv[...]).astype(BF)
    ready("node_n1", "node_r1", "qkv")

    @dm.each_pair
    def _(rows, pair):
        x = io.edges[rows, :]
        centred = x.astype(F32) - nn(x, scr.mean[...])
        r = lax.rsqrt(nn((centred * centred).astype(BF), scr.mean[...]) + NORM_EPS)
        n = centred * r
        res.edge_n1[rows, :] = n.astype(BF)
        res.edge_r1[rows, :] = r.astype(BF)
        xn = (n * w.en[0:1, :] + w.en[1:2, :]).astype(BF)
        both = nn(beside(xn), w.eg[...])
        scr.scores[pair, :] = both[:, :256]
        res.gate[pair, :] = both[:, 256:]

    ready("edge_n1", "edge_r1", "gate")
    t0 = 0
    for bucket in dm.buckets:
        @pl.loop(0, bucket.graphs * bucket.blocks, unroll=True)
        def _(t, bucket=bucket, t0=t0):
            rows, keys, pair_rows = block_of(bucket, t)
            for half in range(2):
                kb = expand(res.qkv[keys, side(512, half)], scr)
                scr.vbig[t0 + t, half] = expand(res.qkv[keys, side(1024, half)], scr)
                s = nt(res.qkv[rows, side(0, half)], kb) * 0.25
                for c in range(2):
                    scr.scores[pair_rows[c], lanes(half)] += s[:, lanes(c)]

        @pl.loop(0, bucket.rows // 32, unroll=True)
        def _(i, bucket=bucket):
            count = counts[bucket.count0 + i * 32 // bucket.slots]
            lane_key = iota((32, 128), 1) >> 4
            row = [
                pl.ds(aligned(bucket.edge0 // 2 + c * bucket.rows + i * 32, 32), 32)
                for c in range(bucket.pairs)
            ]
            for half in range(2):
                at = lanes(half)
                top = jnp.full((32, 128), MASK_FILL, F32)
                for c in range(bucket.pairs):
                    s = scr.scores[row[c], at]
                    res.low[row[c], at] = s.astype(BF)
                    top = jnp.maximum(top, jnp.where(lane_key < count - 8 * c, s, MASK_FILL))
                top = group_max(top)
                sums = jnp.zeros((32, 128), F32)
                for c in range(bucket.pairs):
                    s = jnp.where(lane_key < count - 8 * c, scr.scores[row[c], at], MASK_FILL)
                    e = jnp.exp(s - top)
                    sums = sums + e
                    scr.scores[row[c], at] = e
                inv = 1.0 / group_sum(sums)
                for c in range(bucket.pairs):
                    p = scr.scores[row[c], at] * inv
                    res.prob[row[c], at] = p.astype(BF)
                    scr.attn[row[c], at] = (p * sigmoid(res.gate[row[c], at])).astype(BF)

        @pl.loop(0, bucket.graphs, unroll=True)
        def _(g, bucket=bucket, t0=t0):
            for half in range(2):
                sums = None
                for b in range(bucket.blocks):
                    t = g * bucket.blocks + b
                    rows, _, pair_rows = block_of(bucket, t)
                    part = nn(joined(scr.attn, pair_rows, half), scr.vbig[t0 + t, half])
                    sums = part if sums is None else sums + part
                res.mixed[rows, side(0, half)] = sums.astype(BF)

        t0 += bucket.graphs * bucket.blocks

    ready("low", "prob", "mixed")
    y = io.nodes[...].astype(F32) + nn(res.mixed[...], w.o[...])
    n, r = node_norm(y)
    res.node_n2[...] = n.astype(BF)
    res.node_r2[...] = jnp.broadcast_to(r, (dm.nodes, 128))
    z = (n * w.nn[2:3, :] + w.nn[3:4, :]).astype(BF)
    u = nn(z, w.up[...])
    res.node_u[...] = u
    ready("node_n2", "node_r2", "node_u")
    io.nodes_out[...] = (y + nn(gelu_value(u).astype(BF), w.down[...])).astype(BF)

    @dm.each_pair
    def _(rows, pair):
        m = io.edges[rows, :].astype(F32) + below(nn(res.low[pair, :], w.x[...]))
        high = m.astype(BF)
        rest = (m - high.astype(F32)).astype(BF)
        centred = m - nn(high, scr.mean[...]) - nn(rest, scr.mean[...])
        r = lax.rsqrt(nn((centred * centred).astype(BF), scr.mean[...]) + NORM_EPS)
        n = centred * r
        res.edge_n2[rows, :] = n.astype(BF)
        res.edge_r2[rows, :] = r.astype(BF)
        mn = (n * w.en[2:3, :] + w.en[3:4, :]).astype(BF)
        ua = nn(mn, w.a[...])
        io.edges_out[rows, :] = (m + nn(gelu_value(ua).astype(BF), w.b[...])).astype(BF)

    ready("edge_n2", "edge_r2")


def put_strided(flat, first, value, parts):
    for q in range(parts):
        flat[pl.ds(first + q, value.shape[0], stride=parts), :] = value[:, 128 * q : 128 * (q + 1)]


def back_ffn(dm, w, io, res, scr):
    flat = scr.upper
    gy = io.nodes_cot[...]
    act, slope = gelu_parts(res.node_u[...])
    du = (nt(gy, w.down[...]) * slope).astype(BF)
    put_strided(flat, ROW_DOWN - ROW_O, tn(act.astype(BF), gy), 4)
    n = res.node_n2[...].astype(F32)
    z = (n * w.nn[2:3, :] + w.nn[3:4, :]).astype(BF)
    put_strided(flat, ROW_UP - ROW_O, tn(z, du), 8)
    dz = nt(du, w.up[...])
    gain = jnp.sum(dz * n, axis=0, keepdims=True)
    bias = jnp.sum(dz, axis=0, keepdims=True)
    dy = gy.astype(F32) + node_norm_back(dz * w.nn[2:3, :], n, res.node_r2[:, 0:1])
    io.dy[...] = dy
    dyl = dy.astype(BF)
    put_strided(flat, 0, tn(res.mixed[...], dyl), 4)
    io.do[...] = nt(dyl, w.o[...]).astype(BF)
    for q in range(4):
        io.sums[q : q + 1, :] = gain[:, 128 * q : 128 * (q + 1)]
        io.sums[4 + q : 5 + q, :] = bias[:, 128 * q : 128 * (q + 1)]
    if hasattr(io, "upper"):
        io.upper[...] = flat[...].astype(BF)
    else:
        put_halves(flat, io.keep, io.send)


def put_halves(flat, keep, send):
    half = keep.shape[0]
    core = lax.axis_index("dp") & 1
    keep[...] = flat[pl.ds(aligned(core * half, 16), half), :].astype(BF)
    send[...] = flat[pl.ds(aligned((1 - core) * half, 16), half), :].astype(BF)


def stacked(v, width):
    return jnp.concatenate([v[:, i : i + width] for i in range(0, v.shape[1], width)])


def back_edges(dm, w, io, res, scr):
    io.small[NN + 8 : NN + 16, :] = io.sums[...]
    scr.gb[...] = jnp.zeros((256, 128), F32)
    scr.ga[...] = jnp.zeros((128, 256), F32)
    scr.gx[...] = jnp.zeros((256, 512), F32)
    scr.en[...] = jnp.zeros((2, 8, 256), F32)

    @dm.each_pair
    def _(rows, pair):
        gx = io.edges_cot[rows, :]
        n = res.edge_n2[rows, :].astype(F32)
        mn = (n * w.en[2:3, :] + w.en[3:4, :]).astype(BF)
        act, slope = gelu_parts(nn(mn, w.a[...]))
        dua = (nt(gx, w.b[...]) * slope).astype(BF)
        act = act.astype(BF)
        scr.gb[...] += tn(stacked(act, 256), stacked(gx, 128))
        scr.ga[...] += tn(stacked(mn, 128), stacked(dua, 256))
        dmn = nt(dua, w.a[...])
        scr.en[0] += fold8(dmn * n)
        scr.en[1] += fold8(dmn)
        gdy = dmn * w.en[2:3, :]
        m1 = nn(gdy.astype(BF), scr.mean[...])
        m2 = nn((gdy * n).astype(BF), scr.mean[...])
        dmid = gx.astype(F32) + res.edge_r2[rows, :].astype(F32) * (gdy - m1 - n * m2)
        dml = dmid.astype(BF)
        io.dmid[rows, :] = dml
        dml = beside(dml)
        scr.gx[...] += tn(res.low[pair, :], dml)
        io.scores[pair, :] = nt(dml, w.x[...])

    io.small[EUP : EUP + 64, :] = scr.ga[0:64, 0:128] + scr.ga[64:128, 128:256]
    sums = jnp.where(lane_group(128, 6) == 0, scr.gb[0:128, :], scr.gb[128:256, :])
    fold_halves(sums, scr.tmp, io.small, EDOWN)
    sides = []
    for half in range(2):
        sums = jnp.zeros((16, 128), F32)
        for k in range(8):
            at = 128 * half + 16 * k
            part = scr.gx[at : at + 16, 128 * (k // 2) : 128 * (k // 2 + 1)]
            sums = sums + jnp.where(lane_group(16, 6) == k % 2, part, 0.0)
        sides.append(sums)
    fold_halves(jnp.concatenate(sides), scr.tmp, io.small, EDGE)
    put_edge_norm(scr.en, io.small, EN + 1)
    io.small[SMALL_USED:, :] = jnp.zeros((SMALL_ROWS - SMALL_USED, 128), F32)


def back_attention(dm, io, res, scr):
    t0 = 0
    for bucket in dm.buckets:
        @pl.loop(0, bucket.graphs * bucket.blocks, unroll=True)
        def _(t, bucket=bucket, t0=t0):
            rows, keys, pair_rows = block_of(bucket, t)
            for half in range(2):
                scr.vbig[t0 + t, half] = expand(res.qkv[keys, side(512, half)], scr)
                vb = expand(res.qkv[keys, side(1024, half)], scr)
                da = nt(io.do[rows, side(0, half)], vb)
                for c in range(2):
                    scr.da[pair_rows[c], lanes(half)] = da[:, lanes(c)]

        @pl.loop(0, bucket.rows // 32, unroll=True)
        def _(i, bucket=bucket):
            row = [
                pl.ds(aligned(bucket.edge0 // 2 + c * bucket.rows + i * 32, 32), 32)
                for c in range(bucket.pairs)
            ]
            for half in range(2):
                at = lanes(half)
                sums = jnp.zeros((32, 128), F32)
                for c in range(bucket.pairs):
                    p = res.prob[row[c], at].astype(F32)
                    s = sigmoid(res.gate[row[c], at])
                    scr.attn[row[c], at] = (p * s).astype(BF)
                    pt = p * scr.da[row[c], at] * s
                    scr.da[row[c], at] = pt
                    sums = sums + pt
                    io.dsg[row[c], lanes(2 + half)] = (pt * (1.0 - s)).astype(BF)
                sums = group_sum(sums)
                for c in range(bucket.pairs):
                    p = res.prob[row[c], at].astype(F32)
                    ds = scr.da[row[c], at] - p * sums + io.scores[row[c], at]
                    io.dsg[row[c], at] = ds.astype(BF)

        @pl.loop(0, bucket.graphs, unroll=True)
        def _(g, bucket=bucket, t0=t0):
            for half in range(2):
                sums = None
                for b in range(bucket.blocks):
                    t = g * bucket.blocks + b
                    rows, keys, pair_rows = block_of(bucket, t)
                    ds = joined(io.dsg, pair_rows, half)
                    part = nn(ds, scr.vbig[t0 + t, half])
                    sums = part if sums is None else sums + part
                    gk = collect(tn(ds, res.qkv[rows, side(0, half)]), scr)
                    io.dqkv[keys, side(512, half)] = (gk * 0.25).astype(BF)
                    gv = tn(joined(scr.attn, pair_rows, half), io.do[rows, side(0, half)])
                    io.dqkv[keys, side(1024, half)] = collect(gv, scr).astype(BF)
                io.dqkv[rows, side(0, half)] = (sums * 0.25).astype(BF)

        t0 += bucket.graphs * bucket.blocks


def back_nodes(dm, w, io, res, scr):
    n = res.node_n1[...].astype(F32)
    dhn = nt(io.dqkv[...], w.qkv[...])
    gain = jnp.sum(dhn * n, axis=0, keepdims=True)
    bias = jnp.sum(dhn, axis=0, keepdims=True)
    for q in range(4):
        io.sums_one[q : q + 1, :] = gain[:, 128 * q : 128 * (q + 1)]
        io.sums_one[4 + q : 5 + q, :] = bias[:, 128 * q : 128 * (q + 1)]
    dx = io.dy[...] + node_norm_back(dhn * w.nn[0:1, :], n, res.node_r1[:, 0:1])
    io.nodes_grad[...] = dx.astype(BF)


def back_last(dm, w, io, res, scr):
    flat = scr.lower
    n = res.node_n1[...].astype(F32)
    hn = (n * w.nn[0:1, :] + w.nn[1:2, :]).astype(BF)
    for m in range(3):
        put_strided(flat, 2048 * m, tn(hn, io.dqkv[:, 512 * m : 512 * (m + 1)]), 4)
    small = flat.at[pl.ds(ROW_O, SMALL_ROWS), :]
    small[...] = io.small[...]
    small[NN : NN + 8, :] = io.sums_one[...]

    scr.geg[...] = jnp.zeros((512, 512), F32)
    scr.en[...] = jnp.zeros((2, 8, 256), F32)

    @dm.each_pair
    def _(rows, pair):
        dsg = io.dsg[pair, :]
        n = res.edge_n1[rows, :].astype(F32)
        xn = (n * w.en[0:1, :] + w.en[1:2, :]).astype(BF)
        scr.geg[...] += tn(beside(xn), dsg)
        dxn = below(nt(dsg, w.eg[...]))
        scr.en[0] += fold8(dxn * n)
        scr.en[1] += fold8(dxn)
        gdy = dxn * w.en[0:1, :]
        m1 = nn(gdy.astype(BF), scr.mean[...])
        m2 = nn((gdy * n).astype(BF), scr.mean[...])
        dx = io.dmid[rows, :].astype(F32) + res.edge_r1[rows, :].astype(F32) * (gdy - m1 - n * m2)
        io.edges_grad[rows, :] = dx.astype(BF)

    for which, first in ((0, BIAS), (1, GATE)):
        sides = []
        for half in range(2):
            sums = jnp.zeros((64, 128), F32)
            for k in range(8):
                part = scr.geg[64 * k : 64 * (k + 1), lanes(2 * which + half)]
                sums = sums + jnp.where(lane_group(64, 4) == k, part, 0.0)
            sides.append(group_sum(sums))
        scr.tmp[0:64, :] = jnp.where(lane_group(64, 4) % 2 == 0, sides[0], sides[1])
        rows = jnp.zeros((16, 128), F32)
        for b in range(4):
            rows = jnp.where(lane_group(16, 5) == b, scr.tmp[pl.ds(b, 16, stride=4), :], rows)
        small[first : first + 16, :] = rows
    put_edge_norm(scr.en, small, EN)
    end = ROW_O + SMALL_ROWS
    if dm.lower > end:
        flat[end:, :] = jnp.zeros((dm.lower - end, 128), F32)
    put_halves(flat, io.keep, io.send)


def lane_group(rows, bits):
    return iota((rows, 128), 1) >> bits


def fold_halves(sums, tmp, out, first):
    rows, half = sums.shape[0], sums.shape[0] // 2
    tmp[0:rows, :] = sums + pltpu.roll(sums, 64, 1)
    even = tmp[pl.ds(0, half, stride=2), :]
    odd = tmp[pl.ds(1, half, stride=2), :]
    out[first : first + half, :] = jnp.where(lane_group(half, 6) == 0, even, odd)


def put_edge_norm(sums, out, at):
    ones = []
    for t in range(2):
        both = jnp.sum(sums[t], axis=0, keepdims=True)
        one = both[:, :128] + both[:, 128:]
        ones.append(one + pltpu.roll(one, 64, 1))
    out[at : at + 1, :] = jnp.where(lane_group(1, 6) == 0, ones[0], ones[1])


def assemble_set(off, flat, tmp, w):
    def strided(first, rows, parts, out, lane0=0):
        for q in range(parts):
            out[:, lane0 + 128 * q : lane0 + 128 * (q + 1)] = flat[
                pl.ds(off + first + q, rows, stride=parts), :
            ].astype(BF)

    for m in range(3):
        strided(ROW_QKV + 2048 * m, 512, 4, w.qkv, 512 * m)
    strided(ROW_O, 512, 4, w.o)
    strided(ROW_UP, 512, 8, w.up)
    strided(ROW_DOWN, 1024, 4, w.down)
    w.eg[...] = jnp.zeros((512, 512), BF)
    w.x[...] = jnp.zeros((256, 512), BF)
    w.a[...] = jnp.zeros((256, 512), BF)
    w.b[...] = jnp.zeros((512, 256), BF)
    up = flat[pl.ds(off + ROW_EUP, 64), :].astype(BF)
    for k in range(4):
        w.a[64 * k : 64 * (k + 1), 128 * k : 128 * (k + 1)] = up

    def doubled(first, in_rows):
        v = flat[pl.ds(off + first, in_rows), :]
        other = pltpu.roll(v, 64, 1)
        low = lane_group(in_rows, 6) == 0
        tmp[pl.ds(0, in_rows, stride=2), :] = jnp.where(low, v, other)
        tmp[pl.ds(1, in_rows, stride=2), :] = jnp.where(low, other, v)
        return tmp[0 : 2 * in_rows, :]

    both = doubled(ROW_EDOWN, 64)
    for k in range(4):
        w.b[128 * k : 128 * (k + 1), 128 * (k // 2) : 128 * (k // 2 + 1)] = jnp.where(
            lane_group(128, 6) == k % 2, both, 0.0
        ).astype(BF)
    both = doubled(ROW_EDGE, 16)
    for half in range(2):
        for k in range(8):
            at = 128 * half + 16 * k
            w.x[at : at + 16, 128 * (k // 2) : 128 * (k // 2 + 1)] = jnp.where(
                lane_group(16, 6) == k % 2, both[16 * half : 16 * (half + 1)], 0.0
            ).astype(BF)
    for which, first in ((0, ROW_BIAS), (1, ROW_GATE)):
        v = flat[pl.ds(off + first, 16), :]
        for b in range(4):
            tmp[pl.ds(b, 16, stride=4), :] = group_sum(jnp.where(lane_group(16, 5) == b, v, 0.0), 32)
        both = tmp[0:64, :]
        even = lane_group(64, 4) % 2 == 0
        sides = (
            jnp.where(even, both, pltpu.roll(both, 16, 1)),
            jnp.where(even, pltpu.roll(both, 112, 1), both),
        )
        for half in range(2):
            for k in range(8):
                w.eg[64 * k : 64 * (k + 1), lanes(2 * which + half)] = jnp.where(
                    lane_group(64, 4) == k, sides[half], 0.0
                ).astype(BF)
    for t in range(4):
        for q in range(4):
            w.nn[t : t + 1, 128 * q : 128 * (q + 1)] = flat[pl.ds(off + ROW_NN + 4 * t + q, 1), :]
    for t in range(2):
        v = flat[pl.ds(off + ROW_EN + t, 1), :]
        other = pltpu.roll(v, 64, 1)
        gain = jnp.where(lane_group(1, 6) == 0, v, other)
        bias = jnp.where(lane_group(1, 6) == 0, other, v)
        for half in range(2):
            w.en[2 * t : 2 * t + 1, 128 * half : 128 * (half + 1)] = gain
            w.en[2 * t + 1 : 2 * t + 2, 128 * half : 128 * (half + 1)] = bias


class Group:
    def __init__(self, names, refs):
        for name, ref in zip(names, refs):
            setattr(self, name, ref)


WEIGHTS = {
    "qkv": ((D, 3 * D), BF),
    "o": ((D, D), BF),
    "up": ((D, FF), BF),
    "down": ((FF, D), BF),
    "eg": ((512, 512), BF),
    "x": ((256, 512), BF),
    "a": ((256, 512), BF),
    "b": ((512, 256), BF),
    "nn": ((4, D), F32),
    "en": ((4, 256), F32),
}


def residual_shapes(dm):
    return {
        "node_n1": ((dm.nodes, D), BF),
        "node_r1": ((dm.nodes, 128), F32),
        "qkv": ((dm.nodes, 3 * D), BF),
        "mixed": ((dm.nodes, D), BF),
        "node_n2": ((dm.nodes, D), BF),
        "node_r2": ((dm.nodes, 128), F32),
        "node_u": ((dm.nodes, FF), F32),
        "edge_n1": ((dm.edges, 256), BF),
        "edge_r1": ((dm.edges, 256), BF),
        "gate": ((dm.scores, 256), F32),
        "low": ((dm.scores, 256), BF),
        "prob": ((dm.scores, 256), BF),
        "edge_n2": ((dm.edges, 256), BF),
        "edge_r2": ((dm.edges, 256), BF),
    }


def mean_shapes():
    return {"mean": ((256, 256), BF)}


def head_shapes():
    return {"head": ((16, 256), F32)}


def mask_shapes():
    return {**mean_shapes(), **head_shapes()}


def forward_scratch(dm):
    return {
        "scores": ((dm.scores, 256), F32),
        "attn": ((dm.scores, 256), BF),
        "vbig": ((dm.blocks, 2, 256, 256), BF),
    }


def ffn_shapes(dm, halves):
    half = ((UPPER_ROWS // 2, 128), BF)
    grads = {"keep": half, "send": half} if halves else {"upper": ((UPPER_ROWS, 128), BF)}
    return {
        "dy": ((dm.nodes, D), F32),
        "do": ((dm.nodes, D), BF),
        "sums": ((8, 128), F32),
        **grads,
    }


def edge_shapes(dm):
    return {
        "dmid": ((dm.edges, 256), BF),
        "scores": ((dm.scores, 256), F32),
        "small": ((SMALL_ROWS, 128), F32),
    }


def attention_shapes(dm):
    return {"dsg": ((dm.scores, 512), BF), "dqkv": ((dm.nodes, 3 * D), BF)}


def ffn_scratch():
    return {"upper": ((UPPER_ROWS, 128), F32)}


def edge_scratch():
    return {
        "gb": ((256, 128), F32),
        "ga": ((128, 256), F32),
        "gx": ((256, 512), F32),
        "en": ((2, 8, 256), F32),
        "tmp": ((128, 128), F32),
    }


def attention_scratch(dm):
    return {
        "attn": ((dm.scores, 256), BF),
        "vbig": ((dm.blocks, 2, 256, 256), BF),
        "da": ((dm.scores, 256), F32),
    }


def last_scratch(dm):
    return {
        "geg": ((512, 512), F32),
        "en": ((2, 8, 256), F32),
        "tmp": ((128, 128), F32),
        "lower": ((dm.lower, 128), F32),
    }


def structs(shapes):
    return [jax.ShapeDtypeStruct(s, t) for s, t in shapes.values()]


def vmem(shapes):
    return [pltpu.VMEM(s, t) for s, t in shapes.values()]


def whole(n):
    return [pl.BlockSpec(memory_space=pltpu.VMEM)] * n


def split(refs, *groups):
    out, at = [], 0
    for names in groups:
        out.append(Group(names, refs[at : at + len(names)]))
        at += len(names)
    assert at == len(refs)
    return out


def edge_copies(dm, small, big, big_lane, stacked, sems, out):
    copies = []
    for bucket, ref, lane in ((dm.small, small, 0), (dm.big, big, big_lane)):
        for c in range(bucket.chunks):
            a = ref.at[:, pl.ds(lane + 256 * c, 256)]
            b = stacked.at[pl.ds(bucket.edge0 + c * bucket.rows, bucket.rows), :]
            src, dst = (b, a) if out else (a, b)
            copies.append(pltpu.make_async_copy(src, dst, sems.at[len(copies)]))
    return copies


def node_copies(dm, small, big, big_lane, nodes, sems, at, out):
    copies = []
    for bucket, ref in ((dm.small, small), (dm.big, big.at[:, pl.ds(big_lane, D)])):
        b = nodes.at[pl.ds(bucket.node0, bucket.rows), :]
        src, dst = (b, ref) if out else (ref, b)
        copies.append(pltpu.make_async_copy(src, dst, sems.at[at + len(copies)]))
    return copies


def copy_sems(dm):
    return pltpu.SemaphoreType.DMA((dm.small.chunks + dm.big.chunks + 2,))


def all_copies(dm, small_nodes, small_edges, big, edge_lane, node_lane, nodes, edges, sems, out):
    copies = edge_copies(dm, small_edges, big, edge_lane, edges, sems, out)
    return node_copies(dm, small_nodes, big, node_lane, nodes, sems, len(copies), out) + copies


def start(copies):
    for c in copies:
        c.start()


def wait(copies):
    for c in copies:
        c.wait()


HBM = pl.BlockSpec(memory_space=pl.ANY)
SMEM = pl.BlockSpec(memory_space=pltpu.SMEM)
EDGE_LANES = NB * DE
IN_LANES = 2 * EDGE_LANES + 2 * D
OUT_LANES = EDGE_LANES + D


def compiler_params():
    return pltpu.CompilerParams(vmem_limit_bytes=VMEM_LIMIT)


def cost(us):
    return pl.CostEstimate(flops=0, bytes_accessed=int(us * 3.4e6), transcendentals=0)


def take(group, names):
    return [getattr(group, k) for k in names]


NODE_BACK = ("node_n2", "node_r2", "node_u", "mixed")
EDGE_BACK = ("edge_n2", "edge_r2", "low")
ATTENTION_BACK = ("qkv", "prob", "gate")
LAST_BACK = ("node_n1", "node_r1", "edge_n1", "edge_r1")
W_NODE = ("o", "up", "down", "nn")
W_EDGE = ("x", "a", "b", "en")
W_LAST = ("qkv", "eg", "nn", "en")


def kernel(body, inputs, out, scr, us, counts=None, hbm_in=0, hbm_out=(), sems=()):
    smem = [] if counts is None else [counts]
    return Group(
        out,
        pl.pallas_call(
            body,
            out_shape=structs(out),
            in_specs=[SMEM] * len(smem) + whole(len(inputs) - hbm_in) + [HBM] * hbm_in,
            out_specs=[HBM if k in hbm_out else pl.BlockSpec(memory_space=pltpu.VMEM) for k in out],
            scratch_shapes=vmem(scr) + list(sems),
            compiler_params=compiler_params(),
            cost_estimate=cost(us),
        )(*smem, *inputs),
    )


class Leaving:
    def __init__(self, names, held, outs, sems):
        self.names, self.held, self.outs, self.sems = tuple(names), held, outs, sems
        self.copies = []

    def __call__(self, *names):
        for k in names:
            if k in self.names:
                sem = self.sems.at[len(self.copies)]
                self.copies.append(
                    pltpu.make_async_copy(getattr(self.held, k), getattr(self.outs, k), sem)
                )
                self.copies[-1].start()

    def wait(self):
        assert len(self.copies) == len(self.names)
        wait(self.copies)


def first_forward(dm, counts, weights, small_nodes, small_edges, big):
    res = residual_shapes(dm)
    out = {"nodes_out": ((dm.nodes, D), BF), "edges_out": ((dm.edges, 256), BF), **res}
    scr = {
        **mask_shapes(),
        **forward_scratch(dm),
        "nodes": ((dm.nodes, D), BF),
        "edges": ((dm.edges, 256), BF),
        **res,
    }

    def body(*refs):
        counts_ref, refs, sems, out_sems = refs[0], refs[1:-2], refs[-2], refs[-1]
        w, src, dst, s = split(refs, WEIGHTS, ("sn", "se", "big"), out, scr)
        copies = all_copies(
            dm, src.sn, src.se, src.big, 0, 2 * EDGE_LANES, s.nodes, s.edges, sems, False
        )
        start(copies)
        make_masks(s)
        io = Group(
            ("nodes", "edges", "nodes_out", "edges_out"),
            (s.nodes, s.edges, dst.nodes_out, dst.edges_out),
        )
        leaving = Leaving(res, s, dst, out_sems)
        wait(copies)
        forward(dm, counts_ref, w, io, s, s, leaving)
        leaving.wait()

    inputs = take(weights, WEIGHTS) + [small_nodes, small_edges, big]
    sems = [copy_sems(dm), pltpu.SemaphoreType.DMA((len(res),))]
    got = kernel(body, inputs, out, scr, 16, counts, 3, tuple(res), sems)
    return got.nodes_out, got.edges_out, got


def second_forward(dm, counts, weights, nodes, edges, small_node_cot, small_edge_cot, big):
    res, ffn = residual_shapes(dm), ffn_shapes(dm, False)
    whole_outs = {
        "sno": ((dm.small.rows, D), BF),
        "seo": ((dm.small.rows, dm.small.edge_lanes), BF),
        "bout": ((dm.big.rows, OUT_LANES), BF),
    }
    kept = {k: v for k, v in res.items() if k not in NODE_BACK}
    out = {**whole_outs, "edge_cot": ((dm.edges, 256), BF), **kept, **ffn}
    scr = {
        **mask_shapes(),
        **forward_scratch(dm),
        **ffn_scratch(),
        **res,
        "nodes_out": ((dm.nodes, D), BF),
        "edges_out": ((dm.edges, 256), BF),
        "node_cot": ((dm.nodes, D), BF),
    }

    def body(*refs):
        counts_ref, refs, in_sems, out_sems, res_sems = refs[0], refs[1:-3], *refs[-3:]
        w, src, dst, s = split(refs, WEIGHTS, ("nodes", "edges", "snc", "sec", "big"), out, scr)
        copies = all_copies(
            dm, src.snc, src.sec, src.big, EDGE_LANES, 2 * EDGE_LANES + D, s.node_cot, dst.edge_cot, in_sems, False
        )
        start(copies)
        make_masks(s)
        leaving = Leaving(kept, s, dst, res_sems)
        io = Group(
            ("nodes", "edges", "nodes_out", "edges_out"),
            (src.nodes, src.edges, s.nodes_out, s.edges_out),
        )
        forward(dm, counts_ref, w, io, s, s, leaving)
        outgoing = all_copies(
            dm, dst.sno, dst.seo, dst.bout, D, 0, s.nodes_out, s.edges_out, out_sems, True
        )
        start(outgoing)
        wait(copies)
        back_ffn(dm, w, Group(("nodes_cot", *ffn), (s.node_cot, *take(dst, ffn))), s, s)
        wait(outgoing)
        leaving.wait()

    inputs = take(weights, WEIGHTS) + [nodes, edges, small_node_cot, small_edge_cot, big]
    sems = [copy_sems(dm), copy_sems(dm), pltpu.SemaphoreType.DMA((len(kept),))]
    got = kernel(body, inputs, out, scr, 22, counts, 3, (*whole_outs, *kept), sems)
    return got.sno, got.seo, got.bout, None, got.edge_cot, got, got


def between(dm, weights_two, weights_one, kept_two, kept_one, ffn_two, edges_cot):
    ffn, edge, att = ffn_shapes(dm, True), edge_shapes(dm), attention_shapes(dm)
    handed = {"dmid": edge["dmid"], "small": edge["small"], **att, "sums_one": ((8, 128), F32)}
    out = {**{"two_" + k: v for k, v in handed.items()}, **ffn}
    scr = {
        **mask_shapes(),
        **edge_scratch(),
        **attention_scratch(dm),
        **ffn_scratch(),
        "scores": edge["scores"],
        "nodes_grad": ((dm.nodes, D), BF),
    }
    w_two = ("qkv", *W_EDGE, "nn")
    res_two = EDGE_BACK + ATTENTION_BACK + ("node_n1", "node_r1")

    def body(*refs):
        w, w_one, res, res_one, src, dst, s = split(
            refs, w_two, W_NODE, res_two, NODE_BACK, ("edges_cot", "sums", "do", "dy"), out, scr
        )
        make_masks(s)
        io = Group(
            ("edges_cot", "sums", "do", "dy", "scores", "nodes_grad", *handed),
            (src.edges_cot, src.sums, src.do, src.dy, s.scores, s.nodes_grad)
            + tuple(getattr(dst, "two_" + k) for k in handed),
        )
        back_edges(dm, w, io, res, s)
        back_attention(dm, io, res, s)
        back_nodes(dm, w, io, res, s)
        back_ffn(dm, w_one, Group(("nodes_cot", *ffn), (s.nodes_grad, *take(dst, ffn))), res_one, s)

    inputs = take(weights_two, w_two) + take(weights_one, W_NODE)
    inputs += take(kept_two, res_two) + take(kept_one, NODE_BACK)
    inputs += [edges_cot, ffn_two.sums, ffn_two.do, ffn_two.dy]
    return kernel(body, inputs, out, scr, 25)


def second_last(dm, weights, kept, got):
    half = {k: ((dm.lower // 2, 128), BF) for k in ("keep", "send")}
    out = {"edges_grad": ((dm.edges, 256), BF), **half}
    scr = {**mean_shapes(), **last_scratch(dm)}
    given = ("dmid", "small", "dsg", "dqkv", "sums_one")
    w_last = ("eg", "nn", "en")
    last_res = ("node_n1", "edge_n1", "edge_r1")

    def body(*refs):
        w, res, src, dst, s = split(refs, w_last, last_res, given, out, scr)
        make_mean(s)
        back_last(dm, w, Group((*given, *out), (*take(src, given), *take(dst, out))), res, s)

    inputs = take(weights, w_last) + take(kept, last_res)
    inputs += [getattr(got, "two_" + k) for k in given]
    return kernel(body, inputs, out, scr, 9)


def call_edges(dm, weights, kept, ffn, edges_cot):
    out, scr = edge_shapes(dm), {**mean_shapes(), **edge_scratch()}

    def body(*refs):
        w, res, src, dst, s = split(refs, W_EDGE, EDGE_BACK, ("edges_cot", "sums"), out, scr)
        make_mean(s)
        io = Group(("edges_cot", "sums", *out), (src.edges_cot, src.sums, *take(dst, out)))
        back_edges(dm, w, io, res, s)

    inputs = take(weights, W_EDGE) + take(kept, EDGE_BACK) + [edges_cot, ffn.sums]
    return kernel(body, inputs, out, scr, 16)


def call_attention(dm, kept, ffn, edge):
    out, scr = attention_shapes(dm), {**head_shapes(), **attention_scratch(dm)}

    def body(*refs):
        res, src, dst, s = split(refs, ATTENTION_BACK, ("do", "scores"), out, scr)
        make_heads(s)
        back_attention(dm, Group(("do", "scores", *out), (src.do, src.scores, *take(dst, out))), res, s)

    return kernel(body, take(kept, ATTENTION_BACK) + [ffn.do, edge.scores], out, scr, 14)


def call_last(dm, weights, kept, ffn, edge, att):
    half = {k: ((dm.lower // 2, 128), BF) for k in ("keep", "send")}
    outs = {
        "sng": ((dm.small.rows, D), BF),
        "seg": ((dm.small.rows, dm.small.edge_lanes), BF),
        "bgrad": ((dm.big.rows, OUT_LANES), BF),
    }
    out = {**outs, **half}
    scr = {
        **mean_shapes(),
        **last_scratch(dm),
        "nodes_grad": ((dm.nodes, D), BF),
        "edges_grad": ((dm.edges, 256), BF),
        "sums_one": ((8, 128), F32),
    }
    given = ("dy", "dmid", "small", "dsg", "dqkv")

    def body(*refs):
        refs, sems = refs[:-1], refs[-1]
        w, res, src, dst, s = split(refs, W_LAST, LAST_BACK, given, out, scr)
        make_mean(s)
        io = Group(
            (*given, "nodes_grad", "edges_grad", "keep", "send", "sums_one"),
            (*take(src, given), s.nodes_grad, s.edges_grad, dst.keep, dst.send, s.sums_one),
        )
        back_nodes(dm, w, io, res, s)
        back_last(dm, w, io, res, s)
        outgoing = all_copies(
            dm, dst.sng, dst.seg, dst.bgrad, D, 0, s.nodes_grad, s.edges_grad, sems, True
        )
        start(outgoing)
        wait(outgoing)

    inputs = take(weights, W_LAST) + take(kept, LAST_BACK)
    inputs += [ffn.dy, edge.dmid, edge.small, att.dsg, att.dqkv]
    got = kernel(body, inputs, out, scr, 13, hbm_out=tuple(outs), sems=[copy_sems(dm)])
    return take(got, out)


def round_up(value, by):
    return -(-value // by) * by


def segment_of(owner, rows, index, count):
    name = owner[index]
    first = jnp.int32(0)
    for t in range(count):
        first = first + jnp.where(t < name, rows[t], 0)
    return first, rows[name]


def shifted_segment(owner, segment_rows, master):
    held = master.shape[0]
    count = owner.shape[0]
    padded = round_up(held + 15, 16)
    step = round_up(-(-padded // 2), 16)

    def body(owner_ref, rows_ref, src, dst, window):
        i = pl.program_id(0)
        first, length = segment_of(owner_ref, rows_ref, lax.axis_index("dp"), count)
        shift = first % 16

        @pl.when(i == 0)
        def _():
            window[0:16, :] = jnp.zeros((16, 128), F32)

        window[16:, :] = src[...]
        moved = window[pl.ds(16 - shift, step), :]
        index = i * step - shift + iota((step, 128), 0)
        live = (index >= 0) & (index < length)
        dst[...] = jnp.where(live, moved, 0.0).astype(BF)
        window[0:16, :] = window[step : step + 16, :]

    return pl.pallas_call(
        body,
        grid=(pl.cdiv(padded, step),),
        out_shape=jax.ShapeDtypeStruct((padded, 128), BF),
        in_specs=[
            SMEM,
            SMEM,
            pl.BlockSpec((step, 128), lambda i: (jnp.minimum(i, (held - 1) // step), 0)),
        ],
        out_specs=pl.BlockSpec((step, 128), lambda i: (i, 0)),
        scratch_shapes=[pltpu.VMEM((step + 16, 128), F32)],
        compiler_params=compiler_params(),
    )(owner, segment_rows, master)


def assemble(cube, owner, segment_rows, parts, sources):
    count = len(parts)
    padded = parts[0].shape[0]
    bits = (padded // 16).bit_length()
    tiles = -(-TOTAL_ROWS // 16)
    set_tiles = -(-(SET_ROWS + 2) // 16)
    out = {**{"one_" + k: v for k, v in WEIGHTS.items()}, **{"two_" + k: v for k, v in WEIGHTS.items()}}

    def body(owner_ref, rows_ref, *refs):
        srcs, refs = refs[:count], refs[count:]
        dsts, (rows, flat, tmp, edge, sems, edge_sems) = refs[: len(out)], refs[len(out) :]
        me = lax.axis_index("dp")
        spans = []
        for i in range(count):
            first, length = segment_of(owner_ref, rows_ref, cube.source(me, sources[i]), count)
            spans.append((first // 16, (first + length - 1) // 16))

        def each(act):
            for i, (a, b) in enumerate(spans):
                inner = b - a - 1
                for bit in range(bits):
                    size = 16 << bit
                    if size > padded:
                        continue
                    done = (inner >> (bit + 1)) << (bit + 1)

                    @pl.when((inner > 0) & (((inner >> bit) & 1) == 1))
                    def _(i=i, a=a, done=done, size=size, bit=bit):
                        act(
                            pltpu.make_async_copy(
                                srcs[i].at[pl.ds(aligned(16 * (1 + done), 16), size), :],
                                rows.at[pl.ds(aligned(16 * (a + 1 + done), 16), size), :],
                                sems.at[i, bit],
                            )
                        )

                act(pltpu.make_async_copy(srcs[i].at[pl.ds(0, 16), :], edge.at[2 * i], edge_sems.at[2 * i]))
                act(
                    pltpu.make_async_copy(
                        srcs[i].at[pl.ds(aligned(16 * (b - a), 16), 16), :],
                        edge.at[2 * i + 1],
                        edge_sems.at[2 * i + 1],
                    )
                )

        each(lambda c: c.start())
        each(lambda c: c.wait())
        tile = lambda t: pl.ds(aligned(16 * t, 16), 16)
        for a, b in spans:
            rows[tile(a), :] = jnp.zeros((16, 128), BF)
            rows[tile(b), :] = jnp.zeros((16, 128), BF)
        for i, (a, b) in enumerate(spans):
            rows[tile(a), :] += edge[2 * i]

            @pl.when(b != a)
            def _(i=i, b=b):
                rows[tile(b), :] += edge[2 * i + 1]

        for which in range(2):
            base = which * (SET_ROWS // 16) * 16
            flat[...] = rows[pl.ds(base, 16 * set_tiles), :].astype(F32)
            w = Group(WEIGHTS, dsts[which * len(WEIGHTS) : (which + 1) * len(WEIGHTS)])
            assemble_set(which * (SET_ROWS % 16), flat, tmp, w)

    got = pl.pallas_call(
        body,
        out_shape=structs(out),
        in_specs=[SMEM] * 2 + [HBM] * count,
        out_specs=whole(len(out)),
        scratch_shapes=[
            pltpu.VMEM((16 * tiles, 128), BF),
            pltpu.VMEM((16 * set_tiles, 128), F32),
            pltpu.VMEM((128, 128), F32),
            pltpu.VMEM((2 * count, 16, 128), BF),
            pltpu.SemaphoreType.DMA((count, bits)),
            pltpu.SemaphoreType.DMA((2 * count,)),
        ],
        compiler_params=compiler_params(),
        cost_estimate=cost(10),
    )(owner, segment_rows, *parts)
    return Group(WEIGHTS, got[: len(WEIGHTS)]), Group(WEIGHTS, got[len(WEIGHTS) :])


def adam(n_row, lower, owner, segment_rows, scales, whole_upper, blocks, master, first, second):
    held = master.shape[0]
    step = 2080
    front = step + 16
    count = len(blocks)
    n_dp = owner.shape[0]
    set_rows = ROW_BIAS - ROW_O + lower
    total_rows = front + set_rows + step + 32
    ways = 3
    arrivals = sum(len(keys) for _, _, keys, _ in blocks)

    def body(owner_ref, rows_ref, scale_ref, *refs):
        upper, srcs, refs = refs[0], refs[1 : 1 + count], refs[1 + count :]
        master_ref, first_ref, second_ref, o_master, o_first, o_second, o_norms, rows, window, grad, rate, sems, upper_sem = refs
        i = pl.program_id(0)
        me, row = lax.axis_index("dp"), lax.axis_index("row")
        begin, length = segment_of(owner_ref, rows_ref, me, n_dp)

        @pl.when(i == 0)
        def _():
            def each(act):
                copy = pltpu.make_async_copy(
                    upper, rows.at[1, pl.ds(front + ROW_O, UPPER_ROWS), :], upper_sem
                )
                pl.when(begin + length > SET_ROWS + ROW_O)(functools.partial(act, copy))
                every = [
                    (k, core, key, n, sections)
                    for k, (_, core, keys, sections) in enumerate(blocks)
                    for n, key in enumerate(keys)
                ]
                for at_sem, (k, core, key, n, sections) in enumerate(every):
                    mine = (me ^ core) & 1
                    source = me ^ core ^ jnp.where(mine == 0, key[0], key[1])
                    offset = n * n_row * sum(size for _, _, size in sections)
                    place = (source & 1) * (n_dp // 2) + (source >> 1)
                    for number, (which, part, size) in enumerate(sections):
                        size = size * n_row
                        at = place * size
                        dest = at + ROW_O if part else jnp.where(at >= ROW_O, at - ROW_O + ROW_BIAS, at)
                        wanted = (dest + which * SET_ROWS < begin + length) & (
                            dest + size + which * SET_ROWS > begin
                        )
                        wanted = wanted | (dest + size > ROW_NN)

                        def move(frm, extent, to, way, k=k, which=which, at_sem=at_sem):
                            act(
                                pltpu.make_async_copy(
                                    srcs[k].at[pl.ds(frm, extent), :],
                                    rows.at[which, pl.ds(aligned(front + to, 16), extent), :],
                                    sems.at[at_sem, way],
                                )
                            )

                        cut = 0 if part else ROW_O % size
                        if cut:
                            split_here = (at < ROW_O) & (at + size > ROW_O)
                            wanted = wanted & jnp.logical_not(split_here)

                            @pl.when(split_here)
                            def _(move=move, offset=offset, size=size, at=at, cut=cut, number=number):
                                move(offset, cut, at, number)
                                move(offset + cut, size - cut, ROW_BIAS, 2)

                        pl.when(wanted)(functools.partial(move, offset, size, dest, number))
                        offset += size

            each(lambda c: c.start())
            each(lambda c: c.wait())
            for which in range(2):
                v = rows[which, front + ROW_NN : front + ROW_NN + 32, :].astype(F32)
                for t in range(4):
                    for q in range(4):
                        o_norms[4 * which + t : 4 * which + t + 1, 128 * q : 128 * (q + 1)] = v[
                            4 * t + q : 4 * t + q + 1, :
                        ]
                for t in range(2):
                    both = v[16 + t : 17 + t, :]
                    at = 4 * which + 2 * t
                    o_norms[at : at + 1, 512:576] = both[:, 0:64]
                    o_norms[at + 1 : at + 2, 512:576] = pltpu.roll(both, 64, 1)[:, 0:64]

        low = begin + i * step
        high = low + step
        some = i * step < length

        @pl.when(jnp.logical_not(some))
        def _():
            o_master[...] = master_ref[...]
            o_first[...] = first_ref[...]
            o_second[...] = second_ref[...]

        @pl.when(some)
        def _():
            def shifted(which):
                local = low - which * SET_ROWS + front
                shift = local % 16
                window[...] = rows[which, pl.ds(aligned(local - shift, 16), step + 16), :].astype(F32)
                return window[pl.ds(shift, step), :]

            index = iota((step, 128), 0)

            @pl.when(low < SET_ROWS)
            def _():
                grad[...] = shifted(0)

            @pl.when(low >= SET_ROWS)
            def _():
                grad[...] = shifted(1)

            @pl.when((low < SET_ROWS) & (high > SET_ROWS))
            def _():
                grad[...] = jnp.where(index + low >= SET_ROWS, shifted(1), grad[...])

            at = index + low
            at = jnp.where(at >= SET_ROWS, at - SET_ROWS, at)
            a, b, c = RATES[0][1], RATES[1][1], RATES[3][1]
            far = jnp.where(at < ROW_DOWN, a, c)
            rate[...] = jnp.where(at < ROW_O, a, jnp.where(at < ROW_UP, b, far))
            near = (low < SET_ROWS) & (high > ROW_BIAS)

            @pl.when(near | (high > SET_ROWS + ROW_BIAS))
            def _():
                value = jnp.full((step, 128), 0.25, F32)
                for end, one in reversed(RATES[4:]):
                    value = jnp.where(at < end, one, value)
                rate[...] = jnp.where(at < ROW_BIAS, rate[...], value)

            g = grad[...]
            p, m, v = master_ref[...], first_ref[...], second_ref[...]
            m_new = BETA_ONE * m + (1.0 - BETA_ONE) * g
            v_new = BETA_TWO * v + (1.0 - BETA_TWO) * g * g
            move = (m_new * scale_ref[0]) / (jnp.sqrt(v_new * scale_ref[1]) + ADAM_EPS)
            live = index < length - i * step
            o_master[...] = jnp.where(live, p - rate[...] * (move + WEIGHT_DECAY * p), p)
            o_first[...] = jnp.where(live, m_new, m)
            o_second[...] = jnp.where(live, v_new, v)

    spec = pl.BlockSpec((step, 128), lambda i: (i, 0))
    shape = jax.ShapeDtypeStruct((held, 128), F32)
    return pl.pallas_call(
        body,
        grid=(pl.cdiv(held, step),),
        out_shape=[shape] * 3 + [jax.ShapeDtypeStruct((8, D + DE), F32)],
        in_specs=[SMEM] * 3 + [HBM] * (count + 1) + [spec] * 3,
        out_specs=[spec] * 3 + [pl.BlockSpec((8, D + DE), lambda i: (0, 0))],
        scratch_shapes=[
            pltpu.VMEM((2, total_rows, 128), BF),
            pltpu.VMEM((step + 16, 128), F32),
            pltpu.VMEM((step, 128), F32),
            pltpu.VMEM((step, 128), F32),
            pltpu.SemaphoreType.DMA((arrivals, ways)),
            pltpu.SemaphoreType.DMA(()),
        ],
        compiler_params=compiler_params(),
        cost_estimate=cost(10),
    )(owner, segment_rows, scales, whole_upper, *[b[0] for b in blocks], master, first, second)


RATES = [
    (ROW_O, 0.5 * D ** (-0.5)),
    (ROW_UP, 2.0 * D ** (-0.5)),
    (ROW_DOWN, 0.5 * D ** (-0.5)),
    (ROW_BIAS, 0.5 * FF ** (-0.5)),
    (ROW_EDGE, 0.5 * DE ** (-0.5)),
    (ROW_EUP, 0.5 * H ** (-0.5)),
    (ROW_EDOWN, 0.5 * DE ** (-0.5)),
    (ROW_NN, 0.5 * FFE ** (-0.5)),
]


class Cube:
    def __init__(self, size):
        self.size = size
        self.bits = size.bit_length() - 1
        assert size == 1 << self.bits
        up = list(range(1, self.bits))
        self.order = (up, up[::-1])

    def pairs(self, step):
        return [(i, i ^ (1 << self.order[i & 1][step])) for i in range(self.size)]

    def core_pairs(self):
        return [(i, i ^ 1) for i in range(self.size)]

    def source(self, me, key):
        other, used = key
        even, odd = [sum(1 << self.order[c][s] for s in used) for c in (0, 1)]
        if other:
            even, odd = odd, even
        return me ^ jnp.where(me & 1 == 0, even, odd) ^ other

    def gather(self, value, meanwhile):
        steps = range(self.bits - 1)
        new, done, also = [((), value)], [], None
        while new:
            sent = []
            for used, v in new:
                done.append(((0, used), v))
                for step in steps:
                    if not used or step > used[-1]:
                        sent.append((0, used + (step,), lax.ppermute(v, "dp", self.pairs(step))))
            for used, v in new:
                sent.append((1, used, lax.ppermute(v, "dp", self.core_pairs())))
            beside = None
            if also is None:
                also = meanwhile(lax.ppermute(value[:16], "dp", self.core_pairs()))
            else:
                beside = also
            moved, beside = lax.optimization_barrier(([v for _, _, v in sent], beside))
            also = also if beside is None else beside
            new = []
            for (other, used, _), v in zip(sent, moved):
                if other:
                    done.append(((1, used), v))
                else:
                    new.append((used, v))
        return done, also


def total(values):
    out = values[0].astype(F32)
    for v in values[1:]:
        out = out + v.astype(F32)
    return out.astype(BF)


def side_by_side(parts, sections, row_order):
    count, total_rows = len(parts), len(parts) * parts[0].shape[0]

    def body(*refs):
        srcs, dst, sems = refs[:count], refs[count], refs[count + 1]
        row = lax.axis_index("row")
        copies = []
        for k in range(count):
            inside = 0
            for number, size in enumerate(sections):
                if row_order:
                    to = aligned(count * inside + (row ^ k) * size, 16)
                else:
                    to = k * parts[0].shape[0] + inside
                copies.append(
                    pltpu.make_async_copy(
                        srcs[k].at[pl.ds(inside, size), :],
                        dst.at[pl.ds(to, size), :],
                        sems.at[k, number],
                    )
                )
                inside += size
        start(copies)
        wait(copies)

    return pl.pallas_call(
        body,
        out_shape=jax.ShapeDtypeStruct((total_rows, 128), BF),
        in_specs=[HBM] * count,
        out_specs=HBM,
        scratch_shapes=[pltpu.SemaphoreType.DMA((count, len(sections)))],
        compiler_params=pltpu.CompilerParams(vmem_limit_bytes=4 * 1024 * 1024),
        cost_estimate=cost(1),
    )(*parts)


class Chain:
    def __init__(self, cube, direct, *halves):
        self.cube, self.direct = cube, direct
        self.kept = [k for k, _ in halves]
        self.value = [s for _, s in halves]
        self.step, self.done = 0, False
        self.sides = lax.axis_size("dp") // 2
        self.rows = lax.axis_size("row")

    def swap(self, value):
        return lax.ppermute(value, "dp", [(i, i ^ 1) for i in range(2 * self.sides)])

    def to_chip(self, value, k):
        return lax.ppermute(value, "dp", [(i, i ^ (k << 1)) for i in range(2 * self.sides)])

    def to_row(self, value, k):
        return lax.ppermute(value, "row", [(i, i ^ k) for i in range(self.rows)])

    def scatter(self, index, count, send):
        def at(k):
            parts = [v.reshape(count, v.shape[0] // count, 128) for v in self.value]
            parts = [lax.dynamic_index_in_dim(v, index ^ k, 0, keepdims=False) for v in parts]
            return jnp.concatenate(parts) if len(parts) > 1 else parts[0]

        self.sizes = [v.shape[0] // count for v in self.value]
        self.kept = at(0)
        return [send(at(k), k) for k in range(1, count)]

    def join(self, other):
        assert self.step == other.step == 2
        self.value = self.value + other.value

    def launch(self):
        self.step += 1
        if self.step == 1:
            return [self.swap(v) for v in self.value]
        if self.step == 2:
            return self.scatter(lax.axis_index("dp") >> 1, self.sides, self.to_chip)
        if self.step == 3:
            return self.scatter(lax.axis_index("row"), self.rows, self.to_row)
        if self.step == 4:
            return [self.to_row(self.value, k) for k in range(1, self.rows)]
        if not self.spread():
            return [self.swap(self.value)]
        if self.direct:
            return [self.to_chip(self.value, k) for k in range(1, self.sides)]
        return [lax.ppermute(self.value, "dp", self.cube.pairs(self.step - 5))]

    def spread(self):
        return self.step < 6 if self.direct else self.step < 5 + self.cube.bits - 1

    def land(self, got):
        if self.step == 1:
            self.value = [total(pair) for pair in zip(self.kept, got)]
        elif self.step <= 3:
            value = total([self.kept, *got])
            if self.step == 3:
                self.value = value
            else:
                self.value, at = [], 0
                for size in self.sizes:
                    self.value.append(value[at : at + size])
                    at += size
        elif self.step == 4:
            self.value = side_by_side([self.value, *got], self.sizes, True)
        elif self.spread():
            self.value = side_by_side([self.value, *got], [self.value.shape[0]], False)
            if self.direct:
                self.keys = [(k << 1, k << 1) for k in range(self.sides)]
            else:
                bit = [1 << order[self.step - 5] for order in self.cube.order]
                keys = self.keys if self.step > 5 else [(0, 0)]
                self.keys = keys + [(a ^ bit[0], b ^ bit[1]) for a, b in keys]
        else:
            self.value, self.done = [self.value, *got], True

    def blocks(self, *names):
        sections = [(which, part, size) for (which, part), size in zip(names, self.sizes)]
        return [(v, core, self.keys, sections) for core, v in enumerate(self.value)]


def phase(chains, *ready):
    chains = [c for c in chains if not c.done]
    sent = [c.launch() for c in chains]
    got, ready = lax.optimization_barrier((sent, ready))
    for c, g in zip(chains, got):
        c.land(g)
    return ready


def per_device(
    small_nodes,
    small_edges,
    small_counts,
    big_nodes,
    big_edges,
    big_counts,
    small_node_cot,
    small_edge_cot,
    big_node_cot,
    big_edge_cot,
    master,
    first_moment,
    second_moment,
    owner,
    segment_rows,
    step_count,
):
    n_dp, n_row = lax.axis_size("dp"), lax.axis_size("row")
    cube = Cube(n_dp)
    share = big_nodes.shape[0] // n_row
    dm = Dims(small_nodes.shape[0], share, n_dp * n_row)

    def flat2(v):
        return v.reshape(-1, v.shape[-1])

    def packed(v, first, lanes):
        v = v[:, first : first + lanes].reshape(share, n_row, NB // n_row, lanes)
        return v.swapaxes(0, 1)

    def to_rows(v):
        v = lax.all_to_all(v, "row", split_axis=0, concat_axis=0, tiled=True)
        return v.reshape(n_row * share, NB // n_row, v.shape[-1])

    row = lax.axis_index("row")

    def row_pieces(v):
        v = v.reshape(share, n_row, NB // n_row, OUT_LANES)
        return [lax.dynamic_index_in_dim(v, row ^ k, 1, keepdims=False) for k in range(n_row)]

    def send_pieces(pieces):
        pairs = lambda k: [(i, i ^ k) for i in range(n_row)]
        return pieces[:1] + [lax.ppermute(pieces[k], "row", pairs(k)) for k in range(1, n_row)]

    def in_order(pieces, first, lanes):
        pieces = [p[..., first : first + lanes] for p in pieces]
        for k in range(n_row.bit_length() - 1):
            odd = (row >> k) & 1 == 1
            pieces = [jnp.where(odd, pieces[i ^ (1 << k)], p) for i, p in enumerate(pieces)]
        return jnp.concatenate(pieces)

    def to_whole(first):
        big = (big_edges, big_edge_cot, big_nodes, big_node_cot)
        _, big = lax.optimization_barrier((first, big))
        big = jnp.concatenate(big, axis=2)
        return flat2(lax.all_to_all(big, "row", split_axis=0, concat_axis=1, tiled=True))

    held, big = cube.gather(shifted_segment(owner, segment_rows, master), to_whole)
    one, two = assemble(cube, owner, segment_rows, [v for _, v in held], [k for k, _ in held])

    own_counts = lax.dynamic_slice_in_dim(big_counts, lax.axis_index("row") * share, share)
    counts = jnp.concatenate([small_counts, own_counts])

    mid_nodes, mid_edges, kept = first_forward(
        dm, counts, one, flat2(small_nodes), flat2(small_edges), big
    )
    sno, seo, bout, node_cot, edge_cot, kept_two, ffn_two = second_forward(
        dm, counts, two, mid_nodes, mid_edges, flat2(small_node_cot), flat2(small_edge_cot), big
    )
    spread = lax.psum_scatter(ffn_two.upper, "dp", scatter_dimension=0, tiled=True)
    got = between(dm, two, one, kept_two, kept, ffn_two, edge_cot)
    names = tuple(vars(got))
    values, out_pieces = phase([], take(got, names), send_pieces(row_pieces(bout)))
    got = Group(names, values)
    middle = Chain(cube, False, (got.keep, got.send))
    rest = second_last(dm, two, kept_two, got)
    spread, edge_grad, keep, send = phase([middle], spread, rest.edges_grad, rest.keep, rest.send)
    spread = lax.psum(spread, "row")
    lower_two = Chain(cube, False, (keep, send))
    names = tuple(edge_shapes(dm))
    edge_one = call_edges(dm, one, kept, got, edge_grad)
    edge_one = Group(names, phase([middle, lower_two], *take(edge_one, names)))
    names = tuple(attention_shapes(dm))
    att_one = Group(names, phase([lower_two], *take(call_attention(dm, kept, got, edge_one), names)))
    middle.join(lower_two)
    sng, seg, bgrad, keep, send = call_last(dm, one, kept, got, edge_one, att_one)
    spread, sng, seg, bgrad, keep, send = phase([middle], spread, sng, seg, bgrad, keep, send)
    upper_two = lax.all_gather(spread, "dp", axis=0, tiled=True)
    last = Chain(cube, True, (keep, send))
    sent = middle.launch()
    early = D + EDGE_LANES // 2
    bgrad, = phase([last], bgrad)
    one_part, two_part = packed(bgrad, 0, early), packed(bgrad, early, OUT_LANES - early)
    one_part = to_rows(one_part)
    sent, out_pieces = phase([last], sent, out_pieces)
    bno, beo = in_order(out_pieces, 0, D), in_order(out_pieces, D, EDGE_LANES)
    middle.land(sent)
    phase([last, middle])
    sent = middle.launch()
    one_part, upper_two, bno, beo = phase([last], one_part, upper_two, bno, beo)
    bng, head = one_part[..., :D], one_part[..., D:]
    sent, two_part, bng, head = phase([last], sent, two_part, bng, head)
    middle.land(sent)
    while not (last.done and middle.done):
        two_part, = phase([last, middle], two_part)
    two_part = to_rows(two_part)
    beg = jnp.concatenate([head, two_part], axis=-1)
    blocks = last.blocks((0, 0)) + middle.blocks((0, 1), (1, 0))
    step_value = step_count[0].astype(F32)
    scales = jnp.stack(
        [
            1.0 / (1.0 - jnp.power(F32(BETA_ONE), step_value)),
            1.0 / (1.0 - jnp.power(F32(BETA_TWO), step_value)),
        ]
    )
    new_master, new_first, new_second, norm_grads = adam(
        n_row, dm.lower, owner, segment_rows, scales, upper_two, blocks, master, first_moment, second_moment
    )
    return (
        sno.reshape(small_nodes.shape),
        seo.reshape(small_edges.shape),
        bno,
        beo,
        sng.reshape(small_nodes.shape),
        seg.reshape(small_edges.shape),
        bng,
        beg,
        new_master,
        new_first,
        new_second,
        norm_grads,
    )


def solution(mesh):
    both = P(("dp", "row"), None, None)
    rows = P("dp", "row", None)
    held = P("dp", None)
    in_specs = (
        both, both, P(("dp", "row")), rows, rows, P("dp"), both, both, rows, rows,
        held, held, held, P(), P(), P(),
    )
    out_specs = (both, both, rows, rows, both, both, rows, rows, held, held, held, P())
    return jax.shard_map(
        per_device, mesh=mesh, in_specs=in_specs, out_specs=out_specs, check_vma=False
    )
```

```python
import functools

import jax
import jax.numpy as jnp
from jax import lax
from jax.experimental import pallas as pl
from jax.experimental.pallas import tpu as pltpu
from jax.sharding import PartitionSpec as P

D = 512
H = 32
DE = 64
FF = 1024
FFE = 128
NS = 32
NB = 64
SET_ROWS = 16578
TOTAL_ROWS = 33156
NORM_EPS = 1e-05
BETA_ONE = 0.9
BETA_TWO = 0.95
WEIGHT_DECAY = 0.1
ADAM_EPS = 1e-08
MASK_FILL = -1e30
BF = jnp.bfloat16
F32 = jnp.float32
VMEM_LIMIT = 58 * 1024 * 1024
ROW_QKV, ROW_O, ROW_UP, ROW_DOWN = 0, 6144, 8192, 12288
ROW_BIAS, ROW_GATE, ROW_EDGE, ROW_EUP, ROW_EDOWN = 16384, 16400, 16416, 16432, 16496
ROW_NN, ROW_EN = 16560, 16576
SMALL_USED, SMALL_ROWS = SET_ROWS - ROW_BIAS, 256
BIAS, GATE, EDGE, EUP, EDOWN = 0, 16, 32, 48, 112
NN, EN = ROW_NN - ROW_BIAS, ROW_EN - ROW_BIAS
UPPER_ROWS = ROW_BIAS - ROW_O
GELU_C = 0.7978845608028654
PAIRS = 4


def nn(a, b):
    return lax.dot_general(a, b, (((1,), (0,)), ((), ())), preferred_element_type=F32)


def nt(a, b):
    return lax.dot_general(a, b, (((1,), (1,)), ((), ())), preferred_element_type=F32)


def tn(a, b):
    return lax.dot_general(a, b, (((0,), (0,)), ((), ())), preferred_element_type=F32)


def iota(shape, axis):
    return lax.broadcasted_iota(jnp.int32, shape, axis)


def gelu_parts(u):
    u2 = u * u
    t = jnp.tanh(u * (GELU_C + (GELU_C * 0.044715) * u2))
    half = 0.5 + 0.5 * t
    value = u * half
    slope = half + value * (1.0 - t) * (GELU_C + (3.0 * GELU_C * 0.044715) * u2)
    return value, slope


def gelu_value(u):
    return u * (0.5 + 0.5 * jnp.tanh(u * (GELU_C + (GELU_C * 0.044715) * (u * u))))


def sigmoid(v):
    return 0.5 + 0.5 * jnp.tanh(0.5 * v)


def group_sum(v, first=16):
    while first < 128:
        v = v + pltpu.roll(v, first, 1)
        first *= 2
    return v


def group_max(v):
    for shift in (16, 32, 64):
        v = jnp.maximum(v, pltpu.roll(v, shift, 1))
    return v


def fold8(v):
    return jnp.sum(v.reshape(v.shape[0] // 8, 8, v.shape[1]), axis=0)


class Bucket:
    def __init__(self, graphs, slots, node0, edge0, count0):
        self.graphs, self.slots = graphs, slots
        self.node0, self.edge0, self.count0 = node0, edge0, count0
        self.rows = graphs * slots
        self.chunks = slots // 4
        self.pairs = slots // 8
        self.blocks = slots // 16
        self.edges = self.rows * self.chunks
        self.edge_lanes = slots * DE


class Dims:
    def __init__(self, small_graphs, big_graphs, parts):
        self.lower = round_up(ROW_O + SMALL_ROWS, 16 * parts)
        self.small = Bucket(small_graphs, NS, 0, 0, 0)
        self.big = Bucket(big_graphs, NB, self.small.rows, self.small.edges, small_graphs)
        self.buckets = (self.small, self.big)
        self.nodes = self.small.rows + self.big.rows
        self.edges = self.small.edges + self.big.edges
        self.scores = self.edges // 2
        self.blocks = sum(b.graphs * b.blocks for b in self.buckets)

    def each_pair(self, body):
        for bucket in self.buckets:
            two = 2 * PAIRS * bucket.rows

            @pl.loop(0, bucket.pairs // PAIRS, unroll=True)
            def _(i, bucket=bucket, two=two):
                body(
                    pl.ds(aligned(bucket.edge0 + i * two, 32), two),
                    pl.ds(aligned((bucket.edge0 + i * two) // 2, 16), two // 2),
                )


def beside(v):
    one = v.shape[0] // (2 * PAIRS)
    at = lambda c: v[c * one : (c + 1) * one]
    sides = [[at(2 * p + c) for p in range(PAIRS)] for c in range(2)]
    return jnp.concatenate([jnp.concatenate(s) for s in sides], axis=1)


def below(v):
    one = v.shape[0] // PAIRS
    at = lambda p, c: v[p * one : (p + 1) * one, 256 * c : 256 * (c + 1)]
    return jnp.concatenate([at(p, c) for p in range(PAIRS) for c in range(2)])


def make_masks(scr):
    make_mean(scr)
    make_heads(scr)


def make_mean(scr):
    shape = (256, 256)
    same = (iota(shape, 0) >> 6) == (iota(shape, 1) >> 6)
    scr.mean[...] = jnp.where(same, 1.0 / DE, 0.0).astype(BF)


def make_heads(scr):
    shape = (16, 256)
    scr.head[...] = jnp.where(iota(shape, 0) == (iota(shape, 1) >> 4), 1.0, 0.0)


def node_norm(v):
    centred = v - jnp.mean(v, axis=1, keepdims=True)
    r = lax.rsqrt(jnp.mean(centred * centred, axis=1, keepdims=True) + NORM_EPS)
    return centred * r, r


def node_norm_back(gdy, n, r):
    return r * (gdy - jnp.mean(gdy, axis=1, keepdims=True) - n * jnp.mean(gdy * n, axis=1, keepdims=True))


def aligned(value, by):
    return pl.multiple_of(value, by)


def block_of(bucket, t):
    g = t // bucket.blocks
    b = t % bucket.blocks
    rows = pl.ds(aligned(bucket.node0 + g * bucket.slots, 16), bucket.slots)
    keys = pl.ds(aligned(bucket.node0 + t * 16, 16), 16)
    pair_rows = [
        pl.ds(
            aligned(bucket.edge0 // 2 + (2 * b + c) * bucket.rows + g * bucket.slots, 16),
            bucket.slots,
        )
        for c in range(2)
    ]
    return rows, keys, pair_rows


def side(first, half):
    return slice(first + 256 * half, first + 256 * (half + 1))


def lanes(half):
    return slice(128 * half, 128 * (half + 1))


def expand(values, scr):
    spread = values.astype(F32)[:, None, :] * scr.head[...][None]
    return spread.reshape(256, 256).astype(BF)


def collect(values, scr):
    return jnp.sum(values.reshape(16, 16, 256) * scr.head[...][None], axis=1)


def joined(ref, pair_rows, half):
    return jnp.concatenate([ref[r, lanes(half)] for r in pair_rows], axis=1)


def forward(dm, counts, w, io, res, scr, ready):
    x = io.nodes[...].astype(F32)
    n, r = node_norm(x)
    res.node_n1[...] = n.astype(BF)
    res.node_r1[...] = jnp.broadcast_to(r, (dm.nodes, 128))
    hn = (n * w.nn[0:1, :] + w.nn[1:2, :]).astype(BF)
    res.qkv[...] = nn(hn, w.qkv[...]).astype(BF)
    ready("node_n1", "node_r1", "qkv")

    @dm.each_pair
    def _(rows, pair):
        x = io.edges[rows, :]
        centred = x.astype(F32) - nn(x, scr.mean[...])
        r = lax.rsqrt(nn((centred * centred).astype(BF), scr.mean[...]) + NORM_EPS)
        n = centred * r
        res.edge_n1[rows, :] = n.astype(BF)
        res.edge_r1[rows, :] = r.astype(BF)
        xn = (n * w.en[0:1, :] + w.en[1:2, :]).astype(BF)
        both = nn(beside(xn), w.eg[...])
        scr.scores[pair, :] = both[:, :256]
        res.gate[pair, :] = both[:, 256:]

    ready("edge_n1", "edge_r1", "gate")
    t0 = 0
    for bucket in dm.buckets:
        @pl.loop(0, bucket.graphs * bucket.blocks, unroll=True)
        def _(t, bucket=bucket, t0=t0):
            rows, keys, pair_rows = block_of(bucket, t)
            for half in range(2):
                kb = expand(res.qkv[keys, side(512, half)], scr)
                scr.vbig[t0 + t, half] = expand(res.qkv[keys, side(1024, half)], scr)
                s = nt(res.qkv[rows, side(0, half)], kb) * 0.25
                for c in range(2):
                    scr.scores[pair_rows[c], lanes(half)] += s[:, lanes(c)]

        @pl.loop(0, bucket.rows // 32, unroll=True)
        def _(i, bucket=bucket):
            count = counts[bucket.count0 + i * 32 // bucket.slots]
            lane_key = iota((32, 128), 1) >> 4
            row = [
                pl.ds(aligned(bucket.edge0 // 2 + c * bucket.rows + i * 32, 32), 32)
                for c in range(bucket.pairs)
            ]
            for half in range(2):
                at = lanes(half)
                top = jnp.full((32, 128), MASK_FILL, F32)
                for c in range(bucket.pairs):
                    s = scr.scores[row[c], at]
                    res.low[row[c], at] = s.astype(BF)
                    top = jnp.maximum(top, jnp.where(lane_key < count - 8 * c, s, MASK_FILL))
                top = group_max(top)
                sums = jnp.zeros((32, 128), F32)
                for c in range(bucket.pairs):
                    s = jnp.where(lane_key < count - 8 * c, scr.scores[row[c], at], MASK_FILL)
                    e = jnp.exp(s - top)
                    sums = sums + e
                    scr.scores[row[c], at] = e
                inv = 1.0 / group_sum(sums)
                for c in range(bucket.pairs):
                    p = scr.scores[row[c], at] * inv
                    res.prob[row[c], at] = p.astype(BF)
                    scr.attn[row[c], at] = (p * sigmoid(res.gate[row[c], at])).astype(BF)

        @pl.loop(0, bucket.graphs, unroll=True)
        def _(g, bucket=bucket, t0=t0):
            for half in range(2):
                sums = None
                for b in range(bucket.blocks):
                    t = g * bucket.blocks + b
                    rows, _, pair_rows = block_of(bucket, t)
                    part = nn(joined(scr.attn, pair_rows, half), scr.vbig[t0 + t, half])
                    sums = part if sums is None else sums + part
                res.mixed[rows, side(0, half)] = sums.astype(BF)

        t0 += bucket.graphs * bucket.blocks

    ready("low", "prob", "mixed")
    y = io.nodes[...].astype(F32) + nn(res.mixed[...], w.o[...])
    n, r = node_norm(y)
    res.node_n2[...] = n.astype(BF)
    res.node_r2[...] = jnp.broadcast_to(r, (dm.nodes, 128))
    z = (n * w.nn[2:3, :] + w.nn[3:4, :]).astype(BF)
    u = nn(z, w.up[...])
    res.node_u[...] = u
    ready("node_n2", "node_r2", "node_u")
    io.nodes_out[...] = (y + nn(gelu_value(u).astype(BF), w.down[...])).astype(BF)

    @dm.each_pair
    def _(rows, pair):
        m = io.edges[rows, :].astype(F32) + below(nn(res.low[pair, :], w.x[...]))
        high = m.astype(BF)
        rest = (m - high.astype(F32)).astype(BF)
        centred = m - nn(high, scr.mean[...]) - nn(rest, scr.mean[...])
        r = lax.rsqrt(nn((centred * centred).astype(BF), scr.mean[...]) + NORM_EPS)
        n = centred * r
        res.edge_n2[rows, :] = n.astype(BF)
        res.edge_r2[rows, :] = r.astype(BF)
        mn = (n * w.en[2:3, :] + w.en[3:4, :]).astype(BF)
        ua = nn(mn, w.a[...])
        io.edges_out[rows, :] = (m + nn(gelu_value(ua).astype(BF), w.b[...])).astype(BF)

    ready("edge_n2", "edge_r2")


def put_strided(flat, first, value, parts):
    for q in range(parts):
        flat[pl.ds(first + q, value.shape[0], stride=parts), :] = value[:, 128 * q : 128 * (q + 1)]


def back_ffn(dm, w, io, res, scr):
    flat = scr.upper
    gy = io.nodes_cot[...]
    act, slope = gelu_parts(res.node_u[...])
    du = (nt(gy, w.down[...]) * slope).astype(BF)
    put_strided(flat, ROW_DOWN - ROW_O, tn(act.astype(BF), gy), 4)
    n = res.node_n2[...].astype(F32)
    z = (n * w.nn[2:3, :] + w.nn[3:4, :]).astype(BF)
    put_strided(flat, ROW_UP - ROW_O, tn(z, du), 8)
    dz = nt(du, w.up[...])
    gain = jnp.sum(dz * n, axis=0, keepdims=True)
    bias = jnp.sum(dz, axis=0, keepdims=True)
    dy = gy.astype(F32) + node_norm_back(dz * w.nn[2:3, :], n, res.node_r2[:, 0:1])
    io.dy[...] = dy
    dyl = dy.astype(BF)
    put_strided(flat, 0, tn(res.mixed[...], dyl), 4)
    io.do[...] = nt(dyl, w.o[...]).astype(BF)
    for q in range(4):
        io.sums[q : q + 1, :] = gain[:, 128 * q : 128 * (q + 1)]
        io.sums[4 + q : 5 + q, :] = bias[:, 128 * q : 128 * (q + 1)]
    if hasattr(io, "upper"):
        io.upper[...] = flat[...].astype(BF)
    else:
        put_halves(flat, io.keep, io.send)


def put_halves(flat, keep, send):
    half = keep.shape[0]
    core = lax.axis_index("dp") & 1
    keep[...] = flat[pl.ds(aligned(core * half, 16), half), :].astype(BF)
    send[...] = flat[pl.ds(aligned((1 - core) * half, 16), half), :].astype(BF)


def stacked(v, width):
    return jnp.concatenate([v[:, i : i + width] for i in range(0, v.shape[1], width)])


def back_edges(dm, w, io, res, scr):
    io.small[NN + 8 : NN + 16, :] = io.sums[...]
    scr.gb[...] = jnp.zeros((256, 128), F32)
    scr.ga[...] = jnp.zeros((128, 256), F32)
    scr.gx[...] = jnp.zeros((256, 512), F32)
    scr.en[...] = jnp.zeros((2, 8, 256), F32)

    @dm.each_pair
    def _(rows, pair):
        gx = io.edges_cot[rows, :]
        n = res.edge_n2[rows, :].astype(F32)
        mn = (n * w.en[2:3, :] + w.en[3:4, :]).astype(BF)
        act, slope = gelu_parts(nn(mn, w.a[...]))
        dua = (nt(gx, w.b[...]) * slope).astype(BF)
        act = act.astype(BF)
        scr.gb[...] += tn(stacked(act, 256), stacked(gx, 128))
        scr.ga[...] += tn(stacked(mn, 128), stacked(dua, 256))
        dmn = nt(dua, w.a[...])
        scr.en[0] += fold8(dmn * n)
        scr.en[1] += fold8(dmn)
        gdy = dmn * w.en[2:3, :]
        m1 = nn(gdy.astype(BF), scr.mean[...])
        m2 = nn((gdy * n).astype(BF), scr.mean[...])
        dmid = gx.astype(F32) + res.edge_r2[rows, :].astype(F32) * (gdy - m1 - n * m2)
        dml = dmid.astype(BF)
        io.dmid[rows, :] = dml
        dml = beside(dml)
        scr.gx[...] += tn(res.low[pair, :], dml)
        io.scores[pair, :] = nt(dml, w.x[...])

    io.small[EUP : EUP + 64, :] = scr.ga[0:64, 0:128] + scr.ga[64:128, 128:256]
    sums = jnp.where(lane_group(128, 6) == 0, scr.gb[0:128, :], scr.gb[128:256, :])
    fold_halves(sums, scr.tmp, io.small, EDOWN)
    sides = []
    for half in range(2):
        sums = jnp.zeros((16, 128), F32)
        for k in range(8):
            at = 128 * half + 16 * k
            part = scr.gx[at : at + 16, 128 * (k // 2) : 128 * (k // 2 + 1)]
            sums = sums + jnp.where(lane_group(16, 6) == k % 2, part, 0.0)
        sides.append(sums)
    fold_halves(jnp.concatenate(sides), scr.tmp, io.small, EDGE)
    put_edge_norm(scr.en, io.small, EN + 1)
    io.small[SMALL_USED:, :] = jnp.zeros((SMALL_ROWS - SMALL_USED, 128), F32)


def back_attention(dm, io, res, scr):
    t0 = 0
    for bucket in dm.buckets:
        @pl.loop(0, bucket.graphs * bucket.blocks, unroll=True)
        def _(t, bucket=bucket, t0=t0):
            rows, keys, pair_rows = block_of(bucket, t)
            for half in range(2):
                scr.vbig[t0 + t, half] = expand(res.qkv[keys, side(512, half)], scr)
                vb = expand(res.qkv[keys, side(1024, half)], scr)
                da = nt(io.do[rows, side(0, half)], vb)
                for c in range(2):
                    scr.da[pair_rows[c], lanes(half)] = da[:, lanes(c)]

        @pl.loop(0, bucket.rows // 32, unroll=True)
        def _(i, bucket=bucket):
            row = [
                pl.ds(aligned(bucket.edge0 // 2 + c * bucket.rows + i * 32, 32), 32)
                for c in range(bucket.pairs)
            ]
            for half in range(2):
                at = lanes(half)
                sums = jnp.zeros((32, 128), F32)
                for c in range(bucket.pairs):
                    p = res.prob[row[c], at].astype(F32)
                    s = sigmoid(res.gate[row[c], at])
                    scr.attn[row[c], at] = (p * s).astype(BF)
                    pt = p * scr.da[row[c], at] * s
                    scr.da[row[c], at] = pt
                    sums = sums + pt
                    io.dsg[row[c], lanes(2 + half)] = (pt * (1.0 - s)).astype(BF)
                sums = group_sum(sums)
                for c in range(bucket.pairs):
                    p = res.prob[row[c], at].astype(F32)
                    ds = scr.da[row[c], at] - p * sums + io.scores[row[c], at]
                    io.dsg[row[c], at] = ds.astype(BF)

        @pl.loop(0, bucket.graphs, unroll=True)
        def _(g, bucket=bucket, t0=t0):
            for half in range(2):
                sums = None
                for b in range(bucket.blocks):
                    t = g * bucket.blocks + b
                    rows, keys, pair_rows = block_of(bucket, t)
                    ds = joined(io.dsg, pair_rows, half)
                    part = nn(ds, scr.vbig[t0 + t, half])
                    sums = part if sums is None else sums + part
                    gk = collect(tn(ds, res.qkv[rows, side(0, half)]), scr)
                    io.dqkv[keys, side(512, half)] = (gk * 0.25).astype(BF)
                    gv = tn(joined(scr.attn, pair_rows, half), io.do[rows, side(0, half)])
                    io.dqkv[keys, side(1024, half)] = collect(gv, scr).astype(BF)
                io.dqkv[rows, side(0, half)] = (sums * 0.25).astype(BF)

        t0 += bucket.graphs * bucket.blocks


def back_nodes(dm, w, io, res, scr):
    n = res.node_n1[...].astype(F32)
    dhn = nt(io.dqkv[...], w.qkv[...])
    gain = jnp.sum(dhn * n, axis=0, keepdims=True)
    bias = jnp.sum(dhn, axis=0, keepdims=True)
    for q in range(4):
        io.sums_one[q : q + 1, :] = gain[:, 128 * q : 128 * (q + 1)]
        io.sums_one[4 + q : 5 + q, :] = bias[:, 128 * q : 128 * (q + 1)]
    dx = io.dy[...] + node_norm_back(dhn * w.nn[0:1, :], n, res.node_r1[:, 0:1])
    io.nodes_grad[...] = dx.astype(BF)


def back_last(dm, w, io, res, scr):
    flat = scr.lower
    n = res.node_n1[...].astype(F32)
    hn = (n * w.nn[0:1, :] + w.nn[1:2, :]).astype(BF)
    for m in range(3):
        put_strided(flat, 2048 * m, tn(hn, io.dqkv[:, 512 * m : 512 * (m + 1)]), 4)
    small = flat.at[pl.ds(ROW_O, SMALL_ROWS), :]
    small[...] = io.small[...]
    small[NN : NN + 8, :] = io.sums_one[...]

    scr.geg[...] = jnp.zeros((512, 512), F32)
    scr.en[...] = jnp.zeros((2, 8, 256), F32)

    @dm.each_pair
    def _(rows, pair):
        dsg = io.dsg[pair, :]
        n = res.edge_n1[rows, :].astype(F32)
        xn = (n * w.en[0:1, :] + w.en[1:2, :]).astype(BF)
        scr.geg[...] += tn(beside(xn), dsg)
        dxn = below(nt(dsg, w.eg[...]))
        scr.en[0] += fold8(dxn * n)
        scr.en[1] += fold8(dxn)
        gdy = dxn * w.en[0:1, :]
        m1 = nn(gdy.astype(BF), scr.mean[...])
        m2 = nn((gdy * n).astype(BF), scr.mean[...])
        dx = io.dmid[rows, :].astype(F32) + res.edge_r1[rows, :].astype(F32) * (gdy - m1 - n * m2)
        io.edges_grad[rows, :] = dx.astype(BF)

    for which, first in ((0, BIAS), (1, GATE)):
        sides = []
        for half in range(2):
            sums = jnp.zeros((64, 128), F32)
            for k in range(8):
                part = scr.geg[64 * k : 64 * (k + 1), lanes(2 * which + half)]
                sums = sums + jnp.where(lane_group(64, 4) == k, part, 0.0)
            sides.append(group_sum(sums))
        scr.tmp[0:64, :] = jnp.where(lane_group(64, 4) % 2 == 0, sides[0], sides[1])
        rows = jnp.zeros((16, 128), F32)
        for b in range(4):
            rows = jnp.where(lane_group(16, 5) == b, scr.tmp[pl.ds(b, 16, stride=4), :], rows)
        small[first : first + 16, :] = rows
    put_edge_norm(scr.en, small, EN)
    end = ROW_O + SMALL_ROWS
    if dm.lower > end:
        flat[end:, :] = jnp.zeros((dm.lower - end, 128), F32)
    put_halves(flat, io.keep, io.send)


def lane_group(rows, bits):
    return iota((rows, 128), 1) >> bits


def fold_halves(sums, tmp, out, first):
    rows, half = sums.shape[0], sums.shape[0] // 2
    tmp[0:rows, :] = sums + pltpu.roll(sums, 64, 1)
    even = tmp[pl.ds(0, half, stride=2), :]
    odd = tmp[pl.ds(1, half, stride=2), :]
    out[first : first + half, :] = jnp.where(lane_group(half, 6) == 0, even, odd)


def put_edge_norm(sums, out, at):
    ones = []
    for t in range(2):
        both = jnp.sum(sums[t], axis=0, keepdims=True)
        one = both[:, :128] + both[:, 128:]
        ones.append(one + pltpu.roll(one, 64, 1))
    out[at : at + 1, :] = jnp.where(lane_group(1, 6) == 0, ones[0], ones[1])


def assemble_set(off, flat, tmp, w):
    def strided(first, rows, parts, out, lane0=0):
        for q in range(parts):
            out[:, lane0 + 128 * q : lane0 + 128 * (q + 1)] = flat[
                pl.ds(off + first + q, rows, stride=parts), :
            ].astype(BF)

    for m in range(3):
        strided(ROW_QKV + 2048 * m, 512, 4, w.qkv, 512 * m)
    strided(ROW_O, 512, 4, w.o)
    strided(ROW_UP, 512, 8, w.up)
    strided(ROW_DOWN, 1024, 4, w.down)
    w.eg[...] = jnp.zeros((512, 512), BF)
    w.x[...] = jnp.zeros((256, 512), BF)
    w.a[...] = jnp.zeros((256, 512), BF)
    w.b[...] = jnp.zeros((512, 256), BF)
    up = flat[pl.ds(off + ROW_EUP, 64), :].astype(BF)
    for k in range(4):
        w.a[64 * k : 64 * (k + 1), 128 * k : 128 * (k + 1)] = up

    def doubled(first, in_rows):
        v = flat[pl.ds(off + first, in_rows), :]
        other = pltpu.roll(v, 64, 1)
        low = lane_group(in_rows, 6) == 0
        tmp[pl.ds(0, in_rows, stride=2), :] = jnp.where(low, v, other)
        tmp[pl.ds(1, in_rows, stride=2), :] = jnp.where(low, other, v)
        return tmp[0 : 2 * in_rows, :]

    both = doubled(ROW_EDOWN, 64)
    for k in range(4):
        w.b[128 * k : 128 * (k + 1), 128 * (k // 2) : 128 * (k // 2 + 1)] = jnp.where(
            lane_group(128, 6) == k % 2, both, 0.0
        ).astype(BF)
    both = doubled(ROW_EDGE, 16)
    for half in range(2):
        for k in range(8):
            at = 128 * half + 16 * k
            w.x[at : at + 16, 128 * (k // 2) : 128 * (k // 2 + 1)] = jnp.where(
                lane_group(16, 6) == k % 2, both[16 * half : 16 * (half + 1)], 0.0
            ).astype(BF)
    for which, first in ((0, ROW_BIAS), (1, ROW_GATE)):
        v = flat[pl.ds(off + first, 16), :]
        for b in range(4):
            tmp[pl.ds(b, 16, stride=4), :] = group_sum(jnp.where(lane_group(16, 5) == b, v, 0.0), 32)
        both = tmp[0:64, :]
        even = lane_group(64, 4) % 2 == 0
        sides = (
            jnp.where(even, both, pltpu.roll(both, 16, 1)),
            jnp.where(even, pltpu.roll(both, 112, 1), both),
        )
        for half in range(2):
            for k in range(8):
                w.eg[64 * k : 64 * (k + 1), lanes(2 * which + half)] = jnp.where(
                    lane_group(64, 4) == k, sides[half], 0.0
                ).astype(BF)
    for t in range(4):
        for q in range(4):
            w.nn[t : t + 1, 128 * q : 128 * (q + 1)] = flat[pl.ds(off + ROW_NN + 4 * t + q, 1), :]
    for t in range(2):
        v = flat[pl.ds(off + ROW_EN + t, 1), :]
        other = pltpu.roll(v, 64, 1)
        gain = jnp.where(lane_group(1, 6) == 0, v, other)
        bias = jnp.where(lane_group(1, 6) == 0, other, v)
        for half in range(2):
            w.en[2 * t : 2 * t + 1, 128 * half : 128 * (half + 1)] = gain
            w.en[2 * t + 1 : 2 * t + 2, 128 * half : 128 * (half + 1)] = bias


class Group:
    def __init__(self, names, refs):
        for name, ref in zip(names, refs):
            setattr(self, name, ref)


WEIGHTS = {
    "qkv": ((D, 3 * D), BF),
    "o": ((D, D), BF),
    "up": ((D, FF), BF),
    "down": ((FF, D), BF),
    "eg": ((512, 512), BF),
    "x": ((256, 512), BF),
    "a": ((256, 512), BF),
    "b": ((512, 256), BF),
    "nn": ((4, D), F32),
    "en": ((4, 256), F32),
}


def residual_shapes(dm):
    return {
        "node_n1": ((dm.nodes, D), BF),
        "node_r1": ((dm.nodes, 128), F32),
        "qkv": ((dm.nodes, 3 * D), BF),
        "mixed": ((dm.nodes, D), BF),
        "node_n2": ((dm.nodes, D), BF),
        "node_r2": ((dm.nodes, 128), F32),
        "node_u": ((dm.nodes, FF), F32),
        "edge_n1": ((dm.edges, 256), BF),
        "edge_r1": ((dm.edges, 256), BF),
        "gate": ((dm.scores, 256), F32),
        "low": ((dm.scores, 256), BF),
        "prob": ((dm.scores, 256), BF),
        "edge_n2": ((dm.edges, 256), BF),
        "edge_r2": ((dm.edges, 256), BF),
    }


def mean_shapes():
    return {"mean": ((256, 256), BF)}


def head_shapes():
    return {"head": ((16, 256), F32)}


def mask_shapes():
    return {**mean_shapes(), **head_shapes()}


def forward_scratch(dm):
    return {
        "scores": ((dm.scores, 256), F32),
        "attn": ((dm.scores, 256), BF),
        "vbig": ((dm.blocks, 2, 256, 256), BF),
    }


def ffn_shapes(dm, halves):
    half = ((UPPER_ROWS // 2, 128), BF)
    grads = {"keep": half, "send": half} if halves else {"upper": ((UPPER_ROWS, 128), BF)}
    return {
        "dy": ((dm.nodes, D), F32),
        "do": ((dm.nodes, D), BF),
        "sums": ((8, 128), F32),
        **grads,
    }


def edge_shapes(dm):
    return {
        "dmid": ((dm.edges, 256), BF),
        "scores": ((dm.scores, 256), F32),
        "small": ((SMALL_ROWS, 128), F32),
    }


def attention_shapes(dm):
    return {"dsg": ((dm.scores, 512), BF), "dqkv": ((dm.nodes, 3 * D), BF)}


def ffn_scratch():
    return {"upper": ((UPPER_ROWS, 128), F32)}


def edge_scratch():
    return {
        "gb": ((256, 128), F32),
        "ga": ((128, 256), F32),
        "gx": ((256, 512), F32),
        "en": ((2, 8, 256), F32),
        "tmp": ((128, 128), F32),
    }


def attention_scratch(dm):
    return {
        "attn": ((dm.scores, 256), BF),
        "vbig": ((dm.blocks, 2, 256, 256), BF),
        "da": ((dm.scores, 256), F32),
    }


def last_scratch(dm):
    return {
        "geg": ((512, 512), F32),
        "en": ((2, 8, 256), F32),
        "tmp": ((128, 128), F32),
        "lower": ((dm.lower, 128), F32),
    }


def structs(shapes):
    return [jax.ShapeDtypeStruct(s, t) for s, t in shapes.values()]


def vmem(shapes):
    return [pltpu.VMEM(s, t) for s, t in shapes.values()]


def whole(n):
    return [pl.BlockSpec(memory_space=pltpu.VMEM)] * n


def split(refs, *groups):
    out, at = [], 0
    for names in groups:
        out.append(Group(names, refs[at : at + len(names)]))
        at += len(names)
    assert at == len(refs)
    return out


def edge_copies(dm, small, big, big_lane, stacked, sems, out):
    copies = []
    for bucket, ref, lane in ((dm.small, small, 0), (dm.big, big, big_lane)):
        for c in range(bucket.chunks):
            a = ref.at[:, pl.ds(lane + 256 * c, 256)]
            b = stacked.at[pl.ds(bucket.edge0 + c * bucket.rows, bucket.rows), :]
            src, dst = (b, a) if out else (a, b)
            copies.append(pltpu.make_async_copy(src, dst, sems.at[len(copies)]))
    return copies


def node_copies(dm, small, big, big_lane, nodes, sems, at, out):
    copies = []
    for bucket, ref in ((dm.small, small), (dm.big, big.at[:, pl.ds(big_lane, D)])):
        b = nodes.at[pl.ds(bucket.node0, bucket.rows), :]
        src, dst = (b, ref) if out else (ref, b)
        copies.append(pltpu.make_async_copy(src, dst, sems.at[at + len(copies)]))
    return copies


def copy_sems(dm):
    return pltpu.SemaphoreType.DMA((dm.small.chunks + dm.big.chunks + 2,))


def all_copies(dm, small_nodes, small_edges, big, edge_lane, node_lane, nodes, edges, sems, out):
    copies = edge_copies(dm, small_edges, big, edge_lane, edges, sems, out)
    return node_copies(dm, small_nodes, big, node_lane, nodes, sems, len(copies), out) + copies


def start(copies):
    for c in copies:
        c.start()


def wait(copies):
    for c in copies:
        c.wait()


HBM = pl.BlockSpec(memory_space=pl.ANY)
SMEM = pl.BlockSpec(memory_space=pltpu.SMEM)
EDGE_LANES = NB * DE
IN_LANES = 2 * EDGE_LANES + 2 * D
OUT_LANES = EDGE_LANES + D


def compiler_params():
    return pltpu.CompilerParams(vmem_limit_bytes=VMEM_LIMIT)


def cost(us):
    return pl.CostEstimate(flops=0, bytes_accessed=int(us * 3.4e6), transcendentals=0)


def take(group, names):
    return [getattr(group, k) for k in names]


NODE_BACK = ("node_n2", "node_r2", "node_u", "mixed")
EDGE_BACK = ("edge_n2", "edge_r2", "low")
ATTENTION_BACK = ("qkv", "prob", "gate")
LAST_BACK = ("node_n1", "node_r1", "edge_n1", "edge_r1")
W_NODE = ("o", "up", "down", "nn")
W_EDGE = ("x", "a", "b", "en")
W_LAST = ("qkv", "eg", "nn", "en")


def kernel(body, inputs, out, scr, us, counts=None, hbm_in=0, hbm_out=(), sems=()):
    smem = [] if counts is None else [counts]
    return Group(
        out,
        pl.pallas_call(
            body,
            out_shape=structs(out),
            in_specs=[SMEM] * len(smem) + whole(len(inputs) - hbm_in) + [HBM] * hbm_in,
            out_specs=[HBM if k in hbm_out else pl.BlockSpec(memory_space=pltpu.VMEM) for k in out],
            scratch_shapes=vmem(scr) + list(sems),
            compiler_params=compiler_params(),
            cost_estimate=cost(us),
        )(*smem, *inputs),
    )


class Leaving:
    def __init__(self, names, held, outs, sems):
        self.names, self.held, self.outs, self.sems = tuple(names), held, outs, sems
        self.copies = []

    def __call__(self, *names):
        for k in names:
            if k in self.names:
                sem = self.sems.at[len(self.copies)]
                self.copies.append(
                    pltpu.make_async_copy(getattr(self.held, k), getattr(self.outs, k), sem)
                )
                self.copies[-1].start()

    def wait(self):
        assert len(self.copies) == len(self.names)
        wait(self.copies)


def first_forward(dm, counts, weights, small_nodes, small_edges, big):
    res = residual_shapes(dm)
    out = {"nodes_out": ((dm.nodes, D), BF), "edges_out": ((dm.edges, 256), BF), **res}
    scr = {
        **mask_shapes(),
        **forward_scratch(dm),
        "nodes": ((dm.nodes, D), BF),
        "edges": ((dm.edges, 256), BF),
        **res,
    }

    def body(*refs):
        counts_ref, refs, sems, out_sems = refs[0], refs[1:-2], refs[-2], refs[-1]
        w, src, dst, s = split(refs, WEIGHTS, ("sn", "se", "big"), out, scr)
        copies = all_copies(
            dm, src.sn, src.se, src.big, 0, 2 * EDGE_LANES, s.nodes, s.edges, sems, False
        )
        start(copies)
        make_masks(s)
        io = Group(
            ("nodes", "edges", "nodes_out", "edges_out"),
            (s.nodes, s.edges, dst.nodes_out, dst.edges_out),
        )
        leaving = Leaving(res, s, dst, out_sems)
        wait(copies)
        forward(dm, counts_ref, w, io, s, s, leaving)
        leaving.wait()

    inputs = take(weights, WEIGHTS) + [small_nodes, small_edges, big]
    sems = [copy_sems(dm), pltpu.SemaphoreType.DMA((len(res),))]
    got = kernel(body, inputs, out, scr, 16, counts, 3, tuple(res), sems)
    return got.nodes_out, got.edges_out, got


def second_forward(dm, counts, weights, nodes, edges, small_node_cot, small_edge_cot, big):
    res, ffn = residual_shapes(dm), ffn_shapes(dm, False)
    whole_outs = {
        "sno": ((dm.small.rows, D), BF),
        "seo": ((dm.small.rows, dm.small.edge_lanes), BF),
        "bout": ((dm.big.rows, OUT_LANES), BF),
    }
    kept = {k: v for k, v in res.items() if k not in NODE_BACK}
    out = {**whole_outs, "edge_cot": ((dm.edges, 256), BF), **kept, **ffn}
    scr = {
        **mask_shapes(),
        **forward_scratch(dm),
        **ffn_scratch(),
        **res,
        "nodes_out": ((dm.nodes, D), BF),
        "edges_out": ((dm.edges, 256), BF),
        "node_cot": ((dm.nodes, D), BF),
    }

    def body(*refs):
        counts_ref, refs, in_sems, out_sems, res_sems = refs[0], refs[1:-3], *refs[-3:]
        w, src, dst, s = split(refs, WEIGHTS, ("nodes", "edges", "snc", "sec", "big"), out, scr)
        copies = all_copies(
            dm, src.snc, src.sec, src.big, EDGE_LANES, 2 * EDGE_LANES + D, s.node_cot, dst.edge_cot, in_sems, False
        )
        start(copies)
        make_masks(s)
        leaving = Leaving(kept, s, dst, res_sems)
        io = Group(
            ("nodes", "edges", "nodes_out", "edges_out"),
            (src.nodes, src.edges, s.nodes_out, s.edges_out),
        )
        forward(dm, counts_ref, w, io, s, s, leaving)
        outgoing = all_copies(
            dm, dst.sno, dst.seo, dst.bout, D, 0, s.nodes_out, s.edges_out, out_sems, True
        )
        start(outgoing)
        wait(copies)
        back_ffn(dm, w, Group(("nodes_cot", *ffn), (s.node_cot, *take(dst, ffn))), s, s)
        wait(outgoing)
        leaving.wait()

    inputs = take(weights, WEIGHTS) + [nodes, edges, small_node_cot, small_edge_cot, big]
    sems = [copy_sems(dm), copy_sems(dm), pltpu.SemaphoreType.DMA((len(kept),))]
    got = kernel(body, inputs, out, scr, 22, counts, 3, (*whole_outs, *kept), sems)
    return got.sno, got.seo, got.bout, None, got.edge_cot, got, got


def between(dm, weights_two, weights_one, kept_two, kept_one, ffn_two, edges_cot):
    ffn, edge, att = ffn_shapes(dm, True), edge_shapes(dm), attention_shapes(dm)
    handed = {"dmid": edge["dmid"], "small": edge["small"], **att, "sums_one": ((8, 128), F32)}
    out = {**{"two_" + k: v for k, v in handed.items()}, **ffn}
    scr = {
        **mask_shapes(),
        **edge_scratch(),
        **attention_scratch(dm),
        **ffn_scratch(),
        "scores": edge["scores"],
        "nodes_grad": ((dm.nodes, D), BF),
    }
    w_two = ("qkv", *W_EDGE, "nn")
    res_two = EDGE_BACK + ATTENTION_BACK + ("node_n1", "node_r1")

    def body(*refs):
        w, w_one, res, res_one, src, dst, s = split(
            refs, w_two, W_NODE, res_two, NODE_BACK, ("edges_cot", "sums", "do", "dy"), out, scr
        )
        make_masks(s)
        io = Group(
            ("edges_cot", "sums", "do", "dy", "scores", "nodes_grad", *handed),
            (src.edges_cot, src.sums, src.do, src.dy, s.scores, s.nodes_grad)
            + tuple(getattr(dst, "two_" + k) for k in handed),
        )
        back_edges(dm, w, io, res, s)
        back_attention(dm, io, res, s)
        back_nodes(dm, w, io, res, s)
        back_ffn(dm, w_one, Group(("nodes_cot", *ffn), (s.nodes_grad, *take(dst, ffn))), res_one, s)

    inputs = take(weights_two, w_two) + take(weights_one, W_NODE)
    inputs += take(kept_two, res_two) + take(kept_one, NODE_BACK)
    inputs += [edges_cot, ffn_two.sums, ffn_two.do, ffn_two.dy]
    return kernel(body, inputs, out, scr, 25)


def second_last(dm, weights, kept, got):
    half = {k: ((dm.lower // 2, 128), BF) for k in ("keep", "send")}
    out = {"edges_grad": ((dm.edges, 256), BF), **half}
    scr = {**mean_shapes(), **last_scratch(dm)}
    given = ("dmid", "small", "dsg", "dqkv", "sums_one")
    w_last = ("eg", "nn", "en")
    last_res = ("node_n1", "edge_n1", "edge_r1")

    def body(*refs):
        w, res, src, dst, s = split(refs, w_last, last_res, given, out, scr)
        make_mean(s)
        back_last(dm, w, Group((*given, *out), (*take(src, given), *take(dst, out))), res, s)

    inputs = take(weights, w_last) + take(kept, last_res)
    inputs += [getattr(got, "two_" + k) for k in given]
    return kernel(body, inputs, out, scr, 9)


def call_edges(dm, weights, kept, ffn, edges_cot):
    out, scr = edge_shapes(dm), {**mean_shapes(), **edge_scratch()}

    def body(*refs):
        w, res, src, dst, s = split(refs, W_EDGE, EDGE_BACK, ("edges_cot", "sums"), out, scr)
        make_mean(s)
        io = Group(("edges_cot", "sums", *out), (src.edges_cot, src.sums, *take(dst, out)))
        back_edges(dm, w, io, res, s)

    inputs = take(weights, W_EDGE) + take(kept, EDGE_BACK) + [edges_cot, ffn.sums]
    return kernel(body, inputs, out, scr, 16)


def call_attention(dm, kept, ffn, edge):
    out, scr = attention_shapes(dm), {**head_shapes(), **attention_scratch(dm)}

    def body(*refs):
        res, src, dst, s = split(refs, ATTENTION_BACK, ("do", "scores"), out, scr)
        make_heads(s)
        back_attention(dm, Group(("do", "scores", *out), (src.do, src.scores, *take(dst, out))), res, s)

    return kernel(body, take(kept, ATTENTION_BACK) + [ffn.do, edge.scores], out, scr, 14)


def call_last(dm, weights, kept, ffn, edge, att):
    half = {k: ((dm.lower // 2, 128), BF) for k in ("keep", "send")}
    outs = {
        "sng": ((dm.small.rows, D), BF),
        "seg": ((dm.small.rows, dm.small.edge_lanes), BF),
        "bgrad": ((dm.big.rows, OUT_LANES), BF),
    }
    out = {**outs, **half}
    scr = {
        **mean_shapes(),
        **last_scratch(dm),
        "nodes_grad": ((dm.nodes, D), BF),
        "edges_grad": ((dm.edges, 256), BF),
        "sums_one": ((8, 128), F32),
    }
    given = ("dy", "dmid", "small", "dsg", "dqkv")

    def body(*refs):
        refs, sems = refs[:-1], refs[-1]
        w, res, src, dst, s = split(refs, W_LAST, LAST_BACK, given, out, scr)
        make_mean(s)
        io = Group(
            (*given, "nodes_grad", "edges_grad", "keep", "send", "sums_one"),
            (*take(src, given), s.nodes_grad, s.edges_grad, dst.keep, dst.send, s.sums_one),
        )
        back_nodes(dm, w, io, res, s)
        back_last(dm, w, io, res, s)
        outgoing = all_copies(
            dm, dst.sng, dst.seg, dst.bgrad, D, 0, s.nodes_grad, s.edges_grad, sems, True
        )
        start(outgoing)
        wait(outgoing)

    inputs = take(weights, W_LAST) + take(kept, LAST_BACK)
    inputs += [ffn.dy, edge.dmid, edge.small, att.dsg, att.dqkv]
    got = kernel(body, inputs, out, scr, 13, hbm_out=tuple(outs), sems=[copy_sems(dm)])
    return take(got, out)


def round_up(value, by):
    return -(-value // by) * by


def segment_of(owner, rows, index, count):
    name = owner[index]
    first = jnp.int32(0)
    for t in range(count):
        first = first + jnp.where(t < name, rows[t], 0)
    return first, rows[name]


def shifted_segment(owner, segment_rows, master):
    held = master.shape[0]
    count = owner.shape[0]
    padded = round_up(held + 15, 16)
    step = round_up(-(-padded // 2), 16)

    def body(owner_ref, rows_ref, src, dst, window):
        i = pl.program_id(0)
        first, length = segment_of(owner_ref, rows_ref, lax.axis_index("dp"), count)
        shift = first % 16

        @pl.when(i == 0)
        def _():
            window[0:16, :] = jnp.zeros((16, 128), F32)

        window[16:, :] = src[...]
        moved = window[pl.ds(16 - shift, step), :]
        index = i * step - shift + iota((step, 128), 0)
        live = (index >= 0) & (index < length)
        dst[...] = jnp.where(live, moved, 0.0).astype(BF)
        window[0:16, :] = window[step : step + 16, :]

    return pl.pallas_call(
        body,
        grid=(pl.cdiv(padded, step),),
        out_shape=jax.ShapeDtypeStruct((padded, 128), BF),
        in_specs=[
            SMEM,
            SMEM,
            pl.BlockSpec((step, 128), lambda i: (jnp.minimum(i, (held - 1) // step), 0)),
        ],
        out_specs=pl.BlockSpec((step, 128), lambda i: (i, 0)),
        scratch_shapes=[pltpu.VMEM((step + 16, 128), F32)],
        compiler_params=compiler_params(),
    )(owner, segment_rows, master)


def assemble(cube, owner, segment_rows, parts, sources):
    count = len(parts)
    padded = parts[0].shape[0]
    bits = (padded // 16).bit_length()
    tiles = -(-TOTAL_ROWS // 16)
    set_tiles = -(-(SET_ROWS + 2) // 16)
    out = {**{"one_" + k: v for k, v in WEIGHTS.items()}, **{"two_" + k: v for k, v in WEIGHTS.items()}}

    def body(owner_ref, rows_ref, *refs):
        srcs, refs = refs[:count], refs[count:]
        dsts, (rows, flat, tmp, edge, sems, edge_sems) = refs[: len(out)], refs[len(out) :]
        me = lax.axis_index("dp")
        spans = []
        for i in range(count):
            first, length = segment_of(owner_ref, rows_ref, cube.source(me, sources[i]), count)
            spans.append((first // 16, (first + length - 1) // 16))

        def each(act):
            for i, (a, b) in enumerate(spans):
                inner = b - a - 1
                for bit in range(bits):
                    size = 16 << bit
                    if size > padded:
                        continue
                    done = (inner >> (bit + 1)) << (bit + 1)

                    @pl.when((inner > 0) & (((inner >> bit) & 1) == 1))
                    def _(i=i, a=a, done=done, size=size, bit=bit):
                        act(
                            pltpu.make_async_copy(
                                srcs[i].at[pl.ds(aligned(16 * (1 + done), 16), size), :],
                                rows.at[pl.ds(aligned(16 * (a + 1 + done), 16), size), :],
                                sems.at[i, bit],
                            )
                        )

                act(pltpu.make_async_copy(srcs[i].at[pl.ds(0, 16), :], edge.at[2 * i], edge_sems.at[2 * i]))
                act(
                    pltpu.make_async_copy(
                        srcs[i].at[pl.ds(aligned(16 * (b - a), 16), 16), :],
                        edge.at[2 * i + 1],
                        edge_sems.at[2 * i + 1],
                    )
                )

        each(lambda c: c.start())
        each(lambda c: c.wait())
        tile = lambda t: pl.ds(aligned(16 * t, 16), 16)
        for a, b in spans:
            rows[tile(a), :] = jnp.zeros((16, 128), BF)
            rows[tile(b), :] = jnp.zeros((16, 128), BF)
        for i, (a, b) in enumerate(spans):
            rows[tile(a), :] += edge[2 * i]

            @pl.when(b != a)
            def _(i=i, b=b):
                rows[tile(b), :] += edge[2 * i + 1]

        for which in range(2):
            base = which * (SET_ROWS // 16) * 16
            flat[...] = rows[pl.ds(base, 16 * set_tiles), :].astype(F32)
            w = Group(WEIGHTS, dsts[which * len(WEIGHTS) : (which + 1) * len(WEIGHTS)])
            assemble_set(which * (SET_ROWS % 16), flat, tmp, w)

    got = pl.pallas_call(
        body,
        out_shape=structs(out),
        in_specs=[SMEM] * 2 + [HBM] * count,
        out_specs=whole(len(out)),
        scratch_shapes=[
            pltpu.VMEM((16 * tiles, 128), BF),
            pltpu.VMEM((16 * set_tiles, 128), F32),
            pltpu.VMEM((128, 128), F32),
            pltpu.VMEM((2 * count, 16, 128), BF),
            pltpu.SemaphoreType.DMA((count, bits)),
            pltpu.SemaphoreType.DMA((2 * count,)),
        ],
        compiler_params=compiler_params(),
        cost_estimate=cost(10),
    )(owner, segment_rows, *parts)
    return Group(WEIGHTS, got[: len(WEIGHTS)]), Group(WEIGHTS, got[len(WEIGHTS) :])


def adam(n_row, lower, owner, segment_rows, scales, whole_upper, blocks, master, first, second):
    held = master.shape[0]
    step = 2080
    front = step + 16
    count = len(blocks)
    n_dp = owner.shape[0]
    set_rows = ROW_BIAS - ROW_O + lower
    total_rows = front + set_rows + step + 32
    ways = 3
    arrivals = sum(len(keys) for _, _, keys, _ in blocks)

    def body(owner_ref, rows_ref, scale_ref, *refs):
        upper, srcs, refs = refs[0], refs[1 : 1 + count], refs[1 + count :]
        master_ref, first_ref, second_ref, o_master, o_first, o_second, o_norms, rows, window, grad, rate, sems, upper_sem = refs
        i = pl.program_id(0)
        me, row = lax.axis_index("dp"), lax.axis_index("row")
        begin, length = segment_of(owner_ref, rows_ref, me, n_dp)

        @pl.when(i == 0)
        def _():
            def each(act):
                copy = pltpu.make_async_copy(
                    upper, rows.at[1, pl.ds(front + ROW_O, UPPER_ROWS), :], upper_sem
                )
                pl.when(begin + length > SET_ROWS + ROW_O)(functools.partial(act, copy))
                every = [
                    (k, core, key, n, sections)
                    for k, (_, core, keys, sections) in enumerate(blocks)
                    for n, key in enumerate(keys)
                ]
                for at_sem, (k, core, key, n, sections) in enumerate(every):
                    mine = (me ^ core) & 1
                    source = me ^ core ^ jnp.where(mine == 0, key[0], key[1])
                    offset = n * n_row * sum(size for _, _, size in sections)
                    place = (source & 1) * (n_dp // 2) + (source >> 1)
                    for number, (which, part, size) in enumerate(sections):
                        size = size * n_row
                        at = place * size
                        dest = at + ROW_O if part else jnp.where(at >= ROW_O, at - ROW_O + ROW_BIAS, at)
                        wanted = (dest + which * SET_ROWS < begin + length) & (
                            dest + size + which * SET_ROWS > begin
                        )
                        wanted = wanted | (dest + size > ROW_NN)

                        def move(frm, extent, to, way, k=k, which=which, at_sem=at_sem):
                            act(
                                pltpu.make_async_copy(
                                    srcs[k].at[pl.ds(frm, extent), :],
                                    rows.at[which, pl.ds(aligned(front + to, 16), extent), :],
                                    sems.at[at_sem, way],
                                )
                            )

                        cut = 0 if part else ROW_O % size
                        if cut:
                            split_here = (at < ROW_O) & (at + size > ROW_O)
                            wanted = wanted & jnp.logical_not(split_here)

                            @pl.when(split_here)
                            def _(move=move, offset=offset, size=size, at=at, cut=cut, number=number):
                                move(offset, cut, at, number)
                                move(offset + cut, size - cut, ROW_BIAS, 2)

                        pl.when(wanted)(functools.partial(move, offset, size, dest, number))
                        offset += size

            each(lambda c: c.start())
            each(lambda c: c.wait())
            for which in range(2):
                v = rows[which, front + ROW_NN : front + ROW_NN + 32, :].astype(F32)
                for t in range(4):
                    for q in range(4):
                        o_norms[4 * which + t : 4 * which + t + 1, 128 * q : 128 * (q + 1)] = v[
                            4 * t + q : 4 * t + q + 1, :
                        ]
                for t in range(2):
                    both = v[16 + t : 17 + t, :]
                    at = 4 * which + 2 * t
                    o_norms[at : at + 1, 512:576] = both[:, 0:64]
                    o_norms[at + 1 : at + 2, 512:576] = pltpu.roll(both, 64, 1)[:, 0:64]

        low = begin + i * step
        high = low + step
        some = i * step < length

        @pl.when(jnp.logical_not(some))
        def _():
            o_master[...] = master_ref[...]
            o_first[...] = first_ref[...]
            o_second[...] = second_ref[...]

        @pl.when(some)
        def _():
            def shifted(which):
                local = low - which * SET_ROWS + front
                shift = local % 16
                window[...] = rows[which, pl.ds(aligned(local - shift, 16), step + 16), :].astype(F32)
                return window[pl.ds(shift, step), :]

            index = iota((step, 128), 0)

            @pl.when(low < SET_ROWS)
            def _():
                grad[...] = shifted(0)

            @pl.when(low >= SET_ROWS)
            def _():
                grad[...] = shifted(1)

            @pl.when((low < SET_ROWS) & (high > SET_ROWS))
            def _():
                grad[...] = jnp.where(index + low >= SET_ROWS, shifted(1), grad[...])

            at = index + low
            at = jnp.where(at >= SET_ROWS, at - SET_ROWS, at)
            a, b, c = RATES[0][1], RATES[1][1], RATES[3][1]
            far = jnp.where(at < ROW_DOWN, a, c)
            rate[...] = jnp.where(at < ROW_O, a, jnp.where(at < ROW_UP, b, far))
            near = (low < SET_ROWS) & (high > ROW_BIAS)

            @pl.when(near | (high > SET_ROWS + ROW_BIAS))
            def _():
                value = jnp.full((step, 128), 0.25, F32)
                for end, one in reversed(RATES[4:]):
                    value = jnp.where(at < end, one, value)
                rate[...] = jnp.where(at < ROW_BIAS, rate[...], value)

            g = grad[...]
            p, m, v = master_ref[...], first_ref[...], second_ref[...]
            m_new = BETA_ONE * m + (1.0 - BETA_ONE) * g
            v_new = BETA_TWO * v + (1.0 - BETA_TWO) * g * g
            move = (m_new * scale_ref[0]) / (jnp.sqrt(v_new * scale_ref[1]) + ADAM_EPS)
            live = index < length - i * step
            o_master[...] = jnp.where(live, p - rate[...] * (move + WEIGHT_DECAY * p), p)
            o_first[...] = jnp.where(live, m_new, m)
            o_second[...] = jnp.where(live, v_new, v)

    spec = pl.BlockSpec((step, 128), lambda i: (i, 0))
    shape = jax.ShapeDtypeStruct((held, 128), F32)
    return pl.pallas_call(
        body,
        grid=(pl.cdiv(held, step),),
        out_shape=[shape] * 3 + [jax.ShapeDtypeStruct((8, D + DE), F32)],
        in_specs=[SMEM] * 3 + [HBM] * (count + 1) + [spec] * 3,
        out_specs=[spec] * 3 + [pl.BlockSpec((8, D + DE), lambda i: (0, 0))],
        scratch_shapes=[
            pltpu.VMEM((2, total_rows, 128), BF),
            pltpu.VMEM((step + 16, 128), F32),
            pltpu.VMEM((step, 128), F32),
            pltpu.VMEM((step, 128), F32),
            pltpu.SemaphoreType.DMA((arrivals, ways)),
            pltpu.SemaphoreType.DMA(()),
        ],
        compiler_params=compiler_params(),
        cost_estimate=cost(10),
    )(owner, segment_rows, scales, whole_upper, *[b[0] for b in blocks], master, first, second)


RATES = [
    (ROW_O, 0.5 * D ** (-0.5)),
    (ROW_UP, 2.0 * D ** (-0.5)),
    (ROW_DOWN, 0.5 * D ** (-0.5)),
    (ROW_BIAS, 0.5 * FF ** (-0.5)),
    (ROW_EDGE, 0.5 * DE ** (-0.5)),
    (ROW_EUP, 0.5 * H ** (-0.5)),
    (ROW_EDOWN, 0.5 * DE ** (-0.5)),
    (ROW_NN, 0.5 * FFE ** (-0.5)),
]


class Cube:
    def __init__(self, size):
        self.size = size
        self.bits = size.bit_length() - 1
        assert size == 1 << self.bits
        up = list(range(1, self.bits))
        self.order = (up, up[::-1])

    def pairs(self, step):
        return [(i, i ^ (1 << self.order[i & 1][step])) for i in range(self.size)]

    def core_pairs(self):
        return [(i, i ^ 1) for i in range(self.size)]

    def source(self, me, key):
        other, used = key
        even, odd = [sum(1 << self.order[c][s] for s in used) for c in (0, 1)]
        if other:
            even, odd = odd, even
        return me ^ jnp.where(me & 1 == 0, even, odd) ^ other

    def gather(self, value, meanwhile):
        steps = range(self.bits - 1)
        new, done, also = [((), value)], [], None
        while new:
            sent = []
            for used, v in new:
                done.append(((0, used), v))
                for step in steps:
                    if not used or step > used[-1]:
                        sent.append((0, used + (step,), lax.ppermute(v, "dp", self.pairs(step))))
            for used, v in new:
                sent.append((1, used, lax.ppermute(v, "dp", self.core_pairs())))
            beside = None
            if also is None:
                also = meanwhile(lax.ppermute(value[:16], "dp", self.core_pairs()))
            else:
                beside = also
            moved, beside = lax.optimization_barrier(([v for _, _, v in sent], beside))
            also = also if beside is None else beside
            new = []
            for (other, used, _), v in zip(sent, moved):
                if other:
                    done.append(((1, used), v))
                else:
                    new.append((used, v))
        return done, also


def total(values):
    out = values[0].astype(F32)
    for v in values[1:]:
        out = out + v.astype(F32)
    return out.astype(BF)


def side_by_side(parts, sections, row_order):
    count, total_rows = len(parts), len(parts) * parts[0].shape[0]

    def body(*refs):
        srcs, dst, sems = refs[:count], refs[count], refs[count + 1]
        row = lax.axis_index("row")
        copies = []
        for k in range(count):
            inside = 0
            for number, size in enumerate(sections):
                if row_order:
                    to = aligned(count * inside + (row ^ k) * size, 16)
                else:
                    to = k * parts[0].shape[0] + inside
                copies.append(
                    pltpu.make_async_copy(
                        srcs[k].at[pl.ds(inside, size), :],
                        dst.at[pl.ds(to, size), :],
                        sems.at[k, number],
                    )
                )
                inside += size
        start(copies)
        wait(copies)

    return pl.pallas_call(
        body,
        out_shape=jax.ShapeDtypeStruct((total_rows, 128), BF),
        in_specs=[HBM] * count,
        out_specs=HBM,
        scratch_shapes=[pltpu.SemaphoreType.DMA((count, len(sections)))],
        compiler_params=pltpu.CompilerParams(vmem_limit_bytes=4 * 1024 * 1024),
        cost_estimate=cost(1),
    )(*parts)


class Chain:
    def __init__(self, cube, direct, *halves):
        self.cube, self.direct = cube, direct
        self.kept = [k for k, _ in halves]
        self.value = [s for _, s in halves]
        self.step, self.done = 0, False
        self.sides = lax.axis_size("dp") // 2
        self.rows = lax.axis_size("row")

    def swap(self, value):
        return lax.ppermute(value, "dp", [(i, i ^ 1) for i in range(2 * self.sides)])

    def to_chip(self, value, k):
        return lax.ppermute(value, "dp", [(i, i ^ (k << 1)) for i in range(2 * self.sides)])

    def to_row(self, value, k):
        return lax.ppermute(value, "row", [(i, i ^ k) for i in range(self.rows)])

    def scatter(self, index, count, send):
        def at(k):
            parts = [v.reshape(count, v.shape[0] // count, 128) for v in self.value]
            parts = [lax.dynamic_index_in_dim(v, index ^ k, 0, keepdims=False) for v in parts]
            return jnp.concatenate(parts) if len(parts) > 1 else parts[0]

        self.sizes = [v.shape[0] // count for v in self.value]
        self.kept = at(0)
        return [send(at(k), k) for k in range(1, count)]

    def join(self, other):
        assert self.step == other.step == 2
        self.value = self.value + other.value

    def launch(self):
        self.step += 1
        if self.step == 1:
            return [self.swap(v) for v in self.value]
        if self.step == 2:
            return self.scatter(lax.axis_index("dp") >> 1, self.sides, self.to_chip)
        if self.step == 3:
            return self.scatter(lax.axis_index("row"), self.rows, self.to_row)
        if self.step == 4:
            return [self.to_row(self.value, k) for k in range(1, self.rows)]
        if not self.spread():
            return [self.swap(self.value)]
        if self.direct:
            return [self.to_chip(self.value, k) for k in range(1, self.sides)]
        return [lax.ppermute(self.value, "dp", self.cube.pairs(self.step - 5))]

    def spread(self):
        return self.step < 6 if self.direct else self.step < 5 + self.cube.bits - 1

    def land(self, got):
        if self.step == 1:
            self.value = [total(pair) for pair in zip(self.kept, got)]
        elif self.step <= 3:
            value = total([self.kept, *got])
            if self.step == 3:
                self.value = value
            else:
                self.value, at = [], 0
                for size in self.sizes:
                    self.value.append(value[at : at + size])
                    at += size
        elif self.step == 4:
            self.value = side_by_side([self.value, *got], self.sizes, True)
        elif self.spread():
            self.value = side_by_side([self.value, *got], [self.value.shape[0]], False)
            if self.direct:
                self.keys = [(k << 1, k << 1) for k in range(self.sides)]
            else:
                bit = [1 << order[self.step - 5] for order in self.cube.order]
                keys = self.keys if self.step > 5 else [(0, 0)]
                self.keys = keys + [(a ^ bit[0], b ^ bit[1]) for a, b in keys]
        else:
            self.value, self.done = [self.value, *got], True

    def blocks(self, *names):
        sections = [(which, part, size) for (which, part), size in zip(names, self.sizes)]
        return [(v, core, self.keys, sections) for core, v in enumerate(self.value)]


def phase(chains, *ready):
    chains = [c for c in chains if not c.done]
    sent = [c.launch() for c in chains]
    got, ready = lax.optimization_barrier((sent, ready))
    for c, g in zip(chains, got):
        c.land(g)
    return ready


def per_device(
    small_nodes,
    small_edges,
    small_counts,
    big_nodes,
    big_edges,
    big_counts,
    small_node_cot,
    small_edge_cot,
    big_node_cot,
    big_edge_cot,
    master,
    first_moment,
    second_moment,
    owner,
    segment_rows,
    step_count,
):
    n_dp, n_row = lax.axis_size("dp"), lax.axis_size("row")
    cube = Cube(n_dp)
    share = big_nodes.shape[0] // n_row
    dm = Dims(small_nodes.shape[0], share, n_dp * n_row)

    def flat2(v):
        return v.reshape(-1, v.shape[-1])

    def packed(v, first, lanes):
        v = v[:, first : first + lanes].reshape(share, n_row, NB // n_row, lanes)
        return v.swapaxes(0, 1)

    def to_rows(v):
        v = lax.all_to_all(v, "row", split_axis=0, concat_axis=0, tiled=True)
        return v.reshape(n_row * share, NB // n_row, v.shape[-1])

    row = lax.axis_index("row")

    def row_pieces(v):
        v = v.reshape(share, n_row, NB // n_row, OUT_LANES)
        return [lax.dynamic_index_in_dim(v, row ^ k, 1, keepdims=False) for k in range(n_row)]

    def send_pieces(pieces):
        pairs = lambda k: [(i, i ^ k) for i in range(n_row)]
        return pieces[:1] + [lax.ppermute(pieces[k], "row", pairs(k)) for k in range(1, n_row)]

    def in_order(pieces, first, lanes):
        pieces = [p[..., first : first + lanes] for p in pieces]
        for k in range(n_row.bit_length() - 1):
            odd = (row >> k) & 1 == 1
            pieces = [jnp.where(odd, pieces[i ^ (1 << k)], p) for i, p in enumerate(pieces)]
        return jnp.concatenate(pieces)

    def to_whole(first):
        big = (big_edges, big_edge_cot, big_nodes, big_node_cot)
        _, big = lax.optimization_barrier((first, big))
        big = jnp.concatenate(big, axis=2)
        return flat2(lax.all_to_all(big, "row", split_axis=0, concat_axis=1, tiled=True))

    held, big = cube.gather(shifted_segment(owner, segment_rows, master), to_whole)
    one, two = assemble(cube, owner, segment_rows, [v for _, v in held], [k for k, _ in held])

    own_counts = lax.dynamic_slice_in_dim(big_counts, lax.axis_index("row") * share, share)
    counts = jnp.concatenate([small_counts, own_counts])

    mid_nodes, mid_edges, kept = first_forward(
        dm, counts, one, flat2(small_nodes), flat2(small_edges), big
    )
    sno, seo, bout, node_cot, edge_cot, kept_two, ffn_two = second_forward(
        dm, counts, two, mid_nodes, mid_edges, flat2(small_node_cot), flat2(small_edge_cot), big
    )
    spread = lax.psum_scatter(ffn_two.upper, "dp", scatter_dimension=0, tiled=True)
    got = between(dm, two, one, kept_two, kept, ffn_two, edge_cot)
    names = tuple(vars(got))
    values, out_pieces = phase([], take(got, names), send_pieces(row_pieces(bout)))
    got = Group(names, values)
    middle = Chain(cube, False, (got.keep, got.send))
    rest = second_last(dm, two, kept_two, got)
    spread, edge_grad, keep, send = phase([middle], spread, rest.edges_grad, rest.keep, rest.send)
    spread = lax.psum(spread, "row")
    lower_two = Chain(cube, False, (keep, send))
    names = tuple(edge_shapes(dm))
    edge_one = call_edges(dm, one, kept, got, edge_grad)
    edge_one = Group(names, phase([middle, lower_two], *take(edge_one, names)))
    names = tuple(attention_shapes(dm))
    att_one = Group(names, phase([lower_two], *take(call_attention(dm, kept, got, edge_one), names)))
    middle.join(lower_two)
    sng, seg, bgrad, keep, send = call_last(dm, one, kept, got, edge_one, att_one)
    spread, sng, seg, bgrad, keep, send = phase([middle], spread, sng, seg, bgrad, keep, send)
    upper_two = lax.all_gather(spread, "dp", axis=0, tiled=True)
    last = Chain(cube, True, (keep, send))
    sent = middle.launch()
    early = D + 3 * EDGE_LANES // 8
    bgrad, = phase([last], bgrad)
    one_part, two_part = packed(bgrad, 0, early), packed(bgrad, early, OUT_LANES - early)
    one_part = to_rows(one_part)
    sent, out_pieces = phase([last], sent, out_pieces)
    bno, beo = in_order(out_pieces, 0, D), in_order(out_pieces, D, EDGE_LANES)
    middle.land(sent)
    phase([last, middle])
    sent = middle.launch()
    one_part, upper_two, bno, beo = phase([last], one_part, upper_two, bno, beo)
    bng, head = one_part[..., :D], one_part[..., D:]
    sent, two_part, bng, head = phase([last], sent, two_part, bng, head)
    middle.land(sent)
    while not (last.done and middle.done):
        two_part, = phase([last, middle], two_part)
    two_part = to_rows(two_part)
    beg = jnp.concatenate([head, two_part], axis=-1)
    blocks = last.blocks((0, 0)) + middle.blocks((0, 1), (1, 0))
    step_value = step_count[0].astype(F32)
    scales = jnp.stack(
        [
            1.0 / (1.0 - jnp.power(F32(BETA_ONE), step_value)),
            1.0 / (1.0 - jnp.power(F32(BETA_TWO), step_value)),
        ]
    )
    new_master, new_first, new_second, norm_grads = adam(
        n_row, dm.lower, owner, segment_rows, scales, upper_two, blocks, master, first_moment, second_moment
    )
    return (
        sno.reshape(small_nodes.shape),
        seo.reshape(small_edges.shape),
        bno,
        beo,
        sng.reshape(small_nodes.shape),
        seg.reshape(small_edges.shape),
        bng,
        beg,
        new_master,
        new_first,
        new_second,
        norm_grads,
    )


def solution(mesh):
    both = P(("dp", "row"), None, None)
    rows = P("dp", "row", None)
    held = P("dp", None)
    in_specs = (
        both, both, P(("dp", "row")), rows, rows, P("dp"), both, both, rows, rows,
        held, held, held, P(), P(), P(),
    )
    out_specs = (both, both, rows, rows, both, both, rows, rows, held, held, held, P())
    return jax.shard_map(
        per_device, mesh=mesh, in_specs=in_specs, out_specs=out_specs, check_vma=False
    )
```
